32 devices in a mesh: dp: 16 (over z, y, core), tensor: 2 (over x).
Axes of the slice: x: 2, y: 2, z: 4, core: 2. Of those that a mesh axis runs over, the one named last changes fastest.
Arguments:
- inputs: bfloat16 [2, 16384, 768], P(None, ('dp', 'tensor')), may hold values from -6 to 6
- segments: int32 [2, 16, 1024], P(None, 'dp'), may hold values from 0 to 15, never falling along the last dimension, each value on 1 to 512 neighbouring positions
- norm_attn: float32 [768], replicated, may hold values from 0.25 to 1.75
- norm_ffn: float32 [768], replicated, may hold values from 0.25 to 1.75
- w_query: bfloat16 [768, 768], P('dp', 'tensor'), may hold values from -0.02734375 to 0.02734375
- w_key: bfloat16 [768, 768], P('dp', 'tensor'), may hold values from -0.21875 to 0.21875
- w_value: bfloat16 [768, 768], P('dp', 'tensor'), may hold values from -0.21875 to 0.21875
- w_out: bfloat16 [768, 768], P('dp', 'tensor'), may hold values from -1.75 to 1.75
- w_in: bfloat16 [768, 3072], P('dp', 'tensor'), may hold values from -0.21875 to 0.21875
- w_back: bfloat16 [768, 3072], P('dp', 'tensor'), may hold values from -0.109375 to 0.109375
- rel_table: float32 [32, 12], P(None, 'tensor'), may hold values from -4 to 4
- cotangent: float32 [2, 16384, 768], P(None, ('dp', 'tensor')), may hold values from -6 to 6
Outputs:
- output: float32 [2, 16384, 768], P(None, ('dp', 'tensor'))
- input_grad: float32 [2, 16384, 768], P(None, ('dp', 'tensor'))
- grad_norm_attn: float32 [768], replicated
- grad_norm_ffn: float32 [768], replicated
- grad_w_query: float32 [768, 768], P('dp', 'tensor')
- grad_w_key: float32 [768, 768], P('dp', 'tensor')
- grad_w_value: float32 [768, 768], P('dp', 'tensor')
- grad_w_out: float32 [768, 768], P('dp', 'tensor')
- grad_w_in: float32 [768, 3072], P('dp', 'tensor')
- grad_w_back: float32 [768, 3072], P('dp', 'tensor')
- grad_rel_table: float32 [32, 12], P(None, 'tensor')
The draws below stay inside these ranges and needn't reach their ends.
Inputs may be any that keep to these rules, and one draw needn't show every extreme that they name: `segments`: within each sequence of 1024 tokens the segment numbers never fall, every segment has 1 to 512 tokens, and some segment has exactly 512.
All inputs are finite; a program needn't handle non-finite values.
Results may differ from the reference program's by a relative error of at most 0.014.
Values may be sent and summed in bfloat16 or wider, within the bound.
A program may use at most 384 MiB of HBM per device.

```python
import math
import jax
import jax.numpy as jnp
import numpy as np
from jax import lax

D = 768
H = 12
DH = 64
FF = 3072
NB = 32
LEN = 1024
MICRO = 2
SEQ_MB = 1
SEQS = 16
ROWS = 16384


def spiked(values, own_key, source, target, blocks, factor):
    def block_of(axis_at):
        return (jnp.arange(values.shape[axis_at]) // (values.shape[axis_at] // blocks)).reshape((-1,) + (1,) * (values.ndim - 1 - axis_at))

    near = jax.random.permutation(own_key, blocks)[block_of(target)]
    other_side = (block_of(target) + blocks // 2) % blocks
    return jnp.where((block_of(source) == near) | (block_of(source) == other_side), factor * values, values)


def block_scale(stream_key, extent, split, smallest, high):
    def one(dim, blocks):
        heights = jax.random.uniform(jax.random.fold_in(jax.random.fold_in(stream_key, 6), dim), (blocks,), jnp.float32, smallest / len(split), high / len(split))
        return jnp.repeat(jnp.exp(heights), extent[dim] // blocks).reshape((-1,) + (1,) * (len(extent) - dim - 1))

    gain = one(*split[0])
    for cut in split[1:]:
        gain = gain * one(*cut)
    return gain


def split_up(amount, total, limit, skew):
    weights = [(1 << 20) // math.isqrt(grade ** skew) + 1 for grade in range(2, amount + 1)]
    rest, given = total - limit - (amount - 1), [1] * (amount - 1)
    while rest > 0:
        movable = [i for i in range(amount - 1) if given[i] < limit]
        whole, left = sum([weights[i] for i in movable]), rest
        for i in movable:
            addition = min(limit - given[i], max(1, left * weights[i] // whole), rest)
            given[i] = given[i] + addition
            rest = rest - addition
    return np.array([limit] + given)


def uneven(stream_key, number_of, total, bound, lean):
    if number_of == 2:
        one = jax.random.randint(stream_key, (), max(1, total - bound), min(bound, total - 1) + 1)
        return jnp.stack([one, total - one])
    lengths = jnp.asarray(split_up(number_of, total, bound, lean), jnp.int32)
    twos = (number_of - 1) // 2
    donor, taker = lengths[1:1 + 2 * twos:2], lengths[2:2 + 2 * twos:2]
    margin = jnp.minimum(donor - 1, bound - taker)
    passed = jax.random.randint(jax.random.fold_in(stream_key, 1), (twos,), 0, 1 << 20) % (margin + 1)
    lengths = lengths.at[1:1 + 2 * twos:2].set(donor - passed).at[2:2 + 2 * twos:2].set(taker + passed)
    return lengths[jax.random.permutation(jax.random.fold_in(stream_key, 2), number_of)]


def bell_draw(key, shape, width, reach, pieces=(), held_as=jnp.bfloat16):
    values = jax.random.normal(key, shape, jnp.float32) * width
    if len(pieces) > 0:
        values = block_scale(key, shape, pieces, -0.22, 0.18) * values
    return jnp.clip(values, min=-reach, max=reach).astype(held_as)


def heavy_noise(own_key, extent, deviation, most, shards, heavy, kind=jnp.bfloat16):
    entries = deviation * jax.random.normal(own_key, extent, jnp.float32)
    if shards:
        entries = entries * block_scale(own_key, extent, shards, -0.22, 0.18)
    return jnp.clip(spiked(entries, jax.random.fold_in(own_key, 3), *heavy), -most, most).astype(kind)


def setup_inputs(seed: int = 0) -> dict:
    splits = jax.random.split(jax.random.key(seed), 13)
    return {
        "inputs": bell_draw(splits[0], (MICRO, ROWS, D), 1.0, 6.0, ((1, 32),)),
        "segments": jax.vmap(lambda own: jnp.searchsorted(jnp.cumsum(uneven(own, max(LEN // 64, 4), LEN, LEN // 2, 2)), jnp.arange(LEN), side="right"))(jax.random.split(splits[1], MICRO * SEQS)).reshape((MICRO, SEQS, LEN)).astype(jnp.int32),
        "norm_attn": jnp.clip(1.0 + 0.15 * jax.random.normal(splits[2], (D,), jnp.float32), 0.25, 1.75),
        "norm_ffn": jnp.clip(1.0 + 0.15 * jax.random.normal(splits[3], (D,), jnp.float32), 0.25, 1.75),
        "w_query": bell_draw(splits[4], (D, H * DH), (D * DH) ** -0.5, 0.02734375, ((0, 16), (1, 2))),
        "w_key": bell_draw(splits[5], (D, H * DH), D ** -0.5, 0.21875, ((0, 16), (1, 2))),
        "w_value": bell_draw(splits[6], (D, H * DH), D ** -0.5, 0.21875, ((0, 16), (1, 2))),
        "w_out": bell_draw(splits[7], (D, H * DH), (max(H * DH // 64, 2)) ** -0.5, 1.75, ((0, 16), (1, 2))),
        "w_in": bell_draw(splits[8], (D, FF), D ** -0.5, 0.21875, ((0, 16), (1, 2))),
        "w_back": bell_draw(splits[9], (D, FF), FF ** -0.5, 0.109375, ((0, 16), (1, 2))),
        "rel_table": bell_draw(splits[10], (NB, H), 1.0, 4.0, ((1, 2),), jnp.float32),
        "cotangent": heavy_noise(splits[11], (MICRO, ROWS, D), 1.0, 6.0, ((1, 32),), (1, 2, 32, 2.75), jnp.float32),
    }


HIGHEST = lax.Precision.HIGHEST
EPSILON = 1e-06
MASKED = -1000000000.0
THRESHOLDS = (12, 16, 23, 32, 46, 64, 91)

@jax.custom_vjp
def low(v):
    return lax.optimization_barrier(v.astype(jnp.bfloat16)).astype(jnp.float32)

@jax.custom_vjp
def low_back(v):
    return v

def low_keep(v):
    return (low(v), None)

def low_pass(kept, grad):
    return (grad,)

def back_keep(v):
    return (v, None)

def back_low(kept, grad):
    return (low(grad),)
low.defvjp(low_keep, low_pass)
low_back.defvjp(back_keep, back_low)

def smooth_act(values):
    return 0.5 * values * (1.0 + jnp.tanh(0.7978845608028654 * (values + 0.044715 * values * values * values)))

def bucket_ids(offsets):
    distance = jnp.abs(offsets).astype(jnp.int32)
    far_ids = jnp.full(distance.shape, 8, jnp.int32)
    for threshold in THRESHOLDS:
        far_ids = far_ids + (distance >= threshold).astype(jnp.int32)
    near_ids = jnp.where(distance < 8, distance, far_ids).astype(jnp.int32)
    side = jnp.where(offsets > 0, jnp.int32(16), jnp.int32(0)).astype(jnp.int32)
    return (side + near_ids).astype(jnp.int32)

def norm_rows(values):
    return values * lax.rsqrt(lax.optimization_barrier(jnp.mean(values * values, -1, keepdims=True)) + EPSILON)

def layer_block(params, rows_block, seg_block):
    gain_attn, gain_ffn, w_query, w_key, w_value, w_out, w_in, w_back, rel_table = params
    seq_count = rows_block.shape[0]
    shaped = (seq_count, LEN, H, DH)
    normed = low(norm_rows(rows_block) * gain_attn)
    queries = low_back(low(jnp.einsum('bld,de->ble', normed, w_query, precision=HIGHEST))).reshape(shaped)
    key_rows = low_back(low(jnp.einsum('bld,de->ble', normed, w_key, precision=HIGHEST))).reshape(shaped)
    value_rows = low_back(low(jnp.einsum('bld,de->ble', normed, w_value, precision=HIGHEST))).reshape(shaped)
    positions = jnp.arange(LEN, dtype=jnp.int32)
    offsets = (positions[None, :] - positions[:, None]).astype(jnp.int32)
    buckets = bucket_ids(offsets)
    onehot = (buckets[:, :, None] == jnp.arange(NB, dtype=jnp.int32)[None, None, :]).astype(rel_table.dtype)
    rel_bias = jnp.einsum('qkb,bh->hqk', onehot, rel_table, precision=HIGHEST)
    scores = jnp.einsum('bqhe,bkhe->bhqk', queries, key_rows, precision=HIGHEST) + rel_bias[None]
    scores = low_back(scores)
    same_doc = seg_block[:, :, None] == seg_block[:, None, :]
    scores = jnp.where(same_doc[:, None], scores, jnp.asarray(MASKED, scores.dtype))
    attn_probs = jax.nn.softmax(scores, axis=-1)
    context = jnp.einsum('bhqk,bkhe->bqhe', low(attn_probs), value_rows, precision=HIGHEST)
    context = low_back(low(context.reshape(seq_count, LEN, H * DH)))
    attended = low_back(jnp.einsum('ble,de->bld', context, w_out, precision=HIGHEST))
    middle = rows_block + attended
    normed_ffn = low(norm_rows(middle) * gain_ffn)
    pre_act = low_back(jnp.einsum('bld,df->blf', normed_ffn, w_in, precision=HIGHEST))
    hidden = low(smooth_act(pre_act))
    ffn_out = low_back(jnp.einsum('blf,df->bld', hidden, w_back, precision=HIGHEST))
    return middle + ffn_out

def reference(inputs, segments, norm_attn, norm_ffn, w_query, w_key, w_value, w_out, w_in, w_back, rel_table, cotangent):
    groups = MICRO * SEQS // SEQ_MB
    rows_all = inputs.astype(jnp.float32).reshape(groups, SEQ_MB, LEN, D)
    seg_all = segments.astype(jnp.int32).reshape(groups, SEQ_MB, LEN)
    params = tuple((weight.astype(jnp.float32) for weight in (norm_attn, norm_ffn, w_query, w_key, w_value, w_out, w_in, w_back, rel_table)))

    def forward(params, rows_all):

        def one_group(packed):
            return jax.checkpoint(layer_block)(params, packed[0], packed[1])
        return lax.map(one_group, (rows_all, seg_all))
    result, pullback = jax.vjp(forward, params, rows_all)
    cot_all = cotangent.astype(jnp.float32).reshape(groups, SEQ_MB, LEN, D).astype(result.dtype)
    param_grads, input_grad = pullback(cot_all)
    shape_out = (MICRO, SEQS * LEN, D)
    return (result.reshape(shape_out), input_grad.reshape(shape_out), param_grads[0], param_grads[1], param_grads[2], param_grads[3], param_grads[4], param_grads[5], param_grads[6], param_grads[7], param_grads[8])
```

```python
import functools

import jax
import jax.numpy as jnp
from jax import lax
from jax.experimental import pallas as pl
from jax.experimental.pallas import tpu as pltpu
from jax.sharding import PartitionSpec as P

MESH = pl.DeviceIdType.MESH
BF = jnp.bfloat16
F32 = jnp.float32
HIGHEST = lax.Precision.HIGHEST
EPSILON = 1e-06
THRESHOLDS = (12, 16, 23, 32, 46, 64, 91)
MASK_OUT = -float(2**30)
DH = 64
SPAN = 512
LANES = 128
VMEM_BYTES = 62 * 2**20


def nn(left, right):
    return lax.dot_general(left, right, (((1,), (0,)), ((), ())), preferred_element_type=F32)


def nt(left, right):
    return lax.dot_general(left, right, (((1,), (1,)), ((), ())), preferred_element_type=F32)


def tn(left, right):
    return lax.dot_general(left, right, (((0,), (0,)), ((), ())), preferred_element_type=F32)


def iota(shape, dim):
    return lax.broadcasted_iota(jnp.int32, shape, dim)


def bucket_ids(offsets):
    distance = jnp.abs(offsets)
    far_ids = 8 + sum((distance >= threshold).astype(jnp.int32) for threshold in THRESHOLDS)
    return jnp.where(offsets > 0, 16, 0) + jnp.where(distance < 8, distance, far_ids)


def rms_scale(values):
    return lax.rsqrt(jnp.mean(values * values, -1, keepdims=True) + EPSILON)


def rms_back(grad_normed, normed, scale, gain):
    scaled = grad_normed * gain
    return scale * (scaled - normed * jnp.mean(scaled * normed, -1, keepdims=True))


def gelu_pair(v):
    square = v * v
    half = 0.5 + 0.5 * jnp.tanh(v * (0.7978845608028654 + 0.035677408136300125 * square))
    slope = half + v * half * (1.0 - half) * (1.5957691216057308 + 0.2140644488178007 * square)
    return v * half, slope


class Place:
    def __init__(self, depth):
        d, t = lax.axis_index("dp"), lax.axis_index("tensor")
        self.t = t
        self.z, self.y, self.c = lax.div(d, 4), lax.rem(lax.div(d, 2), 2), lax.rem(d, 2)
        self.depth = depth
        self.sib = (d + 1 - 2 * self.c, t)
        self.ypeer = (d + 2 - 4 * self.y, t)
        self.xpeer = (d, 1 - t)
        rest = lax.rem(d, 4)
        self.zs = [lax.rem(self.z + step, depth) for step in range(1, depth)]
        self.zpeers = [(z * 4 + rest, t) for z in self.zs]

    def barrier(self):
        semaphore = pltpu.get_barrier_semaphore()
        peers = [self.sib, self.ypeer, self.xpeer] + self.zpeers
        for peer in peers:
            pl.semaphore_signal(semaphore, inc=1, device_id=peer, device_id_type=MESH)
        pl.semaphore_wait(semaphore, len(peers))


class Copy:
    def __init__(self, **parts):
        self.parts = parts

    def made(self):
        return pltpu.make_async_remote_copy(device_id_type=MESH, **self.parts)

    def start(self):
        self.made().start()

    def wait_recv(self):
        self.made().wait_recv()

    def wait_send(self):
        self.made().wait_send()


def remote(src, dst, sems, index, peer):
    send, recv = sems
    return Copy(
        src_ref=src, dst_ref=dst, send_sem=send.at[index], recv_sem=recv.at[index], device_id=peer
    )


class Gather:
    def __init__(self, place, ref, width, sems, item, x_first):
        self.p, self.ref, self.width, self.sems, self.item = place, ref, width, sems, item
        self.x_first = x_first
        self.first, self.second = (
            (place.xpeer, place.ypeer) if x_first else (place.ypeer, place.xpeer)
        )

    def cols(self, x):
        return pl.ds(pl.multiple_of(x * self.width, LANES), self.width)

    def region(self, y, x):
        return self.ref.at[:, y, self.p.c, :, self.cols(x)]

    def send(self, index, src, peer):
        return remote(src, src, self.sems, (self.item, index), peer)

    def copies(self):
        p = self.p
        own = self.ref.at[p.z, p.y, p.c, :, self.cols(p.t)]
        regions = [self.region(p.y, p.t)]
        regions.append(self.region(p.y, 1 - p.t) if self.x_first else self.region(1 - p.y, p.t))
        regions.append(self.region(1 - p.y, p.t) if self.x_first else self.region(p.y, 1 - p.t))
        regions.append(self.region(1 - p.y, 1 - p.t))
        n = len(p.zpeers)
        zs = [self.send(i, own, peer) for i, peer in enumerate(p.zpeers)]
        first = self.send(n, regions[0], self.first)
        seconds = [self.send(n + 1 + i, regions[i], self.second) for i in range(2)]
        sibs = [self.send(n + 3 + i, regions[i], p.sib) for i in range(4)]
        return zs, first, seconds, sibs

    def start(self):
        for copy in self.copies()[0]:
            copy.start()

    def step1(self):
        zs, first, seconds, sibs = self.copies()
        for copy in zs:
            copy.wait_recv()
        first.start()
        seconds[0].start()
        sibs[0].start()

    def step2(self):
        _, first, seconds, sibs = self.copies()
        first.wait_recv()
        seconds[1].start()
        sibs[1].start()

    def step3(self):
        _, _, seconds, sibs = self.copies()
        seconds[0].wait_recv()
        sibs[2].start()
        seconds[1].wait_recv()
        sibs[3].start()

    def finish(self):
        zs, first, seconds, sibs = self.copies()
        for copy in sibs:
            copy.wait_recv()
        for copy in zs + [first] + seconds + sibs:
            copy.wait_send()


def gather_sems(items, depth):
    return [pltpu.SemaphoreType.DMA((items, depth + 6))] * 2


class Scatter:
    def __init__(self, place, ref, width, bufs, sems, item, y_first):
        self.p, self.ref, self.width, self.sems, self.item = place, ref, width, sems, item
        self.r0, self.r1, self.r2, self.r3 = bufs
        self.y_first = y_first

    def cols(self, x):
        return pl.ds(pl.multiple_of(x * self.width, LANES), self.width)

    def copies(self):
        p, ref = self.p, self.ref
        sib = remote(ref.at[:, :, 1 - p.c], self.r0, self.sems, (self.item, 0), p.sib)
        if self.y_first:
            half = remote(ref.at[:, 1 - p.y, p.c], self.r1, self.sems, (self.item, 1), p.ypeer)
            quarter = remote(
                ref.at[:, p.y, p.c, :, self.cols(1 - p.t)],
                self.r2,
                self.sems,
                (self.item, 2),
                p.xpeer,
            )
        else:
            half = remote(
                ref.at[:, :, p.c, :, self.cols(1 - p.t)],
                self.r1,
                self.sems,
                (self.item, 1),
                p.xpeer,
            )
            quarter = remote(
                ref.at[:, 1 - p.y, p.c, :, self.cols(p.t)],
                self.r2,
                self.sems,
                (self.item, 2),
                p.ypeer,
            )
        zs = [
            remote(
                ref.at[z, p.y, p.c, :, self.cols(p.t)],
                self.r3.at[i],
                self.sems,
                (self.item, 3 + i),
                peer,
            )
            for i, (z, peer) in enumerate(zip(p.zs, p.zpeers))
        ]
        return sib, half, quarter, zs

    def step0(self):
        self.copies()[0].start()

    def step1(self):
        p = self.p
        sib, half, _, _ = self.copies()
        sib.wait_recv()
        kept = self.ref.at[:, :, p.c]
        kept[...] = (kept[...].astype(F32) + self.r0[...].astype(F32)).astype(BF)
        half.start()

    def step2(self):
        p = self.p
        _, half, quarter, _ = self.copies()
        half.wait_recv()
        if self.y_first:
            kept = self.ref.at[:, p.y, p.c]
        else:
            kept = self.ref.at[:, :, p.c, :, self.cols(p.t)]
        kept[...] = (kept[...].astype(F32) + self.r1[...].astype(F32)).astype(BF)
        quarter.start()

    def step3(self):
        p = self.p
        _, _, quarter, zs = self.copies()
        quarter.wait_recv()
        kept = self.ref.at[:, p.y, p.c, :, self.cols(p.t)]
        kept[...] = (kept[...].astype(F32) + self.r2[...].astype(F32)).astype(BF)
        for copy in zs:
            copy.start()

    def finish(self, out, offset):
        p = self.p
        sib, half, quarter, zs = self.copies()
        for copy in zs:
            copy.wait_recv()
        total = self.ref[p.z, p.y, p.c, :, self.cols(p.t)].astype(F32)
        for i in range(len(zs)):
            total = total + self.r3[i].astype(F32)
        out[:, pl.ds(pl.multiple_of(offset, LANES), self.width)] = total
        for copy in [sib, half, quarter] + zs:
            copy.wait_send()


def scatter_bufs(items, depth, rows, width, y_first):
    lead = () if items is None else (items,)
    return [
        pltpu.VMEM(lead + (depth, 2, rows, 2 * width), BF),
        pltpu.VMEM(lead + ((depth, rows, 2 * width) if y_first else (depth, 2, rows, width)), BF),
        pltpu.VMEM(lead + (depth, rows, width), BF),
        pltpu.VMEM(lead + (depth - 1, rows, width), BF),
    ]


def scatter_sems(items, depth):
    return [pltpu.SemaphoreType.DMA((items, depth + 2))] * 2


def flat(values):
    if len(values.shape) == 2:
        return values
    return values.reshape(-1, values.shape[-1])


def project_rows(x_rows, gain):
    rows = x_rows.astype(F32)
    return (rows * rms_scale(rows) * gain).astype(BF)


def project(low_ref, w_ref, out_ref):
    weight = flat(w_ref[...])
    half = low_ref.shape[0] // 2

    def one(i, carry):
        rows = pl.ds(pl.multiple_of(i * half, half), half)
        out_ref[rows, :] = nn(low_ref[rows, :], weight).astype(BF)
        return carry

    lax.fori_loop(0, 2, one, 0)


def k1_plain(x_ref, gain_ref, wq_ref, wk_ref, wv_ref, q_ref, k_ref, v_ref, low_ref):
    low_ref[...] = project_rows(x_ref[...], gain_ref[...])
    for weight, out in ((wq_ref, q_ref), (wk_ref, k_ref), (wv_ref, v_ref)):
        project(low_ref, weight, out)


def k1_fused(
    depth,
    x_ref,
    cot_ref,
    gain_ref,
    tab_ref,
    wq_shard,
    wk_shard,
    wv_shard,
    xs_ref,
    cots_ref,
    tabs_ref,
    q_ref,
    k_ref,
    v_ref,
    wq_ref,
    wk_ref,
    wv_ref,
    low_ref,
    g_send,
    g_recv,
    x_send,
    x_recv,
):
    p = Place(depth)
    half_rows = x_ref.shape[1]
    width = wq_shard.shape[1]
    weights = (wq_ref, wk_ref, wv_ref)
    items = [
        Gather(p, ref, width, (g_send, g_recv), i, i != 1) for i, ref in enumerate(weights)
    ]
    for item, shard in zip(items, (wq_shard, wk_shard, wv_shard)):
        item.ref[p.z, p.y, p.c, :, item.cols(p.t)] = shard[...]
    xs_ref[p.t] = x_ref[p.t]
    cots_ref[p.t] = cot_ref[p.t].astype(BF)
    cots_ref[1 - p.t] = cot_ref[1 - p.t].astype(BF)
    tabs_ref[p.t] = tab_ref[...]
    p.barrier()
    for item in items:
        item.start()
    sems = (x_send, x_recv)
    moves = [
        remote(x_ref.at[1 - p.t], xs_ref.at[p.t], sems, 0, p.xpeer),
        remote(tabs_ref.at[p.t], tabs_ref.at[p.t], sems, 1, p.xpeer),
    ]
    moves[0] = remote(x_ref.at[1 - p.t], xs_ref.at[p.t], sems, 0, p.xpeer)
    for move in moves:
        move.start()

    def rows_of(half):
        return pl.ds(pl.multiple_of(half * half_rows, half_rows), half_rows)

    for item in items:
        item.step1()
    low_ref[rows_of(p.t), :] = project_rows(x_ref[p.t], gain_ref[...])
    for item in items:
        item.step2()
    for item in items:
        item.step3()
    moves[0].wait_recv()
    low_ref[rows_of(1 - p.t), :] = project_rows(xs_ref[1 - p.t], gain_ref[...])
    for item, weight, out in zip(items, weights, (q_ref, k_ref, v_ref)):
        item.finish()
        project(low_ref, weight, out)
    moves[1].wait_recv()
    for move in moves:
        move.wait_send()


def bias_rows(tabs_ref, out_ref, flipped):
    offsets = iota((LANES, 4 * LANES), 1) - 2 * LANES
    onehot = (bucket_ids(-offsets if flipped else offsets) == iota((LANES, 4 * LANES), 0)).astype(F32)
    for half in range(2):
        out_ref[half * 8 : half * 8 + 8, :] = jnp.dot(
            tabs_ref[half], onehot, precision=HIGHEST, preferred_element_type=F32
        )


def head_row(pair, per_half):
    return 8 * lax.div(pair, per_half) + 2 * lax.rem(pair, per_half)


def bias_strip(row):
    spread = jnp.broadcast_to(row, (LANES, 4 * LANES))
    return pltpu.roll(spread, 3 * LANES, 1, stride=1, stride_axis=0)


def window(tile, rows, length):
    reach = -(-SPAN // rows)
    return max(0, (tile - reach) * rows), min(length, (tile + reach + 1) * rows)


def segment_lanes(seg_ref, pieces):
    onehot = seg_ref[...] == iota((seg_ref.shape[0], LANES), 1)
    inside = iota((seg_ref.shape[0], LANES), 1) < 16
    return onehot, inside


def pair_cols(pair):
    return pl.ds(pl.multiple_of(pair * LANES, LANES), LANES)


def spread3(value):
    top = value.astype(BF).astype(F32)
    mid = (value - top).astype(BF).astype(F32)
    return top, mid, value - top - mid


def fwd_kernel(
    q_ref, k_ref, v_ref, seg_ref, tabs_ref, ctx_ref, ctxf_ref, feat_ref, bias_ref, segq_ref, segk_ref
):
    length, width = q_ref.shape
    pairs = width // LANES
    per_half = pairs // 2
    tile = 256
    near = SPAN // LANES
    bias_rows(tabs_ref, bias_ref, False)
    onehot, inside = segment_lanes(seg_ref, 1)
    segq_ref[...] = jnp.where(onehot, MASK_OUT, 0.0).astype(BF)
    segk_ref[...] = jnp.where(onehot, 0.0, jnp.where(inside, 1.0, 0.0)).astype(BF)

    def one_pair(pair, carry):
        cols = pair_cols(pair)
        row = head_row(pair, per_half)
        lane = iota((tile, LANES), 1)
        low_half = lane < DH
        strips, fars = [], []
        for hh in range(2):
            line = bias_ref[pl.ds(row + hh, 1), :]
            strips.append(bias_strip(line))
            fars.append((line[:, 0:1], line[:, 4 * LANES - 1 : 4 * LANES]))
        for index in range(length // tile):
            rows = slice(index * tile, (index + 1) * tile)
            start, stop = window(index, tile, length)
            queries = q_ref[rows, cols]
            zero = jnp.zeros_like(queries)
            q_feat = segq_ref[rows, :]
            left = jnp.concatenate(
                [
                    jnp.concatenate([jnp.where(low_half, queries, zero), q_feat], 1),
                    jnp.concatenate([jnp.where(low_half, zero, queries), q_feat], 1),
                ],
                0,
            )
            right = jnp.concatenate([k_ref[start:stop, cols], segk_ref[start:stop, :]], 1)
            scores = nt(left, right)
            weights, peaks = [], []
            for hh in range(2):
                for part in range(tile // LANES):
                    at = hh * tile + part * LANES
                    q_block = index * (tile // LANES) + part
                    blocks = []
                    for k_block in range(start // LANES, stop // LANES):
                        delta = k_block - q_block
                        if abs(delta) > near:
                            blocks.append(None)
                            continue
                        col = k_block * LANES - start
                        block = scores[at : at + LANES, col : col + LANES]
                        if abs(delta) <= 1:
                            block = block + strips[hh][:, (delta + 1) * LANES : (delta + 2) * LANES]
                        else:
                            block = block + fars[hh][0 if delta < 0 else 1]
                        blocks.append(block)
                    real = [block for block in blocks if block is not None]
                    peak = functools.reduce(jnp.maximum, real)
                    peak = jnp.max(peak, -1, keepdims=True)
                    peaks.append(peak)
                    weights.append(
                        jnp.concatenate(
                            [
                                jnp.zeros((LANES, LANES), BF)
                                if block is None
                                else jnp.exp(block - peak).astype(BF)
                                for block in blocks
                            ],
                            1,
                        )
                    )
            values = v_ref[start:stop, cols]
            gathered = nn(
                jnp.concatenate(weights, 0), jnp.concatenate([values, jnp.ones_like(values)], 1)
            )
            normal = gathered[:, :LANES] / gathered[:, LANES:]
            context = jnp.where(low_half, normal[:tile], normal[tile:])
            ctx_ref[rows, cols] = context.astype(BF)
            ctxf_ref[rows, cols] = context
            logs = jnp.concatenate(peaks, 0) + jnp.log(gathered[:, LANES:])
            feature = q_feat.astype(F32)
            for hh in range(2):
                for i, piece in enumerate(spread3(logs[hh * tile : (hh + 1) * tile])):
                    feature = jnp.where(lane == 16 + 3 * hh + i, -piece, feature)
            feat_ref[pair, rows, :] = feature.astype(BF)
        return carry

    lax.fori_loop(0, pairs, one_pair, 0)


def bwd_kernel(
    q_ref,
    k_ref,
    v_ref,
    go_ref,
    ctxf_ref,
    feat_ref,
    seg_ref,
    tabs_ref,
    dq_ref,
    dk_ref,
    dv_ref,
    tabg_ref,
    bias_ref,
    sums_ref,
    far_ref,
    segk_ref,
    gofeat_ref,
    near_ref,
    acc_ref,
):
    length, width = q_ref.shape
    pairs = width // LANES
    per_half = pairs // 2
    tile = 256
    near = SPAN // LANES
    bias_rows(tabs_ref, bias_ref, True)
    sums_ref[...] = jnp.zeros_like(sums_ref)
    far_ref[...] = jnp.zeros_like(far_ref)
    onehot, inside = segment_lanes(seg_ref, 1)
    segk_ref[...] = jnp.where(onehot, 0.0, jnp.where(inside, 1.0, 0.0)).astype(BF)
    flip = (iota((LANES, LANES), 0) + iota((LANES, LANES), 1) == LANES - 1).astype(F32)
    block_of = (lax.div(iota((length, LANES), 0), LANES) == iota((length, LANES), 1)).astype(BF)

    def one_pair(pair, carry):
        cols = pair_cols(pair)
        row = head_row(pair, per_half)
        lane = iota((tile, LANES), 1)
        low_half = lane < DH
        strips, fars = [], []
        for hh in range(2):
            line = bias_ref[pl.ds(row + hh, 1), :]
            strips.append(bias_strip(line))
            fars.append((line[:, 0:1], line[:, 4 * LANES - 1 : 4 * LANES]))
        grads_all = go_ref[:, cols]
        product = grads_all.astype(F32) * ctxf_ref[:, cols]
        lane_all = iota((length, LANES), 1)
        feature = jnp.zeros((length, LANES), F32)
        for hh in range(2):
            keep = (lane_all < DH) if hh == 0 else (lane_all >= DH)
            total = jnp.sum(jnp.where(keep, product, 0.0), -1, keepdims=True)
            for i, piece in enumerate(spread3(total)):
                feature = jnp.where(lane_all == 3 * hh + i, -piece, feature)
        gofeat_ref[...] = feature.astype(BF)
        near_ref[...] = jnp.zeros_like(near_ref)
        acc_ref[...] = jnp.zeros_like(acc_ref)
        far_sums = [[jnp.zeros((1, LANES), F32) for _ in range(2)] for _ in range(2)]
        lane_row = iota((1, LANES), 1)
        for index in range(length // tile):
            rows = slice(index * tile, (index + 1) * tile)
            start, stop = window(index, tile, length)
            keys, values = k_ref[rows, cols], v_ref[rows, cols]
            zero = jnp.zeros_like(keys)
            seg_feat = segk_ref[rows, :].astype(F32)

            def ones_at(base, first):
                return jnp.where((lane >= first) & (lane < first + 3), 1.0, base).astype(BF)

            masked_keys = jnp.concatenate(
                [jnp.where(low_half, keys, zero), jnp.where(low_half, zero, keys)], 0
            )
            masked_values = jnp.concatenate(
                [jnp.where(low_half, values, zero), jnp.where(low_half, zero, values)], 0
            )
            key_feats = jnp.concatenate([ones_at(seg_feat, 16), ones_at(seg_feat, 19)], 0)
            value_feats = jnp.concatenate([ones_at(0.0, 0), ones_at(0.0, 3)], 0)
            queries = q_ref[start:stop, cols]
            grads = go_ref[start:stop, cols]
            logits = nt(
                jnp.concatenate([masked_keys, key_feats], 1),
                jnp.concatenate([queries, feat_ref[pair, start:stop, :]], 1),
            )
            shifted = nt(
                jnp.concatenate([masked_values, value_feats], 1),
                jnp.concatenate([grads, gofeat_ref[start:stop, :]], 1),
            )
            probs_rows, score_rows = [], []
            for hh in range(2):
                for part in range(tile // LANES):
                    at = hh * tile + part * LANES
                    k_block = index * (tile // LANES) + part
                    probs, score_grads = [], []
                    for q_block in range(start // LANES, stop // LANES):
                        delta = k_block - q_block
                        if abs(delta) > near:
                            probs.append(jnp.zeros((LANES, LANES), BF))
                            score_grads.append(jnp.zeros((LANES, LANES), BF))
                            continue
                        col = q_block * LANES - start
                        block = logits[at : at + LANES, col : col + LANES]
                        place = (1 - delta) * LANES
                        if abs(delta) <= 1:
                            block = block + strips[hh][:, place : place + LANES]
                        else:
                            block = block + fars[hh][0 if delta > 0 else 1]
                        prob = jnp.exp(block)
                        grad = prob * shifted[at : at + LANES, col : col + LANES]
                        if abs(delta) <= 1:
                            near_ref[hh, :, place : place + LANES] += grad
                        probs.append(prob.astype(BF))
                        score_grads.append(grad.astype(BF))
                    probs_rows.append(jnp.concatenate(probs, 1))
                    score_rows.append(jnp.concatenate(score_grads, 1))
            probs_all = jnp.concatenate(probs_rows, 0)
            scores_all = jnp.concatenate(score_rows, 0)
            value_grad = nn(probs_all, grads)
            dv_ref[rows, cols] = jnp.where(low_half, value_grad[:tile], value_grad[tile:]).astype(BF)
            key_grad = nn(scores_all, jnp.concatenate([queries, block_of[start:stop]], 1))
            dk_ref[rows, cols] = jnp.where(
                low_half, key_grad[:tile, :LANES], key_grad[tile:, :LANES]
            ).astype(BF)
            acc_ref[start:stop, :] += tn(scores_all, masked_keys)
            for hh in range(2):
                for part in range(tile // LANES):
                    at = hh * tile + part * LANES
                    k_block = index * (tile // LANES) + part
                    line = jnp.sum(key_grad[at : at + LANES, LANES:], 0, keepdims=True)
                    far_sums[hh][0] += jnp.where(lane_row <= k_block - 2, line, 0.0)
                    far_sums[hh][1] += jnp.where(lane_row >= k_block + 2, line, 0.0)
        dq_ref[:, cols] = acc_ref[...].astype(BF)
        for hh in range(2):
            turned = jnp.dot(flip, near_ref[hh], precision=HIGHEST, preferred_element_type=F32)
            turned = jnp.concatenate([turned, jnp.zeros((LANES, LANES), F32)], 1)
            turned = pltpu.roll(turned, 1, 1, stride=1, stride_axis=0)
            sums_ref[pl.ds(row + hh, 1), :] = jnp.sum(turned, 0, keepdims=True)
            last = lane_row == 0
            positive = jnp.sum(far_sums[hh][0], -1, keepdims=True)
            negative = jnp.sum(far_sums[hh][1], -1, keepdims=True)
            far_ref[pl.ds(row + hh, 1), :] = jnp.where(last, positive, jnp.where(lane_row == 1, negative, 0.0))
        return carry

    lax.fori_loop(0, pairs, one_pair, 0)
    offsets = 2 * LANES - iota((LANES, 4 * LANES), 1)
    onehot_buckets = (bucket_ids(offsets) == iota((LANES, 4 * LANES), 0)).astype(F32)
    table = lax.dot_general(
        sums_ref[...],
        onehot_buckets,
        (((1,), (1,)), ((), ())),
        precision=HIGHEST,
        preferred_element_type=F32,
    )
    lane = iota(tabg_ref.shape, 1)
    far = far_ref[...]
    table = table + jnp.where(lane == 31, far[:, 0:1], 0.0) + jnp.where(lane == 15, far[:, 1:2], 0.0)
    tabg_ref[...] = table


def k3_before(xs_ref, ctx_ref, wo, gain, middle_ref, ffn_ref, ffnt_ref):
    step = 256

    def one(i, carry):
        rows = pl.ds(pl.multiple_of(i * step, step), step)
        middle = xs_ref[rows, :].astype(F32) + nt(ctx_ref[rows, :], wo)
        middle_ref[rows, :] = middle
        low = (middle * rms_scale(middle) * gain).astype(BF)
        ffn_ref[rows, :] = low
        ffnt_ref[:, rows] = low.T
        return carry

    lax.fori_loop(0, middle_ref.shape[0] // step, one, 0)


def transpose_rows(src_ref, dst_ref):
    step = 256

    def one(i, carry):
        rows = pl.ds(pl.multiple_of(i * step, step), step)
        dst_ref[:, rows] = src_ref[rows, :].T
        return carry

    lax.fori_loop(0, src_ref.shape[0] // step, one, 0)


def ffn_rows(i, half, w_in, w_back, first, ffn_ref, cot_ref, hid_ref, gp_ref, up_ref, down_ref):
    rows = pl.ds(pl.multiple_of(i * half, half), half)
    hidden, slope = gelu_pair(nn(ffn_ref[rows, :], w_in))
    hidden = hidden.astype(BF)
    hid_ref[rows, :] = hidden
    grad_pre = (nn(cot_ref[rows, :], w_back) * slope).astype(BF)
    gp_ref[rows, :] = grad_pre
    up = nt(hidden, w_back)
    down = nt(grad_pre, w_in)
    keep = jnp.where(first, 0.0, 1.0).astype(F32)

    @pl.when(first)
    def _():
        up_ref[rows, :] = up
        down_ref[rows, :] = down

    @pl.when(jnp.logical_not(first))
    def _():
        up_ref[rows, :] += up
        down_ref[rows, :] += down


def after_rows(rows, cot, up_ref, down_ref, gain, gain_ref, gm_ref, ca_ref, cat_ref):
    middle = gm_ref[rows, :]
    scale = rms_scale(middle)
    normed = middle * scale
    down = down_ref[rows, :]
    gain_ref[...] += jnp.sum(down * normed, 0, keepdims=True)
    grad = cot + rms_back(down, normed, scale, gain)
    gm_ref[rows, :] = grad
    low = grad.astype(BF)
    ca_ref[rows, :] = low
    cat_ref[:, rows] = low.T
    return middle + up_ref[rows, :]


def context_grad(ca_ref, wo, go_ref):
    step = 256

    def one(i, carry):
        rows = pl.ds(pl.multiple_of(i * step, step), step)
        go_ref[rows, :] = nn(ca_ref[rows, :], wo).astype(BF)
        return carry

    lax.fori_loop(0, ca_ref.shape[0] // step, one, 0)


def k3_fused(
    depth,
    xs_ref,
    ctx_ref,
    cot_ref,
    cots_ref,
    gain_ref,
    wo_shard,
    wi_shard,
    wb_shard,
    out_ref,
    gm_ref,
    go_ref,
    ggain_ref,
    gwo_ref,
    gwi_ref,
    gwb_ref,
    wo_ref,
    wi_ref,
    wb_ref,
    ffn_ref,
    ffnt_ref,
    cott_ref,
    cotb_ref,
    hid_ref,
    gp_ref,
    up_ref,
    down_ref,
    obuf_ref,
    obuf2_ref,
    o0,
    o1,
    o2,
    o3,
    i0,
    i1,
    i2,
    i3,
    b0,
    b1,
    b2,
    b3,
    g_send,
    g_recv,
    s_send,
    s_recv,
    x_send,
    x_recv,
):
    p = Place(depth)
    length = ctx_ref.shape[0]
    half_rows = length // 2
    width = wo_shard.shape[1]
    chunks = wi_ref.shape[0]
    part = wi_shard.shape[1] // chunks
    g_sems, s_sems, x_sems = (g_send, g_recv), (s_send, s_recv), (x_send, x_recv)

    def part_cols(k):
        return pl.ds(pl.multiple_of(k * part, LANES), part)

    g_out = Gather(p, wo_ref, width, g_sems, 0, True)

    def g_chunk(k):
        return (
            Gather(p, wi_ref.at[k], part, g_sems, 1 + 2 * k, True),
            Gather(p, wb_ref.at[k], part, g_sems, 2 + 2 * k, False),
        )

    def s_chunk(k):
        return (
            Scatter(
                p, wi_ref.at[k], part, [r.at[k] for r in (i0, i1, i2, i3)], s_sems, 1 + 2 * k, True
            ),
            Scatter(
                p, wb_ref.at[k], part, [r.at[k] for r in (b0, b1, b2, b3)], s_sems, 2 + 2 * k, False
            ),
        )

    def when_gather(k, name):
        @pl.when(k < chunks)
        def _():
            for item in g_chunk(k):
                getattr(item, name)()

    def when_scatter(k, name):
        @pl.when((k >= 0) & (k < chunks))
        def _():
            for item, out in zip(s_chunk(k), (gwi_ref, gwb_ref)):
                if name == "finish":
                    item.finish(out, k * part)
                else:
                    getattr(item, name)()

    wo_ref[p.z, p.y, p.c, :, g_out.cols(p.t)] = wo_shard[...]
    for k in range(chunks):
        for item, shard in zip(g_chunk(k), (wi_shard, wb_shard)):
            item.ref[p.z, p.y, p.c, :, item.cols(p.t)] = shard[:, k * part : (k + 1) * part]
    p.barrier()
    g_out.start()
    for k in range(2):
        when_gather(k, "start")
    cot_move = remote(cots_ref.at[1 - p.t], cotb_ref.at[p.t], x_sems, 0, p.xpeer)
    cot_move.start()
    cotb_ref[p.t] = cots_ref[p.t]
    for k in range(2, chunks):
        when_gather(k, "start")
    g_out.step1()
    when_gather(0, "step1")
    when_gather(1, "step1")
    g_out.step2()
    when_gather(0, "step2")
    g_out.step3()
    when_gather(2, "step1")
    when_gather(1, "step2")
    when_gather(0, "step3")
    g_out.finish()
    gain = gain_ref[...]
    k3_before(xs_ref, ctx_ref, flat(wo_ref[...]), gain, gm_ref, ffn_ref, ffnt_ref)
    cot_move.wait_recv()
    cotb = cotb_ref.reshape(length, cotb_ref.shape[2])
    transpose_rows(cotb, cott_ref)

    def one_chunk(k, carry):
        when_gather(k + 3, "step1")
        when_gather(k + 2, "step2")
        when_gather(k + 1, "step3")
        for item in g_chunk(k):
            item.finish()
        when_scatter(k - 2, "step2")
        w_in, w_back = flat(wi_ref[k]), flat(wb_ref[k])
        args = (w_in, w_back, k == 0, ffn_ref, cotb, hid_ref, gp_ref, up_ref, down_ref)
        ffn_rows(0, half_rows, *args)
        when_scatter(k - 1, "step1")
        ffn_rows(1, half_rows, *args)
        when_scatter(k - 3, "step3")
        wb_ref[k] = nn(cott_ref[...], hid_ref[...]).astype(BF).reshape(wb_ref.shape[1:])
        when_scatter(k - 4, "finish")
        wi_ref[k] = nn(ffnt_ref[...], gp_ref[...]).astype(BF).reshape(wi_ref.shape[1:])
        for item in s_chunk(k):
            item.step0()
        return carry

    lax.fori_loop(0, chunks, one_chunk, 0)
    when_scatter(chunks - 1, "step1")
    when_scatter(chunks - 2, "step2")
    when_scatter(chunks - 3, "step3")
    ggain_ref[...] = jnp.zeros_like(ggain_ref)
    step = 256

    def finish_rows(own, i):
        half = p.t if own else 1 - p.t
        at = pl.ds(pl.multiple_of(i * step, step), step)
        rows = pl.ds(pl.multiple_of(half * half_rows + i * step, step), step)
        cot = cot_ref[p.t, at, :] if own else cotb_ref[1 - p.t, at, :].astype(F32)
        out = after_rows(
            rows, cot, up_ref, down_ref, gain, ggain_ref, gm_ref, ffn_ref, cott_ref
        )
        if own:
            out_ref[p.t, at, :] = out
        else:
            obuf_ref[at, :] = out.astype(BF)

    for i in range(half_rows // step):
        finish_rows(False, i)
    out_move = remote(obuf_ref, obuf2_ref, x_sems, 1, p.xpeer)
    out_move.start()
    for i in range(half_rows // step):
        finish_rows(True, i)
    when_scatter(chunks - 4, "finish")
    when_scatter(chunks - 1, "step2")
    context_grad(ffn_ref, flat(wo_ref[...]), go_ref)
    when_scatter(chunks - 2, "step3")
    wo_ref[...] = nn(cott_ref[...], ctx_ref[...]).astype(BF).reshape(wo_ref.shape)
    s_out = Scatter(p, wo_ref, width, (o0, o1, o2, o3), s_sems, 0, True)
    s_out.step0()
    when_scatter(chunks - 3, "finish")
    s_out.step1()
    when_scatter(chunks - 1, "step3")
    when_scatter(chunks - 2, "finish")
    s_out.step2()
    s_out.step3()
    out_move.wait_recv()
    out_ref[1 - p.t] = obuf2_ref[...].astype(F32)
    when_scatter(chunks - 1, "finish")
    s_out.finish(gwo_ref, 0)
    cot_move.wait_send()
    out_move.wait_send()


def k3_plain(
    xs_ref,
    ctx_ref,
    cot_ref,
    gain_ref,
    wo_ref,
    wi_ref,
    wb_ref,
    out_ref,
    gm_ref,
    go_ref,
    ggain_ref,
    gwo_ref,
    gwi_ref,
    gwb_ref,
    ffn_ref,
    ffnt_ref,
    cott_ref,
    cotb_ref,
    hid_ref,
    gp_ref,
    up_ref,
    down_ref,
):
    length = ctx_ref.shape[0]
    half_rows = length // 2
    chunk = hid_ref.shape[1]
    gain = gain_ref[...]
    cotb_ref[...] = cot_ref[...].astype(BF)
    k3_before(xs_ref, ctx_ref, wo_ref[...], gain, gm_ref, ffn_ref, ffnt_ref)
    transpose_rows(cotb_ref, cott_ref)

    def one_chunk(k, carry):
        cols = pl.ds(pl.multiple_of(k * chunk, LANES), chunk)
        w_in, w_back = wi_ref[:, cols], wb_ref[:, cols]
        for i in range(2):
            ffn_rows(
                i, half_rows, w_in, w_back, k == 0, ffn_ref, cotb_ref, hid_ref, gp_ref, up_ref, down_ref
            )
        gwb_ref[:, cols] = nn(cott_ref[...], hid_ref[...]).astype(BF)
        gwi_ref[:, cols] = nn(ffnt_ref[...], gp_ref[...]).astype(BF)
        return carry

    lax.fori_loop(0, wi_ref.shape[1] // chunk, one_chunk, 0)
    ggain_ref[...] = jnp.zeros_like(ggain_ref)
    step = 256

    def finish_rows(i, carry):
        rows = pl.ds(pl.multiple_of(i * step, step), step)
        out_ref[rows, :] = after_rows(
            rows,
            cot_ref[rows, :],
            up_ref,
            down_ref,
            gain,
            ggain_ref,
            gm_ref,
            ffn_ref,
            cott_ref,
        )
        return carry

    lax.fori_loop(0, length // step, finish_rows, 0)
    context_grad(ffn_ref, wo_ref[...], go_ref)
    gwo_ref[...] = nn(cott_ref[...], ctx_ref[...]).astype(BF)


def low_transposed(xs_ref, gain, lowt_ref):
    step = 256

    def one(i, carry):
        rows = pl.ds(pl.multiple_of(i * step, step), step)
        lowt_ref[:, rows] = project_rows(xs_ref[rows, :], gain).T
        return carry

    lax.fori_loop(0, xs_ref.shape[0] // step, one, 0)


def input_rows(rows, xs_ref, gm_ref, grads, weights, gain, gain_out):
    down = sum(nt(grad[rows, :], flat(weight[...])) for grad, weight in zip(grads, weights))
    inputs = xs_ref[rows, :].astype(F32)
    scale = rms_scale(inputs)
    normed = inputs * scale
    gain_out[...] += jnp.sum(down * normed, 0, keepdims=True)
    return gm_ref[rows, :] + rms_back(down, normed, scale, gain)


def k5_fused(
    depth,
    xs_ref,
    gm_ref,
    dq_ref,
    dk_ref,
    dv_ref,
    wq_ref,
    wk_ref,
    wv_ref,
    gain_ref,
    ggain_ref,
    tabg_ref,
    ig_ref,
    gwq_ref,
    gwk_ref,
    gwv_ref,
    small_ref,
    lowt_ref,
    gq_ref,
    gk_ref,
    gv_ref,
    ibuf_ref,
    ibuf2_ref,
    again_ref,
    sm_ref,
    smr_ref,
    a0,
    a1,
    a2,
    a3,
    c0,
    c1,
    c2,
    c3,
    d0,
    d1,
    d2,
    d3,
    s_send,
    s_recv,
    x_send,
    x_recv,
):
    p = Place(depth)
    length = xs_ref.shape[0]
    half_rows = length // 2
    width = gwq_ref.shape[1]
    s_sems, x_sems = (s_send, s_recv), (x_send, x_recv)
    items = [
        Scatter(p, gq_ref, width, (a0, a1, a2, a3), s_sems, 0, True),
        Scatter(p, gk_ref, width, (c0, c1, c2, c3), s_sems, 1, False),
        Scatter(p, gv_ref, width, (d0, d1, d2, d3), s_sems, 2, True),
    ]
    gain = gain_ref[...]
    p.barrier()
    low_transposed(xs_ref, gain, lowt_ref)
    for item, grad in zip(items, (dq_ref, dk_ref, dv_ref)):
        item.ref[...] = nn(lowt_ref[...], grad[...]).astype(BF).reshape(item.ref.shape)
        item.step0()
        if item is not items[0]:
            items[items.index(item) - 1].step1()
    again_ref[...] = jnp.zeros_like(again_ref)
    step = 256
    grads, weights = (dq_ref, dk_ref, dv_ref), (wq_ref, wk_ref, wv_ref)

    def finish_rows(own, i):
        half = p.t if own else 1 - p.t
        at = pl.ds(pl.multiple_of(i * step, step), step)
        rows = pl.ds(pl.multiple_of(half * half_rows + i * step, step), step)
        out = input_rows(rows, xs_ref, gm_ref, grads, weights, gain, again_ref)
        if own:
            ig_ref[p.t, at, :] = out
        else:
            ibuf_ref[at, :] = out.astype(BF)

    for i in range(half_rows // step):
        finish_rows(False, i)
    move = remote(ibuf_ref, ibuf2_ref, x_sems, 0, p.xpeer)
    move.start()
    items[2].step1()
    items[0].step2()
    for i in range(half_rows // step):
        finish_rows(True, i)
    model = again_ref.shape[1]
    sm_ref[0, 0:1, :model] = again_ref[...]
    sm_ref[0, 1:2, :model] = ggain_ref[...]
    sm_ref[0, 2:8, :model] = jnp.zeros((6, model), F32)
    sm_ref[0, :, model : model + LANES] = tabg_ref[0:8, :]
    sm_ref[0, :, model + LANES :] = tabg_ref[8:16, :]
    hops = [(p.sib,), (p.ypeer,), (p.xpeer,), tuple(p.zpeers)]
    slot = 0
    comm = [
        lambda: items[1].step2(),
        lambda: items[0].step3(),
        lambda: items[2].step2(),
        lambda: items[1].step3(),
    ]
    for level, peers in enumerate(hops):
        moves = [
            remote(sm_ref.at[level], smr_ref.at[slot + i], x_sems, 1 + slot + i, peer)
            for i, peer in enumerate(peers)
        ]
        for one in moves:
            one.start()
        comm[level]()
        total = sm_ref[level]
        for i, one in enumerate(moves):
            one.wait_recv()
            total = total + smr_ref[slot + i]
        slot += len(peers)
        if level + 1 < len(hops):
            sm_ref[level + 1] = total
        else:
            small_ref[...] = total
        for one in moves:
            one.wait_send()
    items[2].step3()
    move.wait_recv()
    ig_ref[1 - p.t] = ibuf2_ref[...].astype(F32)
    for item, out in zip(items, (gwq_ref, gwk_ref, gwv_ref)):
        item.finish(out, 0)
    move.wait_send()


def k5_plain(
    xs_ref,
    gm_ref,
    dq_ref,
    dk_ref,
    dv_ref,
    wq_ref,
    wk_ref,
    wv_ref,
    gain_ref,
    ig_ref,
    gwq_ref,
    gwk_ref,
    gwv_ref,
    again_ref,
    lowt_ref,
):
    gain = gain_ref[...]
    low_transposed(xs_ref, gain, lowt_ref)
    grads, weights = (dq_ref, dk_ref, dv_ref), (wq_ref, wk_ref, wv_ref)
    for grad, out in zip(grads, (gwq_ref, gwk_ref, gwv_ref)):
        out[...] = nn(lowt_ref[...], grad[...]).astype(BF)
    again_ref[...] = jnp.zeros_like(again_ref)
    step = 256

    def one(i, carry):
        rows = pl.ds(pl.multiple_of(i * step, step), step)
        ig_ref[rows, :] = input_rows(rows, xs_ref, gm_ref, grads, weights, gain, again_ref)
        return carry

    lax.fori_loop(0, xs_ref.shape[0] // step, one, 0)


def call(kernel, outs, scratch, args, name, collective=None):
    spec = pl.BlockSpec(memory_space=pltpu.VMEM)
    if collective is None:
        params = pltpu.CompilerParams(vmem_limit_bytes=VMEM_BYTES)
    else:
        params = pltpu.CompilerParams(
            vmem_limit_bytes=VMEM_BYTES, collective_id=collective, has_side_effects=True
        )
    return pl.pallas_call(
        kernel,
        out_shape=[jax.ShapeDtypeStruct(shape, dtype) for shape, dtype in outs],
        in_specs=[spec] * len(args),
        out_specs=[spec] * len(outs),
        scratch_shapes=scratch,
        compiler_params=params,
        name=name,
    )(*args)


def shards(
    inputs,
    segments,
    norm_attn,
    norm_ffn,
    w_query,
    w_key,
    w_value,
    w_out,
    w_in,
    w_back,
    rel_table,
    cotangent,
):
    dp, tensor = lax.axis_size("dp"), lax.axis_size("tensor")
    t = lax.axis_index("tensor")
    rows, width = w_query.shape
    hidden_part = w_in.shape[1]
    model = inputs.shape[2]
    length = segments.shape[2]
    half = inputs.shape[1]
    buckets, heads = rel_table.shape
    depth = dp // 4
    fused = rows % 16 == 0 and dp % 4 == 0 and depth >= 2
    gain_attn, gain_ffn = norm_attn.reshape(1, model), norm_ffn.reshape(1, model)
    table = jnp.pad(rel_table.T, ((0, 8 - heads), (0, LANES - buckets)))
    segment = lax.dynamic_index_in_dim(segments[:, 0], t, 0, False).reshape(length, 1)
    full = (length, model)
    inner = (length, width * tensor)
    square = (depth, 2, 2, rows, 2 * width)
    part = 256
    chunks = hidden_part // part
    dma = pltpu.SemaphoreType.DMA
    if fused:
        xs, cots, tabs, queries, keys, values, wq, wk, wv = call(
            functools.partial(k1_fused, depth),
            [
                ((2, half, model), BF),
                ((2, half, model), BF),
                ((2, 8, LANES), F32),
                (inner, BF),
                (inner, BF),
                (inner, BF),
                (square, BF),
                (square, BF),
                (square, BF),
            ],
            [pltpu.VMEM(full, BF)] + gather_sems(3, depth) + [dma((2,)), dma((2,))],
            (inputs, cotangent, gain_attn, table, w_query, w_key, w_value),
            "exchange_project",
            0,
        )
        xs = xs.reshape(full)
    else:

        def whole(weight):
            weight = lax.all_gather(weight, "dp", axis=0, tiled=True)
            return lax.all_gather(weight, "tensor", axis=1, tiled=True)

        def exchanged(local):
            own = lax.dynamic_index_in_dim(local, t, 0, False)
            other = lax.dynamic_index_in_dim(local, 1 - t, 0, False)
            other = lax.ppermute(other, "tensor", [(0, 1), (1, 0)])
            first = jnp.where(t == 0, own, other)
            second = jnp.where(t == 0, other, own)
            return jnp.concatenate([first, second], 0)

        def returned(seq):
            mine = lax.dynamic_slice_in_dim(seq, t * half, half, 0)
            other = lax.dynamic_slice_in_dim(seq, (1 - t) * half, half, 0)
            other = lax.ppermute(other, "tensor", [(0, 1), (1, 0)])
            return jnp.stack([jnp.where(t == 0, mine, other), jnp.where(t == 0, other, mine)])

        def scattered(grad):
            grad = lax.psum_scatter(grad.astype(F32), "tensor", scatter_dimension=1, tiled=True)
            return lax.psum_scatter(grad, "dp", scatter_dimension=0, tiled=True)

        xs = exchanged(inputs)
        tabs = lax.all_gather(table, "tensor", axis=0)
        wq, wk, wv, wo, wi, wb = (
            whole(w) for w in (w_query, w_key, w_value, w_out, w_in, w_back)
        )
        queries, keys, values = call(
            k1_plain,
            [(inner, BF)] * 3,
            [pltpu.VMEM(full, BF)],
            (xs, gain_attn, wq, wk, wv),
            "project",
        )
    pairs = inner[1] // LANES
    ctx, ctxf, feats = call(
        fwd_kernel,
        [(inner, BF), (inner, F32), ((pairs, length, LANES), BF)],
        [pltpu.VMEM((16, 4 * LANES), F32)] + [pltpu.VMEM((length, LANES), BF)] * 2,
        (queries, keys, values, segment, tabs),
        "attention_forward",
    )
    work = [
        pltpu.VMEM(full, BF),
        pltpu.VMEM((model, length), BF),
        pltpu.VMEM((model, length), BF),
    ]
    rest = [
        pltpu.VMEM((length, 2 * part), BF),
        pltpu.VMEM((length, 2 * part), BF),
        pltpu.VMEM(full, F32),
        pltpu.VMEM(full, F32),
    ]
    if fused:
        big = pltpu.VMEM((chunks, depth, 2, 2, rows, 2 * part), BF)
        output, grad_middle, grad_context, ggain, gwo, gwi, gwb = call(
            functools.partial(k3_fused, depth),
            [
                ((2, half, model), F32),
                (full, F32),
                (inner, BF),
                ((1, model), F32),
                ((rows, width), F32),
                ((rows, hidden_part), F32),
                ((rows, hidden_part), F32),
            ],
            [pltpu.VMEM(square, BF), big, big]
            + work
            + [pltpu.VMEM((2, half, model), BF)]
            + rest
            + [pltpu.VMEM((half, model), BF)] * 2
            + scatter_bufs(None, depth, rows, width, True)
            + scatter_bufs(chunks, depth, rows, part, True)
            + scatter_bufs(chunks, depth, rows, part, False)
            + gather_sems(1 + 2 * chunks, depth)
            + scatter_sems(1 + 2 * chunks, depth)
            + [dma((2,)), dma((2,))],
            (xs, ctx, cotangent, cots, gain_ffn, w_out, w_in, w_back),
            "feed_forward",
            1,
        )
    else:
        out_seq, grad_middle, grad_context, ggain, gwo, gwi, gwb = call(
            k3_plain,
            [
                (full, F32),
                (full, F32),
                (inner, BF),
                ((1, model), F32),
                (wo.shape, BF),
                (wi.shape, BF),
                (wb.shape, BF),
            ],
            work + [pltpu.VMEM(full, BF)] + rest,
            (xs, ctx, exchanged(cotangent), gain_ffn, wo, wi, wb),
            "feed_forward",
        )
        output = returned(out_seq)
        gwo, gwi, gwb = scattered(gwo), scattered(gwi), scattered(gwb)
    dq, dk, dv, table_grad = call(
        bwd_kernel,
        [(inner, BF), (inner, BF), (inner, BF), ((16, LANES), F32)],
        [
            pltpu.VMEM((16, 4 * LANES), F32),
            pltpu.VMEM((16, 4 * LANES), F32),
            pltpu.VMEM((16, LANES), F32),
            pltpu.VMEM((length, LANES), BF),
            pltpu.VMEM((length, LANES), BF),
            pltpu.VMEM((2, LANES, 3 * LANES), F32),
            pltpu.VMEM((length, LANES), F32),
        ],
        (queries, keys, values, grad_context, ctxf, feats, segment, tabs),
        "attention_backward",
    )
    if fused:
        input_grad, gwq, gwk, gwv, small = call(
            functools.partial(k5_fused, depth),
            [
                ((2, half, model), F32),
                ((rows, width), F32),
                ((rows, width), F32),
                ((rows, width), F32),
                ((8, model + 2 * LANES), F32),
            ],
            [pltpu.VMEM((model, length), BF)]
            + [pltpu.VMEM(square, BF)] * 3
            + [pltpu.VMEM((half, model), BF)] * 2
            + [
                pltpu.VMEM((1, model), F32),
                pltpu.VMEM((4, 8, model + 2 * LANES), F32),
                pltpu.VMEM((depth + 2, 8, model + 2 * LANES), F32),
            ]
            + scatter_bufs(None, depth, rows, width, True)
            + scatter_bufs(None, depth, rows, width, False)
            + scatter_bufs(None, depth, rows, width, True)
            + scatter_sems(3, depth)
            + [dma((depth + 3,)), dma((depth + 3,))],
            (xs, grad_middle, dq, dk, dv, wq, wk, wv, gain_attn, ggain, table_grad),
            "projection_gradients",
            2,
        )
        gain_attn_grad, gain_ffn_grad = small[0, :model], small[1, :model]
        tables = jnp.stack([small[:, model : model + LANES], small[:, model + LANES :]])
    else:
        ig_seq, gwq, gwk, gwv, again = call(
            k5_plain,
            [(full, F32), (wq.shape, BF), (wk.shape, BF), (wv.shape, BF), ((1, model), F32)],
            [pltpu.VMEM((model, length), BF)],
            (xs, grad_middle, dq, dk, dv, wq, wk, wv, gain_attn),
            "projection_gradients",
        )
        input_grad = returned(ig_seq)
        gwq, gwk, gwv = scattered(gwq), scattered(gwk), scattered(gwv)
        again, ggain, tables = lax.psum((again, ggain, table_grad), ("dp", "tensor"))
        gain_attn_grad, gain_ffn_grad = again[0], ggain[0]
        tables = tables.reshape(2, 8, LANES)
    table_out = lax.dynamic_index_in_dim(tables, t, 0, False)[:heads, :buckets].T
    return (
        output,
        input_grad,
        gain_attn_grad,
        gain_ffn_grad,
        gwq,
        gwk,
        gwv,
        gwo,
        gwi,
        gwb,
        table_out,
    )


def solution(mesh):
    weight = P("dp", "tensor")
    tokens = P(None, ("dp", "tensor"), None)
    return jax.shard_map(
        shards,
        mesh=mesh,
        in_specs=(
            tokens,
            P(None, "dp", None),
            P(),
            P(),
            weight,
            weight,
            weight,
            weight,
            weight,
            weight,
            P(None, "tensor"),
            tokens,
        ),
        out_specs=(
            tokens,
            tokens,
            P(),
            P(),
            weight,
            weight,
            weight,
            weight,
            weight,
            weight,
            P(None, "tensor"),
        ),
        check_vma=False,
    )
```

```python
import functools

import jax
import jax.numpy as jnp
from jax import lax
from jax.experimental import pallas as pl
from jax.experimental.pallas import tpu as pltpu
from jax.sharding import PartitionSpec as P

MESH = pl.DeviceIdType.MESH
BF = jnp.bfloat16
F32 = jnp.float32
HIGHEST = lax.Precision.HIGHEST
EPSILON = 1e-06
THRESHOLDS = (12, 16, 23, 32, 46, 64, 91)
MASK_OUT = -float(2**30)
DH = 64
SPAN = 512
LANES = 128
VMEM_BYTES = 62 * 2**20


def nn(left, right):
    return lax.dot_general(left, right, (((1,), (0,)), ((), ())), preferred_element_type=F32)


def nt(left, right):
    return lax.dot_general(left, right, (((1,), (1,)), ((), ())), preferred_element_type=F32)


def tn(left, right):
    return lax.dot_general(left, right, (((0,), (0,)), ((), ())), preferred_element_type=F32)


def iota(shape, dim):
    return lax.broadcasted_iota(jnp.int32, shape, dim)


def bucket_ids(offsets):
    distance = jnp.abs(offsets)
    far_ids = 8 + sum((distance >= threshold).astype(jnp.int32) for threshold in THRESHOLDS)
    return jnp.where(offsets > 0, 16, 0) + jnp.where(distance < 8, distance, far_ids)


def rms_scale(values):
    return lax.rsqrt(jnp.mean(values * values, -1, keepdims=True) + EPSILON)


def rms_back(grad_normed, normed, scale, gain):
    scaled = grad_normed * gain
    return scale * (scaled - normed * jnp.mean(scaled * normed, -1, keepdims=True))


def gelu_pair(v):
    square = v * v
    half = 0.5 + 0.5 * jnp.tanh(v * (0.7978845608028654 + 0.035677408136300125 * square))
    slope = half + v * half * (1.0 - half) * (1.5957691216057308 + 0.2140644488178007 * square)
    return v * half, slope


class Place:
    def __init__(self, depth):
        d, t = lax.axis_index("dp"), lax.axis_index("tensor")
        self.t = t
        self.z, self.y, self.c = lax.div(d, 4), lax.rem(lax.div(d, 2), 2), lax.rem(d, 2)
        self.depth = depth
        self.sib = (d + 1 - 2 * self.c, t)
        self.ypeer = (d + 2 - 4 * self.y, t)
        self.xpeer = (d, 1 - t)
        rest = lax.rem(d, 4)
        self.zs = [lax.rem(self.z + step, depth) for step in range(1, depth)]
        self.zpeers = [(z * 4 + rest, t) for z in self.zs]

    def barrier(self):
        semaphore = pltpu.get_barrier_semaphore()
        peers = [self.sib, self.ypeer, self.xpeer] + self.zpeers
        for peer in peers:
            pl.semaphore_signal(semaphore, inc=1, device_id=peer, device_id_type=MESH)
        pl.semaphore_wait(semaphore, len(peers))


class Copy:
    def __init__(self, **parts):
        self.parts = parts

    def made(self):
        return pltpu.make_async_remote_copy(device_id_type=MESH, **self.parts)

    def start(self):
        self.made().start()

    def wait_recv(self):
        self.made().wait_recv()

    def wait_send(self):
        self.made().wait_send()


def local(src, dst, sem):
    return pltpu.make_async_copy(src, dst, sem)


def remote(src, dst, sems, index, peer):
    send, recv = sems
    return Copy(
        src_ref=src, dst_ref=dst, send_sem=send.at[index], recv_sem=recv.at[index], device_id=peer
    )


class Gather:
    def __init__(self, place, ref, width, sems, item, x_first):
        self.p, self.ref, self.width, self.sems, self.item = place, ref, width, sems, item
        self.x_first = x_first
        self.first, self.second = (
            (place.xpeer, place.ypeer) if x_first else (place.ypeer, place.xpeer)
        )

    def cols(self, x):
        return pl.ds(pl.multiple_of(x * self.width, LANES), self.width)

    def region(self, y, x):
        return self.ref.at[:, y, self.p.c, :, self.cols(x)]

    def send(self, index, src, peer):
        return remote(src, src, self.sems, (self.item, index), peer)

    def copies(self):
        p = self.p
        own = self.ref.at[p.z, p.y, p.c, :, self.cols(p.t)]
        regions = [self.region(p.y, p.t)]
        regions.append(self.region(p.y, 1 - p.t) if self.x_first else self.region(1 - p.y, p.t))
        regions.append(self.region(1 - p.y, p.t) if self.x_first else self.region(p.y, 1 - p.t))
        regions.append(self.region(1 - p.y, 1 - p.t))
        n = len(p.zpeers)
        zs = [self.send(i, own, peer) for i, peer in enumerate(p.zpeers)]
        first = self.send(n, regions[0], self.first)
        seconds = [self.send(n + 1 + i, regions[i], self.second) for i in range(2)]
        sibs = [self.send(n + 3 + i, regions[i], p.sib) for i in range(4)]
        return zs, first, seconds, sibs

    def start(self):
        for copy in self.copies()[0]:
            copy.start()

    def step1(self):
        zs, first, seconds, sibs = self.copies()
        for copy in zs:
            copy.wait_recv()
        first.start()
        seconds[0].start()
        sibs[0].start()

    def step2(self):
        _, first, seconds, sibs = self.copies()
        first.wait_recv()
        seconds[1].start()
        sibs[1].start()

    def step3(self):
        _, _, seconds, sibs = self.copies()
        seconds[0].wait_recv()
        sibs[2].start()
        seconds[1].wait_recv()
        sibs[3].start()

    def finish(self):
        zs, first, seconds, sibs = self.copies()
        for copy in sibs:
            copy.wait_recv()
        for copy in zs + [first] + seconds + sibs:
            copy.wait_send()


class GatherX(Gather):
    def copies(self):
        p = self.p
        n = len(p.zpeers)
        own = self.ref.at[p.z, p.y, p.c, :, self.cols(p.t)]
        other = self.ref.at[p.z, p.y, p.c, :, self.cols(1 - p.t)]
        regions = [self.region(y, x) for y in (p.y, 1 - p.y) for x in (p.t, 1 - p.t)]
        first = self.send(0, own, p.xpeer)
        zs = [
            [self.send(1 + side * n + i, block, peer) for i, peer in enumerate(p.zpeers)]
            for side, block in enumerate((own, other))
        ]
        lasts = [self.send(1 + 2 * n + i, regions[i], p.ypeer) for i in range(2)]
        sibs = [self.send(3 + 2 * n + i, regions[i], p.sib) for i in range(4)]
        return first, zs, lasts, sibs

    def start(self):
        first, zs, _, _ = self.copies()
        first.start()
        for copy in zs[0]:
            copy.start()

    def step1(self):
        first, zs, _, _ = self.copies()
        first.wait_recv()
        for copy in zs[1]:
            copy.start()

    def step2(self, side):
        _, zs, lasts, sibs = self.copies()
        for copy in zs[side]:
            copy.wait_recv()
        lasts[side].start()
        sibs[side].start()

    def step3(self):
        _, _, lasts, sibs = self.copies()
        for side in range(2):
            lasts[side].wait_recv()
            sibs[2 + side].start()

    def finish(self):
        first, zs, lasts, sibs = self.copies()
        for copy in sibs:
            copy.wait_recv()
        for copy in [first] + zs[0] + zs[1] + lasts + sibs:
            copy.wait_send()


def gather_sems(items, depth):
    return [pltpu.SemaphoreType.DMA((items, depth + 6))] * 2


class Scatter:
    def __init__(self, place, ref, width, bufs, sems, item, y_first):
        self.p, self.ref, self.width, self.sems, self.item = place, ref, width, sems, item
        self.r0, self.r1, self.r2, self.r3 = bufs
        self.y_first = y_first

    def cols(self, x):
        return pl.ds(pl.multiple_of(x * self.width, LANES), self.width)

    def copies(self):
        p, ref = self.p, self.ref
        sib = remote(ref.at[:, :, 1 - p.c], self.r0, self.sems, (self.item, 0), p.sib)
        if self.y_first:
            half = remote(ref.at[:, 1 - p.y, p.c], self.r1, self.sems, (self.item, 1), p.ypeer)
            quarter = remote(
                ref.at[:, p.y, p.c, :, self.cols(1 - p.t)],
                self.r2,
                self.sems,
                (self.item, 2),
                p.xpeer,
            )
        else:
            half = remote(
                ref.at[:, :, p.c, :, self.cols(1 - p.t)],
                self.r1,
                self.sems,
                (self.item, 1),
                p.xpeer,
            )
            quarter = remote(
                ref.at[:, 1 - p.y, p.c, :, self.cols(p.t)],
                self.r2,
                self.sems,
                (self.item, 2),
                p.ypeer,
            )
        zs = [
            remote(
                ref.at[z, p.y, p.c, :, self.cols(p.t)],
                self.r3.at[i],
                self.sems,
                (self.item, 3 + i),
                peer,
            )
            for i, (z, peer) in enumerate(zip(p.zs, p.zpeers))
        ]
        return sib, half, quarter, zs

    def step0(self):
        self.copies()[0].start()

    def step1(self):
        p = self.p
        sib, half, _, _ = self.copies()
        sib.wait_recv()
        kept = self.ref.at[:, :, p.c]
        kept[...] = (kept[...].astype(F32) + self.r0[...].astype(F32)).astype(BF)
        half.start()

    def step2(self):
        p = self.p
        _, half, quarter, _ = self.copies()
        half.wait_recv()
        if self.y_first:
            kept = self.ref.at[:, p.y, p.c]
        else:
            kept = self.ref.at[:, :, p.c, :, self.cols(p.t)]
        kept[...] = (kept[...].astype(F32) + self.r1[...].astype(F32)).astype(BF)
        quarter.start()

    def step3(self):
        p = self.p
        _, _, quarter, zs = self.copies()
        quarter.wait_recv()
        kept = self.ref.at[:, p.y, p.c, :, self.cols(p.t)]
        kept[...] = (kept[...].astype(F32) + self.r2[...].astype(F32)).astype(BF)
        for copy in zs:
            copy.start()

    def finish(self, out, offset):
        p = self.p
        sib, half, quarter, zs = self.copies()
        for copy in zs:
            copy.wait_recv()
        total = self.ref[p.z, p.y, p.c, :, self.cols(p.t)].astype(F32)
        for i in range(len(zs)):
            total = total + self.r3[i].astype(F32)
        out[:, pl.ds(pl.multiple_of(offset, LANES), self.width)] = total
        for copy in [sib, half, quarter] + zs:
            copy.wait_send()


def scatter_bufs(items, depth, rows, width, y_first):
    lead = () if items is None else (items,)
    return [
        pltpu.VMEM(lead + (depth, 2, rows, 2 * width), BF),
        pltpu.VMEM(lead + ((depth, rows, 2 * width) if y_first else (depth, 2, rows, width)), BF),
        pltpu.VMEM(lead + (depth, rows, width), BF),
        pltpu.VMEM(lead + (depth - 1, rows, width), BF),
    ]


def scatter_sems(items, depth):
    return [pltpu.SemaphoreType.DMA((items, depth + 2))] * 2


def flat(values):
    if len(values.shape) == 2:
        return values
    return values.reshape(-1, values.shape[-1])


def project_rows(x_rows, gain):
    rows = x_rows.astype(F32)
    return (rows * rms_scale(rows) * gain).astype(BF)


def project(low_ref, w_ref, out_ref):
    weight = flat(w_ref[...])
    half = low_ref.shape[0] // 2

    def one(i, carry):
        rows = pl.ds(pl.multiple_of(i * half, half), half)
        out_ref[rows, :] = nn(low_ref[rows, :], weight).astype(BF)
        return carry

    lax.fori_loop(0, 2, one, 0)


def k1_plain(x_ref, gain_ref, wq_ref, wk_ref, wv_ref, q_ref, k_ref, v_ref, low_ref):
    low_ref[...] = project_rows(x_ref[...], gain_ref[...])
    for weight, out in ((wq_ref, q_ref), (wk_ref, k_ref), (wv_ref, v_ref)):
        project(low_ref, weight, out)


def bias_rows(tabs_ref, out_ref, flipped):
    offsets = iota((LANES, 4 * LANES), 1) - 2 * LANES
    onehot = (bucket_ids(-offsets if flipped else offsets) == iota((LANES, 4 * LANES), 0)).astype(F32)
    for half in range(2):
        out_ref[half * 8 : half * 8 + 8, :] = jnp.dot(
            tabs_ref[half], onehot, precision=HIGHEST, preferred_element_type=F32
        )


def head_row(pair, per_half):
    return 8 * lax.div(pair, per_half) + 2 * lax.rem(pair, per_half)


def bias_strip(row):
    spread = jnp.broadcast_to(row, (LANES, 4 * LANES))
    return pltpu.roll(spread, 3 * LANES, 1, stride=1, stride_axis=0)


def window(tile, rows, length):
    reach = -(-SPAN // rows)
    return max(0, (tile - reach) * rows), min(length, (tile + reach + 1) * rows)


def segment_lanes(seg_ref):
    onehot = seg_ref[...] == iota((seg_ref.shape[0], LANES), 1)
    inside = iota((seg_ref.shape[0], LANES), 1) < 16
    return onehot, inside


def pair_cols(pair):
    return pl.ds(pl.multiple_of(pair * LANES, LANES), LANES)


def spread3(value):
    top = value.astype(BF).astype(F32)
    mid = (value - top).astype(BF).astype(F32)
    return top, mid, value - top - mid


TILE = 256
NEAR = SPAN // LANES


def key_lanes(seg_ref):
    onehot, inside = segment_lanes(seg_ref)
    return jnp.where(onehot, 0.0, jnp.where(inside, 1.0, 0.0)).astype(BF)


def fwd_setup(seg_ref, tabs_ref, bias_ref, segq_ref, segk_ref):
    bias_rows(tabs_ref, bias_ref, False)
    onehot, _ = segment_lanes(seg_ref)
    segq_ref[...] = jnp.where(onehot, MASK_OUT, 0.0).astype(BF)
    segk_ref[...] = key_lanes(seg_ref)


def fwd_pair(pair, q_ref, k_ref, v_ref, ctx_ref, feat_ref, bias_ref, segq_ref, segk_ref):
    length, width = q_ref.shape
    per_half = width // LANES // 2
    tile, near = TILE, NEAR
    cols = pair_cols(pair)
    row = head_row(pair, per_half)
    lane = iota((tile, LANES), 1)
    low_half = lane < DH
    strips, fars = [], []
    for hh in range(2):
        line = bias_ref[pl.ds(row + hh, 1), :]
        strips.append(bias_strip(line))
        fars.append((line[:, 0:1], line[:, 4 * LANES - 1 : 4 * LANES]))
    for index in range(length // tile):
        rows = slice(index * tile, (index + 1) * tile)
        start, stop = window(index, tile, length)
        queries = q_ref[rows, cols]
        zero = jnp.zeros_like(queries)
        q_feat = segq_ref[rows, :]
        left = jnp.concatenate(
            [
                jnp.concatenate([jnp.where(low_half, queries, zero), q_feat], 1),
                jnp.concatenate([jnp.where(low_half, zero, queries), q_feat], 1),
            ],
            0,
        )
        right = jnp.concatenate([k_ref[start:stop, cols], segk_ref[start:stop, :]], 1)
        scores = nt(left, right)
        weights, peaks = [], []
        for hh in range(2):
            for part in range(tile // LANES):
                at = hh * tile + part * LANES
                q_block = index * (tile // LANES) + part
                blocks = []
                for k_block in range(start // LANES, stop // LANES):
                    delta = k_block - q_block
                    if abs(delta) > near:
                        blocks.append(None)
                        continue
                    col = k_block * LANES - start
                    block = scores[at : at + LANES, col : col + LANES]
                    if abs(delta) <= 1:
                        block = block + strips[hh][:, (delta + 1) * LANES : (delta + 2) * LANES]
                    else:
                        block = block + fars[hh][0 if delta < 0 else 1]
                    blocks.append(block)
                real = [block for block in blocks if block is not None]
                peak = functools.reduce(jnp.maximum, real)
                peak = jnp.max(peak, -1, keepdims=True)
                peaks.append(peak)
                weights.append(
                    jnp.concatenate(
                        [
                            jnp.zeros((LANES, LANES), BF)
                            if block is None
                            else jnp.exp(block - peak).astype(BF)
                            for block in blocks
                        ],
                        1,
                    )
                )
        values = v_ref[start:stop, cols]
        gathered = nn(
            jnp.concatenate(weights, 0), jnp.concatenate([values, jnp.ones_like(values)], 1)
        )
        normal = gathered[:, :LANES] / gathered[:, LANES:]
        context = jnp.where(low_half, normal[:tile], normal[tile:])
        ctx_ref[rows, cols] = context.astype(BF)
        logs = jnp.concatenate(peaks, 0) + jnp.log(gathered[:, LANES:])
        feature = q_feat.astype(F32)
        for hh in range(2):
            for i, piece in enumerate(spread3(logs[hh * tile : (hh + 1) * tile])):
                feature = jnp.where(lane == 16 + 3 * hh + i, -piece, feature)
        feat_ref[pair, rows, :] = feature.astype(BF)


def fwd_kernel(
    q_ref, k_ref, v_ref, seg_ref, tabs_ref, ctx_ref, feat_ref, bias_ref, segq_ref, segk_ref
):
    fwd_setup(seg_ref, tabs_ref, bias_ref, segq_ref, segk_ref)

    def one_pair(pair, carry):
        fwd_pair(pair, q_ref, k_ref, v_ref, ctx_ref, feat_ref, bias_ref, segq_ref, segk_ref)
        return carry

    lax.fori_loop(0, q_ref.shape[1] // LANES, one_pair, 0)


def bwd_setup(seg_ref, tabs_ref, bias_ref, sums_ref, far_ref, segk_ref, blockof_ref):
    length = seg_ref.shape[0]
    bias_rows(tabs_ref, bias_ref, True)
    sums_ref[...] = jnp.zeros_like(sums_ref)
    far_ref[...] = jnp.zeros_like(far_ref)
    segk_ref[...] = key_lanes(seg_ref)
    blockof_ref[...] = (
        lax.div(iota((length, LANES), 0), LANES) == iota((length, LANES), 1)
    ).astype(BF)


def bwd_pair(
    pair,
    q_ref,
    k_ref,
    v_ref,
    go_ref,
    ctx_ref,
    feat_ref,
    dq_ref,
    dk_ref,
    dv_ref,
    bias_ref,
    sums_ref,
    far_ref,
    segk_ref,
    blockof_ref,
    gofeat_ref,
    near_ref,
    acc_ref,
):
    length, width = q_ref.shape
    per_half = width // LANES // 2
    tile, near = TILE, NEAR
    flip = (iota((LANES, LANES), 0) + iota((LANES, LANES), 1) == LANES - 1).astype(F32)
    cols = pair_cols(pair)
    row = head_row(pair, per_half)
    lane = iota((tile, LANES), 1)
    low_half = lane < DH
    strips, fars = [], []
    for hh in range(2):
        line = bias_ref[pl.ds(row + hh, 1), :]
        strips.append(bias_strip(line))
        fars.append((line[:, 0:1], line[:, 4 * LANES - 1 : 4 * LANES]))
    grads_all = go_ref[:, cols]
    product = grads_all.astype(F32) * ctx_ref[:, cols].astype(F32)
    lane_all = iota((length, LANES), 1)
    feature = jnp.zeros((length, LANES), F32)
    for hh in range(2):
        keep = (lane_all < DH) if hh == 0 else (lane_all >= DH)
        total = jnp.sum(jnp.where(keep, product, 0.0), -1, keepdims=True)
        for i, piece in enumerate(spread3(total)):
            feature = jnp.where(lane_all == 3 * hh + i, -piece, feature)
    gofeat_ref[...] = feature.astype(BF)
    near_ref[...] = jnp.zeros_like(near_ref)
    acc_ref[...] = jnp.zeros_like(acc_ref)
    far_sums = [[jnp.zeros((1, LANES), F32) for _ in range(2)] for _ in range(2)]
    lane_row = iota((1, LANES), 1)
    for index in range(length // tile):
        rows = slice(index * tile, (index + 1) * tile)
        start, stop = window(index, tile, length)
        keys, values = k_ref[rows, cols], v_ref[rows, cols]
        zero = jnp.zeros_like(keys)
        seg_feat = segk_ref[rows, :].astype(F32)

        def ones_at(base, first):
            return jnp.where((lane >= first) & (lane < first + 3), 1.0, base).astype(BF)

        masked_keys = jnp.concatenate(
            [jnp.where(low_half, keys, zero), jnp.where(low_half, zero, keys)], 0
        )
        masked_values = jnp.concatenate(
            [jnp.where(low_half, values, zero), jnp.where(low_half, zero, values)], 0
        )
        key_feats = jnp.concatenate([ones_at(seg_feat, 16), ones_at(seg_feat, 19)], 0)
        value_feats = jnp.concatenate([ones_at(0.0, 0), ones_at(0.0, 3)], 0)
        queries = q_ref[start:stop, cols]
        grads = go_ref[start:stop, cols]
        logits = nt(
            jnp.concatenate([masked_keys, key_feats], 1),
            jnp.concatenate([queries, feat_ref[pair, start:stop, :]], 1),
        )
        shifted = nt(
            jnp.concatenate([masked_values, value_feats], 1),
            jnp.concatenate([grads, gofeat_ref[start:stop, :]], 1),
        )
        probs_rows, score_rows = [], []
        for hh in range(2):
            for part in range(tile // LANES):
                at = hh * tile + part * LANES
                k_block = index * (tile // LANES) + part
                probs, score_grads = [], []
                for q_block in range(start // LANES, stop // LANES):
                    delta = k_block - q_block
                    if abs(delta) > near:
                        probs.append(jnp.zeros((LANES, LANES), BF))
                        score_grads.append(jnp.zeros((LANES, LANES), BF))
                        continue
                    col = q_block * LANES - start
                    block = logits[at : at + LANES, col : col + LANES]
                    place = (1 - delta) * LANES
                    if abs(delta) <= 1:
                        block = block + strips[hh][:, place : place + LANES]
                    else:
                        block = block + fars[hh][0 if delta > 0 else 1]
                    prob = jnp.exp(block)
                    grad = prob * shifted[at : at + LANES, col : col + LANES]
                    if abs(delta) <= 1:
                        near_ref[hh, :, place : place + LANES] += grad
                    probs.append(prob.astype(BF))
                    score_grads.append(grad.astype(BF))
                probs_rows.append(jnp.concatenate(probs, 1))
                score_rows.append(jnp.concatenate(score_grads, 1))
        probs_all = jnp.concatenate(probs_rows, 0)
        scores_all = jnp.concatenate(score_rows, 0)
        value_grad = nn(probs_all, grads)
        dv_ref[rows, cols] = jnp.where(low_half, value_grad[:tile], value_grad[tile:]).astype(BF)
        key_grad = nn(scores_all, jnp.concatenate([queries, blockof_ref[start:stop, :]], 1))
        dk_ref[rows, cols] = jnp.where(
            low_half, key_grad[:tile, :LANES], key_grad[tile:, :LANES]
        ).astype(BF)
        acc_ref[start:stop, :] += tn(scores_all, masked_keys)
        for hh in range(2):
            for part in range(tile // LANES):
                at = hh * tile + part * LANES
                k_block = index * (tile // LANES) + part
                line = jnp.sum(key_grad[at : at + LANES, LANES:], 0, keepdims=True)
                far_sums[hh][0] += jnp.where(lane_row <= k_block - 2, line, 0.0)
                far_sums[hh][1] += jnp.where(lane_row >= k_block + 2, line, 0.0)
    dq_ref[:, cols] = acc_ref[...].astype(BF)
    for hh in range(2):
        turned = jnp.dot(flip, near_ref[hh], precision=HIGHEST, preferred_element_type=F32)
        turned = jnp.concatenate([turned, jnp.zeros((LANES, LANES), F32)], 1)
        turned = pltpu.roll(turned, 1, 1, stride=1, stride_axis=0)
        sums_ref[pl.ds(row + hh, 1), :] = jnp.sum(turned, 0, keepdims=True)
        last = lane_row == 0
        positive = jnp.sum(far_sums[hh][0], -1, keepdims=True)
        negative = jnp.sum(far_sums[hh][1], -1, keepdims=True)
        far_ref[pl.ds(row + hh, 1), :] = jnp.where(last, positive, jnp.where(lane_row == 1, negative, 0.0))


def bwd_table(tabg_ref, sums_ref, far_ref):
    offsets = 2 * LANES - iota((LANES, 4 * LANES), 1)
    onehot_buckets = (bucket_ids(offsets) == iota((LANES, 4 * LANES), 0)).astype(F32)
    table = lax.dot_general(
        sums_ref[...],
        onehot_buckets,
        (((1,), (1,)), ((), ())),
        precision=HIGHEST,
        preferred_element_type=F32,
    )
    lane = iota(tabg_ref.shape, 1)
    far = far_ref[...]
    table = table + jnp.where(lane == 31, far[:, 0:1], 0.0) + jnp.where(lane == 15, far[:, 1:2], 0.0)
    tabg_ref[...] = table


def bwd_kernel(
    q_ref,
    k_ref,
    v_ref,
    go_ref,
    ctx_ref,
    feat_ref,
    seg_ref,
    tabs_ref,
    dq_ref,
    dk_ref,
    dv_ref,
    tabg_ref,
    bias_ref,
    sums_ref,
    far_ref,
    segk_ref,
    blockof_ref,
    gofeat_ref,
    near_ref,
    acc_ref,
):
    bwd_setup(seg_ref, tabs_ref, bias_ref, sums_ref, far_ref, segk_ref, blockof_ref)

    def one_pair(pair, carry):
        bwd_pair(
            pair,
            q_ref,
            k_ref,
            v_ref,
            go_ref,
            ctx_ref,
            feat_ref,
            dq_ref,
            dk_ref,
            dv_ref,
            bias_ref,
            sums_ref,
            far_ref,
            segk_ref,
            blockof_ref,
            gofeat_ref,
            near_ref,
            acc_ref,
        )
        return carry

    lax.fori_loop(0, q_ref.shape[1] // LANES, one_pair, 0)
    bwd_table(tabg_ref, sums_ref, far_ref)


def k3_before(xs_ref, ctx_ref, wo, gain, middle_ref, ffn_ref, ffnt_ref):
    step = 256

    def one(i, carry):
        rows = pl.ds(pl.multiple_of(i * step, step), step)
        middle = xs_ref[rows, :].astype(F32) + nt(ctx_ref[rows, :], wo)
        middle_ref[rows, :] = middle
        low = (middle * rms_scale(middle) * gain).astype(BF)
        ffn_ref[rows, :] = low
        ffnt_ref[:, rows] = low.T
        return carry

    lax.fori_loop(0, middle_ref.shape[0] // step, one, 0)


def transpose_rows(src_ref, dst_ref):
    step = 256

    def one(i, carry):
        rows = pl.ds(pl.multiple_of(i * step, step), step)
        dst_ref[:, rows] = src_ref[rows, :].T
        return carry

    lax.fori_loop(0, src_ref.shape[0] // step, one, 0)


def ffn_rows(i, half, w_in, w_back, first, ffn_ref, cot_ref, hid_ref, gp_ref, up_ref, down_ref):
    rows = pl.ds(pl.multiple_of(i * half, half), half)
    hidden, slope = gelu_pair(nn(ffn_ref[rows, :], w_in))
    hidden = hidden.astype(BF)
    hid_ref[rows, :] = hidden
    grad_pre = (nn(cot_ref[rows, :], w_back) * slope).astype(BF)
    gp_ref[rows, :] = grad_pre
    up = nt(hidden, w_back)
    down = nt(grad_pre, w_in)

    @pl.when(first)
    def _():
        up_ref[rows, :] = up
        down_ref[rows, :] = down

    @pl.when(jnp.logical_not(first))
    def _():
        up_ref[rows, :] += up
        down_ref[rows, :] += down


def after_rows(rows, cot, up_ref, down_ref, gain, gain_ref, gm_ref, ca_ref, cat_ref):
    middle = gm_ref[rows, :]
    scale = rms_scale(middle)
    normed = middle * scale
    down = down_ref[rows, :]
    gain_ref[...] += jnp.sum(down * normed, 0, keepdims=True)
    grad = cot + rms_back(down, normed, scale, gain)
    gm_ref[rows, :] = grad
    low = grad.astype(BF)
    ca_ref[rows, :] = low
    cat_ref[:, rows] = low.T
    return middle + up_ref[rows, :]


def context_grad(ca_ref, wo, go_ref):
    step = 256

    def one(i, carry):
        rows = pl.ds(pl.multiple_of(i * step, step), step)
        go_ref[rows, :] = nn(ca_ref[rows, :], wo).astype(BF)
        return carry

    lax.fori_loop(0, ca_ref.shape[0] // step, one, 0)


def k3_plain(
    xs_ref,
    ctx_ref,
    cot_ref,
    gain_ref,
    wo_ref,
    wi_ref,
    wb_ref,
    out_ref,
    gm_ref,
    go_ref,
    ggain_ref,
    gwo_ref,
    gwi_ref,
    gwb_ref,
    ffn_ref,
    ffnt_ref,
    cott_ref,
    cotb_ref,
    hid_ref,
    gp_ref,
    up_ref,
    down_ref,
):
    length = ctx_ref.shape[0]
    half_rows = length // 2
    chunk = hid_ref.shape[1]
    gain = gain_ref[...]
    cotb_ref[...] = cot_ref[...].astype(BF)
    k3_before(xs_ref, ctx_ref, wo_ref[...], gain, gm_ref, ffn_ref, ffnt_ref)
    transpose_rows(cotb_ref, cott_ref)

    def one_chunk(k, carry):
        cols = pl.ds(pl.multiple_of(k * chunk, LANES), chunk)
        w_in, w_back = wi_ref[:, cols], wb_ref[:, cols]
        for i in range(2):
            ffn_rows(
                i, half_rows, w_in, w_back, k == 0, ffn_ref, cotb_ref, hid_ref, gp_ref, up_ref, down_ref
            )
        gwb_ref[:, cols] = nn(cott_ref[...], hid_ref[...]).astype(BF)
        gwi_ref[:, cols] = nn(ffnt_ref[...], gp_ref[...]).astype(BF)
        return carry

    lax.fori_loop(0, wi_ref.shape[1] // chunk, one_chunk, 0)
    ggain_ref[...] = jnp.zeros_like(ggain_ref)
    step = 256

    def finish_rows(i, carry):
        rows = pl.ds(pl.multiple_of(i * step, step), step)
        out_ref[rows, :] = after_rows(
            rows,
            cot_ref[rows, :],
            up_ref,
            down_ref,
            gain,
            ggain_ref,
            gm_ref,
            ffn_ref,
            cott_ref,
        )
        return carry

    lax.fori_loop(0, length // step, finish_rows, 0)
    context_grad(ffn_ref, wo_ref[...], go_ref)
    gwo_ref[...] = nn(cott_ref[...], ctx_ref[...]).astype(BF)


def low_transposed(xs_ref, gain, lowt_ref):
    step = 256

    def one(i, carry):
        rows = pl.ds(pl.multiple_of(i * step, step), step)
        lowt_ref[:, rows] = project_rows(xs_ref[rows, :], gain).T
        return carry

    lax.fori_loop(0, xs_ref.shape[0] // step, one, 0)


def input_rows(rows, xs_ref, gm_ref, grads, weights, gain, gain_out):
    down = sum(nt(grad[rows, :], flat(weight[...])) for grad, weight in zip(grads, weights))
    inputs = xs_ref[rows, :].astype(F32)
    scale = rms_scale(inputs)
    normed = inputs * scale
    gain_out[...] += jnp.sum(down * normed, 0, keepdims=True)
    return gm_ref[rows, :] + rms_back(down, normed, scale, gain)


def k5_plain(
    xs_ref,
    gm_ref,
    dq_ref,
    dk_ref,
    dv_ref,
    wq_ref,
    wk_ref,
    wv_ref,
    gain_ref,
    ig_ref,
    gwq_ref,
    gwk_ref,
    gwv_ref,
    again_ref,
    lowt_ref,
):
    gain = gain_ref[...]
    low_transposed(xs_ref, gain, lowt_ref)
    grads, weights = (dq_ref, dk_ref, dv_ref), (wq_ref, wk_ref, wv_ref)
    for grad, out in zip(grads, (gwq_ref, gwk_ref, gwv_ref)):
        out[...] = nn(lowt_ref[...], grad[...]).astype(BF)
    again_ref[...] = jnp.zeros_like(again_ref)
    step = 256

    def one(i, carry):
        rows = pl.ds(pl.multiple_of(i * step, step), step)
        ig_ref[rows, :] = input_rows(rows, xs_ref, gm_ref, grads, weights, gain, again_ref)
        return carry

    lax.fori_loop(0, xs_ref.shape[0] // step, one, 0)


def run_all(steps):
    for step in steps:
        step()


def at_step(index, plan):
    for number, steps in enumerate(plan):
        if steps:

            @pl.when(index == number)
            def _(steps=steps):
                run_all(steps)


def attend_fused(
    depth,
    x_ref,
    cot_ref,
    gain_ref,
    tab_ref,
    seg_ref,
    wq_shard,
    wk_shard,
    wv_shard,
    wo_shard,
    wi_shard,
    wb_shard,
    xs_out,
    coto_ref,
    tabs_ref,
    q_out,
    k_out,
    v_out,
    ctx_ref,
    feat_ref,
    wq_out,
    wk_out,
    wv_out,
    wo_out,
    wi_out,
    wb_out,
    xs_ref,
    cotf_ref,
    cotb_ref,
    q_ref,
    k_ref,
    v_ref,
    wq_ref,
    wk_ref,
    wv_ref,
    wo_ref,
    wi_ref,
    wb_ref,
    low_ref,
    bias_ref,
    segq_ref,
    segk_ref,
    r_send,
    r_recv,
    g_send,
    g_recv,
    x_send,
    x_recv,
    l_sem,
):
    p = Place(depth)
    half_rows = x_ref.shape[1]
    width = wq_shard.shape[1]
    early, part = wi_ref.shape[0], wi_ref.shape[-1] // 2
    x_sems, g_sems = (x_send, x_recv), (g_send, g_recv)
    weights = (wq_ref, wk_ref, wv_ref)
    heads = [GatherX(p, ref, width, (r_send, r_recv), i, True) for i, ref in enumerate(weights)]
    for item, shard in zip(heads, (wq_shard, wk_shard, wv_shard)):
        item.ref[p.z, p.y, p.c, :, item.cols(p.t)] = shard[...]
    cot_load = local(cot_ref.at[1 - p.t], cotf_ref, l_sem.at[0])
    cot_load.start()
    tabs_ref[p.t] = tab_ref[...]
    p.barrier()
    for item in heads:
        item.start()
    moves = [
        remote(x_ref.at[1 - p.t], xs_ref.at[p.t], x_sems, 0, p.xpeer),
        remote(tabs_ref.at[p.t], tabs_ref.at[p.t], x_sems, 1, p.xpeer),
        remote(cotb_ref, coto_ref, x_sems, 2, p.xpeer),
    ]
    moves[0].start()
    moves[1].start()
    xs_ref[p.t] = x_ref[p.t]
    out_item = Gather(p, wo_ref, width, g_sems, 0, True)
    out_item.ref[p.z, p.y, p.c, :, out_item.cols(p.t)] = wo_shard[...]
    chunks = []
    for k in range(early):
        pair = []
        for side, (ref, shard) in enumerate(((wi_ref, wi_shard), (wb_ref, wb_shard))):
            item = Gather(p, ref.at[k], part, g_sems, 1 + 2 * k + side, True)
            item.ref[p.z, p.y, p.c, :, item.cols(p.t)] = shard[:, k * part : (k + 1) * part]
            pair.append(item)
        chunks.append(pair)

    def chunk(k, name):
        return [getattr(item, name) for item in chunks[k]] if k < early else []

    def rows_of(half):
        return pl.ds(pl.multiple_of(half * half_rows, half_rows), half_rows)

    low_ref[rows_of(p.t), :] = project_rows(x_ref[p.t], gain_ref[...])
    for item in heads:
        item.step1()
    fwd_setup_early = moves[1].wait_recv
    for item in heads:
        item.step2(0)
        item.step2(1)
    out_item.start()
    cot_load.wait()
    cotb_ref[...] = cotf_ref[...].astype(BF)
    fwd_setup_early()
    fwd_setup(seg_ref, tabs_ref, bias_ref, segq_ref, segk_ref)
    moves[0].wait_recv()
    moves[2].start()
    low_ref[rows_of(1 - p.t), :] = project_rows(xs_ref[1 - p.t], gain_ref[...])
    saves = [local(xs_ref, xs_out, l_sem.at[1])]
    saves[0].start()
    heads[0].step3()
    heads[0].finish()
    project(low_ref, wq_ref, q_ref)
    heads[1].step3()
    run_all(chunk(0, "start"))
    heads[1].finish()
    project(low_ref, wk_ref, k_ref)
    heads[2].step3()
    out_item.step1()
    heads[2].finish()
    project(low_ref, wv_ref, v_ref)
    for i, (src, dst) in enumerate(
        zip((q_ref, k_ref, v_ref) + weights, (q_out, k_out, v_out, wq_out, wk_out, wv_out))
    ):
        saves.append(local(src, dst, l_sem.at[2 + i]))
        saves[-1].start()

    def save(src, dst, index):
        return lambda: local(src, dst, l_sem.at[index]).start()

    def save_chunk(k):
        if k >= early:
            return []
        return [
            save(wi_ref.at[k], wi_out.at[k], 9 + 2 * k),
            save(wb_ref.at[k], wb_out.at[k], 10 + 2 * k),
        ]

    plan = [
        chunk(0, "step1") + [out_item.step2] + chunk(1, "start"),
        chunk(0, "step2") + [out_item.step3] + chunk(1, "step1") + chunk(2, "start"),
        chunk(0, "step3") + chunk(1, "step2") + [out_item.finish, save(wo_ref, wo_out, 8)],
        chunk(0, "finish") + save_chunk(0) + chunk(1, "step3") + chunk(2, "step1"),
        chunk(1, "finish") + save_chunk(1) + chunk(2, "step2"),
        chunk(2, "step3"),
    ]

    def one_pair(pair, carry):
        at_step(pair, plan)
        fwd_pair(pair, q_ref, k_ref, v_ref, ctx_ref, feat_ref, bias_ref, segq_ref, segk_ref)
        return carry

    lax.fori_loop(0, q_ref.shape[1] // LANES, one_pair, 0)
    run_all(chunk(2, "finish") + save_chunk(2))
    moves[2].wait_recv()
    for move in moves:
        move.wait_send()
    for one in saves:
        one.wait()
    local(wo_ref, wo_out, l_sem.at[8]).wait()
    for k in range(early):
        local(wi_ref.at[k], wi_out.at[k], l_sem.at[9 + 2 * k]).wait()
        local(wb_ref.at[k], wb_out.at[k], l_sem.at[10 + 2 * k]).wait()


def ffn_fused(
    depth,
    early,
    here,
    xs_ref,
    ctx_ref,
    cot_ref,
    coto_ref,
    gain_ref,
    wo_ref,
    wi_in,
    wb_in,
    wi_shard,
    wb_shard,
    out_ref,
    gm_ref,
    go_ref,
    ggain_ref,
    gwo_ref,
    gwi_ref,
    gwb_ref,
    gi_out,
    gb_out,
    wi_ref,
    wb_ref,
    gout_ref,
    ffn_ref,
    ffnt_ref,
    cott_ref,
    cotf_ref,
    cotb_ref,
    hid_ref,
    gp_ref,
    up_ref,
    down_ref,
    obuf_ref,
    obuf2_ref,
    o0,
    o1,
    o2,
    o3,
    i0,
    i1,
    i2,
    i3,
    b0,
    b1,
    b2,
    b3,
    g_send,
    g_recv,
    s_send,
    s_recv,
    x_send,
    x_recv,
    l_sem,
):
    p = Place(depth)
    length = ctx_ref.shape[0]
    half_rows = length // 2
    chunks = wi_ref.shape[0]
    width = gwo_ref.shape[1]
    part = wi_ref.shape[-1] // 2
    g_sems, s_sems, x_sems = (g_send, g_recv), (s_send, s_recv), (x_send, x_recv)
    late = chunks - early

    def g_chunk(k):
        return (
            Gather(p, wi_ref.at[k], part, g_sems, 2 * (k - early), True),
            Gather(p, wb_ref.at[k], part, g_sems, 1 + 2 * (k - early), False),
        )

    def s_chunk(k):
        return (
            Scatter(
                p, wi_ref.at[k], part, [r.at[k] for r in (i0, i1, i2, i3)], s_sems, 1 + 2 * k, True
            ),
            Scatter(
                p, wb_ref.at[k], part, [r.at[k] for r in (b0, b1, b2, b3)], s_sems, 2 + 2 * k, False
            ),
        )

    def load_chunk(k):
        return (
            local(wi_in.at[k], wi_ref.at[k], l_sem.at[1 + 2 * k]),
            local(wb_in.at[k], wb_ref.at[k], l_sem.at[2 + 2 * k]),
        )

    def save_chunk(k):
        return (
            local(wi_ref.at[k], gi_out.at[k - here], l_sem.at[1 + 2 * k]),
            local(wb_ref.at[k], gb_out.at[k - here], l_sem.at[2 + 2 * k]),
        )

    def when_gather(k, name):
        @pl.when((k >= early) & (k < chunks))
        def _():
            for item in g_chunk(k):
                getattr(item, name)()

    def when_scatter(k, name):
        @pl.when((k >= 0) & (k < here))
        def _():
            for item, out in zip(s_chunk(k), (gwi_ref, gwb_ref)):
                if name == "finish":
                    item.finish(out, k * part)
                else:
                    getattr(item, name)()

    cot_load = local(cot_ref.at[p.t], cotf_ref, l_sem.at[0])
    cot_load.start()
    for k in range(early):
        for one in load_chunk(k):
            one.start()
    for k in range(early, chunks):
        for item, shard in zip(g_chunk(k), (wi_shard, wb_shard)):
            item.ref[p.z, p.y, p.c, :, item.cols(p.t)] = shard[:, k * part : (k + 1) * part]
    p.barrier()
    when_gather(early, "start")
    when_gather(early + 1, "start")
    gain = gain_ref[...]
    k3_before(xs_ref, ctx_ref, flat(wo_ref[...]), gain, gm_ref, ffn_ref, ffnt_ref)
    when_gather(early, "step1")
    cotb_ref[1 - p.t] = coto_ref[...]
    cot_load.wait()
    cotb_ref[p.t] = cotf_ref[...].astype(BF)
    cotb = cotb_ref.reshape(length, cotb_ref.shape[2])
    transpose_rows(cotb, cott_ref)
    when_gather(early, "step2")

    def one_chunk(k, carry):
        when_gather(k + early, "step3")
        when_gather(k + early + 1, "step1")
        when_gather(k + early + 2, "start")

        @pl.when(k < early)
        def _():
            for one in load_chunk(k):
                one.wait()

        @pl.when(k >= early)
        def _():
            for item in g_chunk(k):
                item.finish()

        when_scatter(k - 2, "step2")
        w_in, w_back = flat(wi_ref[k]), flat(wb_ref[k])
        args = (w_in, w_back, k == 0, ffn_ref, cotb, hid_ref, gp_ref, up_ref, down_ref)
        ffn_rows(0, half_rows, *args)
        when_scatter(k - 1, "step1")
        when_gather(k + early + 1, "step2")
        ffn_rows(1, half_rows, *args)
        when_scatter(k - 3, "step3")
        wb_ref[k] = nn(cott_ref[...], hid_ref[...]).astype(BF).reshape(wb_ref.shape[1:])
        when_scatter(k - 4, "finish")
        wi_ref[k] = nn(ffnt_ref[...], gp_ref[...]).astype(BF).reshape(wi_ref.shape[1:])
        when_scatter(k, "step0")

        @pl.when(k >= here)
        def _():
            for one in save_chunk(k):
                one.start()

        return carry

    lax.fori_loop(0, chunks, one_chunk, 0)
    ggain_ref[...] = jnp.zeros_like(ggain_ref)
    step = 256

    def finish_rows(own, i):
        half = p.t if own else 1 - p.t
        at = pl.ds(pl.multiple_of(i * step, step), step)
        rows = pl.ds(pl.multiple_of(half * half_rows + i * step, step), step)
        cot = cotf_ref[at, :] if own else cotb_ref[1 - p.t, at, :].astype(F32)
        out = after_rows(
            rows, cot, up_ref, down_ref, gain, ggain_ref, gm_ref, ffn_ref, cott_ref
        )
        if own:
            out_ref[p.t, at, :] = out
        else:
            obuf_ref[at, :] = out.astype(BF)

    for i in range(half_rows // step):
        finish_rows(False, i)
    out_move = remote(obuf_ref, obuf2_ref, x_sems, 0, p.xpeer)
    out_move.start()
    for stage, name in ((1, "step1"), (2, "step2"), (3, "step3"), (4, "finish")):
        for k in range(max(0, chunks - stage), here):
            when_scatter(k, name)
    for i in range(half_rows // step):
        finish_rows(True, i)
    gout_ref[...] = nn(cott_ref[...], ctx_ref[...]).astype(BF).reshape(gout_ref.shape)
    s_out = Scatter(p, gout_ref, width, (o0, o1, o2, o3), s_sems, 0, True)
    s_out.step0()
    context_grad(ffn_ref, flat(wo_ref[...]), go_ref)
    s_out.step1()
    s_out.step2()
    s_out.step3()
    out_move.wait_recv()
    out_ref[1 - p.t] = obuf2_ref[...].astype(F32)
    s_out.finish(gwo_ref, 0)
    out_move.wait_send()
    for k in range(here, chunks):
        for one in save_chunk(k):
            one.wait()


def back_fused(
    depth,
    q_in,
    k_in,
    v_in,
    go_ref,
    ctx_ref,
    feat_ref,
    seg_ref,
    tabs_ref,
    xs_in,
    gm_in,
    wq_in,
    wk_in,
    wv_in,
    gain_ref,
    ggain_ref,
    gi_in,
    gb_in,
    ig_ref,
    gwq_ref,
    gwk_ref,
    gwv_ref,
    gwi_ref,
    gwb_ref,
    small_ref,
    q_ref,
    k_ref,
    v_ref,
    xs_ref,
    gm_ref,
    wq_ref,
    wk_ref,
    wv_ref,
    gi_ref,
    gb_ref,
    lowt_ref,
    sum_ref,
    gq_ref,
    gk_ref,
    gv_ref,
    ibuf_ref,
    ibuf2_ref,
    again_ref,
    tabg_ref,
    sm_ref,
    smr_ref,
    bias_ref,
    sums_ref,
    far_ref,
    segk_ref,
    blockof_ref,
    gofeat_ref,
    near_ref,
    acc_ref,
    i0,
    i1,
    i2,
    i3,
    b0,
    b1,
    b2,
    b3,
    a0,
    a1,
    a2,
    a3,
    c0,
    c1,
    c2,
    c3,
    d0,
    d1,
    d2,
    d3,
    s_send,
    s_recv,
    x_send,
    x_recv,
    l_sem,
):
    p = Place(depth)
    length = q_ref.shape[0]
    half_rows = length // 2
    groups = gq_ref.shape[0]
    rest, part = gi_ref.shape[0], gi_ref.shape[-1] // 2
    s_sems, x_sems = (s_send, s_recv), (x_send, x_recv)
    pairs = [(q_in, q_ref), (k_in, k_ref), (v_in, v_ref), (xs_in, xs_ref)]
    pairs += [(gi_in, gi_ref), (gb_in, gb_ref), (gm_in, gm_ref)]
    pairs += [(wq_in, wq_ref), (wk_in, wk_ref), (wv_in, wv_ref)]
    loads = [local(src, dst, l_sem.at[i]) for i, (src, dst) in enumerate(pairs)]
    for one in loads:
        one.start()
    bwd_setup(seg_ref, tabs_ref, bias_ref, sums_ref, far_ref, segk_ref, blockof_ref)
    p.barrier()
    rest_items = []
    for k in range(rest):
        rest_items.append(
            [
                Scatter(
                    p, gi_ref.at[k], part, [r.at[k] for r in (i0, i1, i2, i3)], s_sems, 2 * k, True
                ),
                Scatter(
                    p,
                    gb_ref.at[k],
                    part,
                    [r.at[k] for r in (b0, b1, b2, b3)],
                    s_sems,
                    2 * k + 1,
                    False,
                ),
            ]
        )
    group_items = []
    for j in range(groups):
        group_items.append(
            [
                Scatter(
                    p,
                    ref.at[j],
                    LANES,
                    [r.at[j] for r in bufs],
                    s_sems,
                    2 * rest + 3 * j + i,
                    i != 1,
                )
                for i, (ref, bufs) in enumerate(
                    (
                        (gq_ref, (a0, a1, a2, a3)),
                        (gk_ref, (c0, c1, c2, c3)),
                        (gv_ref, (d0, d1, d2, d3)),
                    )
                )
            ]
        )

    def chunk(k, name):
        if k >= rest:
            return []
        if name == "finish":
            return [
                functools.partial(item.finish, out, k * part)
                for item, out in zip(rest_items[k], (gwi_ref, gwb_ref))
            ]
        return [getattr(item, name) for item in rest_items[k]]

    def group(j, name):
        if name == "finish":
            return [
                functools.partial(item.finish, out, j * LANES)
                for item, out in zip(group_items[j], (gwq_ref, gwk_ref, gwv_ref))
            ]
        return [getattr(item, name) for item in group_items[j]]

    for one in loads[:6]:
        one.wait()
    run_all(chunk(0, "step0"))
    xs = xs_ref.reshape(length, xs_ref.shape[2])
    gain = gain_ref[...]
    low_transposed(xs, gain, lowt_ref)
    run_all(chunk(0, "step1") + chunk(1, "step0"))
    for one in loads[6:]:
        one.wait()

    def group_cols(ref, j):
        return [ref[:, pair_cols(j)], ref[:, pair_cols(j + groups)]]

    def weight_grads(j):
        for target, grad in zip((gq_ref, gk_ref, gv_ref), (q_ref, k_ref, v_ref)):
            both = jnp.concatenate(group_cols(grad, j), 1)
            target[j] = nn(lowt_ref[...], both).astype(BF).reshape(target.shape[1:])

    def group_weights(j):
        pieces = []
        for weight in (wq_ref, wk_ref, wv_ref):
            for at in (j, j + groups):
                pieces.append(flat(weight[:, :, :, :, pair_cols(at)]))
        return jnp.concatenate(pieces, 1)

    def group_sum(rows, j):
        pieces = []
        for grad in (q_ref, k_ref, v_ref):
            for at in (j, j + groups):
                pieces.append(grad[rows, pair_cols(at)])
        return nt(jnp.concatenate(pieces, 1), group_weights(j))

    step = 256
    plan = [
        [],
        chunk(0, "step2") + chunk(1, "step1") + chunk(2, "step0"),
        chunk(0, "step3") + chunk(1, "step2") + chunk(2, "step1"),
        chunk(0, "finish") + chunk(1, "step3") + chunk(2, "step2") + group(0, "step1"),
        chunk(1, "finish") + chunk(2, "step3") + group(0, "step2"),
        chunk(2, "finish") + group(0, "step3") + group(1, "step1"),
    ]

    def one_pair(index, carry):
        at_step(index, plan)
        j, side = lax.div(index, 2), lax.rem(index, 2)
        bwd_pair(
            j + groups * side,
            q_ref,
            k_ref,
            v_ref,
            go_ref,
            ctx_ref,
            feat_ref,
            q_ref,
            k_ref,
            v_ref,
            bias_ref,
            sums_ref,
            far_ref,
            segk_ref,
            blockof_ref,
            gofeat_ref,
            near_ref,
            acc_ref,
        )

        @pl.when(side == 1)
        def _():
            weight_grads(j)
            for i in range(groups):

                @pl.when(j == i)
                def _():
                    run_all(group(i, "step0"))

            for i in range(groups - 1):

                @pl.when(j == i)
                def _():
                    for at in range(length // step):
                        rows = slice(at * step, (at + 1) * step)
                        if i == 0:
                            sum_ref[rows, :] = group_sum(rows, i)
                        else:
                            sum_ref[rows, :] += group_sum(rows, i)

        return carry

    lax.fori_loop(0, 2 * groups, one_pair, 0)
    bwd_table(tabg_ref, sums_ref, far_ref)
    again_ref[...] = jnp.zeros_like(again_ref)
    last = groups - 1

    def finish_rows(own, i):
        half = p.t if own else 1 - p.t
        at = pl.ds(pl.multiple_of(i * step, step), step)
        rows = pl.ds(pl.multiple_of(half * half_rows + i * step, step), step)
        down = sum_ref[rows, :] + group_sum(rows, last)
        inputs = xs_ref[half, at, :].astype(F32)
        scale = rms_scale(inputs)
        normed = inputs * scale
        again_ref[...] += jnp.sum(down * normed, 0, keepdims=True)
        out = gm_ref[rows, :] + rms_back(down, normed, scale, gain)
        if own:
            ig_ref[p.t, at, :] = out
        else:
            ibuf_ref[at, :] = out.astype(BF)

    moves = []
    for i in range(half_rows // step):
        finish_rows(False, i)
        at = pl.ds(i * step, step)
        moves.append(remote(ibuf_ref.at[at], ibuf2_ref.at[at], x_sems, i, p.xpeer))
        moves[-1].start()
    run_all(group(last, "step1") + group(1, "step2") + group(0, "finish"))
    for i in range(half_rows // step):
        finish_rows(True, i)
    model = again_ref.shape[1]
    sm_ref[0, 0:1, :model] = again_ref[...]
    sm_ref[0, 1:2, :model] = ggain_ref[...]
    sm_ref[0, 2:8, :model] = jnp.zeros((6, model), F32)
    sm_ref[0, :, model : model + LANES] = tabg_ref[0:8, :]
    sm_ref[0, :, model + LANES :] = tabg_ref[8:16, :]
    hops = [(p.sib,), (p.ypeer,), (p.xpeer,), tuple(p.zpeers)]
    slot = 0
    beside = [
        group(last, "step2"),
        group(1, "step3"),
        group(last, "step3"),
        group(1, "finish"),
    ]
    for level, peers in enumerate(hops):
        hop = [
            remote(sm_ref.at[level], smr_ref.at[slot + i], x_sems, len(moves) + slot + i, peer)
            for i, peer in enumerate(peers)
        ]
        for one in hop:
            one.start()
        run_all(beside[level])
        total = sm_ref[level]
        for i, one in enumerate(hop):
            one.wait_recv()
            total = total + smr_ref[slot + i]
        slot += len(peers)
        if level + 1 < len(hops):
            sm_ref[level + 1] = total
        else:
            small_ref[...] = total
        for one in hop:
            one.wait_send()
    run_all(group(last, "finish"))
    for i, move in enumerate(moves):
        move.wait_recv()
        at = pl.ds(i * step, step)
        ig_ref[1 - p.t, at, :] = ibuf2_ref[at, :].astype(F32)
        move.wait_send()


def call(kernel, outs, scratch, args, name, collective=None, far=()):
    def spec(array):
        return pl.BlockSpec(memory_space=pl.ANY if array in far else pltpu.VMEM)

    if collective is None:
        params = pltpu.CompilerParams(vmem_limit_bytes=VMEM_BYTES)
    else:
        params = pltpu.CompilerParams(
            vmem_limit_bytes=VMEM_BYTES, collective_id=collective, has_side_effects=True
        )
    return pl.pallas_call(
        kernel,
        out_shape=[jax.ShapeDtypeStruct(shape, dtype) for shape, dtype in outs],
        in_specs=[spec(i) for i in range(len(args))],
        out_specs=[spec(len(args) + i) for i in range(len(outs))],
        scratch_shapes=scratch,
        compiler_params=params,
        name=name,
    )(*args)


def shards(
    inputs,
    segments,
    norm_attn,
    norm_ffn,
    w_query,
    w_key,
    w_value,
    w_out,
    w_in,
    w_back,
    rel_table,
    cotangent,
):
    dp, tensor = lax.axis_size("dp"), lax.axis_size("tensor")
    t = lax.axis_index("tensor")
    rows, width = w_query.shape
    hidden_part = w_in.shape[1]
    model = inputs.shape[2]
    length = segments.shape[2]
    half = inputs.shape[1]
    buckets, heads = rel_table.shape
    depth = dp // 4
    fused = rows % 16 == 0 and dp % 4 == 0 and depth >= 2
    gain_attn, gain_ffn = norm_attn.reshape(1, model), norm_ffn.reshape(1, model)
    table = jnp.pad(rel_table.T, ((0, 8 - heads), (0, LANES - buckets)))
    segment = lax.dynamic_index_in_dim(segments[:, 0], t, 0, False).reshape(length, 1)
    full = (length, model)
    inner = (length, width * tensor)
    square = (depth, 2, 2, rows, 2 * width)
    part = 256
    chunks = hidden_part // part
    pairs = inner[1] // LANES
    dma = pltpu.SemaphoreType.DMA
    halves = (2, half, model)
    fwd_work = [pltpu.VMEM((16, 4 * LANES), F32)] + [pltpu.VMEM((length, LANES), BF)] * 2
    bwd_work = [
        pltpu.VMEM((16, 4 * LANES), F32),
        pltpu.VMEM((16, 4 * LANES), F32),
        pltpu.VMEM((16, LANES), F32),
        pltpu.VMEM((length, LANES), BF),
        pltpu.VMEM((length, LANES), BF),
        pltpu.VMEM((length, LANES), BF),
        pltpu.VMEM((2, LANES, 3 * LANES), F32),
        pltpu.VMEM((length, LANES), F32),
    ]
    ffn_work = [pltpu.VMEM(full, BF), pltpu.VMEM(full[::-1], BF), pltpu.VMEM(full[::-1], BF)]
    rest = [pltpu.VMEM((length, 2 * part), BF)] * 2 + [pltpu.VMEM(full, F32)] * 2
    if fused:
        early = chunks // 2
        here = chunks // 2
        late = chunks - early
        block = (depth, 2, 2, rows, 2 * part)
        xs, coto, tabs, queries, keys, values, ctx, feats, wq, wk, wv, wo, wi, wb = call(
            functools.partial(attend_fused, depth),
            [
                (halves, BF),
                ((half, model), BF),
                ((2, 8, LANES), F32),
                (inner, BF),
                (inner, BF),
                (inner, BF),
                (inner, BF),
                ((pairs, length, LANES), BF),
                (square, BF),
                (square, BF),
                (square, BF),
                (square, BF),
                ((early,) + block, BF),
                ((early,) + block, BF),
            ],
            [pltpu.VMEM(halves, BF), pltpu.VMEM((half, model), F32), pltpu.VMEM((half, model), BF)]
            + [pltpu.VMEM(inner, BF)] * 3
            + [pltpu.VMEM(square, BF)] * 4
            + [pltpu.VMEM((early,) + block, BF)] * 2
            + [pltpu.VMEM(full, BF)]
            + fwd_work
            + [dma((3, 2 * depth + 5))] * 2
            + gather_sems(1 + 2 * early, depth)
            + [dma((3,)), dma((3,)), dma((9 + 2 * early,))],
            (
                inputs,
                cotangent,
                gain_attn,
                table,
                segment,
                w_query,
                w_key,
                w_value,
                w_out,
                w_in,
                w_back,
            ),
            "attention_forward",
            0,
            (1, 11, 14, 15, 16, 19, 20, 21, 22, 23, 24),
        )
        output, grad_middle, grad_context, ggain, gwo, gwi, gwb, gi, gb = call(
            functools.partial(ffn_fused, depth, early, here),
            [
                (halves, F32),
                (full, F32),
                (inner, BF),
                ((1, model), F32),
                ((rows, width), F32),
                ((rows, here * part), F32),
                ((rows, here * part), F32),
                ((chunks - here,) + block, BF),
                ((chunks - here,) + block, BF),
            ],
            [pltpu.VMEM((chunks,) + block, BF)] * 2
            + [pltpu.VMEM(square, BF)]
            + ffn_work
            + [pltpu.VMEM((half, model), F32), pltpu.VMEM(halves, BF)]
            + rest
            + [pltpu.VMEM((half, model), BF)] * 2
            + scatter_bufs(None, depth, rows, width, True)
            + scatter_bufs(here, depth, rows, part, True)
            + scatter_bufs(here, depth, rows, part, False)
            + gather_sems(2 * late, depth)
            + scatter_sems(1 + 2 * here, depth)
            + [dma((1,)), dma((1,)), dma((1 + 2 * chunks,))],
            (xs.reshape(full), ctx, cotangent, coto, gain_ffn, wo, wi, wb, w_in, w_back),
            "feed_forward",
            1,
            (2, 6, 7, 17, 18),
        )
        left = chunks - here
        groups = pairs // 2
        narrow = (groups, depth, 2, 2, rows, 2 * LANES)
        input_grad, gwq, gwk, gwv, gwi_rest, gwb_rest, small = call(
            functools.partial(back_fused, depth),
            [
                (halves, F32),
                ((rows, width), F32),
                ((rows, width), F32),
                ((rows, width), F32),
                ((rows, left * part), F32),
                ((rows, left * part), F32),
                ((8, model + 2 * LANES), F32),
            ],
            [pltpu.VMEM(inner, BF)] * 3
            + [pltpu.VMEM(halves, BF), pltpu.VMEM(full, F32)]
            + [pltpu.VMEM(square, BF)] * 3
            + [pltpu.VMEM((left,) + block, BF)] * 2
            + [pltpu.VMEM(full[::-1], BF), pltpu.VMEM(full, F32)]
            + [pltpu.VMEM(narrow, BF)] * 3
            + [pltpu.VMEM((half, model), BF)] * 2
            + [
                pltpu.VMEM((1, model), F32),
                pltpu.VMEM((16, LANES), F32),
                pltpu.VMEM((4, 8, model + 2 * LANES), F32),
                pltpu.VMEM((depth + 2, 8, model + 2 * LANES), F32),
            ]
            + bwd_work
            + scatter_bufs(left, depth, rows, part, True)
            + scatter_bufs(left, depth, rows, part, False)
            + scatter_bufs(groups, depth, rows, LANES, True)
            + scatter_bufs(groups, depth, rows, LANES, False)
            + scatter_bufs(groups, depth, rows, LANES, True)
            + scatter_sems(2 * left + 3 * groups, depth)
            + [dma((depth + 4,)), dma((depth + 4,)), dma((10,))],
            (
                queries,
                keys,
                values,
                grad_context,
                ctx,
                feats,
                segment,
                tabs,
                xs,
                grad_middle,
                wq,
                wk,
                wv,
                gain_attn,
                ggain,
                gi,
                gb,
            ),
            "attention_backward",
            2,
            (0, 1, 2, 8, 9, 10, 11, 12, 15, 16),
        )
        gwi = jnp.concatenate([gwi, gwi_rest], 1)
        gwb = jnp.concatenate([gwb, gwb_rest], 1)
        gain_attn_grad, gain_ffn_grad = small[0, :model], small[1, :model]
        tables = jnp.stack([small[:, model : model + LANES], small[:, model + LANES :]])
    else:

        def whole(weight):
            weight = lax.all_gather(weight, "dp", axis=0, tiled=True)
            return lax.all_gather(weight, "tensor", axis=1, tiled=True)

        def exchanged(local_part):
            own = lax.dynamic_index_in_dim(local_part, t, 0, False)
            other = lax.dynamic_index_in_dim(local_part, 1 - t, 0, False)
            other = lax.ppermute(other, "tensor", [(0, 1), (1, 0)])
            first = jnp.where(t == 0, own, other)
            second = jnp.where(t == 0, other, own)
            return jnp.concatenate([first, second], 0)

        def returned(seq):
            mine = lax.dynamic_slice_in_dim(seq, t * half, half, 0)
            other = lax.dynamic_slice_in_dim(seq, (1 - t) * half, half, 0)
            other = lax.ppermute(other, "tensor", [(0, 1), (1, 0)])
            return jnp.stack([jnp.where(t == 0, mine, other), jnp.where(t == 0, other, mine)])

        def scattered(grad):
            grad = lax.psum_scatter(grad.astype(F32), "tensor", scatter_dimension=1, tiled=True)
            return lax.psum_scatter(grad, "dp", scatter_dimension=0, tiled=True)

        xs = exchanged(inputs)
        tabs = lax.all_gather(table, "tensor", axis=0)
        wq, wk, wv, wo, wi, wb = (
            whole(w) for w in (w_query, w_key, w_value, w_out, w_in, w_back)
        )
        queries, keys, values = call(
            k1_plain,
            [(inner, BF)] * 3,
            [pltpu.VMEM(full, BF)],
            (xs, gain_attn, wq, wk, wv),
            "project",
        )
        ctx, feats = call(
            fwd_kernel,
            [(inner, BF), ((pairs, length, LANES), BF)],
            fwd_work,
            (queries, keys, values, segment, tabs),
            "attention_forward",
        )
        out_seq, grad_middle, grad_context, ggain, gwo, gwi, gwb = call(
            k3_plain,
            [
                (full, F32),
                (full, F32),
                (inner, BF),
                ((1, model), F32),
                (wo.shape, BF),
                (wi.shape, BF),
                (wb.shape, BF),
            ],
            ffn_work + [pltpu.VMEM(full, BF)] + rest,
            (xs, ctx, exchanged(cotangent), gain_ffn, wo, wi, wb),
            "feed_forward",
        )
        output = returned(out_seq)
        gwo, gwi, gwb = scattered(gwo), scattered(gwi), scattered(gwb)
        dq, dk, dv, table_grad = call(
            bwd_kernel,
            [(inner, BF), (inner, BF), (inner, BF), ((16, LANES), F32)],
            bwd_work,
            (queries, keys, values, grad_context, ctx, feats, segment, tabs),
            "attention_backward",
        )
        ig_seq, gwq, gwk, gwv, again = call(
            k5_plain,
            [(full, F32), (wq.shape, BF), (wk.shape, BF), (wv.shape, BF), ((1, model), F32)],
            [pltpu.VMEM((model, length), BF)],
            (xs, grad_middle, dq, dk, dv, wq, wk, wv, gain_attn),
            "projection_gradients",
        )
        input_grad = returned(ig_seq)
        gwq, gwk, gwv = scattered(gwq), scattered(gwk), scattered(gwv)
        again, ggain, tables = lax.psum((again, ggain, table_grad), ("dp", "tensor"))
        gain_attn_grad, gain_ffn_grad = again[0], ggain[0]
        tables = tables.reshape(2, 8, LANES)
    table_out = lax.dynamic_index_in_dim(tables, t, 0, False)[:heads, :buckets].T
    return (
        output,
        input_grad,
        gain_attn_grad,
        gain_ffn_grad,
        gwq,
        gwk,
        gwv,
        gwo,
        gwi,
        gwb,
        table_out,
    )


def solution(mesh):
    weight = P("dp", "tensor")
    tokens = P(None, ("dp", "tensor"), None)
    return jax.shard_map(
        shards,
        mesh=mesh,
        in_specs=(
            tokens,
            P(None, "dp", None),
            P(),
            P(),
            weight,
            weight,
            weight,
            weight,
            weight,
            weight,
            P(None, "tensor"),
            tokens,
        ),
        out_specs=(
            tokens,
            tokens,
            P(),
            P(),
            weight,
            weight,
            weight,
            weight,
            weight,
            weight,
            P(None, "tensor"),
        ),
        check_vma=False,
    )
```

```python
import functools

import jax
import jax.numpy as jnp
from jax import lax
from jax.experimental import pallas as pl
from jax.experimental.pallas import tpu as pltpu
from jax.sharding import PartitionSpec as P

MESH = pl.DeviceIdType.MESH
BF = jnp.bfloat16
F32 = jnp.float32
HIGHEST = lax.Precision.HIGHEST
EPSILON = 1e-06
THRESHOLDS = (12, 16, 23, 32, 46, 64, 91)
MASK_OUT = -float(2**30)
DH = 64
SPAN = 512
LANES = 128
VMEM_BYTES = 62 * 2**20


def nn(left, right):
    return lax.dot_general(left, right, (((1,), (0,)), ((), ())), preferred_element_type=F32)


def nt(left, right):
    return lax.dot_general(left, right, (((1,), (1,)), ((), ())), preferred_element_type=F32)


def tn(left, right):
    return lax.dot_general(left, right, (((0,), (0,)), ((), ())), preferred_element_type=F32)


def iota(shape, dim):
    return lax.broadcasted_iota(jnp.int32, shape, dim)


def bucket_ids(offsets):
    distance = jnp.abs(offsets)
    far_ids = 8 + sum((distance >= threshold).astype(jnp.int32) for threshold in THRESHOLDS)
    return jnp.where(offsets > 0, 16, 0) + jnp.where(distance < 8, distance, far_ids)


def rms_scale(values):
    return lax.rsqrt(jnp.mean(values * values, -1, keepdims=True) + EPSILON)


def rms_back(grad_normed, normed, scale, gain):
    scaled = grad_normed * gain
    return scale * (scaled - normed * jnp.mean(scaled * normed, -1, keepdims=True))


def gelu_pair(v):
    square = v * v
    half = 0.5 + 0.5 * jnp.tanh(v * (0.7978845608028654 + 0.035677408136300125 * square))
    slope = half + v * half * (1.0 - half) * (1.5957691216057308 + 0.2140644488178007 * square)
    return v * half, slope


class Place:
    def __init__(self, depth):
        d, t = lax.axis_index("dp"), lax.axis_index("tensor")
        self.t = t
        self.z, self.y, self.c = lax.div(d, 4), lax.rem(lax.div(d, 2), 2), lax.rem(d, 2)
        self.depth = depth
        self.sib = (d + 1 - 2 * self.c, t)
        self.ypeer = (d + 2 - 4 * self.y, t)
        self.xpeer = (d, 1 - t)
        rest = self.rest = lax.rem(d, 4)
        self.zs = [lax.rem(self.z + step, depth) for step in range(1, depth)]
        self.zpeers = [(z * 4 + rest, t) for z in self.zs]

    def barrier(self):
        semaphore = pltpu.get_barrier_semaphore()
        peers = [self.sib, self.ypeer, self.xpeer] + self.zpeers
        for peer in peers:
            pl.semaphore_signal(semaphore, inc=1, device_id=peer, device_id_type=MESH)
        pl.semaphore_wait(semaphore, len(peers))


class Copy:
    def __init__(self, **parts):
        self.parts = parts

    def made(self):
        return pltpu.make_async_remote_copy(device_id_type=MESH, **self.parts)

    def start(self):
        self.made().start()

    def wait_recv(self):
        self.made().wait_recv()

    def wait_send(self):
        self.made().wait_send()


def local(src, dst, sem):
    return pltpu.make_async_copy(src, dst, sem)


def remote(src, dst, sems, index, peer):
    send, recv = sems
    return Copy(
        src_ref=src, dst_ref=dst, send_sem=send.at[index], recv_sem=recv.at[index], device_id=peer
    )


class Gather:
    def __init__(self, place, ref, width, sems, item, x_first):
        self.p, self.ref, self.width, self.sems, self.item = place, ref, width, sems, item
        p = place
        self.relays = p.depth == 4
        if x_first:
            self.peers, order = (p.xpeer, p.ypeer), ((0, 0), (0, 1), (1, 0), (1, 1))
        else:
            self.peers, order = (p.ypeer, p.xpeer), ((0, 0), (1, 0), (0, 1), (1, 1))
        self.sides = [(p.y + (1 - 2 * p.y) * i, p.t + (1 - 2 * p.t) * j) for i, j in order]

    def cols(self, x):
        return pl.ds(pl.multiple_of(x * self.width, LANES), self.width)

    def block(self, z, side):
        y, x = self.sides[side]
        return self.ref.at[z, y, self.p.c, :, self.cols(x)]

    def region(self, side):
        y, x = self.sides[side]
        return self.ref.at[:, y, self.p.c, :, self.cols(x)]

    def send(self, index, src, peer):
        return remote(src, src, self.sems, (self.item, index), peer)

    def first(self):
        return self.send(0, self.block(self.p.z, 0), self.peers[0])

    def along(self, side):
        p = self.p
        base = 1 + side * len(p.zpeers)
        return [self.send(base + i, self.block(p.z, side), peer) for i, peer in enumerate(p.zpeers)]

    def last(self, side):
        return self.send(1 + 2 * len(self.p.zpeers) + side, self.region(side), self.peers[1])

    def sib(self, side):
        return self.send(3 + 2 * len(self.p.zpeers) + side, self.region(side), self.p.sib)

    def relay(self, side):
        p = self.p
        send, recv = self.sems
        src = self.block(lax.rem(p.z + 2, 4), side)
        low = p.z == 1
        target = jnp.where(low, 0, 3)
        return Copy(
            src_ref=src,
            dst_ref=src,
            send_sem=send.at[self.item, 7 + 2 * len(p.zpeers) + side],
            recv_sem=recv.at[self.item, 1 + side * len(p.zpeers) + jnp.where(low, 0, 2)],
            device_id=(target * 4 + p.rest, p.t),
        )

    def each_along(self, side, method):
        p = self.p
        for i, copy in enumerate(self.along(side)):
            if self.relays and i != 1:
                pl.when(p.z != (3 if i == 0 else 0))(getattr(copy, method))
            else:
                getattr(copy, method)()

    def inside(self, action):
        pl.when((self.p.z == 1) | (self.p.z == 2))(action)

    def start(self):
        self.first().start()

    def start_z(self):
        self.each_along(0, "start")

    def step1(self):
        self.first().wait_recv()
        self.each_along(1, "start")

    def step2(self, side):
        zs = self.along(side)
        if self.relays:
            zs[1].wait_recv()
            self.inside(self.relay(side).start)
            zs = [zs[0], zs[2]]
        for copy in zs:
            copy.wait_recv()
        self.last(side).start()
        self.sib(side).start()

    def step3(self):
        for side in range(2):
            self.last(side).wait_recv()
            self.sib(2 + side).start()

    def finish(self):
        for side in range(4):
            self.sib(side).wait_recv()
        self.first().wait_send()
        for side in range(2):
            self.each_along(side, "wait_send")
            if self.relays:
                self.inside(self.relay(side).wait_send)
            self.last(side).wait_send()
        for side in range(4):
            self.sib(side).wait_send()


def gather_sems(items, depth):
    return [pltpu.SemaphoreType.DMA((items, 2 * depth + 7))] * 2


class Scatter:
    def __init__(self, place, ref, width, bufs, sems, item, y_first):
        self.p, self.ref, self.width, self.sems, self.item = place, ref, width, sems, item
        self.r0, self.r1, self.r2, self.r3 = bufs
        self.y_first = y_first

    def cols(self, x):
        return pl.ds(pl.multiple_of(x * self.width, LANES), self.width)

    def copies(self):
        p, ref = self.p, self.ref
        sib = remote(ref.at[:, :, 1 - p.c], self.r0, self.sems, (self.item, 0), p.sib)
        if self.y_first:
            half = remote(ref.at[:, 1 - p.y, p.c], self.r1, self.sems, (self.item, 1), p.ypeer)
            quarter = remote(
                ref.at[:, p.y, p.c, :, self.cols(1 - p.t)],
                self.r2,
                self.sems,
                (self.item, 2),
                p.xpeer,
            )
        else:
            half = remote(
                ref.at[:, :, p.c, :, self.cols(1 - p.t)],
                self.r1,
                self.sems,
                (self.item, 1),
                p.xpeer,
            )
            quarter = remote(
                ref.at[:, 1 - p.y, p.c, :, self.cols(p.t)],
                self.r2,
                self.sems,
                (self.item, 2),
                p.ypeer,
            )
        zs = [
            remote(
                ref.at[z, p.y, p.c, :, self.cols(p.t)],
                self.r3.at[i],
                self.sems,
                (self.item, 3 + i),
                peer,
            )
            for i, (z, peer) in enumerate(zip(p.zs, p.zpeers))
        ]
        return sib, half, quarter, zs

    def step0(self):
        self.copies()[0].start()

    def step1(self):
        p = self.p
        sib, half, _, _ = self.copies()
        sib.wait_recv()
        kept = self.ref.at[:, :, p.c]
        kept[...] = (kept[...].astype(F32) + self.r0[...].astype(F32)).astype(BF)
        half.start()

    def step2(self):
        p = self.p
        _, half, quarter, _ = self.copies()
        half.wait_recv()
        if self.y_first:
            kept = self.ref.at[:, p.y, p.c]
        else:
            kept = self.ref.at[:, :, p.c, :, self.cols(p.t)]
        kept[...] = (kept[...].astype(F32) + self.r1[...].astype(F32)).astype(BF)
        quarter.start()

    def step3(self):
        p = self.p
        _, _, quarter, zs = self.copies()
        quarter.wait_recv()
        kept = self.ref.at[:, p.y, p.c, :, self.cols(p.t)]
        kept[...] = (kept[...].astype(F32) + self.r2[...].astype(F32)).astype(BF)
        for copy in zs:
            copy.start()

    def finish(self, out, offset):
        p = self.p
        sib, half, quarter, zs = self.copies()
        for copy in zs:
            copy.wait_recv()
        total = self.ref[p.z, p.y, p.c, :, self.cols(p.t)].astype(F32)
        for i in range(len(zs)):
            total = total + self.r3[i].astype(F32)
        out[:, pl.ds(pl.multiple_of(offset, LANES), self.width)] = total
        for copy in [sib, half, quarter] + zs:
            copy.wait_send()


def scatter_bufs(items, depth, rows, width, y_first):
    lead = () if items is None else (items,)
    return [
        pltpu.VMEM(lead + (depth, 2, rows, 2 * width), BF),
        pltpu.VMEM(lead + ((depth, rows, 2 * width) if y_first else (depth, 2, rows, width)), BF),
        pltpu.VMEM(lead + (depth, rows, width), BF),
        pltpu.VMEM(lead + (depth - 1, rows, width), BF),
    ]


def scatter_sems(items, depth):
    return [pltpu.SemaphoreType.DMA((items, depth + 2))] * 2


def flat(values):
    if len(values.shape) == 2:
        return values
    return values.reshape(-1, values.shape[-1])


def project_rows(x_rows, gain):
    rows = x_rows.astype(F32)
    return (rows * rms_scale(rows) * gain).astype(BF)


def project(low_ref, w_ref, out_ref):
    weight = flat(w_ref[...])
    half = low_ref.shape[0] // 2

    def one(i, carry):
        rows = pl.ds(pl.multiple_of(i * half, half), half)
        out_ref[rows, :] = nn(low_ref[rows, :], weight).astype(BF)
        return carry

    lax.fori_loop(0, 2, one, 0)


def k1_plain(x_ref, gain_ref, wq_ref, wk_ref, wv_ref, q_ref, k_ref, v_ref, low_ref):
    low_ref[...] = project_rows(x_ref[...], gain_ref[...])
    for weight, out in ((wq_ref, q_ref), (wk_ref, k_ref), (wv_ref, v_ref)):
        project(low_ref, weight, out)


def bias_rows(tabs_ref, out_ref, flipped):
    offsets = iota((LANES, 4 * LANES), 1) - 2 * LANES
    onehot = (bucket_ids(-offsets if flipped else offsets) == iota((LANES, 4 * LANES), 0)).astype(F32)
    for half in range(2):
        out_ref[half * 8 : half * 8 + 8, :] = jnp.dot(
            tabs_ref[half], onehot, precision=HIGHEST, preferred_element_type=F32
        )


def head_row(pair, per_half):
    return 8 * lax.div(pair, per_half) + 2 * lax.rem(pair, per_half)


def bias_strip(row):
    spread = jnp.broadcast_to(row, (LANES, 4 * LANES))
    return pltpu.roll(spread, 3 * LANES, 1, stride=1, stride_axis=0)


def window(tile, rows, length):
    reach = -(-SPAN // rows)
    return max(0, (tile - reach) * rows), min(length, (tile + reach + 1) * rows)


def segment_lanes(seg):
    length = seg.shape[1]
    onehot = (seg == iota((LANES, length), 0)).astype(F32).T > 0.5
    inside = iota((length, LANES), 1) < 16
    return onehot, inside


def pair_cols(pair):
    return pl.ds(pl.multiple_of(pair * LANES, LANES), LANES)


def spread3(value):
    top = value.astype(BF).astype(F32)
    mid = (value - top).astype(BF).astype(F32)
    return top, mid, value - top - mid


TILE = 256
NEAR = SPAN // LANES


def key_lanes(seg):
    onehot, inside = segment_lanes(seg)
    return jnp.where(onehot, 0.0, jnp.where(inside, 1.0, 0.0)).astype(BF)


def fwd_setup(seg, tabs_ref, bias_ref, segq_ref, segk_ref):
    bias_rows(tabs_ref, bias_ref, False)
    onehot, _ = segment_lanes(seg)
    segq_ref[...] = jnp.where(onehot, MASK_OUT, 0.0).astype(BF)
    segk_ref[...] = key_lanes(seg)


def fwd_pair(pair, q_ref, k_ref, v_ref, ctx_ref, feat_ref, bias_ref, segq_ref, segk_ref):
    length, width = q_ref.shape
    per_half = width // LANES // 2
    tile, near = TILE, NEAR
    cols = pair_cols(pair)
    row = head_row(pair, per_half)
    lane = iota((tile, LANES), 1)
    low_half = lane < DH
    strips, fars = [], []
    for hh in range(2):
        line = bias_ref[pl.ds(row + hh, 1), :]
        strips.append(bias_strip(line))
        fars.append((line[:, 0:1], line[:, 4 * LANES - 1 : 4 * LANES]))
    for index in range(length // tile):
        rows = slice(index * tile, (index + 1) * tile)
        start, stop = window(index, tile, length)
        queries = q_ref[rows, cols]
        zero = jnp.zeros_like(queries)
        q_feat = segq_ref[rows, :]
        left = jnp.concatenate(
            [
                jnp.concatenate([jnp.where(low_half, queries, zero), q_feat], 1),
                jnp.concatenate([jnp.where(low_half, zero, queries), q_feat], 1),
            ],
            0,
        )
        right = jnp.concatenate([k_ref[start:stop, cols], segk_ref[start:stop, :]], 1)
        scores = nt(left, right)
        weights, peaks = [], []
        for hh in range(2):
            for part in range(tile // LANES):
                at = hh * tile + part * LANES
                q_block = index * (tile // LANES) + part
                blocks = []
                for k_block in range(start // LANES, stop // LANES):
                    delta = k_block - q_block
                    if abs(delta) > near:
                        blocks.append(None)
                        continue
                    col = k_block * LANES - start
                    block = scores[at : at + LANES, col : col + LANES]
                    if abs(delta) <= 1:
                        block = block + strips[hh][:, (delta + 1) * LANES : (delta + 2) * LANES]
                    else:
                        block = block + fars[hh][0 if delta < 0 else 1]
                    blocks.append(block)
                real = [block for block in blocks if block is not None]
                peak = functools.reduce(jnp.maximum, real)
                peak = jnp.max(peak, -1, keepdims=True)
                peaks.append(peak)
                weights.append(
                    jnp.concatenate(
                        [
                            jnp.zeros((LANES, LANES), BF)
                            if block is None
                            else jnp.exp(block - peak).astype(BF)
                            for block in blocks
                        ],
                        1,
                    )
                )
        values = v_ref[start:stop, cols]
        gathered = nn(
            jnp.concatenate(weights, 0), jnp.concatenate([values, jnp.ones_like(values)], 1)
        )
        normal = gathered[:, :LANES] / gathered[:, LANES:]
        context = jnp.where(low_half, normal[:tile], normal[tile:])
        ctx_ref[rows, cols] = context.astype(BF)
        logs = jnp.concatenate(peaks, 0) + jnp.log(gathered[:, LANES:])
        feature = q_feat.astype(F32)
        for hh in range(2):
            for i, piece in enumerate(spread3(logs[hh * tile : (hh + 1) * tile])):
                feature = jnp.where(lane == 16 + 3 * hh + i, -piece, feature)
        feat_ref[pair, rows, :] = feature.astype(BF)


def fwd_kernel(
    q_ref, k_ref, v_ref, seg_ref, tabs_ref, ctx_ref, feat_ref, bias_ref, segq_ref, segk_ref
):
    fwd_setup(seg_ref[...], tabs_ref, bias_ref, segq_ref, segk_ref)

    def one_pair(pair, carry):
        fwd_pair(pair, q_ref, k_ref, v_ref, ctx_ref, feat_ref, bias_ref, segq_ref, segk_ref)
        return carry

    lax.fori_loop(0, q_ref.shape[1] // LANES, one_pair, 0)


def bwd_setup(seg, tabs_ref, bias_ref, sums_ref, far_ref, segk_ref, blockof_ref):
    length = seg.shape[1]
    bias_rows(tabs_ref, bias_ref, True)
    sums_ref[...] = jnp.zeros_like(sums_ref)
    far_ref[...] = jnp.zeros_like(far_ref)
    segk_ref[...] = key_lanes(seg)
    blockof_ref[...] = (
        lax.div(iota((length, LANES), 0), LANES) == iota((length, LANES), 1)
    ).astype(BF)


def bwd_pair(
    pair,
    q_ref,
    k_ref,
    v_ref,
    go_ref,
    ctx_ref,
    feat_ref,
    dq_ref,
    dk_ref,
    dv_ref,
    bias_ref,
    sums_ref,
    far_ref,
    segk_ref,
    blockof_ref,
    gofeat_ref,
    near_ref,
    acc_ref,
):
    length, width = q_ref.shape
    per_half = width // LANES // 2
    tile, near = TILE, NEAR
    flip = (iota((LANES, LANES), 0) + iota((LANES, LANES), 1) == LANES - 1).astype(F32)
    cols = pair_cols(pair)
    row = head_row(pair, per_half)
    lane = iota((tile, LANES), 1)
    low_half = lane < DH
    strips, fars = [], []
    for hh in range(2):
        line = bias_ref[pl.ds(row + hh, 1), :]
        strips.append(bias_strip(line))
        fars.append((line[:, 0:1], line[:, 4 * LANES - 1 : 4 * LANES]))
    grads_all = go_ref[:, cols]
    product = grads_all.astype(F32) * ctx_ref[:, cols].astype(F32)
    lane_all = iota((length, LANES), 1)
    feature = jnp.zeros((length, LANES), F32)
    for hh in range(2):
        keep = (lane_all < DH) if hh == 0 else (lane_all >= DH)
        total = jnp.sum(jnp.where(keep, product, 0.0), -1, keepdims=True)
        for i, piece in enumerate(spread3(total)):
            feature = jnp.where(lane_all == 3 * hh + i, -piece, feature)
    gofeat_ref[...] = feature.astype(BF)
    near_ref[...] = jnp.zeros_like(near_ref)
    acc_ref[...] = jnp.zeros_like(acc_ref)
    far_sums = [[jnp.zeros((1, LANES), F32) for _ in range(2)] for _ in range(2)]
    lane_row = iota((1, LANES), 1)
    for index in range(length // tile):
        rows = slice(index * tile, (index + 1) * tile)
        start, stop = window(index, tile, length)
        keys, values = k_ref[rows, cols], v_ref[rows, cols]
        zero = jnp.zeros_like(keys)
        seg_feat = segk_ref[rows, :].astype(F32)

        def ones_at(base, first):
            return jnp.where((lane >= first) & (lane < first + 3), 1.0, base).astype(BF)

        masked_keys = jnp.concatenate(
            [jnp.where(low_half, keys, zero), jnp.where(low_half, zero, keys)], 0
        )
        masked_values = jnp.concatenate(
            [jnp.where(low_half, values, zero), jnp.where(low_half, zero, values)], 0
        )
        key_feats = jnp.concatenate([ones_at(seg_feat, 16), ones_at(seg_feat, 19)], 0)
        value_feats = jnp.concatenate([ones_at(0.0, 0), ones_at(0.0, 3)], 0)
        queries = q_ref[start:stop, cols]
        grads = go_ref[start:stop, cols]
        logits = nt(
            jnp.concatenate([masked_keys, key_feats], 1),
            jnp.concatenate([queries, feat_ref[pair, start:stop, :]], 1),
        )
        shifted = nt(
            jnp.concatenate([masked_values, value_feats], 1),
            jnp.concatenate([grads, gofeat_ref[start:stop, :]], 1),
        )
        probs_rows, score_rows = [], []
        for hh in range(2):
            for part in range(tile // LANES):
                at = hh * tile + part * LANES
                k_block = index * (tile // LANES) + part
                probs, score_grads = [], []
                for q_block in range(start // LANES, stop // LANES):
                    delta = k_block - q_block
                    if abs(delta) > near:
                        probs.append(jnp.zeros((LANES, LANES), BF))
                        score_grads.append(jnp.zeros((LANES, LANES), BF))
                        continue
                    col = q_block * LANES - start
                    block = logits[at : at + LANES, col : col + LANES]
                    place = (1 - delta) * LANES
                    if abs(delta) <= 1:
                        block = block + strips[hh][:, place : place + LANES]
                    else:
                        block = block + fars[hh][0 if delta > 0 else 1]
                    prob = jnp.exp(block)
                    grad = prob * shifted[at : at + LANES, col : col + LANES]
                    if abs(delta) <= 1:
                        near_ref[hh, :, place : place + LANES] += grad
                    probs.append(prob.astype(BF))
                    score_grads.append(grad.astype(BF))
                probs_rows.append(jnp.concatenate(probs, 1))
                score_rows.append(jnp.concatenate(score_grads, 1))
        probs_all = jnp.concatenate(probs_rows, 0)
        scores_all = jnp.concatenate(score_rows, 0)
        value_grad = nn(probs_all, grads)
        dv_ref[rows, cols] = jnp.where(low_half, value_grad[:tile], value_grad[tile:]).astype(BF)
        key_grad = nn(scores_all, jnp.concatenate([queries, blockof_ref[start:stop, :]], 1))
        dk_ref[rows, cols] = jnp.where(
            low_half, key_grad[:tile, :LANES], key_grad[tile:, :LANES]
        ).astype(BF)
        acc_ref[start:stop, :] += tn(scores_all, masked_keys)
        for hh in range(2):
            for part in range(tile // LANES):
                at = hh * tile + part * LANES
                k_block = index * (tile // LANES) + part
                line = jnp.sum(key_grad[at : at + LANES, LANES:], 0, keepdims=True)
                far_sums[hh][0] += jnp.where(lane_row <= k_block - 2, line, 0.0)
                far_sums[hh][1] += jnp.where(lane_row >= k_block + 2, line, 0.0)
    dq_ref[:, cols] = acc_ref[...].astype(BF)
    for hh in range(2):
        turned = jnp.dot(flip, near_ref[hh], precision=HIGHEST, preferred_element_type=F32)
        turned = jnp.concatenate([turned, jnp.zeros((LANES, LANES), F32)], 1)
        turned = pltpu.roll(turned, 1, 1, stride=1, stride_axis=0)
        sums_ref[pl.ds(row + hh, 1), :] = jnp.sum(turned, 0, keepdims=True)
        last = lane_row == 0
        positive = jnp.sum(far_sums[hh][0], -1, keepdims=True)
        negative = jnp.sum(far_sums[hh][1], -1, keepdims=True)
        far_ref[pl.ds(row + hh, 1), :] = jnp.where(last, positive, jnp.where(lane_row == 1, negative, 0.0))


def bwd_table(tabg_ref, sums_ref, far_ref):
    offsets = 2 * LANES - iota((LANES, 4 * LANES), 1)
    onehot_buckets = (bucket_ids(offsets) == iota((LANES, 4 * LANES), 0)).astype(F32)
    table = lax.dot_general(
        sums_ref[...],
        onehot_buckets,
        (((1,), (1,)), ((), ())),
        precision=HIGHEST,
        preferred_element_type=F32,
    )
    lane = iota(tabg_ref.shape, 1)
    far = far_ref[...]
    table = table + jnp.where(lane == 31, far[:, 0:1], 0.0) + jnp.where(lane == 15, far[:, 1:2], 0.0)
    tabg_ref[...] = table


def bwd_kernel(
    q_ref,
    k_ref,
    v_ref,
    go_ref,
    ctx_ref,
    feat_ref,
    seg_ref,
    tabs_ref,
    dq_ref,
    dk_ref,
    dv_ref,
    tabg_ref,
    bias_ref,
    sums_ref,
    far_ref,
    segk_ref,
    blockof_ref,
    gofeat_ref,
    near_ref,
    acc_ref,
):
    bwd_setup(seg_ref[...], tabs_ref, bias_ref, sums_ref, far_ref, segk_ref, blockof_ref)

    def one_pair(pair, carry):
        bwd_pair(
            pair,
            q_ref,
            k_ref,
            v_ref,
            go_ref,
            ctx_ref,
            feat_ref,
            dq_ref,
            dk_ref,
            dv_ref,
            bias_ref,
            sums_ref,
            far_ref,
            segk_ref,
            blockof_ref,
            gofeat_ref,
            near_ref,
            acc_ref,
        )
        return carry

    lax.fori_loop(0, q_ref.shape[1] // LANES, one_pair, 0)
    bwd_table(tabg_ref, sums_ref, far_ref)


def k3_before(xs_ref, ctx_ref, wo, gain, middle_ref, ffn_ref, ffnt_ref):
    step = 256

    def one(i, carry):
        rows = pl.ds(pl.multiple_of(i * step, step), step)
        middle = xs_ref[rows, :].astype(F32) + nt(ctx_ref[rows, :], wo)
        middle_ref[rows, :] = middle
        low = (middle * rms_scale(middle) * gain).astype(BF)
        ffn_ref[rows, :] = low
        ffnt_ref[:, rows] = low.T
        return carry

    lax.fori_loop(0, middle_ref.shape[0] // step, one, 0)


def transpose_rows(src_ref, dst_ref):
    step = 256

    def one(i, carry):
        rows = pl.ds(pl.multiple_of(i * step, step), step)
        dst_ref[:, rows] = src_ref[rows, :].T
        return carry

    lax.fori_loop(0, src_ref.shape[0] // step, one, 0)


def ffn_rows(i, half, w_in, w_back, first, ffn_ref, cot_ref, hid_ref, gp_ref, up_ref, down_ref):
    rows = pl.ds(pl.multiple_of(i * half, half), half)
    hidden, slope = gelu_pair(nn(ffn_ref[rows, :], w_in))
    hidden = hidden.astype(BF)
    hid_ref[rows, :] = hidden
    grad_pre = (nn(cot_ref[rows, :], w_back) * slope).astype(BF)
    gp_ref[rows, :] = grad_pre
    up = nt(hidden, w_back)
    down = nt(grad_pre, w_in)

    @pl.when(first)
    def _():
        up_ref[rows, :] = up
        down_ref[rows, :] = down

    @pl.when(jnp.logical_not(first))
    def _():
        up_ref[rows, :] += up
        down_ref[rows, :] += down


def after_rows(rows, cot, up_ref, down_ref, gain, gain_ref, gm_ref, ca_ref, cat_ref):
    middle = gm_ref[rows, :]
    scale = rms_scale(middle)
    normed = middle * scale
    down = down_ref[rows, :]
    gain_ref[...] += jnp.sum(down * normed, 0, keepdims=True)
    grad = cot + rms_back(down, normed, scale, gain)
    gm_ref[rows, :] = grad
    low = grad.astype(BF)
    ca_ref[rows, :] = low
    cat_ref[:, rows] = low.T
    return middle + up_ref[rows, :]


def context_grad(ca_ref, wo, go_ref):
    step = 256

    def one(i, carry):
        rows = pl.ds(pl.multiple_of(i * step, step), step)
        go_ref[rows, :] = nn(ca_ref[rows, :], wo).astype(BF)
        return carry

    lax.fori_loop(0, ca_ref.shape[0] // step, one, 0)


def k3_plain(
    xs_ref,
    ctx_ref,
    cot_ref,
    gain_ref,
    wo_ref,
    wi_ref,
    wb_ref,
    out_ref,
    gm_ref,
    go_ref,
    ggain_ref,
    gwo_ref,
    gwi_ref,
    gwb_ref,
    ffn_ref,
    ffnt_ref,
    cott_ref,
    cotb_ref,
    hid_ref,
    gp_ref,
    up_ref,
    down_ref,
):
    length = ctx_ref.shape[0]
    half_rows = length // 2
    chunk = hid_ref.shape[1]
    gain = gain_ref[...]
    cotb_ref[...] = cot_ref[...].astype(BF)
    k3_before(xs_ref, ctx_ref, wo_ref[...], gain, gm_ref, ffn_ref, ffnt_ref)
    transpose_rows(cotb_ref, cott_ref)

    def one_chunk(k, carry):
        cols = pl.ds(pl.multiple_of(k * chunk, LANES), chunk)
        w_in, w_back = wi_ref[:, cols], wb_ref[:, cols]
        for i in range(2):
            ffn_rows(
                i, half_rows, w_in, w_back, k == 0, ffn_ref, cotb_ref, hid_ref, gp_ref, up_ref, down_ref
            )
        gwb_ref[:, cols] = nn(cott_ref[...], hid_ref[...]).astype(BF)
        gwi_ref[:, cols] = nn(ffnt_ref[...], gp_ref[...]).astype(BF)
        return carry

    lax.fori_loop(0, wi_ref.shape[1] // chunk, one_chunk, 0)
    ggain_ref[...] = jnp.zeros_like(ggain_ref)
    step = 256

    def finish_rows(i, carry):
        rows = pl.ds(pl.multiple_of(i * step, step), step)
        out_ref[rows, :] = after_rows(
            rows,
            cot_ref[rows, :],
            up_ref,
            down_ref,
            gain,
            ggain_ref,
            gm_ref,
            ffn_ref,
            cott_ref,
        )
        return carry

    lax.fori_loop(0, length // step, finish_rows, 0)
    context_grad(ffn_ref, wo_ref[...], go_ref)
    gwo_ref[...] = nn(cott_ref[...], ctx_ref[...]).astype(BF)


def low_transposed(xs_ref, gain, lowt_ref):
    step = 256

    def one(i, carry):
        rows = pl.ds(pl.multiple_of(i * step, step), step)
        lowt_ref[:, rows] = project_rows(xs_ref[rows, :], gain).T
        return carry

    lax.fori_loop(0, xs_ref.shape[0] // step, one, 0)


def input_rows(rows, xs_ref, gm_ref, grads, weights, gain, gain_out):
    down = sum(nt(grad[rows, :], flat(weight[...])) for grad, weight in zip(grads, weights))
    inputs = xs_ref[rows, :].astype(F32)
    scale = rms_scale(inputs)
    normed = inputs * scale
    gain_out[...] += jnp.sum(down * normed, 0, keepdims=True)
    return gm_ref[rows, :] + rms_back(down, normed, scale, gain)


def k5_plain(
    xs_ref,
    gm_ref,
    dq_ref,
    dk_ref,
    dv_ref,
    wq_ref,
    wk_ref,
    wv_ref,
    gain_ref,
    ig_ref,
    gwq_ref,
    gwk_ref,
    gwv_ref,
    again_ref,
    lowt_ref,
):
    gain = gain_ref[...]
    low_transposed(xs_ref, gain, lowt_ref)
    grads, weights = (dq_ref, dk_ref, dv_ref), (wq_ref, wk_ref, wv_ref)
    for grad, out in zip(grads, (gwq_ref, gwk_ref, gwv_ref)):
        out[...] = nn(lowt_ref[...], grad[...]).astype(BF)
    again_ref[...] = jnp.zeros_like(again_ref)
    step = 256

    def one(i, carry):
        rows = pl.ds(pl.multiple_of(i * step, step), step)
        ig_ref[rows, :] = input_rows(rows, xs_ref, gm_ref, grads, weights, gain, again_ref)
        return carry

    lax.fori_loop(0, xs_ref.shape[0] // step, one, 0)


def as_row(vector):
    return vector.reshape(1, vector.shape[-1])


def turned_table(tab_ref, turn_ref):
    turn_ref[...] = jnp.zeros_like(turn_ref)
    turn_ref[: tab_ref.shape[0], : tab_ref.shape[1]] = tab_ref[...]
    return turn_ref[...].T[:8, :]


def run_all(steps):
    for step in steps:
        step()


def at_step(index, plan):
    for number, steps in enumerate(plan):
        if steps:

            @pl.when(index == number)
            def _(steps=steps):
                run_all(steps)


def forward_fused(
    depth,
    here,
    x_in,
    cot_in,
    gain_in,
    ffn_gain_in,
    tab_ref,
    seg_ref,
    wq_shard,
    wk_shard,
    wv_shard,
    wo_shard,
    wi_shard,
    wb_shard,
    xs_out,
    tabs_ref,
    q_out,
    k_out,
    v_out,
    ctx_out,
    feat_out,
    wq_out,
    wk_out,
    wv_out,
    own_out,
    oth_out,
    gm_out,
    go_out,
    ggain_ref,
    gout_out,
    gwi_ref,
    gwb_ref,
    gi_out,
    gb_out,
    xs_ref,
    cotf_ref,
    cotb_ref,
    obuf_ref,
    q_ref,
    k_ref,
    v_ref,
    ctx_ref,
    feat_ref,
    wq_ref,
    wk_ref,
    wv_ref,
    wo_ref,
    wi_ref,
    wb_ref,
    low_ref,
    turn_ref,
    bias_ref,
    segq_ref,
    segk_ref,
    gm_ref,
    ffnt_ref,
    cott_ref,
    up_ref,
    down_ref,
    i0,
    i1,
    i2,
    i3,
    b0,
    b1,
    b2,
    b3,
    r_send,
    r_recv,
    g_send,
    g_recv,
    s_send,
    s_recv,
    x_send,
    x_recv,
    l_sem,
    c_sem,
):
    p = Place(depth)
    length = q_ref.shape[0]
    half_rows = length // 2
    width = wo_shard.shape[1]
    groups = wq_ref.shape[0]
    chunks, part = wi_ref.shape[0], wi_ref.shape[-1] // 2
    x_sems, g_sems, r_sems, s_sems = (
        (x_send, x_recv),
        (g_send, g_recv),
        (r_send, r_recv),
        (s_send, s_recv),
    )
    gain, ffn_gain = as_row(gain_in[...]), as_row(ffn_gain_in[...])
    weights = (wq_ref, wk_ref, wv_ref)
    x_own = local(x_in.at[p.t], xs_ref.at[p.t], l_sem.at[0])
    x_own.start()
    cot_load = local(cot_in.at[1 - p.t], cotf_ref, l_sem.at[1])
    cot_load.start()
    heads = []
    for j in range(groups):
        trio = []
        for i, (ref, shard) in enumerate(zip(weights, (wq_shard, wk_shard, wv_shard))):
            item = Gather(p, ref.at[j], LANES, r_sems, 3 * j + i, True)
            item.block(p.z, 0)[...] = shard[:, j * LANES : (j + 1) * LANES]
            trio.append(item)
        heads.append(trio)
    tabs_ref[p.t] = turned_table(tab_ref, turn_ref)
    p.barrier()
    moves = [
        remote(x_in.at[1 - p.t], xs_ref.at[p.t], x_sems, 0, p.xpeer),
        remote(tabs_ref.at[p.t], tabs_ref.at[p.t], x_sems, 1, p.xpeer),
        remote(obuf_ref, cotb_ref.at[p.t], x_sems, 2, p.xpeer),
    ]

    def head(j, name):
        return [getattr(item, name) for item in heads[j]]

    def both(items):
        return [functools.partial(item.step2, side) for side in range(2) for item in items]

    run_all(head(0, "start") + head(1, "start") + head(2, "start"))
    moves[1].start()
    moves[0].start()
    run_all(head(0, "start_z") + head(1, "start_z"))
    out_item = Gather(p, wo_ref, width, g_sems, 0, True)
    out_item.block(p.z, 0)[...] = wo_shard[...]
    items = []
    for k in range(chunks):
        pair = []
        for side, (ref, shard) in enumerate(((wi_ref, wi_shard), (wb_ref, wb_shard))):
            item = Gather(p, ref.at[k], part, g_sems, 1 + 2 * k + side, side == 0 or k < 2)
            item.block(p.z, 0)[...] = shard[:, k * part : (k + 1) * part]
            pair.append(item)
        items.append(pair)

    def chunk(k, *names):
        steps = []
        for name in names if k < chunks else ():
            if name == "both":
                steps += both(items[k])
            else:
                steps += [getattr(item, name) for item in items[k]]
        return steps

    def rows_of(half):
        return pl.ds(pl.multiple_of(half * half_rows, half_rows), half_rows)

    run_all(head(0, "step1") + head(1, "step1") + head(2, "start_z"))
    x_own.wait()
    low_ref[rows_of(p.t), :] = project_rows(xs_ref[p.t], gain)
    run_all(both(heads[0]) + head(2, "step1"))
    cot_load.wait()
    obuf_ref[...] = cotf_ref[...].astype(BF)
    own_load = local(cot_in.at[p.t], cotf_ref, l_sem.at[1])
    own_load.start()
    run_all(both(heads[1]))
    moves[1].wait_recv()
    fwd_setup(seg_ref[p.t], tabs_ref, bias_ref, segq_ref, segk_ref)
    run_all(head(0, "step3"))
    moves[0].wait_recv()
    run_all([out_item.start])
    for k in range(chunks):
        run_all(chunk(k, "start"))
    moves[2].start()
    low_ref[rows_of(1 - p.t), :] = project_rows(xs_ref[1 - p.t], gain)
    run_all(both(heads[2]) + [out_item.start_z, out_item.step1] + head(0, "finish"))

    def save(index, src, dst):
        return local(src, dst, l_sem.at[index])

    saves = [
        save(2 + i, src, dst)
        for i, (src, dst) in enumerate(
            (
                (xs_ref, xs_out),
                (wq_ref, wq_out),
                (wk_ref, wk_out),
                (wv_ref, wv_out),
                (ctx_ref, ctx_out),
                (feat_ref, feat_out),
                (obuf_ref, oth_out),
                (cotf_ref, own_out),
                (gm_ref, gm_out),
                (v_ref, go_out),
                (wo_ref, gout_out),
            )
        )
    ]
    qkv_saves = [
        save(13 + i, src, dst)
        for i, (src, dst) in enumerate(((q_ref, q_out), (k_ref, k_out), (v_ref, v_out)))
    ]

    def project_group(j):
        for weight, out in zip(weights, (q_ref, k_ref, v_ref)):
            value = flat(weight[j])

            def one(i, carry):
                rows = pl.ds(pl.multiple_of(i * half_rows, half_rows), half_rows)
                result = nn(low_ref[rows, :], value).astype(BF)
                out[rows, pair_cols(j)] = result[:, :LANES]
                out[rows, pair_cols(j + groups)] = result[:, LANES:]
                return carry

            lax.fori_loop(0, 2, one, 0)

    plan = [
        head(1, "step3") + chunk(0, "start_z", "step1"),
        head(2, "step3") + both([out_item]) + chunk(1, "start_z", "step1"),
        head(1, "finish") + chunk(0, "both") + [out_item.step3] + chunk(2, "start_z", "step1"),
        chunk(1, "both") + chunk(0, "step3") + chunk(3, "start_z", "step1"),
        head(2, "finish") + [out_item.finish] + chunk(2, "both") + chunk(1, "step3"),
        chunk(0, "finish")
        + chunk(3, "both")
        + chunk(2, "step3")
        + chunk(4, "start_z", "step1")
        + [one.start for one in qkv_saves + saves[:4]],
    ]

    def one_pair(index, carry):
        j, side = lax.div(index, 2), lax.rem(index, 2)
        at_step(index, plan)

        @pl.when(side == 0)
        def _():
            project_group(j)

        pair = j + groups * side
        fwd_pair(pair, q_ref, k_ref, v_ref, ctx_ref, feat_ref, bias_ref, segq_ref, segk_ref)
        return carry

    lax.fori_loop(0, 2 * groups, one_pair, 0)
    saves[4].start()
    saves[5].start()
    xs = xs_ref.reshape(length, xs_ref.shape[2])
    k3_before(xs, ctx_ref, flat(wo_ref[...]), ffn_gain, gm_ref, low_ref, ffnt_ref)
    run_all(chunk(3, "step3") + chunk(4, "both"))
    moves[2].wait_recv()
    moves[2].wait_send()
    own_load.wait()
    cotb_ref[p.t] = cotf_ref[...].astype(BF)
    cotb = cotb_ref.reshape(length, cotb_ref.shape[2])
    transpose_rows(cotb, cott_ref)
    for one in qkv_saves:
        one.wait()
    hid_ref, gp_ref = q_ref.at[:, : 2 * part], k_ref.at[:, : 2 * part]

    def s_chunk(k):
        return (
            Scatter(
                p, wi_ref.at[k], part, [r.at[k] for r in (i0, i1, i2, i3)], s_sems, 2 * k, True
            ),
            Scatter(
                p, wb_ref.at[k], part, [r.at[k] for r in (b0, b1, b2, b3)], s_sems, 1 + 2 * k, False
            ),
        )

    def save_chunk(k):
        return (
            local(wi_ref.at[k], gi_out.at[k - here], c_sem.at[2 * k]),
            local(wb_ref.at[k], gb_out.at[k - here], c_sem.at[1 + 2 * k]),
        )

    def when_scatter(k, name):
        @pl.when((k >= 0) & (k < here))
        def _():
            for item, out in zip(s_chunk(k), (gwi_ref, gwb_ref)):
                if name == "finish":
                    item.finish(out, k * part)
                else:
                    getattr(item, name)()

    begin = [chunk(5, "start_z", "step1") + chunk(4, "step3"), chunk(5, "step3")]
    begin = begin[:1] + [begin[1] + chunk(1, "finish")]
    begin += [chunk(k, "finish") for k in range(2, chunks)]
    middle = [chunk(5, "both")]

    def one_chunk(k, carry):
        at_step(k, begin)
        when_scatter(k - 2, "step2")
        w_in, w_back = flat(wi_ref[k]), flat(wb_ref[k])
        args = (w_in, w_back, k == 0, low_ref, cotb, hid_ref, gp_ref, up_ref, down_ref)
        ffn_rows(0, half_rows, *args)
        when_scatter(k - 1, "step1")
        at_step(k, middle)
        ffn_rows(1, half_rows, *args)
        when_scatter(k - 3, "step3")
        wb_ref[k] = nn(cott_ref[...], hid_ref[...]).astype(BF).reshape(wb_ref.shape[1:])
        when_scatter(k - 4, "finish")
        wi_ref[k] = nn(ffnt_ref[...], gp_ref[...]).astype(BF).reshape(wi_ref.shape[1:])
        when_scatter(k, "step0")

        @pl.when(k >= here)
        def _():
            for one in save_chunk(k):
                one.start()

        return carry

    lax.fori_loop(0, chunks, one_chunk, 0)
    ggain_ref[...] = jnp.zeros_like(ggain_ref)
    step = 256

    def finish_rows(own, i):
        half = p.t if own else 1 - p.t
        at = pl.ds(pl.multiple_of(i * step, step), step)
        rows = pl.ds(pl.multiple_of(half * half_rows + i * step, step), step)
        cot = cotf_ref[at, :] if own else cotb_ref[1 - p.t, at, :].astype(F32)
        out = after_rows(
            rows, cot, up_ref, down_ref, ffn_gain, ggain_ref, gm_ref, low_ref, cott_ref
        )
        if own:
            cotf_ref[at, :] = out
        else:
            obuf_ref[at, :] = out.astype(BF)

    for i in range(half_rows // step):
        finish_rows(False, i)
    saves[6].start()
    for stage, name in ((1, "step1"), (2, "step2"), (3, "step3")):
        for k in range(max(0, chunks - stage), here):
            when_scatter(k, name)
    for i in range(half_rows // step):
        finish_rows(True, i)
    saves[7].start()
    saves[8].start()
    context_grad(low_ref, flat(wo_ref[...]), v_ref)
    saves[9].start()
    wo_ref[...] = nn(cott_ref[...], ctx_ref[...]).astype(BF).reshape(wo_ref.shape)
    saves[10].start()
    for k in range(max(0, chunks - 4), here):
        when_scatter(k, "finish")
    for move in moves[:2]:
        move.wait_send()
    for one in saves:
        one.wait()
    for k in range(here, chunks):
        for one in save_chunk(k):
            one.wait()


def back_fused(
    depth,
    q_in,
    k_in,
    v_in,
    go_ref,
    ctx_ref,
    feat_ref,
    seg_ref,
    tabs_ref,
    xs_in,
    gm_in,
    wq_in,
    wk_in,
    wv_in,
    gain_in,
    ggain_ref,
    gi_in,
    gb_in,
    gout_in,
    oth_in,
    oth_out,
    igown_ref,
    ibuf2_ref,
    gwo_ref,
    gwq_ref,
    gwk_ref,
    gwv_ref,
    gwi_ref,
    gwb_ref,
    small_ref,
    q_ref,
    k_ref,
    v_ref,
    xs_ref,
    gm_ref,
    wq_ref,
    wk_ref,
    wv_ref,
    gi_ref,
    gb_ref,
    gout_ref,
    lowt_ref,
    sum_ref,
    gq_ref,
    gk_ref,
    gv_ref,
    ibuf_ref,
    again_ref,
    tabg_ref,
    sm_ref,
    smr_ref,
    bias_ref,
    sums_ref,
    far_ref,
    segk_ref,
    blockof_ref,
    gofeat_ref,
    near_ref,
    acc_ref,
    o0,
    o1,
    o2,
    o3,
    i0,
    i1,
    i2,
    i3,
    b0,
    b1,
    b2,
    b3,
    a0,
    a1,
    a2,
    a3,
    c0,
    c1,
    c2,
    c3,
    d0,
    d1,
    d2,
    d3,
    s_send,
    s_recv,
    x_send,
    x_recv,
    l_sem,
):
    p = Place(depth)
    length = q_ref.shape[0]
    half_rows = length // 2
    groups = gq_ref.shape[0]
    rest, part = gi_ref.shape[0], gi_ref.shape[-1] // 2
    s_sems, x_sems = (s_send, s_recv), (x_send, x_recv)
    pairs = [(q_in, q_ref), (k_in, k_ref), (v_in, v_ref), (xs_in, xs_ref)]
    pairs += [(gi_in, gi_ref), (gb_in, gb_ref), (gout_in, gout_ref), (gm_in, gm_ref)]
    pairs += [(wq_in, wq_ref), (wk_in, wk_ref), (wv_in, wv_ref)]
    loads = [local(src, dst, l_sem.at[i]) for i, (src, dst) in enumerate(pairs)]
    for one in loads:
        one.start()
    bwd_setup(seg_ref[p.t], tabs_ref, bias_ref, sums_ref, far_ref, segk_ref, blockof_ref)
    p.barrier()
    quarter = half_rows // 4
    out_moves = [
        remote(
            oth_in.at[pl.ds(i * quarter, quarter)],
            oth_out.at[pl.ds(i * quarter, quarter)],
            x_sems,
            depth + 6 + i,
            p.xpeer,
        )
        for i in range(4)
    ]
    out_item = Scatter(
        p, gout_ref, gwo_ref.shape[1], (o0, o1, o2, o3), s_sems, 2 * rest + 3 * groups, True
    )
    rest_items = []
    for k in range(rest):
        rest_items.append(
            [
                Scatter(
                    p, gi_ref.at[k], part, [r.at[k] for r in (i0, i1, i2, i3)], s_sems, 2 * k, True
                ),
                Scatter(
                    p,
                    gb_ref.at[k],
                    part,
                    [r.at[k] for r in (b0, b1, b2, b3)],
                    s_sems,
                    2 * k + 1,
                    True,
                ),
            ]
        )
    group_items = []
    for j in range(groups):
        group_items.append(
            [
                Scatter(
                    p,
                    ref.at[j],
                    LANES,
                    [r.at[j] for r in bufs],
                    s_sems,
                    2 * rest + 3 * j + i,
                    True,
                )
                for i, (ref, bufs) in enumerate(
                    (
                        (gq_ref, (a0, a1, a2, a3)),
                        (gk_ref, (c0, c1, c2, c3)),
                        (gv_ref, (d0, d1, d2, d3)),
                    )
                )
            ]
        )

    def chunk(k, name):
        if k >= rest:
            return []
        if name == "finish":
            return [
                functools.partial(item.finish, out, k * part)
                for item, out in zip(rest_items[k], (gwi_ref, gwb_ref))
            ]
        return [getattr(item, name) for item in rest_items[k]]

    def group(j, name):
        if name == "finish":
            return [
                functools.partial(item.finish, out, j * LANES)
                for item, out in zip(group_items[j], (gwq_ref, gwk_ref, gwv_ref))
            ]
        return [getattr(item, name) for item in group_items[j]]

    for one in loads[:7]:
        one.wait()
    run_all(chunk(0, "step0"))
    xs = xs_ref.reshape(length, xs_ref.shape[2])
    gain = as_row(gain_in[...])
    low_transposed(xs, gain, lowt_ref)
    run_all(chunk(0, "step1") + chunk(1, "step0"))
    for one in loads[7:]:
        one.wait()

    def group_cols(ref, j):
        return [ref[:, pair_cols(j)], ref[:, pair_cols(j + groups)]]

    def weight_grads(j):
        for target, grad in zip((gq_ref, gk_ref, gv_ref), (q_ref, k_ref, v_ref)):
            both = jnp.concatenate(group_cols(grad, j), 1)
            target[j] = nn(lowt_ref[...], both).astype(BF).reshape(target.shape[1:])

    def group_weights(j):
        pieces = []
        for weight in (wq_ref, wk_ref, wv_ref):
            pieces.append(flat(weight[j]))
        return jnp.concatenate(pieces, 1)

    def group_sum(rows, j):
        pieces = []
        for grad in (q_ref, k_ref, v_ref):
            for at in (j, j + groups):
                pieces.append(grad[rows, pair_cols(at)])
        return nt(jnp.concatenate(pieces, 1), group_weights(j))

    step = 256
    plan = [
        [out_moves[0].start],
        chunk(0, "step2") + chunk(1, "step1") + [out_item.step0, out_moves[1].start],
        chunk(0, "step3") + chunk(1, "step2") + [out_item.step1, out_moves[2].start],
        chunk(0, "finish") + chunk(1, "step3") + group(0, "step1") + [out_item.step2],
        chunk(1, "finish") + group(0, "step2") + [out_item.step3, out_moves[3].start],
        group(0, "step3") + group(1, "step1") + [functools.partial(out_item.finish, gwo_ref, 0)],
    ]

    def one_pair(index, carry):
        at_step(index, plan)
        j, side = lax.div(index, 2), lax.rem(index, 2)
        bwd_pair(
            j + groups * side,
            q_ref,
            k_ref,
            v_ref,
            go_ref,
            ctx_ref,
            feat_ref,
            q_ref,
            k_ref,
            v_ref,
            bias_ref,
            sums_ref,
            far_ref,
            segk_ref,
            blockof_ref,
            gofeat_ref,
            near_ref,
            acc_ref,
        )

        @pl.when(side == 1)
        def _():
            weight_grads(j)
            for i in range(groups):

                @pl.when(j == i)
                def _():
                    run_all(group(i, "step0"))

            for i in range(groups - 1):

                @pl.when(j == i)
                def _():
                    for at in range(length // step):
                        rows = slice(at * step, (at + 1) * step)
                        if i == 0:
                            sum_ref[rows, :] = group_sum(rows, i)
                        else:
                            sum_ref[rows, :] += group_sum(rows, i)

        return carry

    lax.fori_loop(0, 2 * groups, one_pair, 0)
    bwd_table(tabg_ref, sums_ref, far_ref)
    again_ref[...] = jnp.zeros_like(again_ref)
    last = groups - 1

    def finish_rows(own, i):
        half = p.t if own else 1 - p.t
        at = pl.ds(pl.multiple_of(i * step, step), step)
        rows = pl.ds(pl.multiple_of(half * half_rows + i * step, step), step)
        down = sum_ref[rows, :] + group_sum(rows, last)
        inputs = xs_ref[half, at, :].astype(F32)
        scale = rms_scale(inputs)
        normed = inputs * scale
        again_ref[...] += jnp.sum(down * normed, 0, keepdims=True)
        out = gm_ref[rows, :] + rms_back(down, normed, scale, gain)
        if own:
            igown_ref[at, :] = out
        else:
            ibuf_ref[at, :] = out.astype(BF)

    finish_rows(False, 0)

    def piece(i):
        size = half_rows // 4
        at = pl.ds(i * size, size)
        return remote(ibuf_ref.at[at], ibuf2_ref.at[at], x_sems, i, p.xpeer)

    moves = [piece(i) for i in range(4)]
    moves[0].start()
    moves[1].start()
    run_all(group(last, "step1"))
    finish_rows(False, 1)
    run_all(group(1, "step2"))
    moves[2].start()
    run_all(group(0, "finish"))
    for i in range(half_rows // step):
        finish_rows(True, i)
    run_all(group(last, "step2"))
    moves[3].start()
    model = again_ref.shape[1]
    sm_ref[0, 0:1, :model] = again_ref[...]
    sm_ref[0, 1:2, :model] = ggain_ref[...]
    sm_ref[0, 2:8, :model] = jnp.zeros((6, model), F32)
    sm_ref[0, :, model : model + LANES] = tabg_ref[0:8, :]
    sm_ref[0, :, model + LANES :] = tabg_ref[8:16, :]
    hops = [(p.sib,), (p.ypeer,), (p.xpeer,), tuple(p.zpeers)]
    slot = 0
    beside = [
        group(1, "step3"),
        group(last, "step3"),
        group(1, "finish"),
        [],
    ]
    for level, peers in enumerate(hops):
        hop = [
            remote(sm_ref.at[level], smr_ref.at[slot + i], x_sems, len(moves) + slot + i, peer)
            for i, peer in enumerate(peers)
        ]
        for one in hop:
            one.start()
        run_all(beside[level])
        total = sm_ref[level]
        for i, one in enumerate(hop):
            one.wait_recv()
            total = total + smr_ref[slot + i]
        slot += len(peers)
        if level + 1 < len(hops):
            sm_ref[level + 1] = total
        else:
            small_ref[...] = total
        for one in hop:
            one.wait_send()
    run_all(group(last, "finish"))
    for move in moves + out_moves:
        move.wait_recv()
        move.wait_send()


def collect(
    own_in,
    oth_ref,
    igown_in,
    igoth_ref,
    small_ref,
    gwi_a,
    gwi_b,
    gwb_a,
    gwb_b,
    gwo_in,
    gwq_in,
    gwk_in,
    gwv_in,
    out_ref,
    ig_ref,
    again_ref,
    ggain_ref,
    gwq_ref,
    gwk_ref,
    gwv_ref,
    gwo_ref,
    gwi_ref,
    gwb_ref,
    table_ref,
    wide_ref,
    turn_ref,
    sem,
):
    t = lax.axis_index("tensor")
    loads = [
        local(own_in, wide_ref.at[0], sem.at[0]),
        local(igown_in, wide_ref.at[1], sem.at[1]),
    ]
    for one in loads:
        one.start()
    copies = []
    for i, (src, dst) in enumerate(((oth_ref, out_ref), (igoth_ref, ig_ref))):
        wide_ref[2 + i] = src[...].astype(F32)
        copies.append(local(wide_ref.at[2 + i], dst.at[1 - t], sem.at[2 + i]))
        copies[-1].start()
    for i, dst in enumerate((out_ref, ig_ref)):
        loads[i].wait()
        copies.append(local(wide_ref.at[i], dst.at[t], sem.at[4 + i]))
        copies[-1].start()
    for src, dst in ((gwq_in, gwq_ref), (gwk_in, gwk_ref), (gwv_in, gwv_ref), (gwo_in, gwo_ref)):
        dst[...] = src[...]
    for first, second, dst in ((gwi_a, gwi_b, gwi_ref), (gwb_a, gwb_b, gwb_ref)):
        dst[:, : first.shape[1]] = first[...]
        dst[:, first.shape[1] :] = second[...]
    model = again_ref.shape[0]
    again_ref[...] = small_ref[0:1, :model].reshape(model)
    ggain_ref[...] = small_ref[1:2, :model].reshape(model)
    turn_ref[...] = jnp.zeros_like(turn_ref)
    first = small_ref[:, model : model + LANES]
    second = small_ref[:, model + LANES :]
    turn_ref[0:8, :] = jnp.where(t == 0, first, second)
    table_ref[...] = turn_ref[...].T[: table_ref.shape[0], : table_ref.shape[1]]
    for one in copies:
        one.wait()


def call(kernel, outs, scratch, args, name, collective=None, far=()):
    def spec(array):
        return pl.BlockSpec(memory_space=pl.ANY if array in far else pltpu.VMEM)

    if collective is None:
        params = pltpu.CompilerParams(vmem_limit_bytes=VMEM_BYTES)
    else:
        params = pltpu.CompilerParams(
            vmem_limit_bytes=VMEM_BYTES, collective_id=collective, has_side_effects=True
        )
    return pl.pallas_call(
        kernel,
        out_shape=[jax.ShapeDtypeStruct(shape, dtype) for shape, dtype in outs],
        in_specs=[spec(i) for i in range(len(args))],
        out_specs=[spec(len(args) + i) for i in range(len(outs))],
        scratch_shapes=scratch,
        compiler_params=params,
        name=name,
    )(*args)


def shards(
    inputs,
    segments,
    norm_attn,
    norm_ffn,
    w_query,
    w_key,
    w_value,
    w_out,
    w_in,
    w_back,
    rel_table,
    cotangent,
):
    dp, tensor = lax.axis_size("dp"), lax.axis_size("tensor")
    t = lax.axis_index("tensor")
    rows, width = w_query.shape
    hidden_part = w_in.shape[1]
    model = inputs.shape[2]
    length = segments.shape[2]
    half = inputs.shape[1]
    buckets, heads = rel_table.shape
    depth = dp // 4
    fused = rows % 16 == 0 and dp % 4 == 0 and depth >= 2
    full = (length, model)
    inner = (length, width * tensor)
    square = (depth, 2, 2, rows, 2 * width)
    part = 256
    chunks = hidden_part // part
    pairs = inner[1] // LANES
    dma = pltpu.SemaphoreType.DMA
    halves = (2, half, model)
    fwd_work = [pltpu.VMEM((16, 4 * LANES), F32)] + [pltpu.VMEM((length, LANES), BF)] * 2
    bwd_work = [
        pltpu.VMEM((16, 4 * LANES), F32),
        pltpu.VMEM((16, 4 * LANES), F32),
        pltpu.VMEM((16, LANES), F32),
        pltpu.VMEM((length, LANES), BF),
        pltpu.VMEM((length, LANES), BF),
        pltpu.VMEM((length, LANES), BF),
        pltpu.VMEM((2, LANES, 3 * LANES), F32),
        pltpu.VMEM((length, LANES), F32),
    ]
    ffn_work = [pltpu.VMEM(full, BF), pltpu.VMEM(full[::-1], BF), pltpu.VMEM(full[::-1], BF)]
    rest = [pltpu.VMEM((length, 2 * part), BF)] * 2 + [pltpu.VMEM(full, F32)] * 2
    if fused:
        here = chunks - chunks // 3
        block = (depth, 2, 2, rows, 2 * part)
        groups = pairs // 2
        narrow = (groups, depth, 2, 2, rows, 2 * LANES)
        (
            xs,
            tabs,
            queries,
            keys,
            values,
            ctx,
            feats,
            wq,
            wk,
            wv,
            own,
            oth,
            grad_middle,
            grad_context,
            ggain,
            gout,
            gwi_a,
            gwb_a,
            gi,
            gb,
        ) = call(
            functools.partial(forward_fused, depth, here),
            [
                (halves, BF),
                ((2, 8, LANES), F32),
                (inner, BF),
                (inner, BF),
                (inner, BF),
                (inner, BF),
                ((pairs, length, LANES), BF),
                (narrow, BF),
                (narrow, BF),
                (narrow, BF),
                ((half, model), F32),
                ((half, model), BF),
                (full, F32),
                (inner, BF),
                ((1, model), F32),
                (square, BF),
                ((rows, here * part), F32),
                ((rows, here * part), F32),
                ((chunks - here,) + block, BF),
                ((chunks - here,) + block, BF),
            ],
            [
                pltpu.VMEM(halves, BF),
                pltpu.VMEM((half, model), F32),
                pltpu.VMEM(halves, BF),
                pltpu.VMEM((half, model), BF),
            ]
            + [pltpu.VMEM(inner, BF)] * 4
            + [pltpu.VMEM((pairs, length, LANES), BF)]
            + [pltpu.VMEM(narrow, BF)] * 3
            + [pltpu.VMEM(square, BF)]
            + [pltpu.VMEM((chunks,) + block, BF)] * 2
            + [pltpu.VMEM(full, BF), pltpu.VMEM((LANES, LANES), F32)]
            + fwd_work
            + [pltpu.VMEM(full, F32)]
            + [pltpu.VMEM(full[::-1], BF)] * 2
            + [pltpu.VMEM(full, F32)] * 2
            + scatter_bufs(here, depth, rows, part, True)
            + scatter_bufs(here, depth, rows, part, False)
            + gather_sems(3 * groups, depth)
            + gather_sems(1 + 2 * chunks, depth)
            + scatter_sems(2 * here, depth)
            + [dma((3,)), dma((3,)), dma((16,)), dma((2 * chunks,))],
            (
                inputs,
                cotangent,
                norm_attn,
                norm_ffn,
                rel_table,
                segments,
                w_query,
                w_key,
                w_value,
                w_out,
                w_in,
                w_back,
            ),
            "forward_feed_forward",
            0,
            (0, 1, 12, 14, 15, 16, 17, 18, 19, 20, 21, 22, 23, 24, 25, 27, 30, 31),
        )
        left = chunks - here
        oth, igown, igoth, gwo, gwq, gwk, gwv, gwi_b, gwb_b, small = call(
            functools.partial(back_fused, depth),
            [
                ((half, model), BF),
                ((half, model), F32),
                ((half, model), BF),
                ((rows, width), F32),
                ((rows, width), F32),
                ((rows, width), F32),
                ((rows, width), F32),
                ((rows, left * part), F32),
                ((rows, left * part), F32),
                ((8, model + 2 * LANES), F32),
            ],
            [pltpu.VMEM(inner, BF)] * 3
            + [pltpu.VMEM(halves, BF), pltpu.VMEM(full, F32)]
            + [pltpu.VMEM(narrow, BF)] * 3
            + [pltpu.VMEM((left,) + block, BF)] * 2
            + [pltpu.VMEM(square, BF)]
            + [pltpu.VMEM(full[::-1], BF), pltpu.VMEM(full, F32)]
            + [pltpu.VMEM(narrow, BF)] * 3
            + [pltpu.VMEM((half, model), BF)]
            + [
                pltpu.VMEM((1, model), F32),
                pltpu.VMEM((16, LANES), F32),
                pltpu.VMEM((4, 8, model + 2 * LANES), F32),
                pltpu.VMEM((depth + 2, 8, model + 2 * LANES), F32),
            ]
            + bwd_work
            + scatter_bufs(None, depth, rows, width, True)
            + scatter_bufs(left, depth, rows, part, True)
            + scatter_bufs(left, depth, rows, part, True)
            + scatter_bufs(groups, depth, rows, LANES, True)
            + scatter_bufs(groups, depth, rows, LANES, True)
            + scatter_bufs(groups, depth, rows, LANES, True)
            + scatter_sems(1 + 2 * left + 3 * groups, depth)
            + [dma((depth + 10,)), dma((depth + 10,)), dma((11,))],
            (
                queries,
                keys,
                values,
                grad_context,
                ctx,
                feats,
                segments,
                tabs,
                xs,
                grad_middle,
                wq,
                wk,
                wv,
                norm_attn,
                ggain,
                gi,
                gb,
                gout,
                oth,
            ),
            "attention_backward",
            1,
            (0, 1, 2, 8, 9, 10, 11, 12, 15, 16, 17, 18, 19),
        )
        return tuple(
            call(
                collect,
                [
                    (halves, F32),
                    (halves, F32),
                    ((model,), F32),
                    ((model,), F32),
                    ((rows, width), F32),
                    ((rows, width), F32),
                    ((rows, width), F32),
                    ((rows, width), F32),
                    ((rows, hidden_part), F32),
                    ((rows, hidden_part), F32),
                    ((buckets, heads), F32),
                ],
                [pltpu.VMEM((4, half, model), F32), pltpu.VMEM((LANES, LANES), F32), dma((6,))],
                (own, oth, igown, igoth, small, gwi_a, gwi_b, gwb_a, gwb_b, gwo, gwq, gwk, gwv),
                "collect",
                None,
                (0, 2, 13, 14),
            )
        )
    else:
        gain_attn, gain_ffn = norm_attn.reshape(1, model), norm_ffn.reshape(1, model)
        table = jnp.pad(rel_table.T, ((0, 8 - heads), (0, LANES - buckets)))
        segment = lax.dynamic_index_in_dim(segments, t, 0, False)

        def whole(weight):
            weight = lax.all_gather(weight, "dp", axis=0, tiled=True)
            return lax.all_gather(weight, "tensor", axis=1, tiled=True)

        def exchanged(local_part):
            own = lax.dynamic_index_in_dim(local_part, t, 0, False)
            other = lax.dynamic_index_in_dim(local_part, 1 - t, 0, False)
            other = lax.ppermute(other, "tensor", [(0, 1), (1, 0)])
            first = jnp.where(t == 0, own, other)
            second = jnp.where(t == 0, other, own)
            return jnp.concatenate([first, second], 0)

        def returned(seq):
            mine = lax.dynamic_slice_in_dim(seq, t * half, half, 0)
            other = lax.dynamic_slice_in_dim(seq, (1 - t) * half, half, 0)
            other = lax.ppermute(other, "tensor", [(0, 1), (1, 0)])
            return jnp.stack([jnp.where(t == 0, mine, other), jnp.where(t == 0, other, mine)])

        def scattered(grad):
            grad = lax.psum_scatter(grad.astype(F32), "tensor", scatter_dimension=1, tiled=True)
            return lax.psum_scatter(grad, "dp", scatter_dimension=0, tiled=True)

        xs = exchanged(inputs)
        tabs = lax.all_gather(table, "tensor", axis=0)
        wq, wk, wv, wo, wi, wb = (
            whole(w) for w in (w_query, w_key, w_value, w_out, w_in, w_back)
        )
        queries, keys, values = call(
            k1_plain,
            [(inner, BF)] * 3,
            [pltpu.VMEM(full, BF)],
            (xs, gain_attn, wq, wk, wv),
            "project",
        )
        ctx, feats = call(
            fwd_kernel,
            [(inner, BF), ((pairs, length, LANES), BF)],
            fwd_work,
            (queries, keys, values, segment, tabs),
            "attention_forward",
        )
        out_seq, grad_middle, grad_context, ggain, gwo, gwi, gwb = call(
            k3_plain,
            [
                (full, F32),
                (full, F32),
                (inner, BF),
                ((1, model), F32),
                (wo.shape, BF),
                (wi.shape, BF),
                (wb.shape, BF),
            ],
            ffn_work + [pltpu.VMEM(full, BF)] + rest,
            (xs, ctx, exchanged(cotangent), gain_ffn, wo, wi, wb),
            "feed_forward",
        )
        output = returned(out_seq)
        gwo, gwi, gwb = scattered(gwo), scattered(gwi), scattered(gwb)
        dq, dk, dv, table_grad = call(
            bwd_kernel,
            [(inner, BF), (inner, BF), (inner, BF), ((16, LANES), F32)],
            bwd_work,
            (queries, keys, values, grad_context, ctx, feats, segment, tabs),
            "attention_backward",
        )
        ig_seq, gwq, gwk, gwv, again = call(
            k5_plain,
            [(full, F32), (wq.shape, BF), (wk.shape, BF), (wv.shape, BF), ((1, model), F32)],
            [pltpu.VMEM((model, length), BF)],
            (xs, grad_middle, dq, dk, dv, wq, wk, wv, gain_attn),
            "projection_gradients",
        )
        input_grad = returned(ig_seq)
        gwq, gwk, gwv = scattered(gwq), scattered(gwk), scattered(gwv)
        again, ggain, tables = lax.psum((again, ggain, table_grad), ("dp", "tensor"))
        gain_attn_grad, gain_ffn_grad = again[0], ggain[0]
        tables = tables.reshape(2, 8, LANES)
    table_out = lax.dynamic_index_in_dim(tables, t, 0, False)[:heads, :buckets].T
    return (
        output,
        input_grad,
        gain_attn_grad,
        gain_ffn_grad,
        gwq,
        gwk,
        gwv,
        gwo,
        gwi,
        gwb,
        table_out,
    )


def solution(mesh):
    weight = P("dp", "tensor")
    tokens = P(None, ("dp", "tensor"), None)
    return jax.shard_map(
        shards,
        mesh=mesh,
        in_specs=(
            tokens,
            P(None, "dp", None),
            P(),
            P(),
            weight,
            weight,
            weight,
            weight,
            weight,
            weight,
            P(None, "tensor"),
            tokens,
        ),
        out_specs=(
            tokens,
            tokens,
            P(),
            P(),
            weight,
            weight,
            weight,
            weight,
            weight,
            weight,
            P(None, "tensor"),
        ),
        check_vma=False,
    )
```

```python
import functools

import jax
import jax.numpy as jnp
from jax import lax
from jax.experimental import pallas as pl
from jax.experimental.pallas import tpu as pltpu
from jax.sharding import PartitionSpec as P

MESH = pl.DeviceIdType.MESH
BF = jnp.bfloat16
F32 = jnp.float32
HIGHEST = lax.Precision.HIGHEST
EPSILON = 1e-06
THRESHOLDS = (12, 16, 23, 32, 46, 64, 91)
MASK_OUT = -float(2**30)
DH = 64
SPAN = 512
LANES = 128
VMEM_BYTES = 62 * 2**20


def nn(left, right):
    return lax.dot_general(left, right, (((1,), (0,)), ((), ())), preferred_element_type=F32)


def nt(left, right):
    return lax.dot_general(left, right, (((1,), (1,)), ((), ())), preferred_element_type=F32)


def tn(left, right):
    return lax.dot_general(left, right, (((0,), (0,)), ((), ())), preferred_element_type=F32)


def iota(shape, dim):
    return lax.broadcasted_iota(jnp.int32, shape, dim)


def bucket_ids(offsets):
    distance = jnp.abs(offsets)
    far_ids = 8 + sum((distance >= threshold).astype(jnp.int32) for threshold in THRESHOLDS)
    return jnp.where(offsets > 0, 16, 0) + jnp.where(distance < 8, distance, far_ids)


def rms_scale(values):
    return lax.rsqrt(jnp.mean(values * values, -1, keepdims=True) + EPSILON)


def rms_back(grad_normed, normed, scale, gain):
    scaled = grad_normed * gain
    return scale * (scaled - normed * jnp.mean(scaled * normed, -1, keepdims=True))


def gelu_pair(v):
    square = v * v
    half = 0.5 + 0.5 * jnp.tanh(v * (0.7978845608028654 + 0.035677408136300125 * square))
    slope = half + v * half * (1.0 - half) * (1.5957691216057308 + 0.2140644488178007 * square)
    return v * half, slope


class Place:
    def __init__(self, depth):
        d, t = lax.axis_index("dp"), lax.axis_index("tensor")
        self.t = t
        self.z, self.y, self.c = lax.div(d, 4), lax.rem(lax.div(d, 2), 2), lax.rem(d, 2)
        self.depth = depth
        self.sib = (d + 1 - 2 * self.c, t)
        self.ypeer = (d + 2 - 4 * self.y, t)
        self.xpeer = (d, 1 - t)
        rest = self.rest = lax.rem(d, 4)
        self.zs = [lax.rem(self.z + step, depth) for step in range(1, depth)]
        self.zpeers = [(z * 4 + rest, t) for z in self.zs]

    def barrier(self):
        semaphore = pltpu.get_barrier_semaphore()
        peers = [self.sib, self.ypeer, self.xpeer] + self.zpeers
        for peer in peers:
            pl.semaphore_signal(semaphore, inc=1, device_id=peer, device_id_type=MESH)
        pl.semaphore_wait(semaphore, len(peers))


class Copy:
    def __init__(self, **parts):
        self.parts = parts

    def made(self):
        return pltpu.make_async_remote_copy(device_id_type=MESH, **self.parts)

    def start(self):
        self.made().start()

    def wait_recv(self):
        self.made().wait_recv()

    def wait_send(self):
        self.made().wait_send()


def local(src, dst, sem):
    return pltpu.make_async_copy(src, dst, sem)


def remote(src, dst, sems, index, peer):
    send, recv = sems
    return Copy(
        src_ref=src, dst_ref=dst, send_sem=send.at[index], recv_sem=recv.at[index], device_id=peer
    )


class Gather:
    def __init__(self, place, ref, width, sems, item, x_first):
        self.p, self.ref, self.width, self.sems, self.item = place, ref, width, sems, item
        p = place
        self.relays = p.depth == 4
        if x_first:
            self.peers, order = (p.xpeer, p.ypeer), ((0, 0), (0, 1), (1, 0), (1, 1))
        else:
            self.peers, order = (p.ypeer, p.xpeer), ((0, 0), (1, 0), (0, 1), (1, 1))
        self.sides = [(p.y + (1 - 2 * p.y) * i, p.t + (1 - 2 * p.t) * j) for i, j in order]

    def cols(self, x):
        return pl.ds(pl.multiple_of(x * self.width, LANES), self.width)

    def block(self, z, side):
        y, x = self.sides[side]
        return self.ref.at[z, y, self.p.c, :, self.cols(x)]

    def region(self, side):
        y, x = self.sides[side]
        return self.ref.at[:, y, self.p.c, :, self.cols(x)]

    def send(self, index, src, peer):
        return remote(src, src, self.sems, (self.item, index), peer)

    def first(self):
        return self.send(0, self.block(self.p.z, 0), self.peers[0])

    def along(self, side):
        p = self.p
        base = 1 + side * len(p.zpeers)
        return [self.send(base + i, self.block(p.z, side), peer) for i, peer in enumerate(p.zpeers)]

    def last(self, side):
        return self.send(1 + 2 * len(self.p.zpeers) + side, self.region(side), self.peers[1])

    def sib(self, side):
        return self.send(3 + 2 * len(self.p.zpeers) + side, self.region(side), self.p.sib)

    def relay(self, side):
        p = self.p
        send, recv = self.sems
        src = self.block(lax.rem(p.z + 2, 4), side)
        low = p.z == 1
        target = jnp.where(low, 0, 3)
        return Copy(
            src_ref=src,
            dst_ref=src,
            send_sem=send.at[self.item, 7 + 2 * len(p.zpeers) + side],
            recv_sem=recv.at[self.item, 1 + side * len(p.zpeers) + jnp.where(low, 0, 2)],
            device_id=(target * 4 + p.rest, p.t),
        )

    def each_along(self, side, method):
        p = self.p
        for i, copy in enumerate(self.along(side)):
            if self.relays and i != 1:
                pl.when(p.z != (3 if i == 0 else 0))(getattr(copy, method))
            else:
                getattr(copy, method)()

    def inside(self, action):
        pl.when((self.p.z == 1) | (self.p.z == 2))(action)

    def start(self):
        self.first().start()

    def start_z(self):
        self.each_along(0, "start")

    def step1(self):
        self.first().wait_recv()
        self.each_along(1, "start")

    def step2(self, side):
        zs = self.along(side)
        if self.relays:
            zs[1].wait_recv()
            self.inside(self.relay(side).start)
            zs = [zs[0], zs[2]]
        for copy in zs:
            copy.wait_recv()
        self.last(side).start()
        self.sib(side).start()

    def step3(self):
        for side in range(2):
            self.last(side).wait_recv()
            self.sib(2 + side).start()

    def finish(self):
        for side in range(4):
            self.sib(side).wait_recv()
        self.first().wait_send()
        for side in range(2):
            self.each_along(side, "wait_send")
            if self.relays:
                self.inside(self.relay(side).wait_send)
            self.last(side).wait_send()
        for side in range(4):
            self.sib(side).wait_send()


def gather_sems(items, depth):
    return [pltpu.SemaphoreType.DMA((items, 2 * depth + 7))] * 2


class Scatter:
    def __init__(self, place, ref, width, bufs, sems, item, y_first):
        self.p, self.ref, self.width, self.sems, self.item = place, ref, width, sems, item
        self.r0, self.r1, self.r2, self.r3 = bufs
        self.y_first = y_first

    def cols(self, x):
        return pl.ds(pl.multiple_of(x * self.width, LANES), self.width)

    def copies(self):
        p, ref = self.p, self.ref
        sib = remote(ref.at[:, :, 1 - p.c], self.r0, self.sems, (self.item, 0), p.sib)
        if self.y_first:
            half = remote(ref.at[:, 1 - p.y, p.c], self.r1, self.sems, (self.item, 1), p.ypeer)
            quarter = remote(
                ref.at[:, p.y, p.c, :, self.cols(1 - p.t)],
                self.r2,
                self.sems,
                (self.item, 2),
                p.xpeer,
            )
        else:
            half = remote(
                ref.at[:, :, p.c, :, self.cols(1 - p.t)],
                self.r1,
                self.sems,
                (self.item, 1),
                p.xpeer,
            )
            quarter = remote(
                ref.at[:, 1 - p.y, p.c, :, self.cols(p.t)],
                self.r2,
                self.sems,
                (self.item, 2),
                p.ypeer,
            )
        zs = [
            remote(
                ref.at[z, p.y, p.c, :, self.cols(p.t)],
                self.r3.at[i],
                self.sems,
                (self.item, 3 + i),
                peer,
            )
            for i, (z, peer) in enumerate(zip(p.zs, p.zpeers))
        ]
        return sib, half, quarter, zs

    def step0(self):
        self.copies()[0].start()

    def step1(self):
        p = self.p
        sib, half, _, _ = self.copies()
        sib.wait_recv()
        kept = self.ref.at[:, :, p.c]
        kept[...] = (kept[...].astype(F32) + self.r0[...].astype(F32)).astype(BF)
        half.start()

    def step2(self):
        p = self.p
        _, half, quarter, _ = self.copies()
        half.wait_recv()
        if self.y_first:
            kept = self.ref.at[:, p.y, p.c]
        else:
            kept = self.ref.at[:, :, p.c, :, self.cols(p.t)]
        kept[...] = (kept[...].astype(F32) + self.r1[...].astype(F32)).astype(BF)
        quarter.start()

    def step3(self):
        p = self.p
        _, _, quarter, zs = self.copies()
        quarter.wait_recv()
        kept = self.ref.at[:, p.y, p.c, :, self.cols(p.t)]
        kept[...] = (kept[...].astype(F32) + self.r2[...].astype(F32)).astype(BF)
        for copy in zs:
            copy.start()

    def finish(self, out, offset):
        p = self.p
        sib, half, quarter, zs = self.copies()
        for copy in zs:
            copy.wait_recv()
        total = self.ref[p.z, p.y, p.c, :, self.cols(p.t)].astype(F32)
        for i in range(len(zs)):
            total = total + self.r3[i].astype(F32)
        out[:, pl.ds(pl.multiple_of(offset, LANES), self.width)] = total
        for copy in [sib, half, quarter] + zs:
            copy.wait_send()


def scatter_bufs(items, depth, rows, width, y_first):
    lead = () if items is None else (items,)
    return [
        pltpu.VMEM(lead + (depth, 2, rows, 2 * width), BF),
        pltpu.VMEM(lead + ((depth, rows, 2 * width) if y_first else (depth, 2, rows, width)), BF),
        pltpu.VMEM(lead + (depth, rows, width), BF),
        pltpu.VMEM(lead + (depth - 1, rows, width), BF),
    ]


def scatter_sems(items, depth):
    return [pltpu.SemaphoreType.DMA((items, depth + 2))] * 2


def flat(values):
    if len(values.shape) == 2:
        return values
    return values.reshape(-1, values.shape[-1])


def project_rows(x_rows, gain):
    rows = x_rows.astype(F32)
    return (rows * rms_scale(rows) * gain).astype(BF)


def project(low_ref, w_ref, out_ref):
    weight = flat(w_ref[...])
    half = low_ref.shape[0] // 2

    def one(i, carry):
        rows = pl.ds(pl.multiple_of(i * half, half), half)
        out_ref[rows, :] = nn(low_ref[rows, :], weight).astype(BF)
        return carry

    lax.fori_loop(0, 2, one, 0)


def k1_plain(x_ref, gain_ref, wq_ref, wk_ref, wv_ref, q_ref, k_ref, v_ref, low_ref):
    low_ref[...] = project_rows(x_ref[...], gain_ref[...])
    for weight, out in ((wq_ref, q_ref), (wk_ref, k_ref), (wv_ref, v_ref)):
        project(low_ref, weight, out)


def bias_rows(tabs_ref, out_ref, flipped):
    offsets = iota((LANES, 4 * LANES), 1) - 2 * LANES
    onehot = (bucket_ids(-offsets if flipped else offsets) == iota((LANES, 4 * LANES), 0)).astype(F32)
    for half in range(2):
        out_ref[half * 8 : half * 8 + 8, :] = jnp.dot(
            tabs_ref[half], onehot, precision=HIGHEST, preferred_element_type=F32
        )


def head_row(pair, per_half):
    return 8 * lax.div(pair, per_half) + 2 * lax.rem(pair, per_half)


def bias_strip(row):
    spread = jnp.broadcast_to(row, (LANES, 4 * LANES))
    return pltpu.roll(spread, 3 * LANES, 1, stride=1, stride_axis=0)


def window(tile, rows, length):
    reach = -(-SPAN // rows)
    return max(0, (tile - reach) * rows), min(length, (tile + reach + 1) * rows)


def segment_lanes(seg):
    length = seg.shape[1]
    onehot = (seg == iota((LANES, length), 0)).astype(F32).T > 0.5
    inside = iota((length, LANES), 1) < 16
    return onehot, inside


def pair_cols(pair):
    return pl.ds(pl.multiple_of(pair * LANES, LANES), LANES)


def spread3(value):
    top = value.astype(BF).astype(F32)
    mid = (value - top).astype(BF).astype(F32)
    return top, mid, value - top - mid


TILE = 256
NEAR = SPAN // LANES


def key_lanes(seg):
    onehot, inside = segment_lanes(seg)
    return jnp.where(onehot, 0.0, jnp.where(inside, 1.0, 0.0)).astype(BF)


def fwd_setup(seg, tabs_ref, bias_ref, segq_ref, segk_ref):
    bias_rows(tabs_ref, bias_ref, False)
    onehot, _ = segment_lanes(seg)
    segq_ref[...] = jnp.where(onehot, MASK_OUT, 0.0).astype(BF)
    segk_ref[...] = key_lanes(seg)


def fwd_pair(pair, q_ref, k_ref, v_ref, ctx_ref, feat_ref, bias_ref, segq_ref, segk_ref):
    length, width = q_ref.shape
    per_half = width // LANES // 2
    tile, near = TILE, NEAR
    cols = pair_cols(pair)
    row = head_row(pair, per_half)
    lane = iota((tile, LANES), 1)
    low_half = lane < DH
    strips, fars = [], []
    for hh in range(2):
        line = bias_ref[pl.ds(row + hh, 1), :]
        strips.append(bias_strip(line))
        fars.append((line[:, 0:1], line[:, 4 * LANES - 1 : 4 * LANES]))
    for index in range(length // tile):
        rows = slice(index * tile, (index + 1) * tile)
        start, stop = window(index, tile, length)
        queries = q_ref[rows, cols]
        zero = jnp.zeros_like(queries)
        q_feat = segq_ref[rows, :]
        left = jnp.concatenate(
            [
                jnp.concatenate([jnp.where(low_half, queries, zero), q_feat], 1),
                jnp.concatenate([jnp.where(low_half, zero, queries), q_feat], 1),
            ],
            0,
        )
        right = jnp.concatenate([k_ref[start:stop, cols], segk_ref[start:stop, :]], 1)
        scores = nt(left, right)
        weights, peaks = [], []
        for hh in range(2):
            for part in range(tile // LANES):
                at = hh * tile + part * LANES
                q_block = index * (tile // LANES) + part
                blocks = []
                for k_block in range(start // LANES, stop // LANES):
                    delta = k_block - q_block
                    if abs(delta) > near:
                        blocks.append(None)
                        continue
                    col = k_block * LANES - start
                    block = scores[at : at + LANES, col : col + LANES]
                    if abs(delta) <= 1:
                        block = block + strips[hh][:, (delta + 1) * LANES : (delta + 2) * LANES]
                    else:
                        block = block + fars[hh][0 if delta < 0 else 1]
                    blocks.append(block)
                real = [block for block in blocks if block is not None]
                peak = functools.reduce(jnp.maximum, real)
                peak = jnp.max(peak, -1, keepdims=True)
                peaks.append(peak)
                weights.append(
                    jnp.concatenate(
                        [
                            jnp.zeros((LANES, LANES), BF)
                            if block is None
                            else jnp.exp(block - peak).astype(BF)
                            for block in blocks
                        ],
                        1,
                    )
                )
        values = v_ref[start:stop, cols]
        gathered = nn(
            jnp.concatenate(weights, 0), jnp.concatenate([values, jnp.ones_like(values)], 1)
        )
        normal = gathered[:, :LANES] / gathered[:, LANES:]
        context = jnp.where(low_half, normal[:tile], normal[tile:])
        ctx_ref[rows, cols] = context.astype(BF)
        logs = jnp.concatenate(peaks, 0) + jnp.log(gathered[:, LANES:])
        feature = q_feat.astype(F32)
        for hh in range(2):
            for i, piece in enumerate(spread3(logs[hh * tile : (hh + 1) * tile])):
                feature = jnp.where(lane == 16 + 3 * hh + i, -piece, feature)
        feat_ref[pair, rows, :] = feature.astype(BF)


def fwd_kernel(
    q_ref, k_ref, v_ref, seg_ref, tabs_ref, ctx_ref, feat_ref, bias_ref, segq_ref, segk_ref
):
    fwd_setup(seg_ref[...], tabs_ref, bias_ref, segq_ref, segk_ref)

    def one_pair(pair, carry):
        fwd_pair(pair, q_ref, k_ref, v_ref, ctx_ref, feat_ref, bias_ref, segq_ref, segk_ref)
        return carry

    lax.fori_loop(0, q_ref.shape[1] // LANES, one_pair, 0)


def bwd_setup(seg, tabs_ref, bias_ref, sums_ref, far_ref, segk_ref, blockof_ref):
    length = seg.shape[1]
    bias_rows(tabs_ref, bias_ref, True)
    sums_ref[...] = jnp.zeros_like(sums_ref)
    far_ref[...] = jnp.zeros_like(far_ref)
    segk_ref[...] = key_lanes(seg)
    blockof_ref[...] = (
        lax.div(iota((length, LANES), 0), LANES) == iota((length, LANES), 1)
    ).astype(BF)


def bwd_pair(
    pair,
    q_ref,
    k_ref,
    v_ref,
    go_ref,
    ctx_ref,
    feat_ref,
    dq_ref,
    dk_ref,
    dv_ref,
    bias_ref,
    sums_ref,
    far_ref,
    segk_ref,
    blockof_ref,
    gofeat_ref,
    near_ref,
    acc_ref,
):
    length, width = q_ref.shape
    per_half = width // LANES // 2
    tile, near = TILE, NEAR
    flip = (iota((LANES, LANES), 0) + iota((LANES, LANES), 1) == LANES - 1).astype(F32)
    cols = pair_cols(pair)
    row = head_row(pair, per_half)
    lane = iota((tile, LANES), 1)
    low_half = lane < DH
    strips, fars = [], []
    for hh in range(2):
        line = bias_ref[pl.ds(row + hh, 1), :]
        strips.append(bias_strip(line))
        fars.append((line[:, 0:1], line[:, 4 * LANES - 1 : 4 * LANES]))
    grads_all = go_ref[:, cols]
    product = grads_all.astype(F32) * ctx_ref[:, cols].astype(F32)
    lane_all = iota((length, LANES), 1)
    feature = jnp.zeros((length, LANES), F32)
    for hh in range(2):
        keep = (lane_all < DH) if hh == 0 else (lane_all >= DH)
        total = jnp.sum(jnp.where(keep, product, 0.0), -1, keepdims=True)
        for i, piece in enumerate(spread3(total)):
            feature = jnp.where(lane_all == 3 * hh + i, -piece, feature)
    gofeat_ref[...] = feature.astype(BF)
    near_ref[...] = jnp.zeros_like(near_ref)
    acc_ref[...] = jnp.zeros_like(acc_ref)
    far_sums = [[jnp.zeros((1, LANES), F32) for _ in range(2)] for _ in range(2)]
    lane_row = iota((1, LANES), 1)
    for index in range(length // tile):
        rows = slice(index * tile, (index + 1) * tile)
        start, stop = window(index, tile, length)
        keys, values = k_ref[rows, cols], v_ref[rows, cols]
        zero = jnp.zeros_like(keys)
        seg_feat = segk_ref[rows, :].astype(F32)

        def ones_at(base, first):
            return jnp.where((lane >= first) & (lane < first + 3), 1.0, base).astype(BF)

        masked_keys = jnp.concatenate(
            [jnp.where(low_half, keys, zero), jnp.where(low_half, zero, keys)], 0
        )
        masked_values = jnp.concatenate(
            [jnp.where(low_half, values, zero), jnp.where(low_half, zero, values)], 0
        )
        key_feats = jnp.concatenate([ones_at(seg_feat, 16), ones_at(seg_feat, 19)], 0)
        value_feats = jnp.concatenate([ones_at(0.0, 0), ones_at(0.0, 3)], 0)
        queries = q_ref[start:stop, cols]
        grads = go_ref[start:stop, cols]
        logits = nt(
            jnp.concatenate([masked_keys, key_feats], 1),
            jnp.concatenate([queries, feat_ref[pair, start:stop, :]], 1),
        )
        shifted = nt(
            jnp.concatenate([masked_values, value_feats], 1),
            jnp.concatenate([grads, gofeat_ref[start:stop, :]], 1),
        )
        probs_rows, score_rows = [], []
        for hh in range(2):
            for part in range(tile // LANES):
                at = hh * tile + part * LANES
                k_block = index * (tile // LANES) + part
                probs, score_grads = [], []
                for q_block in range(start // LANES, stop // LANES):
                    delta = k_block - q_block
                    if abs(delta) > near:
                        probs.append(jnp.zeros((LANES, LANES), BF))
                        score_grads.append(jnp.zeros((LANES, LANES), BF))
                        continue
                    col = q_block * LANES - start
                    block = logits[at : at + LANES, col : col + LANES]
                    place = (1 - delta) * LANES
                    if abs(delta) <= 1:
                        block = block + strips[hh][:, place : place + LANES]
                    else:
                        block = block + fars[hh][0 if delta > 0 else 1]
                    prob = jnp.exp(block)
                    grad = prob * shifted[at : at + LANES, col : col + LANES]
                    if abs(delta) <= 1:
                        near_ref[hh, :, place : place + LANES] += grad
                    probs.append(prob.astype(BF))
                    score_grads.append(grad.astype(BF))
                probs_rows.append(jnp.concatenate(probs, 1))
                score_rows.append(jnp.concatenate(score_grads, 1))
        probs_all = jnp.concatenate(probs_rows, 0)
        scores_all = jnp.concatenate(score_rows, 0)
        value_grad = nn(probs_all, grads)
        dv_ref[rows, cols] = jnp.where(low_half, value_grad[:tile], value_grad[tile:]).astype(BF)
        key_grad = nn(scores_all, jnp.concatenate([queries, blockof_ref[start:stop, :]], 1))
        dk_ref[rows, cols] = jnp.where(
            low_half, key_grad[:tile, :LANES], key_grad[tile:, :LANES]
        ).astype(BF)
        acc_ref[start:stop, :] += tn(scores_all, masked_keys)
        for hh in range(2):
            for part in range(tile // LANES):
                at = hh * tile + part * LANES
                k_block = index * (tile // LANES) + part
                line = jnp.sum(key_grad[at : at + LANES, LANES:], 0, keepdims=True)
                far_sums[hh][0] += jnp.where(lane_row <= k_block - 2, line, 0.0)
                far_sums[hh][1] += jnp.where(lane_row >= k_block + 2, line, 0.0)
    dq_ref[:, cols] = acc_ref[...].astype(BF)
    for hh in range(2):
        turned = jnp.dot(flip, near_ref[hh], precision=HIGHEST, preferred_element_type=F32)
        turned = jnp.concatenate([turned, jnp.zeros((LANES, LANES), F32)], 1)
        turned = pltpu.roll(turned, 1, 1, stride=1, stride_axis=0)
        sums_ref[pl.ds(row + hh, 1), :] = jnp.sum(turned, 0, keepdims=True)
        last = lane_row == 0
        positive = jnp.sum(far_sums[hh][0], -1, keepdims=True)
        negative = jnp.sum(far_sums[hh][1], -1, keepdims=True)
        far_ref[pl.ds(row + hh, 1), :] = jnp.where(last, positive, jnp.where(lane_row == 1, negative, 0.0))


def bwd_table(tabg_ref, sums_ref, far_ref):
    offsets = 2 * LANES - iota((LANES, 4 * LANES), 1)
    onehot_buckets = (bucket_ids(offsets) == iota((LANES, 4 * LANES), 0)).astype(F32)
    table = lax.dot_general(
        sums_ref[...],
        onehot_buckets,
        (((1,), (1,)), ((), ())),
        precision=HIGHEST,
        preferred_element_type=F32,
    )
    lane = iota(tabg_ref.shape, 1)
    far = far_ref[...]
    table = table + jnp.where(lane == 31, far[:, 0:1], 0.0) + jnp.where(lane == 15, far[:, 1:2], 0.0)
    tabg_ref[...] = table


def bwd_kernel(
    q_ref,
    k_ref,
    v_ref,
    go_ref,
    ctx_ref,
    feat_ref,
    seg_ref,
    tabs_ref,
    dq_ref,
    dk_ref,
    dv_ref,
    tabg_ref,
    bias_ref,
    sums_ref,
    far_ref,
    segk_ref,
    blockof_ref,
    gofeat_ref,
    near_ref,
    acc_ref,
):
    bwd_setup(seg_ref[...], tabs_ref, bias_ref, sums_ref, far_ref, segk_ref, blockof_ref)

    def one_pair(pair, carry):
        bwd_pair(
            pair,
            q_ref,
            k_ref,
            v_ref,
            go_ref,
            ctx_ref,
            feat_ref,
            dq_ref,
            dk_ref,
            dv_ref,
            bias_ref,
            sums_ref,
            far_ref,
            segk_ref,
            blockof_ref,
            gofeat_ref,
            near_ref,
            acc_ref,
        )
        return carry

    lax.fori_loop(0, q_ref.shape[1] // LANES, one_pair, 0)
    bwd_table(tabg_ref, sums_ref, far_ref)


def k3_before(xs_ref, ctx_ref, wo, gain, middle_ref, ffn_ref, ffnt_ref):
    step = 256

    def one(i, carry):
        rows = pl.ds(pl.multiple_of(i * step, step), step)
        middle = xs_ref[rows, :].astype(F32) + nt(ctx_ref[rows, :], wo)
        middle_ref[rows, :] = middle
        low = (middle * rms_scale(middle) * gain).astype(BF)
        ffn_ref[rows, :] = low
        ffnt_ref[:, rows] = low.T
        return carry

    lax.fori_loop(0, middle_ref.shape[0] // step, one, 0)


def transpose_rows(src_ref, dst_ref):
    step = 256

    def one(i, carry):
        rows = pl.ds(pl.multiple_of(i * step, step), step)
        dst_ref[:, rows] = src_ref[rows, :].T
        return carry

    lax.fori_loop(0, src_ref.shape[0] // step, one, 0)


def ffn_rows(i, half, w_in, w_back, first, ffn_ref, cot_ref, hid_ref, gp_ref, up_ref, down_ref):
    rows = pl.ds(pl.multiple_of(i * half, half), half)
    hidden, slope = gelu_pair(nn(ffn_ref[rows, :], w_in))
    hidden = hidden.astype(BF)
    hid_ref[rows, :] = hidden
    grad_pre = (nn(cot_ref[rows, :], w_back) * slope).astype(BF)
    gp_ref[rows, :] = grad_pre
    up = nt(hidden, w_back)
    down = nt(grad_pre, w_in)

    @pl.when(first)
    def _():
        up_ref[rows, :] = up
        down_ref[rows, :] = down

    @pl.when(jnp.logical_not(first))
    def _():
        up_ref[rows, :] += up
        down_ref[rows, :] += down


def after_rows(rows, cot, up_ref, down_ref, gain, gain_ref, gm_ref, ca_ref, cat_ref):
    middle = gm_ref[rows, :]
    scale = rms_scale(middle)
    normed = middle * scale
    down = down_ref[rows, :]
    gain_ref[...] += jnp.sum(down * normed, 0, keepdims=True)
    grad = cot + rms_back(down, normed, scale, gain)
    gm_ref[rows, :] = grad
    low = grad.astype(BF)
    ca_ref[rows, :] = low
    cat_ref[:, rows] = low.T
    return middle + up_ref[rows, :]


def context_grad(ca_ref, wo, go_ref):
    step = 256

    def one(i, carry):
        rows = pl.ds(pl.multiple_of(i * step, step), step)
        go_ref[rows, :] = nn(ca_ref[rows, :], wo).astype(BF)
        return carry

    lax.fori_loop(0, ca_ref.shape[0] // step, one, 0)


def k3_plain(
    xs_ref,
    ctx_ref,
    cot_ref,
    gain_ref,
    wo_ref,
    wi_ref,
    wb_ref,
    out_ref,
    gm_ref,
    go_ref,
    ggain_ref,
    gwo_ref,
    gwi_ref,
    gwb_ref,
    ffn_ref,
    ffnt_ref,
    cott_ref,
    cotb_ref,
    hid_ref,
    gp_ref,
    up_ref,
    down_ref,
):
    length = ctx_ref.shape[0]
    half_rows = length // 2
    chunk = hid_ref.shape[1]
    gain = gain_ref[...]
    cotb_ref[...] = cot_ref[...].astype(BF)
    k3_before(xs_ref, ctx_ref, wo_ref[...], gain, gm_ref, ffn_ref, ffnt_ref)
    transpose_rows(cotb_ref, cott_ref)

    def one_chunk(k, carry):
        cols = pl.ds(pl.multiple_of(k * chunk, LANES), chunk)
        w_in, w_back = wi_ref[:, cols], wb_ref[:, cols]
        for i in range(2):
            ffn_rows(
                i, half_rows, w_in, w_back, k == 0, ffn_ref, cotb_ref, hid_ref, gp_ref, up_ref, down_ref
            )
        gwb_ref[:, cols] = nn(cott_ref[...], hid_ref[...]).astype(BF)
        gwi_ref[:, cols] = nn(ffnt_ref[...], gp_ref[...]).astype(BF)
        return carry

    lax.fori_loop(0, wi_ref.shape[1] // chunk, one_chunk, 0)
    ggain_ref[...] = jnp.zeros_like(ggain_ref)
    step = 256

    def finish_rows(i, carry):
        rows = pl.ds(pl.multiple_of(i * step, step), step)
        out_ref[rows, :] = after_rows(
            rows,
            cot_ref[rows, :],
            up_ref,
            down_ref,
            gain,
            ggain_ref,
            gm_ref,
            ffn_ref,
            cott_ref,
        )
        return carry

    lax.fori_loop(0, length // step, finish_rows, 0)
    context_grad(ffn_ref, wo_ref[...], go_ref)
    gwo_ref[...] = nn(cott_ref[...], ctx_ref[...]).astype(BF)


def low_transposed(xs_ref, gain, lowt_ref):
    step = 256

    def one(i, carry):
        rows = pl.ds(pl.multiple_of(i * step, step), step)
        lowt_ref[:, rows] = project_rows(xs_ref[rows, :], gain).T
        return carry

    lax.fori_loop(0, xs_ref.shape[0] // step, one, 0)


def input_rows(rows, xs_ref, gm_ref, grads, weights, gain, gain_out):
    down = sum(nt(grad[rows, :], flat(weight[...])) for grad, weight in zip(grads, weights))
    inputs = xs_ref[rows, :].astype(F32)
    scale = rms_scale(inputs)
    normed = inputs * scale
    gain_out[...] += jnp.sum(down * normed, 0, keepdims=True)
    return gm_ref[rows, :] + rms_back(down, normed, scale, gain)


def k5_plain(
    xs_ref,
    gm_ref,
    dq_ref,
    dk_ref,
    dv_ref,
    wq_ref,
    wk_ref,
    wv_ref,
    gain_ref,
    ig_ref,
    gwq_ref,
    gwk_ref,
    gwv_ref,
    again_ref,
    lowt_ref,
):
    gain = gain_ref[...]
    low_transposed(xs_ref, gain, lowt_ref)
    grads, weights = (dq_ref, dk_ref, dv_ref), (wq_ref, wk_ref, wv_ref)
    for grad, out in zip(grads, (gwq_ref, gwk_ref, gwv_ref)):
        out[...] = nn(lowt_ref[...], grad[...]).astype(BF)
    again_ref[...] = jnp.zeros_like(again_ref)
    step = 256

    def one(i, carry):
        rows = pl.ds(pl.multiple_of(i * step, step), step)
        ig_ref[rows, :] = input_rows(rows, xs_ref, gm_ref, grads, weights, gain, again_ref)
        return carry

    lax.fori_loop(0, xs_ref.shape[0] // step, one, 0)


def as_row(vector):
    return vector.reshape(1, vector.shape[-1])


def turned_table(tab_ref, turn_ref):
    turn_ref[...] = jnp.zeros_like(turn_ref)
    turn_ref[: tab_ref.shape[0], : tab_ref.shape[1]] = tab_ref[...]
    return turn_ref[...].T[:8, :]


def run_all(steps):
    for step in steps:
        step()


def at_step(index, plan):
    for number, steps in enumerate(plan):
        if steps:

            @pl.when(index == number)
            def _(steps=steps):
                run_all(steps)


def forward_fused(
    depth,
    here,
    x_in,
    cot_in,
    gain_in,
    ffn_gain_in,
    tab_ref,
    seg_ref,
    wq_shard,
    wk_shard,
    wv_shard,
    wo_shard,
    wi_shard,
    wb_shard,
    xs_out,
    tabs_ref,
    q_out,
    k_out,
    v_out,
    ctx_out,
    feat_out,
    wq_out,
    wk_out,
    wv_out,
    own_out,
    oth_out,
    gm_out,
    go_out,
    ggain_ref,
    gout_out,
    gwi_ref,
    gwb_ref,
    gi_out,
    gb_out,
    xs_ref,
    cotf_ref,
    cotb_ref,
    obuf_ref,
    q_ref,
    k_ref,
    v_ref,
    ctx_ref,
    feat_ref,
    wq_ref,
    wk_ref,
    wv_ref,
    wo_ref,
    wi_ref,
    wb_ref,
    low_ref,
    turn_ref,
    bias_ref,
    segq_ref,
    segk_ref,
    gm_ref,
    ffnt_ref,
    cott_ref,
    up_ref,
    down_ref,
    i0,
    i1,
    i2,
    i3,
    b0,
    b1,
    b2,
    b3,
    r_send,
    r_recv,
    g_send,
    g_recv,
    s_send,
    s_recv,
    x_send,
    x_recv,
    l_sem,
    c_sem,
):
    p = Place(depth)
    length = q_ref.shape[0]
    half_rows = length // 2
    width = wo_shard.shape[1]
    groups = wq_ref.shape[0]
    chunks, part = wi_ref.shape[0], wi_ref.shape[-1] // 2
    x_sems, g_sems, r_sems, s_sems = (
        (x_send, x_recv),
        (g_send, g_recv),
        (r_send, r_recv),
        (s_send, s_recv),
    )
    gain, ffn_gain = as_row(gain_in[...]), as_row(ffn_gain_in[...])
    weights = (wq_ref, wk_ref, wv_ref)
    x_own = local(x_in.at[p.t], xs_ref.at[p.t], l_sem.at[0])
    x_own.start()
    cot_load = local(cot_in.at[1 - p.t], cotf_ref, l_sem.at[1])
    cot_load.start()
    heads = []
    for j in range(groups):
        trio = []
        for i, (ref, shard) in enumerate(zip(weights, (wq_shard, wk_shard, wv_shard))):
            item = Gather(p, ref.at[j], LANES, r_sems, 3 * j + i, True)
            item.block(p.z, 0)[...] = shard[:, j * LANES : (j + 1) * LANES]
            trio.append(item)
        heads.append(trio)
    out_item = Gather(p, wo_ref, width, g_sems, 0, True)
    out_item.block(p.z, 0)[...] = wo_shard[...]
    items = []
    for k in range(chunks):
        pair = []
        for side, (ref, shard) in enumerate(((wi_ref, wi_shard), (wb_ref, wb_shard))):
            item = Gather(p, ref.at[k], part, g_sems, 1 + 2 * k + side, side == 0 or k < 2)
            item.block(p.z, 0)[...] = shard[:, k * part : (k + 1) * part]
            pair.append(item)
        items.append(pair)

    tabs_ref[p.t] = turned_table(tab_ref, turn_ref)
    p.barrier()
    moves = [
        remote(x_in.at[1 - p.t], xs_ref.at[p.t], x_sems, 0, p.xpeer),
        remote(tabs_ref.at[p.t], tabs_ref.at[p.t], x_sems, 1, p.xpeer),
        remote(obuf_ref, cotb_ref.at[p.t], x_sems, 2, p.xpeer),
    ]

    def head(j, name):
        return [getattr(item, name) for item in heads[j]]

    def both(items):
        return [functools.partial(item.step2, side) for side in range(2) for item in items]

    run_all(head(0, "start") + head(1, "start") + head(2, "start"))
    run_all([out_item.start])
    for item in items[0]:
        item.start()
    moves[1].start()
    moves[0].start()
    run_all(head(0, "start_z") + head(1, "start_z"))
    def chunk(k, *names):
        steps = []
        for name in names if k < chunks else ():
            if name == "both":
                steps += both(items[k])
            else:
                steps += [getattr(item, name) for item in items[k]]
        return steps

    def rows_of(half):
        return pl.ds(pl.multiple_of(half * half_rows, half_rows), half_rows)

    def project_group(j, half):
        rows = rows_of(half)
        for weight, out in zip(weights, (q_ref, k_ref, v_ref)):
            result = nn(low_ref[rows, :], flat(weight[j])).astype(BF)
            out[rows, pair_cols(j)] = result[:, :LANES]
            out[rows, pair_cols(j + groups)] = result[:, LANES:]

    run_all(head(0, "step1") + head(1, "step1") + head(2, "start_z"))
    x_own.wait()
    low_ref[rows_of(p.t), :] = project_rows(xs_ref[p.t], gain)
    run_all(both(heads[0]) + head(2, "step1"))
    cot_load.wait()
    obuf_ref[...] = cotf_ref[...].astype(BF)
    own_load = local(cot_in.at[p.t], cotf_ref, l_sem.at[1])
    own_load.start()
    run_all(both(heads[1]))
    moves[1].wait_recv()
    fwd_setup(seg_ref[p.t], tabs_ref, bias_ref, segq_ref, segk_ref)
    run_all(head(0, "step3") + [out_item.start_z, out_item.step1])
    run_all(both(heads[2]) + head(0, "finish"))
    project_group(0, p.t)
    run_all(chunk(0, "start_z", "step1"))
    moves[0].wait_recv()
    for k in range(1, chunks):
        run_all(chunk(k, "start"))
    moves[2].start()
    low_ref[rows_of(1 - p.t), :] = project_rows(xs_ref[1 - p.t], gain)
    project_group(0, 1 - p.t)

    def save(index, src, dst):
        return local(src, dst, l_sem.at[index])

    saves = [
        save(2 + i, src, dst)
        for i, (src, dst) in enumerate(
            (
                (xs_ref, xs_out),
                (wq_ref, wq_out),
                (wk_ref, wk_out),
                (wv_ref, wv_out),
                (ctx_ref, ctx_out),
                (feat_ref, feat_out),
                (obuf_ref, oth_out),
                (cotf_ref, own_out),
                (gm_ref, gm_out),
                (v_ref, go_out),
                (wo_ref, gout_out),
            )
        )
    ]
    qkv_saves = [
        save(13 + i, src, dst)
        for i, (src, dst) in enumerate(((q_ref, q_out), (k_ref, k_out), (v_ref, v_out)))
    ]

    plan = [
        head(1, "step3") + both([out_item]) + chunk(1, "start_z", "step1"),
        head(2, "step3") + chunk(0, "both"),
        head(1, "finish") + chunk(2, "start_z", "step1"),
        [out_item.step3] + chunk(1, "both"),
        head(2, "finish") + chunk(0, "step3") + chunk(3, "start_z", "step1") + chunk(2, "both"),
        [out_item.finish] + [one.start for one in qkv_saves + saves[:4]],
    ]

    def one_pair(index, carry):
        j, side = lax.div(index, 2), lax.rem(index, 2)
        at_step(index, plan)

        @pl.when((side == 0) & (j > 0))
        def _():
            def one(half, carry):
                project_group(j, half)
                return carry

            lax.fori_loop(0, 2, one, 0)

        pair = j + groups * side
        fwd_pair(pair, q_ref, k_ref, v_ref, ctx_ref, feat_ref, bias_ref, segq_ref, segk_ref)
        return carry

    lax.fori_loop(0, 2 * groups, one_pair, 0)
    saves[4].start()
    saves[5].start()
    run_all(chunk(1, "step3") + chunk(3, "both") + chunk(4, "start_z", "step1"))
    xs = xs_ref.reshape(length, xs_ref.shape[2])
    k3_before(xs, ctx_ref, flat(wo_ref[...]), ffn_gain, gm_ref, low_ref, ffnt_ref)
    run_all(chunk(0, "finish") + chunk(2, "step3"))
    moves[2].wait_recv()
    moves[2].wait_send()
    own_load.wait()
    cotb_ref[p.t] = cotf_ref[...].astype(BF)
    cotb = cotb_ref.reshape(length, cotb_ref.shape[2])
    transpose_rows(cotb, cott_ref)
    for one in qkv_saves:
        one.wait()
    hid_ref, gp_ref = q_ref.at[:, : 2 * part], k_ref.at[:, : 2 * part]

    def s_chunk(k):
        return (
            Scatter(
                p, wi_ref.at[k], part, [r.at[k] for r in (i0, i1, i2, i3)], s_sems, 2 * k, True
            ),
            Scatter(
                p, wb_ref.at[k], part, [r.at[k] for r in (b0, b1, b2, b3)], s_sems, 1 + 2 * k, False
            ),
        )

    def save_chunk(k):
        return (
            local(wi_ref.at[k], gi_out.at[k - here], c_sem.at[2 * k]),
            local(wb_ref.at[k], gb_out.at[k - here], c_sem.at[1 + 2 * k]),
        )

    def when_scatter(k, name):
        @pl.when((k >= 0) & (k < here))
        def _():
            for item, out in zip(s_chunk(k), (gwi_ref, gwb_ref)):
                if name == "finish":
                    item.finish(out, k * part)
                else:
                    getattr(item, name)()

    begin = [
        chunk(4, "both") + chunk(5, "start_z", "step1"),
        chunk(1, "finish") + chunk(5, "both") + chunk(4, "step3"),
        chunk(2, "finish") + chunk(5, "step3"),
    ]
    begin += [chunk(k, "finish") for k in range(3, chunks)]
    middle = [chunk(3, "step3")]

    def one_chunk(k, carry):
        at_step(k, begin)
        w_in, w_back = flat(wi_ref[k]), flat(wb_ref[k])
        args = (w_in, w_back, k == 0, low_ref, cotb, hid_ref, gp_ref, up_ref, down_ref)
        ffn_rows(0, half_rows, *args)
        when_scatter(k - 3, "step3")
        when_scatter(k - 2, "step2")
        when_scatter(k - 1, "step1")
        at_step(k, middle)
        ffn_rows(1, half_rows, *args)
        wb_ref[k] = nn(cott_ref[...], hid_ref[...]).astype(BF).reshape(wb_ref.shape[1:])
        when_scatter(k - 4, "finish")
        wi_ref[k] = nn(ffnt_ref[...], gp_ref[...]).astype(BF).reshape(wi_ref.shape[1:])
        when_scatter(k, "step0")

        @pl.when(k >= here)
        def _():
            for one in save_chunk(k):
                one.start()

        return carry

    lax.fori_loop(0, chunks, one_chunk, 0)
    ggain_ref[...] = jnp.zeros_like(ggain_ref)
    step = 256

    def finish_rows(own, i):
        half = p.t if own else 1 - p.t
        at = pl.ds(pl.multiple_of(i * step, step), step)
        rows = pl.ds(pl.multiple_of(half * half_rows + i * step, step), step)
        cot = cotf_ref[at, :] if own else cotb_ref[1 - p.t, at, :].astype(F32)
        out = after_rows(
            rows, cot, up_ref, down_ref, ffn_gain, ggain_ref, gm_ref, low_ref, cott_ref
        )
        if own:
            cotf_ref[at, :] = out
        else:
            obuf_ref[at, :] = out.astype(BF)

    for i in range(half_rows // step):
        finish_rows(False, i)
    saves[6].start()
    for stage, name in ((1, "step1"), (2, "step2"), (3, "step3")):
        for k in range(max(0, chunks - stage), here):
            when_scatter(k, name)
    for i in range(half_rows // step):
        finish_rows(True, i)
    saves[7].start()
    saves[8].start()
    context_grad(low_ref, flat(wo_ref[...]), v_ref)
    saves[9].start()
    wo_ref[...] = nn(cott_ref[...], ctx_ref[...]).astype(BF).reshape(wo_ref.shape)
    saves[10].start()
    for k in range(max(0, chunks - 4), here):
        when_scatter(k, "finish")
    for move in moves[:2]:
        move.wait_send()
    for one in saves:
        one.wait()
    for k in range(here, chunks):
        for one in save_chunk(k):
            one.wait()


def back_fused(
    depth,
    q_in,
    k_in,
    v_in,
    go_ref,
    ctx_ref,
    feat_ref,
    seg_ref,
    tabs_ref,
    xs_in,
    gm_in,
    wq_in,
    wk_in,
    wv_in,
    gain_in,
    ggain_ref,
    gi_in,
    gb_in,
    gout_in,
    oth_in,
    oth_out,
    igown_ref,
    ibuf2_ref,
    gwo_ref,
    gwq_ref,
    gwk_ref,
    gwv_ref,
    gwi_ref,
    gwb_ref,
    small_ref,
    q_ref,
    k_ref,
    v_ref,
    xs_ref,
    gm_ref,
    wq_ref,
    wk_ref,
    wv_ref,
    gi_ref,
    gb_ref,
    gout_ref,
    lowt_ref,
    sum_ref,
    gq_ref,
    gk_ref,
    gv_ref,
    ibuf_ref,
    again_ref,
    tabg_ref,
    sm_ref,
    smr_ref,
    bias_ref,
    sums_ref,
    far_ref,
    segk_ref,
    blockof_ref,
    gofeat_ref,
    near_ref,
    acc_ref,
    o0,
    o1,
    o2,
    o3,
    i0,
    i1,
    i2,
    i3,
    b0,
    b1,
    b2,
    b3,
    a0,
    a1,
    a2,
    a3,
    c0,
    c1,
    c2,
    c3,
    d0,
    d1,
    d2,
    d3,
    s_send,
    s_recv,
    x_send,
    x_recv,
    l_sem,
):
    p = Place(depth)
    length = q_ref.shape[0]
    half_rows = length // 2
    groups = gq_ref.shape[0]
    rest, part = gi_ref.shape[0], gi_ref.shape[-1] // 2
    s_sems, x_sems = (s_send, s_recv), (x_send, x_recv)
    pairs = [(q_in, q_ref), (k_in, k_ref), (v_in, v_ref), (xs_in, xs_ref)]
    pairs += [(gi_in, gi_ref), (gb_in, gb_ref), (gout_in, gout_ref), (gm_in, gm_ref)]
    pairs += [(wq_in, wq_ref), (wk_in, wk_ref), (wv_in, wv_ref)]
    loads = [local(src, dst, l_sem.at[i]) for i, (src, dst) in enumerate(pairs)]
    for one in loads:
        one.start()
    bwd_setup(seg_ref[p.t], tabs_ref, bias_ref, sums_ref, far_ref, segk_ref, blockof_ref)
    p.barrier()
    quarter = half_rows // 4
    out_moves = [
        remote(
            oth_in.at[pl.ds(i * quarter, quarter)],
            oth_out.at[pl.ds(i * quarter, quarter)],
            x_sems,
            depth + 6 + i,
            p.xpeer,
        )
        for i in range(4)
    ]
    out_item = Scatter(
        p, gout_ref, gwo_ref.shape[1], (o0, o1, o2, o3), s_sems, 2 * rest + 3 * groups, True
    )
    rest_items = []
    for k in range(rest):
        rest_items.append(
            [
                Scatter(
                    p, gi_ref.at[k], part, [r.at[k] for r in (i0, i1, i2, i3)], s_sems, 2 * k, True
                ),
                Scatter(
                    p,
                    gb_ref.at[k],
                    part,
                    [r.at[k] for r in (b0, b1, b2, b3)],
                    s_sems,
                    2 * k + 1,
                    True,
                ),
            ]
        )
    group_items = []
    for j in range(groups):
        group_items.append(
            [
                Scatter(
                    p,
                    ref.at[j],
                    LANES,
                    [r.at[j] for r in bufs],
                    s_sems,
                    2 * rest + 3 * j + i,
                    True,
                )
                for i, (ref, bufs) in enumerate(
                    (
                        (gq_ref, (a0, a1, a2, a3)),
                        (gk_ref, (c0, c1, c2, c3)),
                        (gv_ref, (d0, d1, d2, d3)),
                    )
                )
            ]
        )

    def chunk(k, name):
        if k >= rest:
            return []
        if name == "finish":
            return [
                functools.partial(item.finish, out, k * part)
                for item, out in zip(rest_items[k], (gwi_ref, gwb_ref))
            ]
        return [getattr(item, name) for item in rest_items[k]]

    def group(j, name):
        if name == "finish":
            return [
                functools.partial(item.finish, out, j * LANES)
                for item, out in zip(group_items[j], (gwq_ref, gwk_ref, gwv_ref))
            ]
        return [getattr(item, name) for item in group_items[j]]

    for one in loads[:7]:
        one.wait()
    run_all(chunk(0, "step0"))
    xs = xs_ref.reshape(length, xs_ref.shape[2])
    gain = as_row(gain_in[...])
    low_transposed(xs, gain, lowt_ref)
    run_all(chunk(0, "step1") + chunk(1, "step0"))
    for one in loads[7:]:
        one.wait()

    def group_cols(ref, j):
        return [ref[:, pair_cols(j)], ref[:, pair_cols(j + groups)]]

    def weight_grads(j):
        for target, grad in zip((gq_ref, gk_ref, gv_ref), (q_ref, k_ref, v_ref)):
            both = jnp.concatenate(group_cols(grad, j), 1)
            target[j] = nn(lowt_ref[...], both).astype(BF).reshape(target.shape[1:])

    def group_weights(j):
        pieces = []
        for weight in (wq_ref, wk_ref, wv_ref):
            pieces.append(flat(weight[j]))
        return jnp.concatenate(pieces, 1)

    def group_sum(rows, j):
        pieces = []
        for grad in (q_ref, k_ref, v_ref):
            for at in (j, j + groups):
                pieces.append(grad[rows, pair_cols(at)])
        return nt(jnp.concatenate(pieces, 1), group_weights(j))

    step = 256
    plan = [
        [out_moves[0].start],
        chunk(0, "step2") + chunk(1, "step1") + [out_item.step0, out_moves[1].start],
        chunk(0, "step3") + chunk(1, "step2") + [out_item.step1, out_moves[2].start],
        chunk(0, "finish") + chunk(1, "step3") + group(0, "step1") + [out_item.step2],
        chunk(1, "finish") + group(0, "step2") + [out_item.step3, out_moves[3].start],
        group(0, "step3") + group(1, "step1") + [functools.partial(out_item.finish, gwo_ref, 0)],
    ]

    def one_pair(index, carry):
        at_step(index, plan)
        j, side = lax.div(index, 2), lax.rem(index, 2)
        bwd_pair(
            j + groups * side,
            q_ref,
            k_ref,
            v_ref,
            go_ref,
            ctx_ref,
            feat_ref,
            q_ref,
            k_ref,
            v_ref,
            bias_ref,
            sums_ref,
            far_ref,
            segk_ref,
            blockof_ref,
            gofeat_ref,
            near_ref,
            acc_ref,
        )

        @pl.when((side == 1) & (j < groups - 1))
        def _():
            weight_grads(j)
            for i in range(groups - 1):

                @pl.when(j == i)
                def _():
                    run_all(group(i, "step0"))

            for i in range(groups - 1):

                @pl.when(j == i)
                def _():
                    for at in range(length // step):
                        rows = slice(at * step, (at + 1) * step)
                        if i == 0:
                            sum_ref[rows, :] = group_sum(rows, i)
                        else:
                            sum_ref[rows, :] += group_sum(rows, i)

        return carry

    lax.fori_loop(0, 2 * groups, one_pair, 0)
    again_ref[...] = jnp.zeros_like(again_ref)
    last = groups - 1

    def finish_rows(own, i):
        half = p.t if own else 1 - p.t
        at = pl.ds(pl.multiple_of(i * step, step), step)
        rows = pl.ds(pl.multiple_of(half * half_rows + i * step, step), step)
        down = sum_ref[rows, :] + group_sum(rows, last)
        inputs = xs_ref[half, at, :].astype(F32)
        scale = rms_scale(inputs)
        normed = inputs * scale
        again_ref[...] += jnp.sum(down * normed, 0, keepdims=True)
        out = gm_ref[rows, :] + rms_back(down, normed, scale, gain)
        if own:
            igown_ref[at, :] = out
        else:
            ibuf_ref[at, :] = out.astype(BF)

    def piece(i):
        size = half_rows // 4
        at = pl.ds(i * size, size)
        return remote(ibuf_ref.at[at], ibuf2_ref.at[at], x_sems, i, p.xpeer)

    moves = [piece(i) for i in range(4)]
    finish_rows(False, 0)
    moves[0].start()
    moves[1].start()
    weight_grads(last)
    run_all(group(last, "step0") + group(1, "step2"))
    finish_rows(False, 1)
    moves[2].start()
    run_all(group(last, "step1"))
    for i in range(half_rows // step):
        finish_rows(True, i)
    bwd_table(tabg_ref, sums_ref, far_ref)
    run_all(group(0, "finish") + group(last, "step2"))
    moves[3].start()
    model = again_ref.shape[1]
    sm_ref[0, 0:1, :model] = again_ref[...]
    sm_ref[0, 1:2, :model] = ggain_ref[...]
    sm_ref[0, 2:8, :model] = jnp.zeros((6, model), F32)
    sm_ref[0, :, model : model + LANES] = tabg_ref[0:8, :]
    sm_ref[0, :, model + LANES :] = tabg_ref[8:16, :]
    hops = [(p.sib,), (p.ypeer,), (p.xpeer,), tuple(p.zpeers)]
    slot = 0
    beside = [
        group(1, "step3"),
        group(last, "step3"),
        group(1, "finish"),
        [],
    ]
    for level, peers in enumerate(hops):
        hop = [
            remote(sm_ref.at[level], smr_ref.at[slot + i], x_sems, len(moves) + slot + i, peer)
            for i, peer in enumerate(peers)
        ]
        for one in hop:
            one.start()
        run_all(beside[level])
        total = sm_ref[level]
        for i, one in enumerate(hop):
            one.wait_recv()
            total = total + smr_ref[slot + i]
        slot += len(peers)
        if level + 1 < len(hops):
            sm_ref[level + 1] = total
        else:
            small_ref[...] = total
        for one in hop:
            one.wait_send()
    run_all(group(last, "finish"))
    for move in moves + out_moves:
        move.wait_recv()
        move.wait_send()


def collect(
    own_in,
    oth_ref,
    igown_in,
    igoth_ref,
    small_ref,
    gwi_a,
    gwi_b,
    gwb_a,
    gwb_b,
    gwo_in,
    gwq_in,
    gwk_in,
    gwv_in,
    out_ref,
    ig_ref,
    again_ref,
    ggain_ref,
    gwq_ref,
    gwk_ref,
    gwv_ref,
    gwo_ref,
    gwi_ref,
    gwb_ref,
    table_ref,
    wide_ref,
    turn_ref,
    sem,
):
    t = lax.axis_index("tensor")
    loads = [
        local(own_in, wide_ref.at[0], sem.at[0]),
        local(igown_in, wide_ref.at[1], sem.at[1]),
    ]
    for one in loads:
        one.start()
    copies = []
    for i, (src, dst) in enumerate(((oth_ref, out_ref), (igoth_ref, ig_ref))):
        wide_ref[2 + i] = src[...].astype(F32)
        copies.append(local(wide_ref.at[2 + i], dst.at[1 - t], sem.at[2 + i]))
        copies[-1].start()
    for i, dst in enumerate((out_ref, ig_ref)):
        loads[i].wait()
        copies.append(local(wide_ref.at[i], dst.at[t], sem.at[4 + i]))
        copies[-1].start()
    for src, dst in ((gwq_in, gwq_ref), (gwk_in, gwk_ref), (gwv_in, gwv_ref), (gwo_in, gwo_ref)):
        dst[...] = src[...]
    for first, second, dst in ((gwi_a, gwi_b, gwi_ref), (gwb_a, gwb_b, gwb_ref)):
        dst[:, : first.shape[1]] = first[...]
        dst[:, first.shape[1] :] = second[...]
    model = again_ref.shape[0]
    again_ref[...] = small_ref[0:1, :model].reshape(model)
    ggain_ref[...] = small_ref[1:2, :model].reshape(model)
    turn_ref[...] = jnp.zeros_like(turn_ref)
    first = small_ref[:, model : model + LANES]
    second = small_ref[:, model + LANES :]
    turn_ref[0:8, :] = jnp.where(t == 0, first, second)
    table_ref[...] = turn_ref[...].T[: table_ref.shape[0], : table_ref.shape[1]]
    for one in copies:
        one.wait()


def call(kernel, outs, scratch, args, name, collective=None, far=()):
    def spec(array):
        return pl.BlockSpec(memory_space=pl.ANY if array in far else pltpu.VMEM)

    if collective is None:
        params = pltpu.CompilerParams(vmem_limit_bytes=VMEM_BYTES)
    else:
        params = pltpu.CompilerParams(
            vmem_limit_bytes=VMEM_BYTES, collective_id=collective, has_side_effects=True
        )
    return pl.pallas_call(
        kernel,
        out_shape=[jax.ShapeDtypeStruct(shape, dtype) for shape, dtype in outs],
        in_specs=[spec(i) for i in range(len(args))],
        out_specs=[spec(len(args) + i) for i in range(len(outs))],
        scratch_shapes=scratch,
        compiler_params=params,
        name=name,
    )(*args)


def shards(
    inputs,
    segments,
    norm_attn,
    norm_ffn,
    w_query,
    w_key,
    w_value,
    w_out,
    w_in,
    w_back,
    rel_table,
    cotangent,
):
    dp, tensor = lax.axis_size("dp"), lax.axis_size("tensor")
    t = lax.axis_index("tensor")
    rows, width = w_query.shape
    hidden_part = w_in.shape[1]
    model = inputs.shape[2]
    length = segments.shape[2]
    half = inputs.shape[1]
    buckets, heads = rel_table.shape
    depth = dp // 4
    fused = rows % 16 == 0 and dp % 4 == 0 and depth >= 2
    full = (length, model)
    inner = (length, width * tensor)
    square = (depth, 2, 2, rows, 2 * width)
    part = 256
    chunks = hidden_part // part
    pairs = inner[1] // LANES
    dma = pltpu.SemaphoreType.DMA
    halves = (2, half, model)
    fwd_work = [pltpu.VMEM((16, 4 * LANES), F32)] + [pltpu.VMEM((length, LANES), BF)] * 2
    bwd_work = [
        pltpu.VMEM((16, 4 * LANES), F32),
        pltpu.VMEM((16, 4 * LANES), F32),
        pltpu.VMEM((16, LANES), F32),
        pltpu.VMEM((length, LANES), BF),
        pltpu.VMEM((length, LANES), BF),
        pltpu.VMEM((length, LANES), BF),
        pltpu.VMEM((2, LANES, 3 * LANES), F32),
        pltpu.VMEM((length, LANES), F32),
    ]
    ffn_work = [pltpu.VMEM(full, BF), pltpu.VMEM(full[::-1], BF), pltpu.VMEM(full[::-1], BF)]
    rest = [pltpu.VMEM((length, 2 * part), BF)] * 2 + [pltpu.VMEM(full, F32)] * 2
    if fused:
        here = chunks - chunks // 3
        block = (depth, 2, 2, rows, 2 * part)
        groups = pairs // 2
        narrow = (groups, depth, 2, 2, rows, 2 * LANES)
        (
            xs,
            tabs,
            queries,
            keys,
            values,
            ctx,
            feats,
            wq,
            wk,
            wv,
            own,
            oth,
            grad_middle,
            grad_context,
            ggain,
            gout,
            gwi_a,
            gwb_a,
            gi,
            gb,
        ) = call(
            functools.partial(forward_fused, depth, here),
            [
                (halves, BF),
                ((2, 8, LANES), F32),
                (inner, BF),
                (inner, BF),
                (inner, BF),
                (inner, BF),
                ((pairs, length, LANES), BF),
                (narrow, BF),
                (narrow, BF),
                (narrow, BF),
                ((half, model), F32),
                ((half, model), BF),
                (full, F32),
                (inner, BF),
                ((1, model), F32),
                (square, BF),
                ((rows, here * part), F32),
                ((rows, here * part), F32),
                ((chunks - here,) + block, BF),
                ((chunks - here,) + block, BF),
            ],
            [
                pltpu.VMEM(halves, BF),
                pltpu.VMEM((half, model), F32),
                pltpu.VMEM(halves, BF),
                pltpu.VMEM((half, model), BF),
            ]
            + [pltpu.VMEM(inner, BF)] * 4
            + [pltpu.VMEM((pairs, length, LANES), BF)]
            + [pltpu.VMEM(narrow, BF)] * 3
            + [pltpu.VMEM(square, BF)]
            + [pltpu.VMEM((chunks,) + block, BF)] * 2
            + [pltpu.VMEM(full, BF), pltpu.VMEM((LANES, LANES), F32)]
            + fwd_work
            + [pltpu.VMEM(full, F32)]
            + [pltpu.VMEM(full[::-1], BF)] * 2
            + [pltpu.VMEM(full, F32)] * 2
            + scatter_bufs(here, depth, rows, part, True)
            + scatter_bufs(here, depth, rows, part, False)
            + gather_sems(3 * groups, depth)
            + gather_sems(1 + 2 * chunks, depth)
            + scatter_sems(2 * here, depth)
            + [dma((3,)), dma((3,)), dma((16,)), dma((2 * chunks,))],
            (
                inputs,
                cotangent,
                norm_attn,
                norm_ffn,
                rel_table,
                segments,
                w_query,
                w_key,
                w_value,
                w_out,
                w_in,
                w_back,
            ),
            "forward_feed_forward",
            0,
            (0, 1, 12, 14, 15, 16, 17, 18, 19, 20, 21, 22, 23, 24, 25, 27, 30, 31),
        )
        left = chunks - here
        oth, igown, igoth, gwo, gwq, gwk, gwv, gwi_b, gwb_b, small = call(
            functools.partial(back_fused, depth),
            [
                ((half, model), BF),
                ((half, model), F32),
                ((half, model), BF),
                ((rows, width), F32),
                ((rows, width), F32),
                ((rows, width), F32),
                ((rows, width), F32),
                ((rows, left * part), F32),
                ((rows, left * part), F32),
                ((8, model + 2 * LANES), F32),
            ],
            [pltpu.VMEM(inner, BF)] * 3
            + [pltpu.VMEM(halves, BF), pltpu.VMEM(full, F32)]
            + [pltpu.VMEM(narrow, BF)] * 3
            + [pltpu.VMEM((left,) + block, BF)] * 2
            + [pltpu.VMEM(square, BF)]
            + [pltpu.VMEM(full[::-1], BF), pltpu.VMEM(full, F32)]
            + [pltpu.VMEM(narrow, BF)] * 3
            + [pltpu.VMEM((half, model), BF)]
            + [
                pltpu.VMEM((1, model), F32),
                pltpu.VMEM((16, LANES), F32),
                pltpu.VMEM((4, 8, model + 2 * LANES), F32),
                pltpu.VMEM((depth + 2, 8, model + 2 * LANES), F32),
            ]
            + bwd_work
            + scatter_bufs(None, depth, rows, width, True)
            + scatter_bufs(left, depth, rows, part, True)
            + scatter_bufs(left, depth, rows, part, True)
            + scatter_bufs(groups, depth, rows, LANES, True)
            + scatter_bufs(groups, depth, rows, LANES, True)
            + scatter_bufs(groups, depth, rows, LANES, True)
            + scatter_sems(1 + 2 * left + 3 * groups, depth)
            + [dma((depth + 10,)), dma((depth + 10,)), dma((11,))],
            (
                queries,
                keys,
                values,
                grad_context,
                ctx,
                feats,
                segments,
                tabs,
                xs,
                grad_middle,
                wq,
                wk,
                wv,
                norm_attn,
                ggain,
                gi,
                gb,
                gout,
                oth,
            ),
            "attention_backward",
            1,
            (0, 1, 2, 8, 9, 10, 11, 12, 15, 16, 17, 18, 19),
        )
        return tuple(
            call(
                collect,
                [
                    (halves, F32),
                    (halves, F32),
                    ((model,), F32),
                    ((model,), F32),
                    ((rows, width), F32),
                    ((rows, width), F32),
                    ((rows, width), F32),
                    ((rows, width), F32),
                    ((rows, hidden_part), F32),
                    ((rows, hidden_part), F32),
                    ((buckets, heads), F32),
                ],
                [pltpu.VMEM((4, half, model), F32), pltpu.VMEM((LANES, LANES), F32), dma((6,))],
                (own, oth, igown, igoth, small, gwi_a, gwi_b, gwb_a, gwb_b, gwo, gwq, gwk, gwv),
                "collect",
                None,
                (0, 2, 13, 14),
            )
        )
    else:
        gain_attn, gain_ffn = norm_attn.reshape(1, model), norm_ffn.reshape(1, model)
        table = jnp.pad(rel_table.T, ((0, 8 - heads), (0, LANES - buckets)))
        segment = lax.dynamic_index_in_dim(segments, t, 0, False)

        def whole(weight):
            weight = lax.all_gather(weight, "dp", axis=0, tiled=True)
            return lax.all_gather(weight, "tensor", axis=1, tiled=True)

        def exchanged(local_part):
            own = lax.dynamic_index_in_dim(local_part, t, 0, False)
            other = lax.dynamic_index_in_dim(local_part, 1 - t, 0, False)
            other = lax.ppermute(other, "tensor", [(0, 1), (1, 0)])
            first = jnp.where(t == 0, own, other)
            second = jnp.where(t == 0, other, own)
            return jnp.concatenate([first, second], 0)

        def returned(seq):
            mine = lax.dynamic_slice_in_dim(seq, t * half, half, 0)
            other = lax.dynamic_slice_in_dim(seq, (1 - t) * half, half, 0)
            other = lax.ppermute(other, "tensor", [(0, 1), (1, 0)])
            return jnp.stack([jnp.where(t == 0, mine, other), jnp.where(t == 0, other, mine)])

        def scattered(grad):
            grad = lax.psum_scatter(grad.astype(F32), "tensor", scatter_dimension=1, tiled=True)
            return lax.psum_scatter(grad, "dp", scatter_dimension=0, tiled=True)

        xs = exchanged(inputs)
        tabs = lax.all_gather(table, "tensor", axis=0)
        wq, wk, wv, wo, wi, wb = (
            whole(w) for w in (w_query, w_key, w_value, w_out, w_in, w_back)
        )
        queries, keys, values = call(
            k1_plain,
            [(inner, BF)] * 3,
            [pltpu.VMEM(full, BF)],
            (xs, gain_attn, wq, wk, wv),
            "project",
        )
        ctx, feats = call(
            fwd_kernel,
            [(inner, BF), ((pairs, length, LANES), BF)],
            fwd_work,
            (queries, keys, values, segment, tabs),
            "attention_forward",
        )
        out_seq, grad_middle, grad_context, ggain, gwo, gwi, gwb = call(
            k3_plain,
            [
                (full, F32),
                (full, F32),
                (inner, BF),
                ((1, model), F32),
                (wo.shape, BF),
                (wi.shape, BF),
                (wb.shape, BF),
            ],
            ffn_work + [pltpu.VMEM(full, BF)] + rest,
            (xs, ctx, exchanged(cotangent), gain_ffn, wo, wi, wb),
            "feed_forward",
        )
        output = returned(out_seq)
        gwo, gwi, gwb = scattered(gwo), scattered(gwi), scattered(gwb)
        dq, dk, dv, table_grad = call(
            bwd_kernel,
            [(inner, BF), (inner, BF), (inner, BF), ((16, LANES), F32)],
            bwd_work,
            (queries, keys, values, grad_context, ctx, feats, segment, tabs),
            "attention_backward",
        )
        ig_seq, gwq, gwk, gwv, again = call(
            k5_plain,
            [(full, F32), (wq.shape, BF), (wk.shape, BF), (wv.shape, BF), ((1, model), F32)],
            [pltpu.VMEM((model, length), BF)],
            (xs, grad_middle, dq, dk, dv, wq, wk, wv, gain_attn),
            "projection_gradients",
        )
        input_grad = returned(ig_seq)
        gwq, gwk, gwv = scattered(gwq), scattered(gwk), scattered(gwv)
        again, ggain, tables = lax.psum((again, ggain, table_grad), ("dp", "tensor"))
        gain_attn_grad, gain_ffn_grad = again[0], ggain[0]
        tables = tables.reshape(2, 8, LANES)
    table_out = lax.dynamic_index_in_dim(tables, t, 0, False)[:heads, :buckets].T
    return (
        output,
        input_grad,
        gain_attn_grad,
        gain_ffn_grad,
        gwq,
        gwk,
        gwv,
        gwo,
        gwi,
        gwb,
        table_out,
    )


def solution(mesh):
    weight = P("dp", "tensor")
    tokens = P(None, ("dp", "tensor"), None)
    return jax.shard_map(
        shards,
        mesh=mesh,
        in_specs=(
            tokens,
            P(None, "dp", None),
            P(),
            P(),
            weight,
            weight,
            weight,
            weight,
            weight,
            weight,
            P(None, "tensor"),
            tokens,
        ),
        out_specs=(
            tokens,
            tokens,
            P(),
            P(),
            weight,
            weight,
            weight,
            weight,
            weight,
            weight,
            P(None, "tensor"),
        ),
        check_vma=False,
    )
```

```python
import functools

import jax
import jax.numpy as jnp
from jax import lax
from jax.experimental import pallas as pl
from jax.experimental.pallas import tpu as pltpu
from jax.sharding import PartitionSpec as P

MESH = pl.DeviceIdType.MESH
BF = jnp.bfloat16
F32 = jnp.float32
HIGHEST = lax.Precision.HIGHEST
EPSILON = 1e-06
THRESHOLDS = (12, 16, 23, 32, 46, 64, 91)
MASK_OUT = -float(2**30)
DH = 64
SPAN = 512
LANES = 128
VMEM_BYTES = 62 * 2**20


def nn(left, right):
    return lax.dot_general(left, right, (((1,), (0,)), ((), ())), preferred_element_type=F32)


def nt(left, right):
    return lax.dot_general(left, right, (((1,), (1,)), ((), ())), preferred_element_type=F32)


def tn(left, right):
    return lax.dot_general(left, right, (((0,), (0,)), ((), ())), preferred_element_type=F32)


def iota(shape, dim):
    return lax.broadcasted_iota(jnp.int32, shape, dim)


def bucket_ids(offsets):
    distance = jnp.abs(offsets)
    far_ids = 8 + sum((distance >= threshold).astype(jnp.int32) for threshold in THRESHOLDS)
    return jnp.where(offsets > 0, 16, 0) + jnp.where(distance < 8, distance, far_ids)


def rms_scale(values):
    return lax.rsqrt(jnp.mean(values * values, -1, keepdims=True) + EPSILON)


def rms_back(grad_normed, normed, scale, gain):
    scaled = grad_normed * gain
    return scale * (scaled - normed * jnp.mean(scaled * normed, -1, keepdims=True))


def gelu_pair(v):
    square = v * v
    half = 0.5 + 0.5 * jnp.tanh(v * (0.7978845608028654 + 0.035677408136300125 * square))
    slope = half + v * half * (1.0 - half) * (1.5957691216057308 + 0.2140644488178007 * square)
    return v * half, slope


class Place:
    def __init__(self, depth):
        d, t = lax.axis_index("dp"), lax.axis_index("tensor")
        self.t = t
        self.z, self.y, self.c = lax.div(d, 4), lax.rem(lax.div(d, 2), 2), lax.rem(d, 2)
        self.depth = depth
        self.sib = (d + 1 - 2 * self.c, t)
        self.ypeer = (d + 2 - 4 * self.y, t)
        self.xpeer = (d, 1 - t)
        rest = self.rest = lax.rem(d, 4)
        self.zs = [lax.rem(self.z + step, depth) for step in range(1, depth)]
        self.zpeers = [(z * 4 + rest, t) for z in self.zs]

    def barrier(self):
        semaphore = pltpu.get_barrier_semaphore()
        peers = [self.sib, self.ypeer, self.xpeer] + self.zpeers
        for peer in peers:
            pl.semaphore_signal(semaphore, inc=1, device_id=peer, device_id_type=MESH)
        pl.semaphore_wait(semaphore, len(peers))


class Copy:
    def __init__(self, **parts):
        self.parts = parts

    def made(self):
        return pltpu.make_async_remote_copy(device_id_type=MESH, **self.parts)

    def start(self):
        self.made().start()

    def wait_recv(self):
        self.made().wait_recv()

    def wait_send(self):
        self.made().wait_send()


def local(src, dst, sem):
    return pltpu.make_async_copy(src, dst, sem)


def remote(src, dst, sems, index, peer):
    send, recv = sems
    return Copy(
        src_ref=src, dst_ref=dst, send_sem=send.at[index], recv_sem=recv.at[index], device_id=peer
    )


class Gather:
    def __init__(self, place, ref, width, sems, item, x_first):
        self.p, self.ref, self.width, self.sems, self.item = place, ref, width, sems, item
        p = place
        self.relays = p.depth == 4
        if x_first:
            self.peers, order = (p.xpeer, p.ypeer), ((0, 0), (0, 1), (1, 0), (1, 1))
        else:
            self.peers, order = (p.ypeer, p.xpeer), ((0, 0), (1, 0), (0, 1), (1, 1))
        self.sides = [(p.y + (1 - 2 * p.y) * i, p.t + (1 - 2 * p.t) * j) for i, j in order]

    def cols(self, x):
        return pl.ds(pl.multiple_of(x * self.width, LANES), self.width)

    def block(self, z, side):
        y, x = self.sides[side]
        return self.ref.at[z, y, self.p.c, :, self.cols(x)]

    def region(self, side):
        y, x = self.sides[side]
        return self.ref.at[:, y, self.p.c, :, self.cols(x)]

    def send(self, index, src, peer):
        return remote(src, src, self.sems, (self.item, index), peer)

    def first(self):
        return self.send(0, self.block(self.p.z, 0), self.peers[0])

    def along(self, side):
        p = self.p
        base = 1 + side * len(p.zpeers)
        return [self.send(base + i, self.block(p.z, side), peer) for i, peer in enumerate(p.zpeers)]

    def last(self, side):
        return self.send(1 + 2 * len(self.p.zpeers) + side, self.region(side), self.peers[1])

    def sib(self, side):
        return self.send(3 + 2 * len(self.p.zpeers) + side, self.region(side), self.p.sib)

    def relay(self, side):
        p = self.p
        send, recv = self.sems
        src = self.block(lax.rem(p.z + 2, 4), side)
        low = p.z == 1
        target = jnp.where(low, 0, 3)
        return Copy(
            src_ref=src,
            dst_ref=src,
            send_sem=send.at[self.item, 7 + 2 * len(p.zpeers) + side],
            recv_sem=recv.at[self.item, 1 + side * len(p.zpeers) + jnp.where(low, 0, 2)],
            device_id=(target * 4 + p.rest, p.t),
        )

    def each_along(self, side, method):
        p = self.p
        for i, copy in enumerate(self.along(side)):
            if self.relays and i != 1:
                pl.when(p.z != (3 if i == 0 else 0))(getattr(copy, method))
            else:
                getattr(copy, method)()

    def inside(self, action):
        pl.when((self.p.z == 1) | (self.p.z == 2))(action)

    def start(self):
        self.first().start()

    def start_z(self):
        self.each_along(0, "start")

    def step1(self):
        self.first().wait_recv()
        self.each_along(1, "start")

    def step2(self, side):
        zs = self.along(side)
        if self.relays:
            zs[1].wait_recv()
            self.inside(self.relay(side).start)
            zs = [zs[0], zs[2]]
        for copy in zs:
            copy.wait_recv()
        self.last(side).start()
        self.sib(side).start()

    def step3(self):
        for side in range(2):
            self.last(side).wait_recv()
            self.sib(2 + side).start()

    def finish(self):
        for side in range(4):
            self.sib(side).wait_recv()
        self.first().wait_send()
        for side in range(2):
            self.each_along(side, "wait_send")
            if self.relays:
                self.inside(self.relay(side).wait_send)
            self.last(side).wait_send()
        for side in range(4):
            self.sib(side).wait_send()


def gather_sems(items, depth):
    return [pltpu.SemaphoreType.DMA((items, 2 * depth + 7))] * 2


class Scatter:
    def __init__(self, place, ref, width, bufs, sems, item, y_first):
        self.p, self.ref, self.width, self.sems, self.item = place, ref, width, sems, item
        self.r0, self.r1, self.r2, self.r3 = bufs
        self.y_first = y_first

    def cols(self, x):
        return pl.ds(pl.multiple_of(x * self.width, LANES), self.width)

    def copies(self):
        p, ref = self.p, self.ref
        sib = remote(ref.at[:, :, 1 - p.c], self.r0, self.sems, (self.item, 0), p.sib)
        if self.y_first:
            half = remote(ref.at[:, 1 - p.y, p.c], self.r1, self.sems, (self.item, 1), p.ypeer)
            quarter = remote(
                ref.at[:, p.y, p.c, :, self.cols(1 - p.t)],
                self.r2,
                self.sems,
                (self.item, 2),
                p.xpeer,
            )
        else:
            half = remote(
                ref.at[:, :, p.c, :, self.cols(1 - p.t)],
                self.r1,
                self.sems,
                (self.item, 1),
                p.xpeer,
            )
            quarter = remote(
                ref.at[:, 1 - p.y, p.c, :, self.cols(p.t)],
                self.r2,
                self.sems,
                (self.item, 2),
                p.ypeer,
            )
        zs = [
            remote(
                ref.at[z, p.y, p.c, :, self.cols(p.t)],
                self.r3.at[i],
                self.sems,
                (self.item, 3 + i),
                peer,
            )
            for i, (z, peer) in enumerate(zip(p.zs, p.zpeers))
        ]
        return sib, half, quarter, zs

    def step0(self):
        self.copies()[0].start()

    def step1(self):
        p = self.p
        sib, half, _, _ = self.copies()
        sib.wait_recv()
        kept = self.ref.at[:, :, p.c]
        kept[...] = (kept[...].astype(F32) + self.r0[...].astype(F32)).astype(BF)
        half.start()

    def step2(self):
        p = self.p
        _, half, quarter, _ = self.copies()
        half.wait_recv()
        if self.y_first:
            kept = self.ref.at[:, p.y, p.c]
        else:
            kept = self.ref.at[:, :, p.c, :, self.cols(p.t)]
        kept[...] = (kept[...].astype(F32) + self.r1[...].astype(F32)).astype(BF)
        quarter.start()

    def step3(self):
        p = self.p
        _, _, quarter, zs = self.copies()
        quarter.wait_recv()
        kept = self.ref.at[:, p.y, p.c, :, self.cols(p.t)]
        kept[...] = (kept[...].astype(F32) + self.r2[...].astype(F32)).astype(BF)
        for copy in zs:
            copy.start()

    def finish(self, out, offset):
        p = self.p
        sib, half, quarter, zs = self.copies()
        for copy in zs:
            copy.wait_recv()
        total = self.ref[p.z, p.y, p.c, :, self.cols(p.t)].astype(F32)
        for i in range(len(zs)):
            total = total + self.r3[i].astype(F32)
        out[:, pl.ds(pl.multiple_of(offset, LANES), self.width)] = total
        for copy in [sib, half, quarter] + zs:
            copy.wait_send()


def scatter_bufs(items, depth, rows, width, y_first):
    lead = () if items is None else (items,)
    return [
        pltpu.VMEM(lead + (depth, 2, rows, 2 * width), BF),
        pltpu.VMEM(lead + ((depth, rows, 2 * width) if y_first else (depth, 2, rows, width)), BF),
        pltpu.VMEM(lead + (depth, rows, width), BF),
        pltpu.VMEM(lead + (depth - 1, rows, width), BF),
    ]


def scatter_sems(items, depth):
    return [pltpu.SemaphoreType.DMA((items, depth + 2))] * 2


def flat(values):
    if len(values.shape) == 2:
        return values
    return values.reshape(-1, values.shape[-1])


def project_rows(x_rows, gain):
    rows = x_rows.astype(F32)
    return (rows * rms_scale(rows) * gain).astype(BF)


def project(low_ref, w_ref, out_ref):
    weight = flat(w_ref[...])
    half = low_ref.shape[0] // 2

    def one(i, carry):
        rows = pl.ds(pl.multiple_of(i * half, half), half)
        out_ref[rows, :] = nn(low_ref[rows, :], weight).astype(BF)
        return carry

    lax.fori_loop(0, 2, one, 0)


def k1_plain(x_ref, gain_ref, wq_ref, wk_ref, wv_ref, q_ref, k_ref, v_ref, low_ref):
    low_ref[...] = project_rows(x_ref[...], gain_ref[...])
    for weight, out in ((wq_ref, q_ref), (wk_ref, k_ref), (wv_ref, v_ref)):
        project(low_ref, weight, out)


def bias_rows(tabs_ref, out_ref, flipped):
    offsets = iota((LANES, 4 * LANES), 1) - 2 * LANES
    onehot = (bucket_ids(-offsets if flipped else offsets) == iota((LANES, 4 * LANES), 0)).astype(F32)
    for half in range(2):
        out_ref[half * 8 : half * 8 + 8, :] = jnp.dot(
            tabs_ref[half], onehot, precision=HIGHEST, preferred_element_type=F32
        )


def head_row(pair, per_half):
    return 8 * lax.div(pair, per_half) + 2 * lax.rem(pair, per_half)


def bias_strip(row):
    spread = jnp.broadcast_to(row, (LANES, 4 * LANES))
    return pltpu.roll(spread, 3 * LANES, 1, stride=1, stride_axis=0)


def window(tile, rows, length):
    reach = -(-SPAN // rows)
    return max(0, (tile - reach) * rows), min(length, (tile + reach + 1) * rows)


def segment_lanes(seg):
    length = seg.shape[1]
    onehot = (seg == iota((LANES, length), 0)).astype(F32).T > 0.5
    inside = iota((length, LANES), 1) < 16
    return onehot, inside


def pair_cols(pair):
    return pl.ds(pl.multiple_of(pair * LANES, LANES), LANES)


def spread3(value):
    top = value.astype(BF).astype(F32)
    mid = (value - top).astype(BF).astype(F32)
    return top, mid, value - top - mid


TILE = 256
NEAR = SPAN // LANES


def key_lanes(seg):
    onehot, inside = segment_lanes(seg)
    return jnp.where(onehot, 0.0, jnp.where(inside, 1.0, 0.0)).astype(BF)


def fwd_setup(seg, tabs_ref, bias_ref, segq_ref, segk_ref):
    bias_rows(tabs_ref, bias_ref, False)
    onehot, _ = segment_lanes(seg)
    segq_ref[...] = jnp.where(onehot, MASK_OUT, 0.0).astype(BF)
    segk_ref[...] = key_lanes(seg)


def fwd_pair(pair, q_ref, k_ref, v_ref, ctx_ref, feat_ref, bias_ref, segq_ref, segk_ref):
    length, width = q_ref.shape
    per_half = width // LANES // 2
    tile, near = TILE, NEAR
    cols = pair_cols(pair)
    row = head_row(pair, per_half)
    lane = iota((tile, LANES), 1)
    low_half = lane < DH
    strips, fars = [], []
    for hh in range(2):
        line = bias_ref[pl.ds(row + hh, 1), :]
        strips.append(bias_strip(line))
        fars.append((line[:, 0:1], line[:, 4 * LANES - 1 : 4 * LANES]))
    for index in range(length // tile):
        rows = slice(index * tile, (index + 1) * tile)
        start, stop = window(index, tile, length)
        queries = q_ref[rows, cols]
        zero = jnp.zeros_like(queries)
        q_feat = segq_ref[rows, :]
        left = jnp.concatenate(
            [
                jnp.concatenate([jnp.where(low_half, queries, zero), q_feat], 1),
                jnp.concatenate([jnp.where(low_half, zero, queries), q_feat], 1),
            ],
            0,
        )
        right = jnp.concatenate([k_ref[start:stop, cols], segk_ref[start:stop, :]], 1)
        scores = nt(left, right)
        weights, peaks = [], []
        for hh in range(2):
            for part in range(tile // LANES):
                at = hh * tile + part * LANES
                q_block = index * (tile // LANES) + part
                blocks = []
                for k_block in range(start // LANES, stop // LANES):
                    delta = k_block - q_block
                    if abs(delta) > near:
                        blocks.append(None)
                        continue
                    col = k_block * LANES - start
                    block = scores[at : at + LANES, col : col + LANES]
                    if abs(delta) <= 1:
                        block = block + strips[hh][:, (delta + 1) * LANES : (delta + 2) * LANES]
                    else:
                        block = block + fars[hh][0 if delta < 0 else 1]
                    blocks.append(block)
                real = [block for block in blocks if block is not None]
                peak = functools.reduce(jnp.maximum, real)
                peak = jnp.max(peak, -1, keepdims=True)
                peaks.append(peak)
                weights.append(
                    jnp.concatenate(
                        [
                            jnp.zeros((LANES, LANES), BF)
                            if block is None
                            else jnp.exp(block - peak).astype(BF)
                            for block in blocks
                        ],
                        1,
                    )
                )
        values = v_ref[start:stop, cols]
        gathered = nn(
            jnp.concatenate(weights, 0), jnp.concatenate([values, jnp.ones_like(values)], 1)
        )
        normal = gathered[:, :LANES] / gathered[:, LANES:]
        context = jnp.where(low_half, normal[:tile], normal[tile:])
        ctx_ref[rows, cols] = context.astype(BF)
        logs = jnp.concatenate(peaks, 0) + jnp.log(gathered[:, LANES:])
        feature = q_feat.astype(F32)
        for hh in range(2):
            for i, piece in enumerate(spread3(logs[hh * tile : (hh + 1) * tile])):
                feature = jnp.where(lane == 16 + 3 * hh + i, -piece, feature)
        feat_ref[pair, rows, :] = feature.astype(BF)


def fwd_kernel(
    q_ref, k_ref, v_ref, seg_ref, tabs_ref, ctx_ref, feat_ref, bias_ref, segq_ref, segk_ref
):
    fwd_setup(seg_ref[...], tabs_ref, bias_ref, segq_ref, segk_ref)

    def one_pair(pair, carry):
        fwd_pair(pair, q_ref, k_ref, v_ref, ctx_ref, feat_ref, bias_ref, segq_ref, segk_ref)
        return carry

    lax.fori_loop(0, q_ref.shape[1] // LANES, one_pair, 0)


def bwd_setup(seg, tabs_ref, bias_ref, sums_ref, far_ref, segk_ref, blockof_ref):
    length = seg.shape[1]
    bias_rows(tabs_ref, bias_ref, True)
    sums_ref[...] = jnp.zeros_like(sums_ref)
    far_ref[...] = jnp.zeros_like(far_ref)
    segk_ref[...] = key_lanes(seg)
    blockof_ref[...] = (
        lax.div(iota((length, LANES), 0), LANES) == iota((length, LANES), 1)
    ).astype(BF)


def bwd_pair(
    pair,
    q_ref,
    k_ref,
    v_ref,
    go_ref,
    ctx_ref,
    feat_ref,
    dq_ref,
    dk_ref,
    dv_ref,
    bias_ref,
    sums_ref,
    far_ref,
    segk_ref,
    blockof_ref,
    gofeat_ref,
    near_ref,
    acc_ref,
):
    length, width = q_ref.shape
    per_half = width // LANES // 2
    tile, near = TILE, NEAR
    flip = (iota((LANES, LANES), 0) + iota((LANES, LANES), 1) == LANES - 1).astype(F32)
    cols = pair_cols(pair)
    row = head_row(pair, per_half)
    lane = iota((tile, LANES), 1)
    low_half = lane < DH
    strips, fars = [], []
    for hh in range(2):
        line = bias_ref[pl.ds(row + hh, 1), :]
        strips.append(bias_strip(line))
        fars.append((line[:, 0:1], line[:, 4 * LANES - 1 : 4 * LANES]))
    grads_all = go_ref[:, cols]
    product = grads_all.astype(F32) * ctx_ref[:, cols].astype(F32)
    lane_all = iota((length, LANES), 1)
    feature = jnp.zeros((length, LANES), F32)
    for hh in range(2):
        keep = (lane_all < DH) if hh == 0 else (lane_all >= DH)
        total = jnp.sum(jnp.where(keep, product, 0.0), -1, keepdims=True)
        for i, piece in enumerate(spread3(total)):
            feature = jnp.where(lane_all == 3 * hh + i, -piece, feature)
    gofeat_ref[...] = feature.astype(BF)
    near_ref[...] = jnp.zeros_like(near_ref)
    acc_ref[...] = jnp.zeros_like(acc_ref)
    far_sums = [[jnp.zeros((1, LANES), F32) for _ in range(2)] for _ in range(2)]
    lane_row = iota((1, LANES), 1)
    for index in range(length // tile):
        rows = slice(index * tile, (index + 1) * tile)
        start, stop = window(index, tile, length)
        keys, values = k_ref[rows, cols], v_ref[rows, cols]
        zero = jnp.zeros_like(keys)
        seg_feat = segk_ref[rows, :].astype(F32)

        def ones_at(base, first):
            return jnp.where((lane >= first) & (lane < first + 3), 1.0, base).astype(BF)

        masked_keys = jnp.concatenate(
            [jnp.where(low_half, keys, zero), jnp.where(low_half, zero, keys)], 0
        )
        masked_values = jnp.concatenate(
            [jnp.where(low_half, values, zero), jnp.where(low_half, zero, values)], 0
        )
        key_feats = jnp.concatenate([ones_at(seg_feat, 16), ones_at(seg_feat, 19)], 0)
        value_feats = jnp.concatenate([ones_at(0.0, 0), ones_at(0.0, 3)], 0)
        queries = q_ref[start:stop, cols]
        grads = go_ref[start:stop, cols]
        logits = nt(
            jnp.concatenate([masked_keys, key_feats], 1),
            jnp.concatenate([queries, feat_ref[pair, start:stop, :]], 1),
        )
        shifted = nt(
            jnp.concatenate([masked_values, value_feats], 1),
            jnp.concatenate([grads, gofeat_ref[start:stop, :]], 1),
        )
        probs_rows, score_rows = [], []
        for hh in range(2):
            for part in range(tile // LANES):
                at = hh * tile + part * LANES
                k_block = index * (tile // LANES) + part
                probs, score_grads = [], []
                for q_block in range(start // LANES, stop // LANES):
                    delta = k_block - q_block
                    if abs(delta) > near:
                        probs.append(jnp.zeros((LANES, LANES), BF))
                        score_grads.append(jnp.zeros((LANES, LANES), BF))
                        continue
                    col = q_block * LANES - start
                    block = logits[at : at + LANES, col : col + LANES]
                    place = (1 - delta) * LANES
                    if abs(delta) <= 1:
                        block = block + strips[hh][:, place : place + LANES]
                    else:
                        block = block + fars[hh][0 if delta > 0 else 1]
                    prob = jnp.exp(block)
                    grad = prob * shifted[at : at + LANES, col : col + LANES]
                    if abs(delta) <= 1:
                        near_ref[hh, :, place : place + LANES] += grad
                    probs.append(prob.astype(BF))
                    score_grads.append(grad.astype(BF))
                probs_rows.append(jnp.concatenate(probs, 1))
                score_rows.append(jnp.concatenate(score_grads, 1))
        probs_all = jnp.concatenate(probs_rows, 0)
        scores_all = jnp.concatenate(score_rows, 0)
        value_grad = nn(probs_all, grads)
        dv_ref[rows, cols] = jnp.where(low_half, value_grad[:tile], value_grad[tile:]).astype(BF)
        key_grad = nn(scores_all, jnp.concatenate([queries, blockof_ref[start:stop, :]], 1))
        dk_ref[rows, cols] = jnp.where(
            low_half, key_grad[:tile, :LANES], key_grad[tile:, :LANES]
        ).astype(BF)
        acc_ref[start:stop, :] += tn(scores_all, masked_keys)
        for hh in range(2):
            for part in range(tile // LANES):
                at = hh * tile + part * LANES
                k_block = index * (tile // LANES) + part
                line = jnp.sum(key_grad[at : at + LANES, LANES:], 0, keepdims=True)
                far_sums[hh][0] += jnp.where(lane_row <= k_block - 2, line, 0.0)
                far_sums[hh][1] += jnp.where(lane_row >= k_block + 2, line, 0.0)
    dq_ref[:, cols] = acc_ref[...].astype(BF)
    for hh in range(2):
        turned = jnp.dot(flip, near_ref[hh], precision=HIGHEST, preferred_element_type=F32)
        turned = jnp.concatenate([turned, jnp.zeros((LANES, LANES), F32)], 1)
        turned = pltpu.roll(turned, 1, 1, stride=1, stride_axis=0)
        sums_ref[pl.ds(row + hh, 1), :] = jnp.sum(turned, 0, keepdims=True)
        last = lane_row == 0
        positive = jnp.sum(far_sums[hh][0], -1, keepdims=True)
        negative = jnp.sum(far_sums[hh][1], -1, keepdims=True)
        far_ref[pl.ds(row + hh, 1), :] = jnp.where(last, positive, jnp.where(lane_row == 1, negative, 0.0))


def bwd_table(tabg_ref, sums_ref, far_ref):
    offsets = 2 * LANES - iota((LANES, 4 * LANES), 1)
    onehot_buckets = (bucket_ids(offsets) == iota((LANES, 4 * LANES), 0)).astype(F32)
    table = lax.dot_general(
        sums_ref[...],
        onehot_buckets,
        (((1,), (1,)), ((), ())),
        precision=HIGHEST,
        preferred_element_type=F32,
    )
    lane = iota(tabg_ref.shape, 1)
    far = far_ref[...]
    table = table + jnp.where(lane == 31, far[:, 0:1], 0.0) + jnp.where(lane == 15, far[:, 1:2], 0.0)
    tabg_ref[...] = table


def bwd_kernel(
    q_ref,
    k_ref,
    v_ref,
    go_ref,
    ctx_ref,
    feat_ref,
    seg_ref,
    tabs_ref,
    dq_ref,
    dk_ref,
    dv_ref,
    tabg_ref,
    bias_ref,
    sums_ref,
    far_ref,
    segk_ref,
    blockof_ref,
    gofeat_ref,
    near_ref,
    acc_ref,
):
    bwd_setup(seg_ref[...], tabs_ref, bias_ref, sums_ref, far_ref, segk_ref, blockof_ref)

    def one_pair(pair, carry):
        bwd_pair(
            pair,
            q_ref,
            k_ref,
            v_ref,
            go_ref,
            ctx_ref,
            feat_ref,
            dq_ref,
            dk_ref,
            dv_ref,
            bias_ref,
            sums_ref,
            far_ref,
            segk_ref,
            blockof_ref,
            gofeat_ref,
            near_ref,
            acc_ref,
        )
        return carry

    lax.fori_loop(0, q_ref.shape[1] // LANES, one_pair, 0)
    bwd_table(tabg_ref, sums_ref, far_ref)


def k3_before(xs_ref, ctx_ref, wo, gain, middle_ref, ffn_ref, ffnt_ref):
    step = 256

    def one(i, carry):
        rows = pl.ds(pl.multiple_of(i * step, step), step)
        middle = xs_ref[rows, :].astype(F32) + nt(ctx_ref[rows, :], wo)
        middle_ref[rows, :] = middle
        low = (middle * rms_scale(middle) * gain).astype(BF)
        ffn_ref[rows, :] = low
        ffnt_ref[:, rows] = low.T
        return carry

    lax.fori_loop(0, middle_ref.shape[0] // step, one, 0)


def transpose_rows(src_ref, dst_ref):
    step = 256

    def one(i, carry):
        rows = pl.ds(pl.multiple_of(i * step, step), step)
        dst_ref[:, rows] = src_ref[rows, :].T
        return carry

    lax.fori_loop(0, src_ref.shape[0] // step, one, 0)


def ffn_rows(i, half, w_in, w_back, first, ffn_ref, cot_ref, hid_ref, gp_ref, up_ref, down_ref):
    rows = pl.ds(pl.multiple_of(i * half, half), half)
    hidden, slope = gelu_pair(nn(ffn_ref[rows, :], w_in))
    hidden = hidden.astype(BF)
    hid_ref[rows, :] = hidden
    grad_pre = (nn(cot_ref[rows, :], w_back) * slope).astype(BF)
    gp_ref[rows, :] = grad_pre
    up = nt(hidden, w_back)
    down = nt(grad_pre, w_in)

    @pl.when(first)
    def _():
        up_ref[rows, :] = up
        down_ref[rows, :] = down

    @pl.when(jnp.logical_not(first))
    def _():
        up_ref[rows, :] += up
        down_ref[rows, :] += down


def after_rows(rows, cot, up_ref, down_ref, gain, gain_ref, gm_ref, ca_ref, cat_ref):
    middle = gm_ref[rows, :]
    scale = rms_scale(middle)
    normed = middle * scale
    down = down_ref[rows, :]
    gain_ref[...] += jnp.sum(down * normed, 0, keepdims=True)
    grad = cot + rms_back(down, normed, scale, gain)
    gm_ref[rows, :] = grad
    low = grad.astype(BF)
    ca_ref[rows, :] = low
    cat_ref[:, rows] = low.T
    return middle + up_ref[rows, :]


def context_grad(ca_ref, wo, go_ref):
    step = 256

    def one(i, carry):
        rows = pl.ds(pl.multiple_of(i * step, step), step)
        go_ref[rows, :] = nn(ca_ref[rows, :], wo).astype(BF)
        return carry

    lax.fori_loop(0, ca_ref.shape[0] // step, one, 0)


def k3_plain(
    xs_ref,
    ctx_ref,
    cot_ref,
    gain_ref,
    wo_ref,
    wi_ref,
    wb_ref,
    out_ref,
    gm_ref,
    go_ref,
    ggain_ref,
    gwo_ref,
    gwi_ref,
    gwb_ref,
    ffn_ref,
    ffnt_ref,
    cott_ref,
    cotb_ref,
    hid_ref,
    gp_ref,
    up_ref,
    down_ref,
):
    length = ctx_ref.shape[0]
    half_rows = length // 2
    chunk = hid_ref.shape[1]
    gain = gain_ref[...]
    cotb_ref[...] = cot_ref[...].astype(BF)
    k3_before(xs_ref, ctx_ref, wo_ref[...], gain, gm_ref, ffn_ref, ffnt_ref)
    transpose_rows(cotb_ref, cott_ref)

    def one_chunk(k, carry):
        cols = pl.ds(pl.multiple_of(k * chunk, LANES), chunk)
        w_in, w_back = wi_ref[:, cols], wb_ref[:, cols]
        for i in range(2):
            ffn_rows(
                i, half_rows, w_in, w_back, k == 0, ffn_ref, cotb_ref, hid_ref, gp_ref, up_ref, down_ref
            )
        gwb_ref[:, cols] = nn(cott_ref[...], hid_ref[...]).astype(BF)
        gwi_ref[:, cols] = nn(ffnt_ref[...], gp_ref[...]).astype(BF)
        return carry

    lax.fori_loop(0, wi_ref.shape[1] // chunk, one_chunk, 0)
    ggain_ref[...] = jnp.zeros_like(ggain_ref)
    step = 256

    def finish_rows(i, carry):
        rows = pl.ds(pl.multiple_of(i * step, step), step)
        out_ref[rows, :] = after_rows(
            rows,
            cot_ref[rows, :],
            up_ref,
            down_ref,
            gain,
            ggain_ref,
            gm_ref,
            ffn_ref,
            cott_ref,
        )
        return carry

    lax.fori_loop(0, length // step, finish_rows, 0)
    context_grad(ffn_ref, wo_ref[...], go_ref)
    gwo_ref[...] = nn(cott_ref[...], ctx_ref[...]).astype(BF)


def low_transposed(xs_ref, gain, lowt_ref):
    step = 256

    def one(i, carry):
        rows = pl.ds(pl.multiple_of(i * step, step), step)
        lowt_ref[:, rows] = project_rows(xs_ref[rows, :], gain).T
        return carry

    lax.fori_loop(0, xs_ref.shape[0] // step, one, 0)


def input_rows(rows, xs_ref, gm_ref, grads, weights, gain, gain_out):
    down = sum(nt(grad[rows, :], flat(weight[...])) for grad, weight in zip(grads, weights))
    inputs = xs_ref[rows, :].astype(F32)
    scale = rms_scale(inputs)
    normed = inputs * scale
    gain_out[...] += jnp.sum(down * normed, 0, keepdims=True)
    return gm_ref[rows, :] + rms_back(down, normed, scale, gain)


def k5_plain(
    xs_ref,
    gm_ref,
    dq_ref,
    dk_ref,
    dv_ref,
    wq_ref,
    wk_ref,
    wv_ref,
    gain_ref,
    ig_ref,
    gwq_ref,
    gwk_ref,
    gwv_ref,
    again_ref,
    lowt_ref,
):
    gain = gain_ref[...]
    low_transposed(xs_ref, gain, lowt_ref)
    grads, weights = (dq_ref, dk_ref, dv_ref), (wq_ref, wk_ref, wv_ref)
    for grad, out in zip(grads, (gwq_ref, gwk_ref, gwv_ref)):
        out[...] = nn(lowt_ref[...], grad[...]).astype(BF)
    again_ref[...] = jnp.zeros_like(again_ref)
    step = 256

    def one(i, carry):
        rows = pl.ds(pl.multiple_of(i * step, step), step)
        ig_ref[rows, :] = input_rows(rows, xs_ref, gm_ref, grads, weights, gain, again_ref)
        return carry

    lax.fori_loop(0, xs_ref.shape[0] // step, one, 0)


def as_row(vector):
    return vector.reshape(1, vector.shape[-1])


def turned_table(tab_ref, turn_ref):
    turn_ref[...] = jnp.zeros_like(turn_ref)
    turn_ref[: tab_ref.shape[0], : tab_ref.shape[1]] = tab_ref[...]
    return turn_ref[0:8, :]


def run_all(steps):
    for step in steps:
        step()


def at_step(index, plan):
    for number, steps in enumerate(plan):
        if steps:

            @pl.when(index == number)
            def _(steps=steps):
                run_all(steps)


def forward_fused(
    depth,
    here,
    x_in,
    cot_in,
    gain_in,
    ffn_gain_in,
    tab_ref,
    seg_ref,
    wq_shard,
    wk_shard,
    wv_shard,
    wo_shard,
    wi_shard,
    wb_shard,
    xs_out,
    tabs_ref,
    q_out,
    k_out,
    v_out,
    ctx_out,
    feat_out,
    wq_out,
    wk_out,
    wv_out,
    own_out,
    oth_out,
    gm_out,
    go_out,
    ggain_ref,
    gout_out,
    gwi_ref,
    gwb_ref,
    gi_out,
    gb_out,
    xs_ref,
    cotf_ref,
    cotb_ref,
    obuf_ref,
    q_ref,
    k_ref,
    v_ref,
    ctx_ref,
    feat_ref,
    wq_ref,
    wk_ref,
    wv_ref,
    wo_ref,
    wi_ref,
    wb_ref,
    low_ref,
    turn_ref,
    bias_ref,
    segq_ref,
    segk_ref,
    gm_ref,
    ffnt_ref,
    cott_ref,
    up_ref,
    down_ref,
    i0,
    i1,
    i2,
    i3,
    b0,
    b1,
    b2,
    b3,
    r_send,
    r_recv,
    g_send,
    g_recv,
    s_send,
    s_recv,
    x_send,
    x_recv,
    l_sem,
    c_sem,
):
    p = Place(depth)
    length = q_ref.shape[0]
    half_rows = length // 2
    width = wo_shard.shape[1]
    groups = wq_ref.shape[0]
    chunks, part = wi_ref.shape[0], wi_ref.shape[-1] // 2
    x_sems, g_sems, r_sems, s_sems = (
        (x_send, x_recv),
        (g_send, g_recv),
        (r_send, r_recv),
        (s_send, s_recv),
    )
    gain, ffn_gain = as_row(gain_in[...]), as_row(ffn_gain_in[...])
    weights = (wq_ref, wk_ref, wv_ref)
    x_own = local(x_in.at[p.t], xs_ref.at[p.t], l_sem.at[0])
    x_own.start()
    cot_load = local(cot_in.at[1 - p.t], cotf_ref, l_sem.at[1])
    cot_load.start()
    heads = []
    for j in range(groups):
        trio = []
        for i, (ref, shard) in enumerate(zip(weights, (wq_shard, wk_shard, wv_shard))):
            item = Gather(p, ref.at[j], LANES, r_sems, 3 * j + i, True)
            item.block(p.z, 0)[...] = shard[:, j * LANES : (j + 1) * LANES]
            trio.append(item)
        heads.append(trio)
    out_item = Gather(p, wo_ref, width, g_sems, 0, True)
    out_item.block(p.z, 0)[...] = wo_shard[...]
    items = []
    for k in range(chunks):
        pair = []
        for side, (ref, shard) in enumerate(((wi_ref, wi_shard), (wb_ref, wb_shard))):
            item = Gather(p, ref.at[k], part, g_sems, 1 + 2 * k + side, side == 0 or k < 2)
            item.block(p.z, 0)[...] = shard[:, k * part : (k + 1) * part]
            pair.append(item)
        items.append(pair)

    tabs_ref[p.t] = turned_table(tab_ref, turn_ref)
    p.barrier()
    moves = [
        remote(x_in.at[1 - p.t], xs_ref.at[p.t], x_sems, 0, p.xpeer),
        remote(tabs_ref.at[p.t], tabs_ref.at[p.t], x_sems, 1, p.xpeer),
        remote(obuf_ref, cotb_ref.at[p.t], x_sems, 2, p.xpeer),
    ]

    def head(j, name):
        return [getattr(item, name) for item in heads[j]]

    def both(items):
        return [functools.partial(item.step2, side) for side in range(2) for item in items]

    run_all(head(0, "start") + head(1, "start") + head(2, "start"))
    run_all([out_item.start])
    for item in items[0]:
        item.start()
    moves[1].start()
    moves[0].start()
    run_all(head(0, "start_z") + head(1, "start_z"))
    def chunk(k, *names):
        steps = []
        for name in names if k < chunks else ():
            if name == "both":
                steps += both(items[k])
            else:
                steps += [getattr(item, name) for item in items[k]]
        return steps

    def rows_of(half):
        return pl.ds(pl.multiple_of(half * half_rows, half_rows), half_rows)

    def project_group(j, half):
        rows = rows_of(half)
        for weight, out in zip(weights, (q_ref, k_ref, v_ref)):
            result = nn(low_ref[rows, :], flat(weight[j])).astype(BF)
            out[rows, pair_cols(j)] = result[:, :LANES]
            out[rows, pair_cols(j + groups)] = result[:, LANES:]

    run_all(head(0, "step1") + head(1, "step1") + head(2, "start_z"))
    x_own.wait()
    low_ref[rows_of(p.t), :] = project_rows(xs_ref[p.t], gain)
    run_all(both(heads[0]) + head(2, "step1"))
    cot_load.wait()
    obuf_ref[...] = cotf_ref[...].astype(BF)
    own_load = local(cot_in.at[p.t], cotf_ref, l_sem.at[1])
    own_load.start()
    run_all(both(heads[1]))
    moves[1].wait_recv()
    fwd_setup(seg_ref[p.t], tabs_ref, bias_ref, segq_ref, segk_ref)
    run_all(head(0, "step3") + [out_item.start_z, out_item.step1])
    run_all(both(heads[2]) + head(0, "finish"))
    project_group(0, p.t)
    run_all(chunk(0, "start_z", "step1"))
    moves[0].wait_recv()
    for k in range(1, chunks):
        run_all(chunk(k, "start"))
    moves[2].start()
    low_ref[rows_of(1 - p.t), :] = project_rows(xs_ref[1 - p.t], gain)
    project_group(0, 1 - p.t)

    def save(index, src, dst):
        return local(src, dst, l_sem.at[index])

    saves = [
        save(2 + i, src, dst)
        for i, (src, dst) in enumerate(
            (
                (xs_ref, xs_out),
                (wq_ref, wq_out),
                (wk_ref, wk_out),
                (wv_ref, wv_out),
                (ctx_ref, ctx_out),
                (feat_ref, feat_out),
                (obuf_ref, oth_out),
                (cotf_ref, own_out),
                (gm_ref, gm_out),
                (v_ref, go_out),
                (wo_ref, gout_out),
            )
        )
    ]
    qkv_saves = [
        save(13 + i, src, dst)
        for i, (src, dst) in enumerate(((q_ref, q_out), (k_ref, k_out), (v_ref, v_out)))
    ]

    plan = [
        head(1, "step3") + both([out_item]) + chunk(1, "start_z", "step1"),
        head(2, "step3") + chunk(0, "both"),
        head(1, "finish") + chunk(2, "start_z", "step1"),
        [out_item.step3] + chunk(1, "both"),
        head(2, "finish") + chunk(0, "step3") + chunk(3, "start_z", "step1") + chunk(2, "both"),
        [out_item.finish] + [one.start for one in qkv_saves + saves[:4]],
    ]

    def one_pair(index, carry):
        j, side = lax.div(index, 2), lax.rem(index, 2)
        at_step(index, plan)

        @pl.when((side == 0) & (j > 0))
        def _():
            def one(half, carry):
                project_group(j, half)
                return carry

            lax.fori_loop(0, 2, one, 0)

        pair = j + groups * side
        fwd_pair(pair, q_ref, k_ref, v_ref, ctx_ref, feat_ref, bias_ref, segq_ref, segk_ref)
        return carry

    lax.fori_loop(0, 2 * groups, one_pair, 0)
    saves[4].start()
    saves[5].start()
    run_all(chunk(1, "step3") + chunk(3, "both") + chunk(4, "start_z", "step1"))
    xs = xs_ref.reshape(length, xs_ref.shape[2])
    k3_before(xs, ctx_ref, flat(wo_ref[...]), ffn_gain, gm_ref, low_ref, ffnt_ref)
    run_all(chunk(0, "finish") + chunk(2, "step3"))
    moves[2].wait_recv()
    moves[2].wait_send()
    own_load.wait()
    cotb_ref[p.t] = cotf_ref[...].astype(BF)
    cotb = cotb_ref.reshape(length, cotb_ref.shape[2])
    transpose_rows(cotb, cott_ref)
    for one in qkv_saves:
        one.wait()
    hid_ref, gp_ref = q_ref.at[:, : 2 * part], k_ref.at[:, : 2 * part]

    def s_chunk(k):
        return (
            Scatter(
                p, wi_ref.at[k], part, [r.at[k] for r in (i0, i1, i2, i3)], s_sems, 2 * k, True
            ),
            Scatter(
                p, wb_ref.at[k], part, [r.at[k] for r in (b0, b1, b2, b3)], s_sems, 1 + 2 * k, False
            ),
        )

    def save_chunk(k):
        return (
            local(wi_ref.at[k], gi_out.at[k - here], c_sem.at[2 * k]),
            local(wb_ref.at[k], gb_out.at[k - here], c_sem.at[1 + 2 * k]),
        )

    def when_scatter(k, name):
        @pl.when((k >= 0) & (k < here))
        def _():
            for item, out in zip(s_chunk(k), (gwi_ref, gwb_ref)):
                if name == "finish":
                    item.finish(out, k * part)
                else:
                    getattr(item, name)()

    begin = [
        chunk(4, "both") + chunk(5, "start_z", "step1"),
        chunk(1, "finish") + chunk(5, "both") + chunk(4, "step3"),
        chunk(2, "finish") + chunk(5, "step3"),
    ]
    begin += [chunk(k, "finish") for k in range(3, chunks)]
    middle = [chunk(3, "step3")]

    def one_chunk(k, carry):
        at_step(k, begin)
        w_in, w_back = flat(wi_ref[k]), flat(wb_ref[k])
        args = (w_in, w_back, k == 0, low_ref, cotb, hid_ref, gp_ref, up_ref, down_ref)
        ffn_rows(0, half_rows, *args)
        when_scatter(k - 3, "step3")
        when_scatter(k - 2, "step2")
        when_scatter(k - 1, "step1")
        at_step(k, middle)
        ffn_rows(1, half_rows, *args)
        wb_ref[k] = nn(cott_ref[...], hid_ref[...]).astype(BF).reshape(wb_ref.shape[1:])
        when_scatter(k - 4, "finish")
        wi_ref[k] = nn(ffnt_ref[...], gp_ref[...]).astype(BF).reshape(wi_ref.shape[1:])
        when_scatter(k, "step0")

        @pl.when(k >= here)
        def _():
            for one in save_chunk(k):
                one.start()

        return carry

    lax.fori_loop(0, chunks, one_chunk, 0)
    ggain_ref[...] = jnp.zeros_like(ggain_ref)
    step = 256

    def finish_rows(own, i):
        half = p.t if own else 1 - p.t
        at = pl.ds(pl.multiple_of(i * step, step), step)
        rows = pl.ds(pl.multiple_of(half * half_rows + i * step, step), step)
        cot = cotf_ref[at, :] if own else cotb_ref[1 - p.t, at, :].astype(F32)
        out = after_rows(
            rows, cot, up_ref, down_ref, ffn_gain, ggain_ref, gm_ref, low_ref, cott_ref
        )
        if own:
            cotf_ref[at, :] = out
        else:
            obuf_ref[at, :] = out.astype(BF)

    for i in range(half_rows // step):
        finish_rows(False, i)
    saves[6].start()
    for stage, name in ((1, "step1"), (2, "step2"), (3, "step3")):
        for k in range(max(0, chunks - stage), here):
            when_scatter(k, name)
    for i in range(half_rows // step):
        finish_rows(True, i)
    saves[7].start()
    saves[8].start()
    context_grad(low_ref, flat(wo_ref[...]), v_ref)
    saves[9].start()
    wo_ref[...] = nn(cott_ref[...], ctx_ref[...]).astype(BF).reshape(wo_ref.shape)
    saves[10].start()
    for k in range(max(0, chunks - 4), here):
        when_scatter(k, "finish")
    for move in moves[:2]:
        move.wait_send()
    for one in saves:
        one.wait()
    for k in range(here, chunks):
        for one in save_chunk(k):
            one.wait()


def back_fused(
    depth,
    q_in,
    k_in,
    v_in,
    go_ref,
    ctx_ref,
    feat_ref,
    seg_ref,
    tabs_ref,
    xs_in,
    gm_in,
    wq_in,
    wk_in,
    wv_in,
    gain_in,
    ggain_ref,
    gi_in,
    gb_in,
    gout_in,
    oth_in,
    oth_out,
    igown_ref,
    ibuf2_ref,
    gwo_ref,
    gwq_ref,
    gwk_ref,
    gwv_ref,
    gwi_ref,
    gwb_ref,
    small_ref,
    q_ref,
    k_ref,
    v_ref,
    xs_ref,
    gm_ref,
    wq_ref,
    wk_ref,
    wv_ref,
    gi_ref,
    gb_ref,
    gout_ref,
    lowt_ref,
    sum_ref,
    gq_ref,
    gk_ref,
    gv_ref,
    ibuf_ref,
    again_ref,
    tabg_ref,
    sm_ref,
    smr_ref,
    bias_ref,
    sums_ref,
    far_ref,
    segk_ref,
    blockof_ref,
    gofeat_ref,
    near_ref,
    acc_ref,
    o0,
    o1,
    o2,
    o3,
    i0,
    i1,
    i2,
    i3,
    b0,
    b1,
    b2,
    b3,
    a0,
    a1,
    a2,
    a3,
    c0,
    c1,
    c2,
    c3,
    d0,
    d1,
    d2,
    d3,
    s_send,
    s_recv,
    x_send,
    x_recv,
    l_sem,
):
    p = Place(depth)
    length = q_ref.shape[0]
    half_rows = length // 2
    groups = gq_ref.shape[0]
    rest, part = gi_ref.shape[0], gi_ref.shape[-1] // 2
    s_sems, x_sems = (s_send, s_recv), (x_send, x_recv)
    pairs = [(q_in, q_ref), (k_in, k_ref), (v_in, v_ref), (xs_in, xs_ref)]
    pairs += [(gi_in, gi_ref), (gb_in, gb_ref), (gout_in, gout_ref), (gm_in, gm_ref)]
    pairs += [(wq_in, wq_ref), (wk_in, wk_ref), (wv_in, wv_ref)]
    loads = [local(src, dst, l_sem.at[i]) for i, (src, dst) in enumerate(pairs)]
    for one in loads:
        one.start()
    bwd_setup(seg_ref[p.t], tabs_ref, bias_ref, sums_ref, far_ref, segk_ref, blockof_ref)
    p.barrier()
    quarter = half_rows // 4
    out_moves = [
        remote(
            oth_in.at[pl.ds(i * quarter, quarter)],
            oth_out.at[pl.ds(i * quarter, quarter)],
            x_sems,
            depth + 6 + i,
            p.xpeer,
        )
        for i in range(4)
    ]
    out_item = Scatter(
        p, gout_ref, gwo_ref.shape[1], (o0, o1, o2, o3), s_sems, 2 * rest + 3 * groups, True
    )
    rest_items = []
    for k in range(rest):
        rest_items.append(
            [
                Scatter(
                    p, gi_ref.at[k], part, [r.at[k] for r in (i0, i1, i2, i3)], s_sems, 2 * k, True
                ),
                Scatter(
                    p,
                    gb_ref.at[k],
                    part,
                    [r.at[k] for r in (b0, b1, b2, b3)],
                    s_sems,
                    2 * k + 1,
                    True,
                ),
            ]
        )
    group_items = []
    for j in range(groups):
        group_items.append(
            [
                Scatter(
                    p,
                    ref.at[j],
                    LANES,
                    [r.at[j] for r in bufs],
                    s_sems,
                    2 * rest + 3 * j + i,
                    True,
                )
                for i, (ref, bufs) in enumerate(
                    (
                        (gq_ref, (a0, a1, a2, a3)),
                        (gk_ref, (c0, c1, c2, c3)),
                        (gv_ref, (d0, d1, d2, d3)),
                    )
                )
            ]
        )

    def chunk(k, name):
        if k >= rest:
            return []
        if name == "finish":
            return [
                functools.partial(item.finish, out, k * part)
                for item, out in zip(rest_items[k], (gwi_ref, gwb_ref))
            ]
        return [getattr(item, name) for item in rest_items[k]]

    def group(j, name):
        if name == "finish":
            return [
                functools.partial(item.finish, out, j * LANES)
                for item, out in zip(group_items[j], (gwq_ref, gwk_ref, gwv_ref))
            ]
        return [getattr(item, name) for item in group_items[j]]

    for one in loads[:7]:
        one.wait()
    run_all(chunk(0, "step0"))
    xs = xs_ref.reshape(length, xs_ref.shape[2])
    gain = as_row(gain_in[...])
    low_transposed(xs, gain, lowt_ref)
    run_all(chunk(0, "step1") + chunk(1, "step0"))
    for one in loads[7:]:
        one.wait()

    def group_cols(ref, j):
        return [ref[:, pair_cols(j)], ref[:, pair_cols(j + groups)]]

    def weight_grads(j):
        for target, grad in zip((gq_ref, gk_ref, gv_ref), (q_ref, k_ref, v_ref)):
            both = jnp.concatenate(group_cols(grad, j), 1)
            target[j] = nn(lowt_ref[...], both).astype(BF).reshape(target.shape[1:])

    def group_weights(j):
        pieces = []
        for weight in (wq_ref, wk_ref, wv_ref):
            pieces.append(flat(weight[j]))
        return jnp.concatenate(pieces, 1)

    def group_sum(rows, j):
        pieces = []
        for grad in (q_ref, k_ref, v_ref):
            for at in (j, j + groups):
                pieces.append(grad[rows, pair_cols(at)])
        return nt(jnp.concatenate(pieces, 1), group_weights(j))

    step = 256
    plan = [
        [out_moves[0].start],
        chunk(0, "step2") + chunk(1, "step1") + [out_item.step0, out_moves[1].start],
        chunk(0, "step3") + chunk(1, "step2") + [out_item.step1, out_moves[2].start],
        chunk(0, "finish") + chunk(1, "step3") + group(0, "step1") + [out_item.step2],
        chunk(1, "finish") + group(0, "step2") + [out_item.step3, out_moves[3].start],
        group(0, "step3") + group(1, "step1") + [functools.partial(out_item.finish, gwo_ref, 0)],
    ]

    def one_pair(index, carry):
        at_step(index, plan)
        j, side = lax.div(index, 2), lax.rem(index, 2)
        bwd_pair(
            j + groups * side,
            q_ref,
            k_ref,
            v_ref,
            go_ref,
            ctx_ref,
            feat_ref,
            q_ref,
            k_ref,
            v_ref,
            bias_ref,
            sums_ref,
            far_ref,
            segk_ref,
            blockof_ref,
            gofeat_ref,
            near_ref,
            acc_ref,
        )

        @pl.when((side == 1) & (j < groups - 1))
        def _():
            weight_grads(j)
            for i in range(groups - 1):

                @pl.when(j == i)
                def _():
                    run_all(group(i, "step0"))

            for i in range(groups - 1):

                @pl.when(j == i)
                def _():
                    for at in range(length // step):
                        rows = slice(at * step, (at + 1) * step)
                        if i == 0:
                            sum_ref[rows, :] = group_sum(rows, i)
                        else:
                            sum_ref[rows, :] += group_sum(rows, i)

        return carry

    lax.fori_loop(0, 2 * groups, one_pair, 0)
    again_ref[...] = jnp.zeros_like(again_ref)
    last = groups - 1

    def finish_rows(own, i):
        half = p.t if own else 1 - p.t
        at = pl.ds(pl.multiple_of(i * step, step), step)
        rows = pl.ds(pl.multiple_of(half * half_rows + i * step, step), step)
        down = sum_ref[rows, :] + group_sum(rows, last)
        inputs = xs_ref[half, at, :].astype(F32)
        scale = rms_scale(inputs)
        normed = inputs * scale
        again_ref[...] += jnp.sum(down * normed, 0, keepdims=True)
        out = gm_ref[rows, :] + rms_back(down, normed, scale, gain)
        if own:
            igown_ref[at, :] = out
        else:
            ibuf_ref[at, :] = out.astype(BF)

    def piece(i):
        size = half_rows // 4
        at = pl.ds(i * size, size)
        return remote(ibuf_ref.at[at], ibuf2_ref.at[at], x_sems, i, p.xpeer)

    moves = [piece(i) for i in range(4)]
    finish_rows(False, 0)
    moves[0].start()
    moves[1].start()
    weight_grads(last)
    run_all(group(last, "step0") + group(1, "step2"))
    finish_rows(False, 1)
    moves[2].start()
    run_all(group(last, "step1"))
    for i in range(half_rows // step):
        finish_rows(True, i)
    bwd_table(tabg_ref, sums_ref, far_ref)
    run_all(group(0, "finish") + group(last, "step2"))
    moves[3].start()
    model = again_ref.shape[1]
    sm_ref[0, 0:1, :model] = again_ref[...]
    sm_ref[0, 1:2, :model] = ggain_ref[...]
    sm_ref[0, 2:8, :model] = jnp.zeros((6, model), F32)
    sm_ref[0, :, model : model + LANES] = tabg_ref[0:8, :]
    sm_ref[0, :, model + LANES :] = tabg_ref[8:16, :]
    hops = [(p.sib,), (p.ypeer,), (p.xpeer,), tuple(p.zpeers)]
    slot = 0
    beside = [
        group(1, "step3"),
        group(last, "step3"),
        group(1, "finish"),
        [],
    ]
    for level, peers in enumerate(hops):
        hop = [
            remote(sm_ref.at[level], smr_ref.at[slot + i], x_sems, len(moves) + slot + i, peer)
            for i, peer in enumerate(peers)
        ]
        for one in hop:
            one.start()
        run_all(beside[level])
        total = sm_ref[level]
        for i, one in enumerate(hop):
            one.wait_recv()
            total = total + smr_ref[slot + i]
        slot += len(peers)
        if level + 1 < len(hops):
            sm_ref[level + 1] = total
        else:
            small_ref[...] = total
        for one in hop:
            one.wait_send()
    run_all(group(last, "finish"))
    for move in moves + out_moves:
        move.wait_recv()
        move.wait_send()


def collect(
    own_in,
    oth_ref,
    igown_in,
    igoth_ref,
    small_ref,
    gwi_a,
    gwi_b,
    gwb_a,
    gwb_b,
    gwo_in,
    gwq_in,
    gwk_in,
    gwv_in,
    out_ref,
    ig_ref,
    again_ref,
    ggain_ref,
    gwq_ref,
    gwk_ref,
    gwv_ref,
    gwo_ref,
    gwi_ref,
    gwb_ref,
    table_ref,
    wide_ref,
    turn_ref,
    sem,
):
    t = lax.axis_index("tensor")
    loads = [
        local(own_in, wide_ref.at[0], sem.at[0]),
        local(igown_in, wide_ref.at[1], sem.at[1]),
    ]
    for one in loads:
        one.start()
    copies = []
    for i, (src, dst) in enumerate(((oth_ref, out_ref), (igoth_ref, ig_ref))):
        wide_ref[2 + i] = src[...].astype(F32)
        copies.append(local(wide_ref.at[2 + i], dst.at[1 - t], sem.at[2 + i]))
        copies[-1].start()
    for i, dst in enumerate((out_ref, ig_ref)):
        loads[i].wait()
        copies.append(local(wide_ref.at[i], dst.at[t], sem.at[4 + i]))
        copies[-1].start()
    for src, dst in ((gwq_in, gwq_ref), (gwk_in, gwk_ref), (gwv_in, gwv_ref), (gwo_in, gwo_ref)):
        dst[...] = src[...]
    for first, second, dst in ((gwi_a, gwi_b, gwi_ref), (gwb_a, gwb_b, gwb_ref)):
        dst[:, : first.shape[1]] = first[...]
        dst[:, first.shape[1] :] = second[...]
    model = again_ref.shape[0]
    again_ref[...] = small_ref[0:1, :model].reshape(model)
    ggain_ref[...] = small_ref[1:2, :model].reshape(model)
    turn_ref[...] = jnp.zeros_like(turn_ref)
    first = small_ref[:, model : model + LANES]
    second = small_ref[:, model + LANES :]
    turn_ref[0:8, :] = jnp.where(t == 0, first, second)
    table_ref[...] = turn_ref[: table_ref.shape[0], : table_ref.shape[1]]
    for one in copies:
        one.wait()


def call(kernel, outs, scratch, args, name, collective=None, far=()):
    def spec(array):
        return pl.BlockSpec(memory_space=pl.ANY if array in far else pltpu.VMEM)

    if collective is None:
        params = pltpu.CompilerParams(vmem_limit_bytes=VMEM_BYTES)
    else:
        params = pltpu.CompilerParams(
            vmem_limit_bytes=VMEM_BYTES, collective_id=collective, has_side_effects=True
        )
    return pl.pallas_call(
        kernel,
        out_shape=[jax.ShapeDtypeStruct(shape, dtype) for shape, dtype in outs],
        in_specs=[spec(i) for i in range(len(args))],
        out_specs=[spec(len(args) + i) for i in range(len(outs))],
        scratch_shapes=scratch,
        compiler_params=params,
        name=name,
    )(*args)


def shards(
    inputs,
    segments,
    norm_attn,
    norm_ffn,
    w_query,
    w_key,
    w_value,
    w_out,
    w_in,
    w_back,
    rel_table,
    cotangent,
):
    dp, tensor = lax.axis_size("dp"), lax.axis_size("tensor")
    t = lax.axis_index("tensor")
    rows, width = w_query.shape
    hidden_part = w_in.shape[1]
    model = inputs.shape[2]
    length = segments.shape[2]
    half = inputs.shape[1]
    buckets, heads = rel_table.shape
    depth = dp // 4
    fused = rows % 16 == 0 and dp % 4 == 0 and depth >= 2
    full = (length, model)
    inner = (length, width * tensor)
    square = (depth, 2, 2, rows, 2 * width)
    part = 256
    chunks = hidden_part // part
    pairs = inner[1] // LANES
    dma = pltpu.SemaphoreType.DMA
    halves = (2, half, model)
    fwd_work = [pltpu.VMEM((16, 4 * LANES), F32)] + [pltpu.VMEM((length, LANES), BF)] * 2
    bwd_work = [
        pltpu.VMEM((16, 4 * LANES), F32),
        pltpu.VMEM((16, 4 * LANES), F32),
        pltpu.VMEM((16, LANES), F32),
        pltpu.VMEM((length, LANES), BF),
        pltpu.VMEM((length, LANES), BF),
        pltpu.VMEM((length, LANES), BF),
        pltpu.VMEM((2, LANES, 3 * LANES), F32),
        pltpu.VMEM((length, LANES), F32),
    ]
    ffn_work = [pltpu.VMEM(full, BF), pltpu.VMEM(full[::-1], BF), pltpu.VMEM(full[::-1], BF)]
    rest = [pltpu.VMEM((length, 2 * part), BF)] * 2 + [pltpu.VMEM(full, F32)] * 2
    if fused:
        here = chunks - chunks // 3
        block = (depth, 2, 2, rows, 2 * part)
        groups = pairs // 2
        narrow = (groups, depth, 2, 2, rows, 2 * LANES)
        (
            xs,
            tabs,
            queries,
            keys,
            values,
            ctx,
            feats,
            wq,
            wk,
            wv,
            own,
            oth,
            grad_middle,
            grad_context,
            ggain,
            gout,
            gwi_a,
            gwb_a,
            gi,
            gb,
        ) = call(
            functools.partial(forward_fused, depth, here),
            [
                (halves, BF),
                ((2, 8, LANES), F32),
                (inner, BF),
                (inner, BF),
                (inner, BF),
                (inner, BF),
                ((pairs, length, LANES), BF),
                (narrow, BF),
                (narrow, BF),
                (narrow, BF),
                ((half, model), F32),
                ((half, model), BF),
                (full, F32),
                (inner, BF),
                ((1, model), F32),
                (square, BF),
                ((rows, here * part), F32),
                ((rows, here * part), F32),
                ((chunks - here,) + block, BF),
                ((chunks - here,) + block, BF),
            ],
            [
                pltpu.VMEM(halves, BF),
                pltpu.VMEM((half, model), F32),
                pltpu.VMEM(halves, BF),
                pltpu.VMEM((half, model), BF),
            ]
            + [pltpu.VMEM(inner, BF)] * 4
            + [pltpu.VMEM((pairs, length, LANES), BF)]
            + [pltpu.VMEM(narrow, BF)] * 3
            + [pltpu.VMEM(square, BF)]
            + [pltpu.VMEM((chunks,) + block, BF)] * 2
            + [pltpu.VMEM(full, BF), pltpu.VMEM((LANES, LANES), F32)]
            + fwd_work
            + [pltpu.VMEM(full, F32)]
            + [pltpu.VMEM(full[::-1], BF)] * 2
            + [pltpu.VMEM(full, F32)] * 2
            + scatter_bufs(here, depth, rows, part, True)
            + scatter_bufs(here, depth, rows, part, False)
            + gather_sems(3 * groups, depth)
            + gather_sems(1 + 2 * chunks, depth)
            + scatter_sems(2 * here, depth)
            + [dma((3,)), dma((3,)), dma((16,)), dma((2 * chunks,))],
            (
                inputs,
                cotangent,
                norm_attn,
                norm_ffn,
                rel_table.T,
                segments,
                w_query,
                w_key,
                w_value,
                w_out,
                w_in,
                w_back,
            ),
            "forward_feed_forward",
            0,
            (0, 1, 12, 14, 15, 16, 17, 18, 19, 20, 21, 22, 23, 24, 25, 27, 30, 31),
        )
        left = chunks - here
        oth, igown, igoth, gwo, gwq, gwk, gwv, gwi_b, gwb_b, small = call(
            functools.partial(back_fused, depth),
            [
                ((half, model), BF),
                ((half, model), F32),
                ((half, model), BF),
                ((rows, width), F32),
                ((rows, width), F32),
                ((rows, width), F32),
                ((rows, width), F32),
                ((rows, left * part), F32),
                ((rows, left * part), F32),
                ((8, model + 2 * LANES), F32),
            ],
            [pltpu.VMEM(inner, BF)] * 3
            + [pltpu.VMEM(halves, BF), pltpu.VMEM(full, F32)]
            + [pltpu.VMEM(narrow, BF)] * 3
            + [pltpu.VMEM((left,) + block, BF)] * 2
            + [pltpu.VMEM(square, BF)]
            + [pltpu.VMEM(full[::-1], BF), pltpu.VMEM(full, F32)]
            + [pltpu.VMEM(narrow, BF)] * 3
            + [pltpu.VMEM((half, model), BF)]
            + [
                pltpu.VMEM((1, model), F32),
                pltpu.VMEM((16, LANES), F32),
                pltpu.VMEM((4, 8, model + 2 * LANES), F32),
                pltpu.VMEM((depth + 2, 8, model + 2 * LANES), F32),
            ]
            + bwd_work
            + scatter_bufs(None, depth, rows, width, True)
            + scatter_bufs(left, depth, rows, part, True)
            + scatter_bufs(left, depth, rows, part, True)
            + scatter_bufs(groups, depth, rows, LANES, True)
            + scatter_bufs(groups, depth, rows, LANES, True)
            + scatter_bufs(groups, depth, rows, LANES, True)
            + scatter_sems(1 + 2 * left + 3 * groups, depth)
            + [dma((depth + 10,)), dma((depth + 10,)), dma((11,))],
            (
                queries,
                keys,
                values,
                grad_context,
                ctx,
                feats,
                segments,
                tabs,
                xs,
                grad_middle,
                wq,
                wk,
                wv,
                norm_attn,
                ggain,
                gi,
                gb,
                gout,
                oth,
            ),
            "attention_backward",
            1,
            (0, 1, 2, 8, 9, 10, 11, 12, 15, 16, 17, 18, 19),
        )
        results = call(
            collect,
            [
                (halves, F32),
                (halves, F32),
                ((model,), F32),
                ((model,), F32),
                ((rows, width), F32),
                ((rows, width), F32),
                ((rows, width), F32),
                ((rows, width), F32),
                ((rows, hidden_part), F32),
                ((rows, hidden_part), F32),
                ((heads, buckets), F32),
            ],
            [pltpu.VMEM((4, half, model), F32), pltpu.VMEM((LANES, LANES), F32), dma((6,))],
            (own, oth, igown, igoth, small, gwi_a, gwi_b, gwb_a, gwb_b, gwo, gwq, gwk, gwv),
            "collect",
            None,
            (0, 2, 13, 14),
        )
        return tuple(results[:-1]) + (results[-1].T,)
    else:
        gain_attn, gain_ffn = norm_attn.reshape(1, model), norm_ffn.reshape(1, model)
        table = jnp.pad(rel_table.T, ((0, 8 - heads), (0, LANES - buckets)))
        segment = lax.dynamic_index_in_dim(segments, t, 0, False)

        def whole(weight):
            weight = lax.all_gather(weight, "dp", axis=0, tiled=True)
            return lax.all_gather(weight, "tensor", axis=1, tiled=True)

        def exchanged(local_part):
            own = lax.dynamic_index_in_dim(local_part, t, 0, False)
            other = lax.dynamic_index_in_dim(local_part, 1 - t, 0, False)
            other = lax.ppermute(other, "tensor", [(0, 1), (1, 0)])
            first = jnp.where(t == 0, own, other)
            second = jnp.where(t == 0, other, own)
            return jnp.concatenate([first, second], 0)

        def returned(seq):
            mine = lax.dynamic_slice_in_dim(seq, t * half, half, 0)
            other = lax.dynamic_slice_in_dim(seq, (1 - t) * half, half, 0)
            other = lax.ppermute(other, "tensor", [(0, 1), (1, 0)])
            return jnp.stack([jnp.where(t == 0, mine, other), jnp.where(t == 0, other, mine)])

        def scattered(grad):
            grad = lax.psum_scatter(grad.astype(F32), "tensor", scatter_dimension=1, tiled=True)
            return lax.psum_scatter(grad, "dp", scatter_dimension=0, tiled=True)

        xs = exchanged(inputs)
        tabs = lax.all_gather(table, "tensor", axis=0)
        wq, wk, wv, wo, wi, wb = (
            whole(w) for w in (w_query, w_key, w_value, w_out, w_in, w_back)
        )
        queries, keys, values = call(
            k1_plain,
            [(inner, BF)] * 3,
            [pltpu.VMEM(full, BF)],
            (xs, gain_attn, wq, wk, wv),
            "project",
        )
        ctx, feats = call(
            fwd_kernel,
            [(inner, BF), ((pairs, length, LANES), BF)],
            fwd_work,
            (queries, keys, values, segment, tabs),
            "attention_forward",
        )
        out_seq, grad_middle, grad_context, ggain, gwo, gwi, gwb = call(
            k3_plain,
            [
                (full, F32),
                (full, F32),
                (inner, BF),
                ((1, model), F32),
                (wo.shape, BF),
                (wi.shape, BF),
                (wb.shape, BF),
            ],
            ffn_work + [pltpu.VMEM(full, BF)] + rest,
            (xs, ctx, exchanged(cotangent), gain_ffn, wo, wi, wb),
            "feed_forward",
        )
        output = returned(out_seq)
        gwo, gwi, gwb = scattered(gwo), scattered(gwi), scattered(gwb)
        dq, dk, dv, table_grad = call(
            bwd_kernel,
            [(inner, BF), (inner, BF), (inner, BF), ((16, LANES), F32)],
            bwd_work,
            (queries, keys, values, grad_context, ctx, feats, segment, tabs),
            "attention_backward",
        )
        ig_seq, gwq, gwk, gwv, again = call(
            k5_plain,
            [(full, F32), (wq.shape, BF), (wk.shape, BF), (wv.shape, BF), ((1, model), F32)],
            [pltpu.VMEM((model, length), BF)],
            (xs, grad_middle, dq, dk, dv, wq, wk, wv, gain_attn),
            "projection_gradients",
        )
        input_grad = returned(ig_seq)
        gwq, gwk, gwv = scattered(gwq), scattered(gwk), scattered(gwv)
        again, ggain, tables = lax.psum((again, ggain, table_grad), ("dp", "tensor"))
        gain_attn_grad, gain_ffn_grad = again[0], ggain[0]
        tables = tables.reshape(2, 8, LANES)
    table_out = lax.dynamic_index_in_dim(tables, t, 0, False)[:heads, :buckets].T
    return (
        output,
        input_grad,
        gain_attn_grad,
        gain_ffn_grad,
        gwq,
        gwk,
        gwv,
        gwo,
        gwi,
        gwb,
        table_out,
    )


def solution(mesh):
    weight = P("dp", "tensor")
    tokens = P(None, ("dp", "tensor"), None)
    return jax.shard_map(
        shards,
        mesh=mesh,
        in_specs=(
            tokens,
            P(None, "dp", None),
            P(),
            P(),
            weight,
            weight,
            weight,
            weight,
            weight,
            weight,
            P(None, "tensor"),
            tokens,
        ),
        out_specs=(
            tokens,
            tokens,
            P(),
            P(),
            weight,
            weight,
            weight,
            weight,
            weight,
            weight,
            P(None, "tensor"),
        ),
        check_vma=False,
    )
```

```python
import functools

import jax
import jax.numpy as jnp
from jax import lax
from jax.experimental import pallas as pl
from jax.experimental.pallas import tpu as pltpu
from jax.sharding import PartitionSpec as P

MESH = pl.DeviceIdType.MESH
BF = jnp.bfloat16
F32 = jnp.float32
HIGHEST = lax.Precision.HIGHEST
EPSILON = 1e-06
THRESHOLDS = (12, 16, 23, 32, 46, 64, 91)
MASK_OUT = -float(2**30)
DH = 64
SPAN = 512
LANES = 128
VMEM_BYTES = 62 * 2**20


def nn(left, right):
    return lax.dot_general(left, right, (((1,), (0,)), ((), ())), preferred_element_type=F32)


def nt(left, right):
    return lax.dot_general(left, right, (((1,), (1,)), ((), ())), preferred_element_type=F32)


def tn(left, right):
    return lax.dot_general(left, right, (((0,), (0,)), ((), ())), preferred_element_type=F32)


def iota(shape, dim):
    return lax.broadcasted_iota(jnp.int32, shape, dim)


def bucket_ids(offsets):
    distance = jnp.abs(offsets)
    far_ids = 8 + sum((distance >= threshold).astype(jnp.int32) for threshold in THRESHOLDS)
    return jnp.where(offsets > 0, 16, 0) + jnp.where(distance < 8, distance, far_ids)


def rms_scale(values):
    return lax.rsqrt(jnp.mean(values * values, -1, keepdims=True) + EPSILON)


def rms_back(grad_normed, normed, scale, gain):
    scaled = grad_normed * gain
    return scale * (scaled - normed * jnp.mean(scaled * normed, -1, keepdims=True))


def gelu_pair(v):
    square = v * v
    half = 0.5 + 0.5 * jnp.tanh(v * (0.7978845608028654 + 0.035677408136300125 * square))
    slope = half + v * half * (1.0 - half) * (1.5957691216057308 + 0.2140644488178007 * square)
    return v * half, slope


class Place:
    def __init__(self, depth):
        d, t = lax.axis_index("dp"), lax.axis_index("tensor")
        self.t = t
        self.z, self.y, self.c = lax.div(d, 4), lax.rem(lax.div(d, 2), 2), lax.rem(d, 2)
        self.depth = depth
        self.sib = (d + 1 - 2 * self.c, t)
        self.ypeer = (d + 2 - 4 * self.y, t)
        self.xpeer = (d, 1 - t)
        rest = self.rest = lax.rem(d, 4)
        self.zs = [lax.rem(self.z + step, depth) for step in range(1, depth)]
        self.zpeers = [(z * 4 + rest, t) for z in self.zs]

    def barrier(self):
        semaphore = pltpu.get_barrier_semaphore()
        peers = [self.sib, self.ypeer, self.xpeer] + self.zpeers
        for peer in peers:
            pl.semaphore_signal(semaphore, inc=1, device_id=peer, device_id_type=MESH)
        pl.semaphore_wait(semaphore, len(peers))


class Copy:
    def __init__(self, **parts):
        self.parts = parts

    def made(self):
        return pltpu.make_async_remote_copy(device_id_type=MESH, **self.parts)

    def start(self):
        self.made().start()

    def wait_recv(self):
        self.made().wait_recv()

    def wait_send(self):
        self.made().wait_send()


def local(src, dst, sem):
    return pltpu.make_async_copy(src, dst, sem)


def remote(src, dst, sems, index, peer):
    send, recv = sems
    return Copy(
        src_ref=src, dst_ref=dst, send_sem=send.at[index], recv_sem=recv.at[index], device_id=peer
    )


class Gather:
    def __init__(self, place, ref, width, sems, item, x_first):
        self.p, self.ref, self.width, self.sems, self.item = place, ref, width, sems, item
        p = place
        self.relays = p.depth == 4
        if x_first:
            self.peers, order = (p.xpeer, p.ypeer), ((0, 0), (0, 1), (1, 0), (1, 1))
        else:
            self.peers, order = (p.ypeer, p.xpeer), ((0, 0), (1, 0), (0, 1), (1, 1))
        self.sides = [(p.y + (1 - 2 * p.y) * i, p.t + (1 - 2 * p.t) * j) for i, j in order]

    def cols(self, x):
        return pl.ds(pl.multiple_of(x * self.width, LANES), self.width)

    def block(self, z, side):
        y, x = self.sides[side]
        return self.ref.at[z, y, self.p.c, :, self.cols(x)]

    def region(self, side):
        y, x = self.sides[side]
        return self.ref.at[:, y, self.p.c, :, self.cols(x)]

    def send(self, index, src, peer):
        return remote(src, src, self.sems, (self.item, index), peer)

    def first(self):
        return self.send(0, self.block(self.p.z, 0), self.peers[0])

    def along(self, side):
        p = self.p
        base = 1 + side * len(p.zpeers)
        return [self.send(base + i, self.block(p.z, side), peer) for i, peer in enumerate(p.zpeers)]

    def last(self, side):
        return self.send(1 + 2 * len(self.p.zpeers) + side, self.region(side), self.peers[1])

    def sib(self, side):
        return self.send(3 + 2 * len(self.p.zpeers) + side, self.region(side), self.p.sib)

    def relay(self, side):
        p = self.p
        send, recv = self.sems
        src = self.block(lax.rem(p.z + 2, 4), side)
        low = p.z == 1
        target = jnp.where(low, 0, 3)
        return Copy(
            src_ref=src,
            dst_ref=src,
            send_sem=send.at[self.item, 7 + 2 * len(p.zpeers) + side],
            recv_sem=recv.at[self.item, 1 + side * len(p.zpeers) + jnp.where(low, 0, 2)],
            device_id=(target * 4 + p.rest, p.t),
        )

    def each_along(self, side, method):
        p = self.p
        for i, copy in enumerate(self.along(side)):
            if self.relays and i != 1:
                pl.when(p.z != (3 if i == 0 else 0))(getattr(copy, method))
            else:
                getattr(copy, method)()

    def inside(self, action):
        pl.when((self.p.z == 1) | (self.p.z == 2))(action)

    def start(self):
        self.first().start()

    def start_z(self):
        self.each_along(0, "start")

    def step1(self):
        self.first().wait_recv()
        self.each_along(1, "start")

    def step2(self, side):
        zs = self.along(side)
        if self.relays:
            zs[1].wait_recv()
            self.inside(self.relay(side).start)
            zs = [zs[0], zs[2]]
        for copy in zs:
            copy.wait_recv()
        self.last(side).start()
        self.sib(side).start()

    def step3(self):
        for side in range(2):
            self.last(side).wait_recv()
            self.sib(2 + side).start()

    def finish(self):
        for side in range(4):
            self.sib(side).wait_recv()
        self.first().wait_send()
        for side in range(2):
            self.each_along(side, "wait_send")
            if self.relays:
                self.inside(self.relay(side).wait_send)
            self.last(side).wait_send()
        for side in range(4):
            self.sib(side).wait_send()


def gather_sems(items, depth):
    return [pltpu.SemaphoreType.DMA((items, 2 * depth + 7))] * 2


class Scatter:
    def __init__(self, place, ref, width, bufs, sems, item, y_first):
        self.p, self.ref, self.width, self.sems, self.item = place, ref, width, sems, item
        self.r0, self.r1, self.r2, self.r3 = bufs
        self.y_first = y_first

    def cols(self, x):
        return pl.ds(pl.multiple_of(x * self.width, LANES), self.width)

    def copies(self):
        p, ref = self.p, self.ref
        sib = remote(ref.at[:, :, 1 - p.c], self.r0, self.sems, (self.item, 0), p.sib)
        if self.y_first:
            half = remote(ref.at[:, 1 - p.y, p.c], self.r1, self.sems, (self.item, 1), p.ypeer)
            quarter = remote(
                ref.at[:, p.y, p.c, :, self.cols(1 - p.t)],
                self.r2,
                self.sems,
                (self.item, 2),
                p.xpeer,
            )
        else:
            half = remote(
                ref.at[:, :, p.c, :, self.cols(1 - p.t)],
                self.r1,
                self.sems,
                (self.item, 1),
                p.xpeer,
            )
            quarter = remote(
                ref.at[:, 1 - p.y, p.c, :, self.cols(p.t)],
                self.r2,
                self.sems,
                (self.item, 2),
                p.ypeer,
            )
        zs = [
            remote(
                ref.at[z, p.y, p.c, :, self.cols(p.t)],
                self.r3.at[i],
                self.sems,
                (self.item, 3 + i),
                peer,
            )
            for i, (z, peer) in enumerate(zip(p.zs, p.zpeers))
        ]
        return sib, half, quarter, zs

    def step0(self):
        self.copies()[0].start()

    def step1(self):
        p = self.p
        sib, half, _, _ = self.copies()
        sib.wait_recv()
        kept = self.ref.at[:, :, p.c]
        kept[...] = (kept[...].astype(F32) + self.r0[...].astype(F32)).astype(BF)
        half.start()

    def step2(self):
        p = self.p
        _, half, quarter, _ = self.copies()
        half.wait_recv()
        if self.y_first:
            kept = self.ref.at[:, p.y, p.c]
        else:
            kept = self.ref.at[:, :, p.c, :, self.cols(p.t)]
        kept[...] = (kept[...].astype(F32) + self.r1[...].astype(F32)).astype(BF)
        quarter.start()

    def step3(self):
        p = self.p
        _, _, quarter, zs = self.copies()
        quarter.wait_recv()
        kept = self.ref.at[:, p.y, p.c, :, self.cols(p.t)]
        kept[...] = (kept[...].astype(F32) + self.r2[...].astype(F32)).astype(BF)
        for copy in zs:
            copy.start()

    def finish(self, out, offset):
        p = self.p
        sib, half, quarter, zs = self.copies()
        for copy in zs:
            copy.wait_recv()
        total = self.ref[p.z, p.y, p.c, :, self.cols(p.t)].astype(F32)
        for i in range(len(zs)):
            total = total + self.r3[i].astype(F32)
        out[:, pl.ds(pl.multiple_of(offset, LANES), self.width)] = total
        for copy in [sib, half, quarter] + zs:
            copy.wait_send()


def scatter_bufs(items, depth, rows, width, y_first):
    lead = () if items is None else (items,)
    return [
        pltpu.VMEM(lead + (depth, 2, rows, 2 * width), BF),
        pltpu.VMEM(lead + ((depth, rows, 2 * width) if y_first else (depth, 2, rows, width)), BF),
        pltpu.VMEM(lead + (depth, rows, width), BF),
        pltpu.VMEM(lead + (depth - 1, rows, width), BF),
    ]


def scatter_sems(items, depth):
    return [pltpu.SemaphoreType.DMA((items, depth + 2))] * 2


def flat(values):
    if len(values.shape) == 2:
        return values
    return values.reshape(-1, values.shape[-1])


def project_rows(x_rows, gain):
    rows = x_rows.astype(F32)
    return (rows * rms_scale(rows) * gain).astype(BF)


def project(low_ref, w_ref, out_ref):
    weight = flat(w_ref[...])
    half = low_ref.shape[0] // 2

    def one(i, carry):
        rows = pl.ds(pl.multiple_of(i * half, half), half)
        out_ref[rows, :] = nn(low_ref[rows, :], weight).astype(BF)
        return carry

    lax.fori_loop(0, 2, one, 0)


def k1_plain(x_ref, gain_ref, wq_ref, wk_ref, wv_ref, q_ref, k_ref, v_ref, low_ref):
    low_ref[...] = project_rows(x_ref[...], gain_ref[...])
    for weight, out in ((wq_ref, q_ref), (wk_ref, k_ref), (wv_ref, v_ref)):
        project(low_ref, weight, out)


def bias_rows(tabs_ref, out_ref, flipped):
    offsets = iota((LANES, 4 * LANES), 1) - 2 * LANES
    onehot = (bucket_ids(-offsets if flipped else offsets) == iota((LANES, 4 * LANES), 0)).astype(F32)
    for half in range(2):
        out_ref[half * 8 : half * 8 + 8, :] = jnp.dot(
            tabs_ref[half], onehot, precision=HIGHEST, preferred_element_type=F32
        )


def head_row(pair, per_half):
    return 8 * lax.div(pair, per_half) + 2 * lax.rem(pair, per_half)


def bias_strip(row):
    spread = jnp.broadcast_to(row, (LANES, 4 * LANES))
    return pltpu.roll(spread, 3 * LANES, 1, stride=1, stride_axis=0)


def window(tile, rows, length):
    reach = -(-SPAN // rows)
    return max(0, (tile - reach) * rows), min(length, (tile + reach + 1) * rows)


def segment_lanes(seg):
    length = seg.shape[1]
    onehot = (seg == iota((LANES, length), 0)).astype(F32).T > 0.5
    inside = iota((length, LANES), 1) < 16
    return onehot, inside


def pair_cols(pair):
    return pl.ds(pl.multiple_of(pair * LANES, LANES), LANES)


def spread3(value):
    top = value.astype(BF).astype(F32)
    mid = (value - top).astype(BF).astype(F32)
    return top, mid, value - top - mid


TILE = 256
NEAR = SPAN // LANES


def key_lanes(seg):
    onehot, inside = segment_lanes(seg)
    return jnp.where(onehot, 0.0, jnp.where(inside, 1.0, 0.0)).astype(BF)


def fwd_setup(seg, tabs_ref, bias_ref, segq_ref, segk_ref):
    bias_rows(tabs_ref, bias_ref, False)
    onehot, _ = segment_lanes(seg)
    segq_ref[...] = jnp.where(onehot, MASK_OUT, 0.0).astype(BF)
    segk_ref[...] = key_lanes(seg)


def fwd_pair(pair, q_ref, k_ref, v_ref, ctx_ref, feat_ref, bias_ref, segq_ref, segk_ref):
    length, width = q_ref.shape
    per_half = width // LANES // 2
    tile, near = TILE, NEAR
    cols = pair_cols(pair)
    row = head_row(pair, per_half)
    lane = iota((tile, LANES), 1)
    low_half = lane < DH
    strips, fars = [], []
    for hh in range(2):
        line = bias_ref[pl.ds(row + hh, 1), :]
        strips.append(bias_strip(line))
        fars.append((line[:, 0:1], line[:, 4 * LANES - 1 : 4 * LANES]))
    for index in range(length // tile):
        rows = slice(index * tile, (index + 1) * tile)
        start, stop = window(index, tile, length)
        queries = q_ref[rows, cols]
        zero = jnp.zeros_like(queries)
        q_feat = segq_ref[rows, :]
        left = jnp.concatenate(
            [
                jnp.concatenate([jnp.where(low_half, queries, zero), q_feat], 1),
                jnp.concatenate([jnp.where(low_half, zero, queries), q_feat], 1),
            ],
            0,
        )
        right = jnp.concatenate([k_ref[start:stop, cols], segk_ref[start:stop, :]], 1)
        scores = nt(left, right)
        weights, peaks = [], []
        for hh in range(2):
            for part in range(tile // LANES):
                at = hh * tile + part * LANES
                q_block = index * (tile // LANES) + part
                blocks = []
                for k_block in range(start // LANES, stop // LANES):
                    delta = k_block - q_block
                    if abs(delta) > near:
                        blocks.append(None)
                        continue
                    col = k_block * LANES - start
                    block = scores[at : at + LANES, col : col + LANES]
                    if abs(delta) <= 1:
                        block = block + strips[hh][:, (delta + 1) * LANES : (delta + 2) * LANES]
                    else:
                        block = block + fars[hh][0 if delta < 0 else 1]
                    blocks.append(block)
                real = [block for block in blocks if block is not None]
                peak = functools.reduce(jnp.maximum, real)
                peak = jnp.max(peak, -1, keepdims=True)
                peaks.append(peak)
                weights.append(
                    jnp.concatenate(
                        [
                            jnp.zeros((LANES, LANES), BF)
                            if block is None
                            else jnp.exp(block - peak).astype(BF)
                            for block in blocks
                        ],
                        1,
                    )
                )
        values = v_ref[start:stop, cols]
        gathered = nn(
            jnp.concatenate(weights, 0), jnp.concatenate([values, jnp.ones_like(values)], 1)
        )
        normal = gathered[:, :LANES] / gathered[:, LANES:]
        context = jnp.where(low_half, normal[:tile], normal[tile:])
        ctx_ref[rows, cols] = context.astype(BF)
        logs = jnp.concatenate(peaks, 0) + jnp.log(gathered[:, LANES:])
        feature = q_feat.astype(F32)
        for hh in range(2):
            for i, piece in enumerate(spread3(logs[hh * tile : (hh + 1) * tile])):
                feature = jnp.where(lane == 16 + 3 * hh + i, -piece, feature)
        feat_ref[pair, rows, :] = feature.astype(BF)


def fwd_kernel(
    q_ref, k_ref, v_ref, seg_ref, tabs_ref, ctx_ref, feat_ref, bias_ref, segq_ref, segk_ref
):
    fwd_setup(seg_ref[...], tabs_ref, bias_ref, segq_ref, segk_ref)

    def one_pair(pair, carry):
        fwd_pair(pair, q_ref, k_ref, v_ref, ctx_ref, feat_ref, bias_ref, segq_ref, segk_ref)
        return carry

    lax.fori_loop(0, q_ref.shape[1] // LANES, one_pair, 0)


def bwd_setup(seg, tabs_ref, bias_ref, sums_ref, far_ref, segk_ref, blockof_ref):
    length = seg.shape[1]
    bias_rows(tabs_ref, bias_ref, True)
    sums_ref[...] = jnp.zeros_like(sums_ref)
    far_ref[...] = jnp.zeros_like(far_ref)
    segk_ref[...] = key_lanes(seg)
    blockof_ref[...] = (
        lax.div(iota((length, LANES), 0), LANES) == iota((length, LANES), 1)
    ).astype(BF)


def bwd_pair(
    pair,
    q_ref,
    k_ref,
    v_ref,
    go_ref,
    ctx_ref,
    feat_ref,
    dq_ref,
    dk_ref,
    dv_ref,
    bias_ref,
    sums_ref,
    far_ref,
    segk_ref,
    blockof_ref,
    gofeat_ref,
    near_ref,
    acc_ref,
):
    length, width = q_ref.shape
    per_half = width // LANES // 2
    tile, near = TILE, NEAR
    flip = (iota((LANES, LANES), 0) + iota((LANES, LANES), 1) == LANES - 1).astype(F32)
    cols = pair_cols(pair)
    row = head_row(pair, per_half)
    lane = iota((tile, LANES), 1)
    low_half = lane < DH
    strips, fars = [], []
    for hh in range(2):
        line = bias_ref[pl.ds(row + hh, 1), :]
        strips.append(bias_strip(line))
        fars.append((line[:, 0:1], line[:, 4 * LANES - 1 : 4 * LANES]))
    grads_all = go_ref[:, cols]
    product = grads_all.astype(F32) * ctx_ref[:, cols].astype(F32)
    lane_all = iota((length, LANES), 1)
    feature = jnp.zeros((length, LANES), F32)
    for hh in range(2):
        keep = (lane_all < DH) if hh == 0 else (lane_all >= DH)
        total = jnp.sum(jnp.where(keep, product, 0.0), -1, keepdims=True)
        for i, piece in enumerate(spread3(total)):
            feature = jnp.where(lane_all == 3 * hh + i, -piece, feature)
    gofeat_ref[...] = feature.astype(BF)
    near_ref[...] = jnp.zeros_like(near_ref)
    acc_ref[...] = jnp.zeros_like(acc_ref)
    far_sums = [[jnp.zeros((1, LANES), F32) for _ in range(2)] for _ in range(2)]
    lane_row = iota((1, LANES), 1)
    for index in range(length // tile):
        rows = slice(index * tile, (index + 1) * tile)
        start, stop = window(index, tile, length)
        keys, values = k_ref[rows, cols], v_ref[rows, cols]
        zero = jnp.zeros_like(keys)
        seg_feat = segk_ref[rows, :].astype(F32)

        def ones_at(base, first):
            return jnp.where((lane >= first) & (lane < first + 3), 1.0, base).astype(BF)

        masked_keys = jnp.concatenate(
            [jnp.where(low_half, keys, zero), jnp.where(low_half, zero, keys)], 0
        )
        masked_values = jnp.concatenate(
            [jnp.where(low_half, values, zero), jnp.where(low_half, zero, values)], 0
        )
        key_feats = jnp.concatenate([ones_at(seg_feat, 16), ones_at(seg_feat, 19)], 0)
        value_feats = jnp.concatenate([ones_at(0.0, 0), ones_at(0.0, 3)], 0)
        queries = q_ref[start:stop, cols]
        grads = go_ref[start:stop, cols]
        logits = nt(
            jnp.concatenate([masked_keys, key_feats], 1),
            jnp.concatenate([queries, feat_ref[pair, start:stop, :]], 1),
        )
        shifted = nt(
            jnp.concatenate([masked_values, value_feats], 1),
            jnp.concatenate([grads, gofeat_ref[start:stop, :]], 1),
        )
        probs_rows, score_rows = [], []
        for hh in range(2):
            for part in range(tile // LANES):
                at = hh * tile + part * LANES
                k_block = index * (tile // LANES) + part
                probs, score_grads = [], []
                for q_block in range(start // LANES, stop // LANES):
                    delta = k_block - q_block
                    if abs(delta) > near:
                        probs.append(jnp.zeros((LANES, LANES), BF))
                        score_grads.append(jnp.zeros((LANES, LANES), BF))
                        continue
                    col = q_block * LANES - start
                    block = logits[at : at + LANES, col : col + LANES]
                    place = (1 - delta) * LANES
                    if abs(delta) <= 1:
                        block = block + strips[hh][:, place : place + LANES]
                    else:
                        block = block + fars[hh][0 if delta > 0 else 1]
                    prob = jnp.exp(block)
                    grad = prob * shifted[at : at + LANES, col : col + LANES]
                    if abs(delta) <= 1:
                        near_ref[hh, :, place : place + LANES] += grad
                    probs.append(prob.astype(BF))
                    score_grads.append(grad.astype(BF))
                probs_rows.append(jnp.concatenate(probs, 1))
                score_rows.append(jnp.concatenate(score_grads, 1))
        probs_all = jnp.concatenate(probs_rows, 0)
        scores_all = jnp.concatenate(score_rows, 0)
        value_grad = nn(probs_all, grads)
        dv_ref[rows, cols] = jnp.where(low_half, value_grad[:tile], value_grad[tile:]).astype(BF)
        key_grad = nn(scores_all, jnp.concatenate([queries, blockof_ref[start:stop, :]], 1))
        dk_ref[rows, cols] = jnp.where(
            low_half, key_grad[:tile, :LANES], key_grad[tile:, :LANES]
        ).astype(BF)
        acc_ref[start:stop, :] += tn(scores_all, masked_keys)
        for hh in range(2):
            for part in range(tile // LANES):
                at = hh * tile + part * LANES
                k_block = index * (tile // LANES) + part
                line = jnp.sum(key_grad[at : at + LANES, LANES:], 0, keepdims=True)
                far_sums[hh][0] += jnp.where(lane_row <= k_block - 2, line, 0.0)
                far_sums[hh][1] += jnp.where(lane_row >= k_block + 2, line, 0.0)
    dq_ref[:, cols] = acc_ref[...].astype(BF)
    for hh in range(2):
        turned = jnp.dot(flip, near_ref[hh], precision=HIGHEST, preferred_element_type=F32)
        turned = jnp.concatenate([turned, jnp.zeros((LANES, LANES), F32)], 1)
        turned = pltpu.roll(turned, 1, 1, stride=1, stride_axis=0)
        sums_ref[pl.ds(row + hh, 1), :] = jnp.sum(turned, 0, keepdims=True)
        last = lane_row == 0
        positive = jnp.sum(far_sums[hh][0], -1, keepdims=True)
        negative = jnp.sum(far_sums[hh][1], -1, keepdims=True)
        far_ref[pl.ds(row + hh, 1), :] = jnp.where(last, positive, jnp.where(lane_row == 1, negative, 0.0))


def bwd_table(tabg_ref, sums_ref, far_ref):
    offsets = 2 * LANES - iota((LANES, 4 * LANES), 1)
    onehot_buckets = (bucket_ids(offsets) == iota((LANES, 4 * LANES), 0)).astype(F32)
    table = lax.dot_general(
        sums_ref[...],
        onehot_buckets,
        (((1,), (1,)), ((), ())),
        precision=HIGHEST,
        preferred_element_type=F32,
    )
    lane = iota(tabg_ref.shape, 1)
    far = far_ref[...]
    table = table + jnp.where(lane == 31, far[:, 0:1], 0.0) + jnp.where(lane == 15, far[:, 1:2], 0.0)
    tabg_ref[...] = table


def bwd_kernel(
    q_ref,
    k_ref,
    v_ref,
    go_ref,
    ctx_ref,
    feat_ref,
    seg_ref,
    tabs_ref,
    dq_ref,
    dk_ref,
    dv_ref,
    tabg_ref,
    bias_ref,
    sums_ref,
    far_ref,
    segk_ref,
    blockof_ref,
    gofeat_ref,
    near_ref,
    acc_ref,
):
    bwd_setup(seg_ref[...], tabs_ref, bias_ref, sums_ref, far_ref, segk_ref, blockof_ref)

    def one_pair(pair, carry):
        bwd_pair(
            pair,
            q_ref,
            k_ref,
            v_ref,
            go_ref,
            ctx_ref,
            feat_ref,
            dq_ref,
            dk_ref,
            dv_ref,
            bias_ref,
            sums_ref,
            far_ref,
            segk_ref,
            blockof_ref,
            gofeat_ref,
            near_ref,
            acc_ref,
        )
        return carry

    lax.fori_loop(0, q_ref.shape[1] // LANES, one_pair, 0)
    bwd_table(tabg_ref, sums_ref, far_ref)


def k3_before(xs_ref, ctx_ref, wo, gain, middle_ref, ffn_ref, ffnt_ref):
    step = 256

    def one(i, carry):
        rows = pl.ds(pl.multiple_of(i * step, step), step)
        middle = xs_ref[rows, :].astype(F32) + nt(ctx_ref[rows, :], wo)
        middle_ref[rows, :] = middle
        low = (middle * rms_scale(middle) * gain).astype(BF)
        ffn_ref[rows, :] = low
        ffnt_ref[:, rows] = low.T
        return carry

    lax.fori_loop(0, middle_ref.shape[0] // step, one, 0)


def transpose_rows(src_ref, dst_ref):
    step = 256

    def one(i, carry):
        rows = pl.ds(pl.multiple_of(i * step, step), step)
        dst_ref[:, rows] = src_ref[rows, :].T
        return carry

    lax.fori_loop(0, src_ref.shape[0] // step, one, 0)


def ffn_rows(i, half, w_in, w_back, first, ffn_ref, cot_ref, hid_ref, gp_ref, up_ref, down_ref):
    rows = pl.ds(pl.multiple_of(i * half, half), half)
    hidden, slope = gelu_pair(nn(ffn_ref[rows, :], w_in))
    hidden = hidden.astype(BF)
    hid_ref[rows, :] = hidden
    grad_pre = (nn(cot_ref[rows, :], w_back) * slope).astype(BF)
    gp_ref[rows, :] = grad_pre
    up = nt(hidden, w_back)
    down = nt(grad_pre, w_in)

    @pl.when(first)
    def _():
        up_ref[rows, :] = up
        down_ref[rows, :] = down

    @pl.when(jnp.logical_not(first))
    def _():
        up_ref[rows, :] += up
        down_ref[rows, :] += down


def after_rows(rows, cot, up_ref, down_ref, gain, gain_ref, gm_ref, ca_ref, cat_ref):
    middle = gm_ref[rows, :]
    scale = rms_scale(middle)
    normed = middle * scale
    down = down_ref[rows, :]
    gain_ref[...] += jnp.sum(down * normed, 0, keepdims=True)
    grad = cot + rms_back(down, normed, scale, gain)
    gm_ref[rows, :] = grad
    low = grad.astype(BF)
    ca_ref[rows, :] = low
    cat_ref[:, rows] = low.T
    return middle + up_ref[rows, :]


def context_grad(ca_ref, wo, go_ref):
    step = 256

    def one(i, carry):
        rows = pl.ds(pl.multiple_of(i * step, step), step)
        go_ref[rows, :] = nn(ca_ref[rows, :], wo).astype(BF)
        return carry

    lax.fori_loop(0, ca_ref.shape[0] // step, one, 0)


def k3_plain(
    xs_ref,
    ctx_ref,
    cot_ref,
    gain_ref,
    wo_ref,
    wi_ref,
    wb_ref,
    out_ref,
    gm_ref,
    go_ref,
    ggain_ref,
    gwo_ref,
    gwi_ref,
    gwb_ref,
    ffn_ref,
    ffnt_ref,
    cott_ref,
    cotb_ref,
    hid_ref,
    gp_ref,
    up_ref,
    down_ref,
):
    length = ctx_ref.shape[0]
    half_rows = length // 2
    chunk = hid_ref.shape[1]
    gain = gain_ref[...]
    cotb_ref[...] = cot_ref[...].astype(BF)
    k3_before(xs_ref, ctx_ref, wo_ref[...], gain, gm_ref, ffn_ref, ffnt_ref)
    transpose_rows(cotb_ref, cott_ref)

    def one_chunk(k, carry):
        cols = pl.ds(pl.multiple_of(k * chunk, LANES), chunk)
        w_in, w_back = wi_ref[:, cols], wb_ref[:, cols]
        for i in range(2):
            ffn_rows(
                i, half_rows, w_in, w_back, k == 0, ffn_ref, cotb_ref, hid_ref, gp_ref, up_ref, down_ref
            )
        gwb_ref[:, cols] = nn(cott_ref[...], hid_ref[...]).astype(BF)
        gwi_ref[:, cols] = nn(ffnt_ref[...], gp_ref[...]).astype(BF)
        return carry

    lax.fori_loop(0, wi_ref.shape[1] // chunk, one_chunk, 0)
    ggain_ref[...] = jnp.zeros_like(ggain_ref)
    step = 256

    def finish_rows(i, carry):
        rows = pl.ds(pl.multiple_of(i * step, step), step)
        out_ref[rows, :] = after_rows(
            rows,
            cot_ref[rows, :],
            up_ref,
            down_ref,
            gain,
            ggain_ref,
            gm_ref,
            ffn_ref,
            cott_ref,
        )
        return carry

    lax.fori_loop(0, length // step, finish_rows, 0)
    context_grad(ffn_ref, wo_ref[...], go_ref)
    gwo_ref[...] = nn(cott_ref[...], ctx_ref[...]).astype(BF)


def low_transposed(xs_ref, gain, lowt_ref):
    step = 256

    def one(i, carry):
        rows = pl.ds(pl.multiple_of(i * step, step), step)
        lowt_ref[:, rows] = project_rows(xs_ref[rows, :], gain).T
        return carry

    lax.fori_loop(0, xs_ref.shape[0] // step, one, 0)


def input_rows(rows, xs_ref, gm_ref, grads, weights, gain, gain_out):
    down = sum(nt(grad[rows, :], flat(weight[...])) for grad, weight in zip(grads, weights))
    inputs = xs_ref[rows, :].astype(F32)
    scale = rms_scale(inputs)
    normed = inputs * scale
    gain_out[...] += jnp.sum(down * normed, 0, keepdims=True)
    return gm_ref[rows, :] + rms_back(down, normed, scale, gain)


def k5_plain(
    xs_ref,
    gm_ref,
    dq_ref,
    dk_ref,
    dv_ref,
    wq_ref,
    wk_ref,
    wv_ref,
    gain_ref,
    ig_ref,
    gwq_ref,
    gwk_ref,
    gwv_ref,
    again_ref,
    lowt_ref,
):
    gain = gain_ref[...]
    low_transposed(xs_ref, gain, lowt_ref)
    grads, weights = (dq_ref, dk_ref, dv_ref), (wq_ref, wk_ref, wv_ref)
    for grad, out in zip(grads, (gwq_ref, gwk_ref, gwv_ref)):
        out[...] = nn(lowt_ref[...], grad[...]).astype(BF)
    again_ref[...] = jnp.zeros_like(again_ref)
    step = 256

    def one(i, carry):
        rows = pl.ds(pl.multiple_of(i * step, step), step)
        ig_ref[rows, :] = input_rows(rows, xs_ref, gm_ref, grads, weights, gain, again_ref)
        return carry

    lax.fori_loop(0, xs_ref.shape[0] // step, one, 0)


def as_row(vector):
    return vector.reshape(1, vector.shape[-1])


def turned_table(tab_ref, turn_ref):
    turn_ref[...] = jnp.zeros_like(turn_ref)
    turn_ref[: tab_ref.shape[0], : tab_ref.shape[1]] = tab_ref[...]
    return turn_ref[0:8, :]


def run_all(steps):
    for step in steps:
        step()


def at_step(index, plan):
    for number, steps in enumerate(plan):
        if steps:

            @pl.when(index == number)
            def _(steps=steps):
                run_all(steps)


def forward_fused(
    depth,
    here,
    x_in,
    cot_in,
    gain_in,
    ffn_gain_in,
    tab_ref,
    seg_ref,
    wq_shard,
    wk_shard,
    wv_shard,
    wo_shard,
    wi_shard,
    wb_shard,
    xs_out,
    tabs_ref,
    q_out,
    k_out,
    v_out,
    ctx_out,
    feat_out,
    wq_out,
    wk_out,
    wv_out,
    own_out,
    oth_out,
    gm_out,
    go_out,
    ggain_ref,
    gout_out,
    gwi_ref,
    gwb_ref,
    gi_out,
    gb_out,
    xs_ref,
    cotf_ref,
    cotb_ref,
    obuf_ref,
    q_ref,
    k_ref,
    v_ref,
    ctx_ref,
    feat_ref,
    wq_ref,
    wk_ref,
    wv_ref,
    wo_ref,
    wi_ref,
    wb_ref,
    low_ref,
    turn_ref,
    bias_ref,
    segq_ref,
    segk_ref,
    gm_ref,
    ffnt_ref,
    cott_ref,
    up_ref,
    down_ref,
    i0,
    i1,
    i2,
    i3,
    b0,
    b1,
    b2,
    b3,
    r_send,
    r_recv,
    g_send,
    g_recv,
    s_send,
    s_recv,
    x_send,
    x_recv,
    l_sem,
    c_sem,
):
    p = Place(depth)
    length = q_ref.shape[0]
    half_rows = length // 2
    width = wo_shard.shape[1]
    groups = wq_ref.shape[0]
    chunks, part = wi_ref.shape[0], wi_ref.shape[-1] // 2
    x_sems, g_sems, r_sems, s_sems = (
        (x_send, x_recv),
        (g_send, g_recv),
        (r_send, r_recv),
        (s_send, s_recv),
    )
    gain, ffn_gain = as_row(gain_in[...]), as_row(ffn_gain_in[...])
    weights = (wq_ref, wk_ref, wv_ref)
    x_own = local(x_in.at[p.t], xs_ref.at[p.t], l_sem.at[0])
    x_own.start()
    cot_load = local(cot_in.at[1 - p.t], cotf_ref, l_sem.at[1])
    cot_load.start()
    heads = []
    for j in range(groups):
        trio = []
        for i, (ref, shard) in enumerate(zip(weights, (wq_shard, wk_shard, wv_shard))):
            item = Gather(p, ref.at[j], LANES, r_sems, 3 * j + i, True)
            item.block(p.z, 0)[...] = shard[:, j * LANES : (j + 1) * LANES]
            trio.append(item)
        heads.append(trio)
    out_item = Gather(p, wo_ref, width, g_sems, 0, True)
    out_item.block(p.z, 0)[...] = wo_shard[...]
    items = []
    for k in range(chunks):
        pair = []
        for side, (ref, shard) in enumerate(((wi_ref, wi_shard), (wb_ref, wb_shard))):
            item = Gather(p, ref.at[k], part, g_sems, 1 + 2 * k + side, side == 0 or k < 2)
            item.block(p.z, 0)[...] = shard[:, k * part : (k + 1) * part]
            pair.append(item)
        items.append(pair)

    tabs_ref[p.t] = turned_table(tab_ref, turn_ref)
    p.barrier()
    moves = [
        remote(x_in.at[1 - p.t], xs_ref.at[p.t], x_sems, 0, p.xpeer),
        remote(tabs_ref.at[p.t], tabs_ref.at[p.t], x_sems, 1, p.xpeer),
        remote(obuf_ref, cotb_ref.at[p.t], x_sems, 2, p.xpeer),
    ]

    def head(j, name):
        return [getattr(item, name) for item in heads[j]]

    def both(items):
        return [functools.partial(item.step2, side) for side in range(2) for item in items]

    run_all(head(0, "start") + head(1, "start") + head(2, "start"))
    run_all([out_item.start])
    for item in items[0]:
        item.start()
    moves[1].start()
    moves[0].start()
    run_all(head(0, "start_z") + head(1, "start_z"))
    def chunk(k, *names):
        steps = []
        for name in names if k < chunks else ():
            if name == "both":
                steps += both(items[k])
            else:
                steps += [getattr(item, name) for item in items[k]]
        return steps

    def rows_of(half):
        return pl.ds(pl.multiple_of(half * half_rows, half_rows), half_rows)

    def project_group(j, half):
        rows = rows_of(half)
        for weight, out in zip(weights, (q_ref, k_ref, v_ref)):
            result = nn(low_ref[rows, :], flat(weight[j])).astype(BF)
            out[rows, pair_cols(j)] = result[:, :LANES]
            out[rows, pair_cols(j + groups)] = result[:, LANES:]

    run_all(head(0, "step1") + head(1, "step1") + head(2, "start_z"))
    x_own.wait()
    low_ref[rows_of(p.t), :] = project_rows(xs_ref[p.t], gain)
    run_all(both(heads[0]) + head(2, "step1"))
    cot_load.wait()
    obuf_ref[...] = cotf_ref[...].astype(BF)
    own_load = local(cot_in.at[p.t], cotf_ref, l_sem.at[1])
    own_load.start()
    run_all(both(heads[1]))
    moves[1].wait_recv()
    fwd_setup(seg_ref[p.t], tabs_ref, bias_ref, segq_ref, segk_ref)
    run_all(head(0, "step3") + [out_item.start_z, out_item.step1])
    run_all(both(heads[2]) + head(0, "finish"))
    project_group(0, p.t)
    run_all(chunk(0, "start_z", "step1"))
    moves[0].wait_recv()
    for k in range(1, chunks):
        run_all(chunk(k, "start"))
    moves[2].start()
    low_ref[rows_of(1 - p.t), :] = project_rows(xs_ref[1 - p.t], gain)
    project_group(0, 1 - p.t)

    def save(index, src, dst):
        return local(src, dst, l_sem.at[index])

    saves = [
        save(2 + i, src, dst)
        for i, (src, dst) in enumerate(
            (
                (xs_ref, xs_out),
                (wq_ref, wq_out),
                (wk_ref, wk_out),
                (wv_ref, wv_out),
                (ctx_ref, ctx_out),
                (feat_ref, feat_out),
                (obuf_ref, oth_out),
                (cotf_ref, own_out),
                (gm_ref, gm_out),
                (v_ref, go_out),
                (wo_ref, gout_out),
            )
        )
    ]
    qkv_saves = [
        save(13 + i, src, dst)
        for i, (src, dst) in enumerate(((q_ref, q_out), (k_ref, k_out), (v_ref, v_out)))
    ]

    plan = [
        head(1, "step3") + both([out_item]) + chunk(1, "start_z", "step1"),
        head(2, "step3") + chunk(0, "both"),
        head(1, "finish") + chunk(2, "start_z", "step1"),
        [out_item.step3] + chunk(1, "both"),
        head(2, "finish") + chunk(0, "step3") + chunk(3, "start_z", "step1") + chunk(2, "both"),
        [out_item.finish] + [one.start for one in qkv_saves + saves[:4]],
    ]

    def one_pair(index, carry):
        j, side = lax.div(index, 2), lax.rem(index, 2)
        at_step(index, plan)

        @pl.when((side == 0) & (j > 0))
        def _():
            def one(half, carry):
                project_group(j, half)
                return carry

            lax.fori_loop(0, 2, one, 0)

        pair = j + groups * side
        fwd_pair(pair, q_ref, k_ref, v_ref, ctx_ref, feat_ref, bias_ref, segq_ref, segk_ref)
        return carry

    lax.fori_loop(0, 2 * groups, one_pair, 0)
    saves[4].start()
    saves[5].start()
    run_all(chunk(1, "step3") + chunk(3, "both") + chunk(4, "start_z", "step1"))
    xs = xs_ref.reshape(length, xs_ref.shape[2])
    k3_before(xs, ctx_ref, flat(wo_ref[...]), ffn_gain, gm_ref, low_ref, ffnt_ref)
    run_all(chunk(0, "finish") + chunk(2, "step3"))
    moves[2].wait_recv()
    moves[2].wait_send()
    own_load.wait()
    cotb_ref[p.t] = cotf_ref[...].astype(BF)
    cotb = cotb_ref.reshape(length, cotb_ref.shape[2])
    transpose_rows(cotb, cott_ref)
    for one in qkv_saves:
        one.wait()
    hid_ref, gp_ref = q_ref.at[:, : 2 * part], k_ref.at[:, : 2 * part]

    def s_chunk(k):
        return (
            Scatter(
                p, wi_ref.at[k], part, [r.at[k] for r in (i0, i1, i2, i3)], s_sems, 2 * k, True
            ),
            Scatter(
                p, wb_ref.at[k], part, [r.at[k] for r in (b0, b1, b2, b3)], s_sems, 1 + 2 * k, False
            ),
        )

    def save_chunk(k):
        return (
            local(wi_ref.at[k], gi_out.at[k - here], c_sem.at[2 * k]),
            local(wb_ref.at[k], gb_out.at[k - here], c_sem.at[1 + 2 * k]),
        )

    def when_scatter(k, name):
        @pl.when((k >= 0) & (k < here))
        def _():
            for item, out in zip(s_chunk(k), (gwi_ref, gwb_ref)):
                if name == "finish":
                    item.finish(out, k * part)
                else:
                    getattr(item, name)()

    begin = [
        chunk(4, "both") + chunk(5, "start_z", "step1"),
        chunk(1, "finish") + chunk(5, "both") + chunk(4, "step3"),
        chunk(2, "finish") + chunk(5, "step3"),
    ]
    begin += [chunk(k, "finish") for k in range(3, chunks)]
    middle = [chunk(3, "step3")]

    def one_chunk(k, carry):
        at_step(k, begin)
        w_in, w_back = flat(wi_ref[k]), flat(wb_ref[k])
        args = (w_in, w_back, k == 0, low_ref, cotb, hid_ref, gp_ref, up_ref, down_ref)
        ffn_rows(0, half_rows, *args)
        when_scatter(k - 3, "step3")
        when_scatter(k - 2, "step2")
        when_scatter(k - 1, "step1")
        at_step(k, middle)
        ffn_rows(1, half_rows, *args)
        wb_ref[k] = nn(cott_ref[...], hid_ref[...]).astype(BF).reshape(wb_ref.shape[1:])
        when_scatter(k - 4, "finish")
        wi_ref[k] = nn(ffnt_ref[...], gp_ref[...]).astype(BF).reshape(wi_ref.shape[1:])
        when_scatter(k, "step0")

        @pl.when(k >= here)
        def _():
            for one in save_chunk(k):
                one.start()

        return carry

    lax.fori_loop(0, chunks, one_chunk, 0)
    ggain_ref[...] = jnp.zeros_like(ggain_ref)
    step = 256

    def finish_rows(own, i):
        half = p.t if own else 1 - p.t
        at = pl.ds(pl.multiple_of(i * step, step), step)
        rows = pl.ds(pl.multiple_of(half * half_rows + i * step, step), step)
        cot = cotf_ref[at, :] if own else cotb_ref[1 - p.t, at, :].astype(F32)
        out = after_rows(
            rows, cot, up_ref, down_ref, ffn_gain, ggain_ref, gm_ref, low_ref, cott_ref
        )
        if own:
            cotf_ref[at, :] = out
        else:
            obuf_ref[at, :] = out.astype(BF)

    for i in range(half_rows // step):
        finish_rows(False, i)
    saves[6].start()
    for stage, name in ((1, "step1"), (2, "step2"), (3, "step3")):
        for k in range(max(0, chunks - stage), here):
            when_scatter(k, name)
    for i in range(half_rows // step):
        finish_rows(True, i)
    saves[7].start()
    saves[8].start()
    context_grad(low_ref, flat(wo_ref[...]), v_ref)
    saves[9].start()
    wo_ref[...] = nn(cott_ref[...], ctx_ref[...]).astype(BF).reshape(wo_ref.shape)
    saves[10].start()
    for k in range(max(0, chunks - 4), here):
        when_scatter(k, "finish")
    for move in moves[:2]:
        move.wait_send()
    for one in saves:
        one.wait()
    for k in range(here, chunks):
        for one in save_chunk(k):
            one.wait()


def back_fused(
    depth,
    q_in,
    k_in,
    v_in,
    go_ref,
    ctx_ref,
    feat_ref,
    seg_ref,
    tabs_ref,
    xs_in,
    gm_in,
    wq_in,
    wk_in,
    wv_in,
    gain_in,
    ggain_ref,
    gi_in,
    gb_in,
    gout_in,
    oth_in,
    oth_out,
    igown_ref,
    ibuf2_ref,
    gwo_ref,
    gwq_ref,
    gwk_ref,
    gwv_ref,
    gwi_ref,
    gwb_ref,
    small_ref,
    q_ref,
    k_ref,
    v_ref,
    xs_ref,
    gm_ref,
    wq_ref,
    wk_ref,
    wv_ref,
    gi_ref,
    gb_ref,
    gout_ref,
    lowt_ref,
    sum_ref,
    gq_ref,
    gk_ref,
    gv_ref,
    ibuf_ref,
    again_ref,
    tabg_ref,
    sm_ref,
    smr_ref,
    bias_ref,
    sums_ref,
    far_ref,
    segk_ref,
    blockof_ref,
    gofeat_ref,
    near_ref,
    acc_ref,
    o0,
    o1,
    o2,
    o3,
    i0,
    i1,
    i2,
    i3,
    b0,
    b1,
    b2,
    b3,
    a0,
    a1,
    a2,
    a3,
    c0,
    c1,
    c2,
    c3,
    d0,
    d1,
    d2,
    d3,
    s_send,
    s_recv,
    x_send,
    x_recv,
    l_sem,
):
    p = Place(depth)
    length = q_ref.shape[0]
    half_rows = length // 2
    groups = gq_ref.shape[0]
    rest, part = gi_ref.shape[0], gi_ref.shape[-1] // 2
    s_sems, x_sems = (s_send, s_recv), (x_send, x_recv)
    pairs = [(q_in, q_ref), (k_in, k_ref), (v_in, v_ref), (xs_in, xs_ref)]
    pairs += [(gi_in, gi_ref), (gb_in, gb_ref), (gout_in, gout_ref), (gm_in, gm_ref)]
    pairs += [(wq_in, wq_ref), (wk_in, wk_ref), (wv_in, wv_ref)]
    loads = [local(src, dst, l_sem.at[i]) for i, (src, dst) in enumerate(pairs)]
    for one in loads:
        one.start()
    bwd_setup(seg_ref[p.t], tabs_ref, bias_ref, sums_ref, far_ref, segk_ref, blockof_ref)
    p.barrier()
    quarter = half_rows // 4
    out_moves = [
        remote(
            oth_in.at[pl.ds(i * quarter, quarter)],
            oth_out.at[pl.ds(i * quarter, quarter)],
            x_sems,
            depth + 6 + i,
            p.xpeer,
        )
        for i in range(4)
    ]
    out_item = Scatter(
        p, gout_ref, gwo_ref.shape[1], (o0, o1, o2, o3), s_sems, 2 * rest + 3 * groups, True
    )
    rest_items = []
    for k in range(rest):
        rest_items.append(
            [
                Scatter(
                    p, gi_ref.at[k], part, [r.at[k] for r in (i0, i1, i2, i3)], s_sems, 2 * k, True
                ),
                Scatter(
                    p,
                    gb_ref.at[k],
                    part,
                    [r.at[k] for r in (b0, b1, b2, b3)],
                    s_sems,
                    2 * k + 1,
                    True,
                ),
            ]
        )
    group_items = []
    for j in range(groups):
        group_items.append(
            [
                Scatter(
                    p,
                    ref.at[j],
                    LANES,
                    [r.at[j] for r in bufs],
                    s_sems,
                    2 * rest + 3 * j + i,
                    True,
                )
                for i, (ref, bufs) in enumerate(
                    (
                        (gq_ref, (a0, a1, a2, a3)),
                        (gk_ref, (c0, c1, c2, c3)),
                        (gv_ref, (d0, d1, d2, d3)),
                    )
                )
            ]
        )

    def chunk(k, name):
        if k >= rest:
            return []
        if name == "finish":
            return [
                functools.partial(item.finish, out, k * part)
                for item, out in zip(rest_items[k], (gwi_ref, gwb_ref))
            ]
        return [getattr(item, name) for item in rest_items[k]]

    def group(j, name):
        if name == "finish":
            return [
                functools.partial(item.finish, out, j * LANES)
                for item, out in zip(group_items[j], (gwq_ref, gwk_ref, gwv_ref))
            ]
        return [getattr(item, name) for item in group_items[j]]

    for one in loads[:7]:
        one.wait()
    run_all(chunk(0, "step0"))
    xs = xs_ref.reshape(length, xs_ref.shape[2])
    gain = as_row(gain_in[...])
    low_transposed(xs, gain, lowt_ref)
    run_all(chunk(0, "step1") + chunk(1, "step0"))
    for one in loads[7:]:
        one.wait()

    def group_cols(ref, j):
        return [ref[:, pair_cols(j)], ref[:, pair_cols(j + groups)]]

    def weight_grads(j):
        for target, grad in zip((gq_ref, gk_ref, gv_ref), (q_ref, k_ref, v_ref)):
            both = jnp.concatenate(group_cols(grad, j), 1)
            target[j] = nn(lowt_ref[...], both).astype(BF).reshape(target.shape[1:])

    def group_weights(j):
        pieces = []
        for weight in (wq_ref, wk_ref, wv_ref):
            pieces.append(flat(weight[j]))
        return jnp.concatenate(pieces, 1)

    def group_sum(rows, j):
        pieces = []
        for grad in (q_ref, k_ref, v_ref):
            for at in (j, j + groups):
                pieces.append(grad[rows, pair_cols(at)])
        return nt(jnp.concatenate(pieces, 1), group_weights(j))

    step = 256
    plan = [
        [out_moves[0].start],
        chunk(1, "step1") + [out_item.step0, out_moves[1].start],
        chunk(0, "step2") + [out_item.step1, out_moves[2].start],
        chunk(0, "step3") + chunk(1, "step2") + group(0, "step1") + [out_item.step2],
        chunk(0, "finish")
        + chunk(1, "step3")
        + group(0, "step2")
        + [out_item.step3, out_moves[3].start],
        chunk(1, "finish")
        + group(0, "step3")
        + group(1, "step1")
        + [functools.partial(out_item.finish, gwo_ref, 0)],
    ]

    def one_pair(index, carry):
        at_step(index, plan)
        j, side = lax.div(index, 2), lax.rem(index, 2)
        bwd_pair(
            j + groups * side,
            q_ref,
            k_ref,
            v_ref,
            go_ref,
            ctx_ref,
            feat_ref,
            q_ref,
            k_ref,
            v_ref,
            bias_ref,
            sums_ref,
            far_ref,
            segk_ref,
            blockof_ref,
            gofeat_ref,
            near_ref,
            acc_ref,
        )

        @pl.when((side == 1) & (j < groups - 1))
        def _():
            weight_grads(j)
            for i in range(groups - 1):

                @pl.when(j == i)
                def _():
                    run_all(group(i, "step0"))

            for i in range(groups - 1):

                @pl.when(j == i)
                def _():
                    for at in range(length // step):
                        rows = slice(at * step, (at + 1) * step)
                        if i == 0:
                            sum_ref[rows, :] = group_sum(rows, i)
                        else:
                            sum_ref[rows, :] += group_sum(rows, i)

        return carry

    lax.fori_loop(0, 2 * groups, one_pair, 0)
    again_ref[...] = jnp.zeros_like(again_ref)
    last = groups - 1

    def finish_rows(own, i):
        half = p.t if own else 1 - p.t
        at = pl.ds(pl.multiple_of(i * step, step), step)
        rows = pl.ds(pl.multiple_of(half * half_rows + i * step, step), step)
        down = sum_ref[rows, :] + group_sum(rows, last)
        inputs = xs_ref[half, at, :].astype(F32)
        scale = rms_scale(inputs)
        normed = inputs * scale
        again_ref[...] += jnp.sum(down * normed, 0, keepdims=True)
        out = gm_ref[rows, :] + rms_back(down, normed, scale, gain)
        if own:
            igown_ref[at, :] = out
        else:
            ibuf_ref[at, :] = out.astype(BF)

    def piece(i):
        size = half_rows // 4
        at = pl.ds(i * size, size)
        return remote(ibuf_ref.at[at], ibuf2_ref.at[at], x_sems, i, p.xpeer)

    moves = [piece(i) for i in range(4)]
    finish_rows(False, 0)
    moves[0].start()
    moves[1].start()
    weight_grads(last)
    run_all(group(last, "step0") + group(1, "step2"))
    finish_rows(False, 1)
    moves[2].start()
    run_all(group(last, "step1"))
    for i in range(half_rows // step):
        finish_rows(True, i)
    bwd_table(tabg_ref, sums_ref, far_ref)
    run_all(group(0, "finish") + group(last, "step2"))
    moves[3].start()
    model = again_ref.shape[1]
    sm_ref[0, 0:1, :model] = again_ref[...]
    sm_ref[0, 1:2, :model] = ggain_ref[...]
    sm_ref[0, 2:8, :model] = jnp.zeros((6, model), F32)
    sm_ref[0, :, model : model + LANES] = tabg_ref[0:8, :]
    sm_ref[0, :, model + LANES :] = tabg_ref[8:16, :]
    hops = [(p.sib,), (p.ypeer,), (p.xpeer,), tuple(p.zpeers)]
    slot = 0
    beside = [
        group(1, "step3"),
        group(last, "step3"),
        group(1, "finish"),
        [],
    ]
    for level, peers in enumerate(hops):
        hop = [
            remote(sm_ref.at[level], smr_ref.at[slot + i], x_sems, len(moves) + slot + i, peer)
            for i, peer in enumerate(peers)
        ]
        for one in hop:
            one.start()
        run_all(beside[level])
        total = sm_ref[level]
        for i, one in enumerate(hop):
            one.wait_recv()
            total = total + smr_ref[slot + i]
        slot += len(peers)
        if level + 1 < len(hops):
            sm_ref[level + 1] = total
        else:
            small_ref[...] = total
        for one in hop:
            one.wait_send()
    run_all(group(last, "finish"))
    for move in moves + out_moves:
        move.wait_recv()
        move.wait_send()


def collect(
    own_in,
    oth_ref,
    igown_in,
    igoth_ref,
    small_ref,
    gwi_a,
    gwi_b,
    gwb_a,
    gwb_b,
    gwo_in,
    gwq_in,
    gwk_in,
    gwv_in,
    out_ref,
    ig_ref,
    again_ref,
    ggain_ref,
    gwq_ref,
    gwk_ref,
    gwv_ref,
    gwo_ref,
    gwi_ref,
    gwb_ref,
    table_ref,
    wide_ref,
    turn_ref,
    sem,
):
    t = lax.axis_index("tensor")
    loads = [
        local(own_in, wide_ref.at[0], sem.at[0]),
        local(igown_in, wide_ref.at[1], sem.at[1]),
    ]
    for one in loads:
        one.start()
    copies = []
    for i, (src, dst) in enumerate(((oth_ref, out_ref), (igoth_ref, ig_ref))):
        wide_ref[2 + i] = src[...].astype(F32)
        copies.append(local(wide_ref.at[2 + i], dst.at[1 - t], sem.at[2 + i]))
        copies[-1].start()
    for i, dst in enumerate((out_ref, ig_ref)):
        loads[i].wait()
        copies.append(local(wide_ref.at[i], dst.at[t], sem.at[4 + i]))
        copies[-1].start()
    for src, dst in ((gwq_in, gwq_ref), (gwk_in, gwk_ref), (gwv_in, gwv_ref), (gwo_in, gwo_ref)):
        dst[...] = src[...]
    for first, second, dst in ((gwi_a, gwi_b, gwi_ref), (gwb_a, gwb_b, gwb_ref)):
        dst[:, : first.shape[1]] = first[...]
        dst[:, first.shape[1] :] = second[...]
    model = again_ref.shape[0]
    again_ref[...] = small_ref[0:1, :model].reshape(model)
    ggain_ref[...] = small_ref[1:2, :model].reshape(model)
    turn_ref[...] = jnp.zeros_like(turn_ref)
    first = small_ref[:, model : model + LANES]
    second = small_ref[:, model + LANES :]
    turn_ref[0:8, :] = jnp.where(t == 0, first, second)
    table_ref[...] = turn_ref[: table_ref.shape[0], : table_ref.shape[1]]
    for one in copies:
        one.wait()


def call(kernel, outs, scratch, args, name, collective=None, far=()):
    def spec(array):
        return pl.BlockSpec(memory_space=pl.ANY if array in far else pltpu.VMEM)

    if collective is None:
        params = pltpu.CompilerParams(vmem_limit_bytes=VMEM_BYTES)
    else:
        params = pltpu.CompilerParams(
            vmem_limit_bytes=VMEM_BYTES, collective_id=collective, has_side_effects=True
        )
    return pl.pallas_call(
        kernel,
        out_shape=[jax.ShapeDtypeStruct(shape, dtype) for shape, dtype in outs],
        in_specs=[spec(i) for i in range(len(args))],
        out_specs=[spec(len(args) + i) for i in range(len(outs))],
        scratch_shapes=scratch,
        compiler_params=params,
        name=name,
    )(*args)


def shards(
    inputs,
    segments,
    norm_attn,
    norm_ffn,
    w_query,
    w_key,
    w_value,
    w_out,
    w_in,
    w_back,
    rel_table,
    cotangent,
):
    dp, tensor = lax.axis_size("dp"), lax.axis_size("tensor")
    t = lax.axis_index("tensor")
    rows, width = w_query.shape
    hidden_part = w_in.shape[1]
    model = inputs.shape[2]
    length = segments.shape[2]
    half = inputs.shape[1]
    buckets, heads = rel_table.shape
    depth = dp // 4
    fused = rows % 16 == 0 and dp % 4 == 0 and depth >= 2
    full = (length, model)
    inner = (length, width * tensor)
    square = (depth, 2, 2, rows, 2 * width)
    part = 256
    chunks = hidden_part // part
    pairs = inner[1] // LANES
    dma = pltpu.SemaphoreType.DMA
    halves = (2, half, model)
    fwd_work = [pltpu.VMEM((16, 4 * LANES), F32)] + [pltpu.VMEM((length, LANES), BF)] * 2
    bwd_work = [
        pltpu.VMEM((16, 4 * LANES), F32),
        pltpu.VMEM((16, 4 * LANES), F32),
        pltpu.VMEM((16, LANES), F32),
        pltpu.VMEM((length, LANES), BF),
        pltpu.VMEM((length, LANES), BF),
        pltpu.VMEM((length, LANES), BF),
        pltpu.VMEM((2, LANES, 3 * LANES), F32),
        pltpu.VMEM((length, LANES), F32),
    ]
    ffn_work = [pltpu.VMEM(full, BF), pltpu.VMEM(full[::-1], BF), pltpu.VMEM(full[::-1], BF)]
    rest = [pltpu.VMEM((length, 2 * part), BF)] * 2 + [pltpu.VMEM(full, F32)] * 2
    if fused:
        here = chunks - chunks // 3
        block = (depth, 2, 2, rows, 2 * part)
        groups = pairs // 2
        narrow = (groups, depth, 2, 2, rows, 2 * LANES)
        (
            xs,
            tabs,
            queries,
            keys,
            values,
            ctx,
            feats,
            wq,
            wk,
            wv,
            own,
            oth,
            grad_middle,
            grad_context,
            ggain,
            gout,
            gwi_a,
            gwb_a,
            gi,
            gb,
        ) = call(
            functools.partial(forward_fused, depth, here),
            [
                (halves, BF),
                ((2, 8, LANES), F32),
                (inner, BF),
                (inner, BF),
                (inner, BF),
                (inner, BF),
                ((pairs, length, LANES), BF),
                (narrow, BF),
                (narrow, BF),
                (narrow, BF),
                ((half, model), F32),
                ((half, model), BF),
                (full, F32),
                (inner, BF),
                ((1, model), F32),
                (square, BF),
                ((rows, here * part), F32),
                ((rows, here * part), F32),
                ((chunks - here,) + block, BF),
                ((chunks - here,) + block, BF),
            ],
            [
                pltpu.VMEM(halves, BF),
                pltpu.VMEM((half, model), F32),
                pltpu.VMEM(halves, BF),
                pltpu.VMEM((half, model), BF),
            ]
            + [pltpu.VMEM(inner, BF)] * 4
            + [pltpu.VMEM((pairs, length, LANES), BF)]
            + [pltpu.VMEM(narrow, BF)] * 3
            + [pltpu.VMEM(square, BF)]
            + [pltpu.VMEM((chunks,) + block, BF)] * 2
            + [pltpu.VMEM(full, BF), pltpu.VMEM((LANES, LANES), F32)]
            + fwd_work
            + [pltpu.VMEM(full, F32)]
            + [pltpu.VMEM(full[::-1], BF)] * 2
            + [pltpu.VMEM(full, F32)] * 2
            + scatter_bufs(here, depth, rows, part, True)
            + scatter_bufs(here, depth, rows, part, False)
            + gather_sems(3 * groups, depth)
            + gather_sems(1 + 2 * chunks, depth)
            + scatter_sems(2 * here, depth)
            + [dma((3,)), dma((3,)), dma((16,)), dma((2 * chunks,))],
            (
                inputs,
                cotangent,
                norm_attn,
                norm_ffn,
                rel_table.T,
                segments,
                w_query,
                w_key,
                w_value,
                w_out,
                w_in,
                w_back,
            ),
            "forward_feed_forward",
            0,
            (0, 1, 12, 14, 15, 16, 17, 18, 19, 20, 21, 22, 23, 24, 25, 27, 30, 31),
        )
        left = chunks - here
        oth, igown, igoth, gwo, gwq, gwk, gwv, gwi_b, gwb_b, small = call(
            functools.partial(back_fused, depth),
            [
                ((half, model), BF),
                ((half, model), F32),
                ((half, model), BF),
                ((rows, width), F32),
                ((rows, width), F32),
                ((rows, width), F32),
                ((rows, width), F32),
                ((rows, left * part), F32),
                ((rows, left * part), F32),
                ((8, model + 2 * LANES), F32),
            ],
            [pltpu.VMEM(inner, BF)] * 3
            + [pltpu.VMEM(halves, BF), pltpu.VMEM(full, F32)]
            + [pltpu.VMEM(narrow, BF)] * 3
            + [pltpu.VMEM((left,) + block, BF)] * 2
            + [pltpu.VMEM(square, BF)]
            + [pltpu.VMEM(full[::-1], BF), pltpu.VMEM(full, F32)]
            + [pltpu.VMEM(narrow, BF)] * 3
            + [pltpu.VMEM((half, model), BF)]
            + [
                pltpu.VMEM((1, model), F32),
                pltpu.VMEM((16, LANES), F32),
                pltpu.VMEM((4, 8, model + 2 * LANES), F32),
                pltpu.VMEM((depth + 2, 8, model + 2 * LANES), F32),
            ]
            + bwd_work
            + scatter_bufs(None, depth, rows, width, True)
            + scatter_bufs(left, depth, rows, part, True)
            + scatter_bufs(left, depth, rows, part, True)
            + scatter_bufs(groups, depth, rows, LANES, True)
            + scatter_bufs(groups, depth, rows, LANES, True)
            + scatter_bufs(groups, depth, rows, LANES, True)
            + scatter_sems(1 + 2 * left + 3 * groups, depth)
            + [dma((depth + 10,)), dma((depth + 10,)), dma((11,))],
            (
                queries,
                keys,
                values,
                grad_context,
                ctx,
                feats,
                segments,
                tabs,
                xs,
                grad_middle,
                wq,
                wk,
                wv,
                norm_attn,
                ggain,
                gi,
                gb,
                gout,
                oth,
            ),
            "attention_backward",
            1,
            (0, 1, 2, 8, 9, 10, 11, 12, 15, 16, 17, 18, 19),
        )
        results = call(
            collect,
            [
                (halves, F32),
                (halves, F32),
                ((model,), F32),
                ((model,), F32),
                ((rows, width), F32),
                ((rows, width), F32),
                ((rows, width), F32),
                ((rows, width), F32),
                ((rows, hidden_part), F32),
                ((rows, hidden_part), F32),
                ((heads, buckets), F32),
            ],
            [pltpu.VMEM((4, half, model), F32), pltpu.VMEM((LANES, LANES), F32), dma((6,))],
            (own, oth, igown, igoth, small, gwi_a, gwi_b, gwb_a, gwb_b, gwo, gwq, gwk, gwv),
            "collect",
            None,
            (0, 2, 13, 14),
        )
        return tuple(results[:-1]) + (results[-1].T,)
    else:
        gain_attn, gain_ffn = norm_attn.reshape(1, model), norm_ffn.reshape(1, model)
        table = jnp.pad(rel_table.T, ((0, 8 - heads), (0, LANES - buckets)))
        segment = lax.dynamic_index_in_dim(segments, t, 0, False)

        def whole(weight):
            weight = lax.all_gather(weight, "dp", axis=0, tiled=True)
            return lax.all_gather(weight, "tensor", axis=1, tiled=True)

        def exchanged(local_part):
            own = lax.dynamic_index_in_dim(local_part, t, 0, False)
            other = lax.dynamic_index_in_dim(local_part, 1 - t, 0, False)
            other = lax.ppermute(other, "tensor", [(0, 1), (1, 0)])
            first = jnp.where(t == 0, own, other)
            second = jnp.where(t == 0, other, own)
            return jnp.concatenate([first, second], 0)

        def returned(seq):
            mine = lax.dynamic_slice_in_dim(seq, t * half, half, 0)
            other = lax.dynamic_slice_in_dim(seq, (1 - t) * half, half, 0)
            other = lax.ppermute(other, "tensor", [(0, 1), (1, 0)])
            return jnp.stack([jnp.where(t == 0, mine, other), jnp.where(t == 0, other, mine)])

        def scattered(grad):
            grad = lax.psum_scatter(grad.astype(F32), "tensor", scatter_dimension=1, tiled=True)
            return lax.psum_scatter(grad, "dp", scatter_dimension=0, tiled=True)

        xs = exchanged(inputs)
        tabs = lax.all_gather(table, "tensor", axis=0)
        wq, wk, wv, wo, wi, wb = (
            whole(w) for w in (w_query, w_key, w_value, w_out, w_in, w_back)
        )
        queries, keys, values = call(
            k1_plain,
            [(inner, BF)] * 3,
            [pltpu.VMEM(full, BF)],
            (xs, gain_attn, wq, wk, wv),
            "project",
        )
        ctx, feats = call(
            fwd_kernel,
            [(inner, BF), ((pairs, length, LANES), BF)],
            fwd_work,
            (queries, keys, values, segment, tabs),
            "attention_forward",
        )
        out_seq, grad_middle, grad_context, ggain, gwo, gwi, gwb = call(
            k3_plain,
            [
                (full, F32),
                (full, F32),
                (inner, BF),
                ((1, model), F32),
                (wo.shape, BF),
                (wi.shape, BF),
                (wb.shape, BF),
            ],
            ffn_work + [pltpu.VMEM(full, BF)] + rest,
            (xs, ctx, exchanged(cotangent), gain_ffn, wo, wi, wb),
            "feed_forward",
        )
        output = returned(out_seq)
        gwo, gwi, gwb = scattered(gwo), scattered(gwi), scattered(gwb)
        dq, dk, dv, table_grad = call(
            bwd_kernel,
            [(inner, BF), (inner, BF), (inner, BF), ((16, LANES), F32)],
            bwd_work,
            (queries, keys, values, grad_context, ctx, feats, segment, tabs),
            "attention_backward",
        )
        ig_seq, gwq, gwk, gwv, again = call(
            k5_plain,
            [(full, F32), (wq.shape, BF), (wk.shape, BF), (wv.shape, BF), ((1, model), F32)],
            [pltpu.VMEM((model, length), BF)],
            (xs, grad_middle, dq, dk, dv, wq, wk, wv, gain_attn),
            "projection_gradients",
        )
        input_grad = returned(ig_seq)
        gwq, gwk, gwv = scattered(gwq), scattered(gwk), scattered(gwv)
        again, ggain, tables = lax.psum((again, ggain, table_grad), ("dp", "tensor"))
        gain_attn_grad, gain_ffn_grad = again[0], ggain[0]
        tables = tables.reshape(2, 8, LANES)
    table_out = lax.dynamic_index_in_dim(tables, t, 0, False)[:heads, :buckets].T
    return (
        output,
        input_grad,
        gain_attn_grad,
        gain_ffn_grad,
        gwq,
        gwk,
        gwv,
        gwo,
        gwi,
        gwb,
        table_out,
    )


def solution(mesh):
    weight = P("dp", "tensor")
    tokens = P(None, ("dp", "tensor"), None)
    return jax.shard_map(
        shards,
        mesh=mesh,
        in_specs=(
            tokens,
            P(None, "dp", None),
            P(),
            P(),
            weight,
            weight,
            weight,
            weight,
            weight,
            weight,
            P(None, "tensor"),
            tokens,
        ),
        out_specs=(
            tokens,
            tokens,
            P(),
            P(),
            weight,
            weight,
            weight,
            weight,
            weight,
            weight,
            P(None, "tensor"),
        ),
        check_vma=False,
    )
```
